32 devices in a mesh: seq: 4 (over y, x), fsdp: 8 (over z, core).
Axes of the slice: x: 2, y: 2, z: 4, core: 2. Of those that a mesh axis runs over, the one named last changes fastest.
Arguments:
- latents: bfloat16 [8, 1024, 1408], P('fsdp', 'seq'), may hold values from -6 to 6
- skip_input: bfloat16 [8, 1024, 1408], P('fsdp', 'seq'), may hold values from -6 to 6
- text_tokens: bfloat16 [8, 333, 1024], P('fsdp'), may hold values from -6 to 6
- text_lengths: int32 [8], P('fsdp'), may hold values from 83 to 333, as said below
- condition: bfloat16 [8, 1408], P('fsdp'), may hold values from -6 to 6
- cotangent: bfloat16 [8, 1024, 1408], P('fsdp', 'seq'), may hold values from -6 to 6
- mod_weight: bfloat16 [2, 1408, 1408], P(None, 'fsdp'), may hold values from -0.15625 to 0.15625
- norm_gains: bfloat16 [2, 3, 1408], P(None, None, 'fsdp'), may hold values from 0.5 to 1.5
- qkv_weight: bfloat16 [2, 1408, 4224], P(None, 'fsdp'), may hold values from -0.15625 to 0.15625
- query_weight: bfloat16 [2, 1408, 1408], P(None, 'fsdp'), may hold values from -0.15625 to 0.15625
- text_kv_weight: bfloat16 [2, 1024, 2816], P(None, 'fsdp'), may hold values from -0.1875 to 0.1875
- self_out_weight: bfloat16 [2, 1408, 1408], P(None, 'fsdp'), may hold values from -3 to 3
- cross_out_weight: bfloat16 [2, 1408, 1408], P(None, 'fsdp'), may hold values from -1.25 to 1.25
- up_weight: bfloat16 [2, 1408, 6144], P(None, 'fsdp'), may hold values from -0.15625 to 0.15625
- down_weight: bfloat16 [2, 6144, 1408], P(None, 'fsdp'), may hold values from -0.078125 to 0.078125
- skip_gain: bfloat16 [2816], P('fsdp'), may hold values from 0.5 to 1.5
- skip_weight: bfloat16 [2816, 1408], P('fsdp'), may hold values from -0.109375 to 0.109375
Outputs:
- output: bfloat16 [8, 1024, 1408], P('fsdp', 'seq')
- grad_latents: float32 [8, 1024, 1408], P('fsdp', 'seq')
- grad_skip: float32 [8, 1024, 1408], P('fsdp', 'seq')
- grad_text: float32 [8, 333, 1024], P('fsdp')
- grad_condition: float32 [8, 1408], P('fsdp')
- grad_mod_weight: float32 [2, 1408, 1408], P(None, 'fsdp')
- grad_norm_gains: float32 [2, 3, 1408], P(None, None, 'fsdp')
- grad_qkv_weight: float32 [2, 1408, 4224], P(None, 'fsdp')
- grad_query_weight: float32 [2, 1408, 1408], P(None, 'fsdp')
- grad_text_kv_weight: float32 [2, 1024, 2816], P(None, 'fsdp')
- grad_self_out_weight: float32 [2, 1408, 1408], P(None, 'fsdp')
- grad_cross_out_weight: float32 [2, 1408, 1408], P(None, 'fsdp')
- grad_up_weight: float32 [2, 1408, 6144], P(None, 'fsdp')
- grad_down_weight: float32 [2, 6144, 1408], P(None, 'fsdp')
- grad_skip_gain: float32 [2816], P('fsdp')
- grad_skip_weight: float32 [2816, 1408], P('fsdp')
The draws below stay inside these ranges and needn't reach their ends.
Inputs may be any that keep to these rules, and one draw needn't show every extreme that they name: `text_lengths`: some latent's text has all 333 tokens.
All inputs are finite; a program needn't handle non-finite values.
Results may differ from the reference program's by a relative error of at most 0.022.
Values may be sent and summed in bfloat16 or wider, within the bound.
No kernel may reach another device: no remote copies, remote signals or barrier semaphores. Data moves between devices by JAX's collectives and lax.ppermute only.
A program may use at most 576 MiB of HBM per device.

```python
import math
import jax
import jax.numpy as jnp
from jax import lax

D = 1408
H = 16
FF = 6144
TXTD = 1024
TXT = 333
LAT_TOK = 1024
LATENTS = 8


def draw_text_lengths(key, part):
    key = jax.random.fold_in(key, 11)
    first_key, second_key = jax.random.split(key)
    drawn = jax.random.randint(first_key, (LATENTS,), TXT // 4, TXT + 1)
    chosen = jax.random.randint(second_key, (), 0, LATENTS)
    return jnp.where(jnp.arange(LATENTS) == chosen, TXT, drawn).astype(jnp.int32)


def levels(rng, extent, cuts, low, largest):
    factor_of, own = 1.0, jax.random.fold_in(rng, 6)
    for position, blocks in cuts:
        draws = jnp.exp(jax.random.uniform(jax.random.fold_in(own, position), (blocks,), jnp.float32, low / len(cuts), largest / len(cuts)))
        factor_of = factor_of * jnp.repeat(draws, extent[position] // blocks).reshape([-1 if axis == position else 1 for axis in range(len(extent))])
    return factor_of


def scatter_about(key, shape, scale, bound, cuts=(), held_as=jnp.bfloat16):
    factor_of = levels(key, shape, cuts, -0.22, 0.18) if cuts else 1.0
    array = jax.random.normal(key, shape, jnp.float32) * scale * factor_of
    return jnp.minimum(jnp.maximum(array, -bound), bound).astype(held_as)


def setup_inputs(seed: int = 0) -> dict:
    key_list = jax.random.split(jax.random.key(seed), 18)
    return {
        "latents": scatter_about(key_list[0], (LATENTS, LAT_TOK, D), 1.0, 6.0, ((0, 8), (1, 4))),
        "skip_input": scatter_about(key_list[1], (LATENTS, LAT_TOK, D), 1.0, 6.0, ((0, 8), (1, 4))),
        "text_tokens": scatter_about(key_list[2], (LATENTS, TXT, TXTD), 1.0, 6.0, ((0, 8),)),
        "text_lengths": draw_text_lengths(jax.random.fold_in(key_list[17], 71), 0),
        "condition": scatter_about(key_list[4], (LATENTS, D), 1.0, 6.0, ((0, 8),)),
        "cotangent": scatter_about(key_list[5], (LATENTS, LAT_TOK, D), 1.0, 6.0, ((0, 8), (1, 4))),
        "mod_weight": scatter_about(key_list[6], (2, D, D), D ** -0.5, 0.15625, ((1, 8),)),
        "norm_gains": jnp.clip(1.0 + 0.1 * jax.random.normal(key_list[7], (2, 3, D), jnp.float32), 0.5, 1.5).astype(jnp.bfloat16),
        "qkv_weight": scatter_about(key_list[8], (2, D, 3 * D), D ** -0.5, 0.15625, ((1, 8),)),
        "query_weight": scatter_about(key_list[9], (2, D, D), D ** -0.5, 0.15625, ((1, 8),)),
        "text_kv_weight": scatter_about(key_list[10], (2, TXTD, 2 * D), TXTD ** -0.5, 0.1875, ((1, 8),)),
        "self_out_weight": scatter_about(key_list[11], (2, D, D), (max(3 * D // LAT_TOK, 1)) ** -0.5, 3.0, ((1, 8),)),
        "cross_out_weight": scatter_about(key_list[12], (2, D, D), (max(D // 64, 1)) ** -0.5, 1.25, ((1, 8),)),
        "up_weight": scatter_about(key_list[13], (2, D, FF), D ** -0.5, 0.15625, ((1, 8),)),
        "down_weight": scatter_about(key_list[14], (2, FF, D), FF ** -0.5, 0.078125, ((1, 8),)),
        "skip_gain": jnp.clip(1.0 + 0.1 * jax.random.normal(key_list[15], (2 * D,), jnp.float32), 0.5, 1.5).astype(jnp.bfloat16),
        "skip_weight": scatter_about(key_list[16], (2 * D, D), (2 * D) ** -0.5, 0.109375, ((0, 8),)),
    }


NORM_EPSILON = 1e-06
EXACT = lax.Precision.HIGHEST

@jax.custom_vjp
def low(v):
    return lax.optimization_barrier(v.astype(jnp.bfloat16)).astype(jnp.float32)

@jax.custom_vjp
def low_back(v):
    return v

def low_keep(v):
    return (low(v), None)

def low_pass(kept, grad):
    return (grad,)

def back_keep(v):
    return (v, None)

def back_low(kept, grad):
    return (low(grad),)
low.defvjp(low_keep, low_pass)
low_back.defvjp(back_keep, back_low)

def layer_norm(values, gain_vec):
    row_mean = lax.optimization_barrier(jnp.mean(values, axis=-1, keepdims=True))
    centered = values - row_mean
    row_var = lax.optimization_barrier(jnp.mean(centered * centered, axis=-1, keepdims=True))
    return centered * lax.rsqrt(row_var + NORM_EPSILON) * gain_vec

def product(left_in, right_in):
    return jnp.dot(left_in, right_in, precision=EXACT)

def attention(queries, key_rows, values, key_validity_mask):
    score_scale = 1.0 / math.sqrt(queries.shape[-1])
    scores = low_back(score_scale * jnp.einsum('qhd,khd->hqk', queries, key_rows, precision=EXACT))
    if key_validity_mask is not None:
        scores = jnp.where(key_validity_mask[None, None, :], scores, -1e+30)
    weights = low(jax.nn.softmax(scores, axis=-1))
    return jnp.einsum('hqk,khd->qhd', weights, values, precision=EXACT)

def diffusion_transformer_block(hidden_state, condition_vector_row, caption_token_row, key_validity_mask, block_parameters):
    mod_matrix, gain_rows, qkv_matrix, query_matrix, kv_matrix, self_matrix, cross_matrix, up_matrix, down_matrix = block_parameters
    tok_count, model_width = hidden_state.shape
    head_size = model_width // H
    shift_vec = product(jax.nn.silu(condition_vector_row), mod_matrix)
    first_norm = low(layer_norm(hidden_state, gain_rows[0]) + shift_vec)
    triples = low(low_back(product(first_norm, qkv_matrix))).reshape(tok_count, 3, H, head_size)
    attended = low(low_back(attention(triples[:, 0], triples[:, 1], triples[:, 2], None)))
    hidden_state = hidden_state + low_back(product(attended.reshape(tok_count, model_width), self_matrix))
    cross_norm = low(layer_norm(hidden_state, gain_rows[1]))
    queries = low(low_back(product(cross_norm, query_matrix))).reshape(tok_count, H, head_size)
    text_pairs = low(low_back(product(caption_token_row, kv_matrix))).reshape(caption_token_row.shape[0], 2, H, head_size)
    attended = low(low_back(attention(queries, text_pairs[:, 0], text_pairs[:, 1], key_validity_mask)))
    hidden_state = hidden_state + low_back(product(attended.reshape(tok_count, model_width), cross_matrix))
    mlp_norm = low(layer_norm(hidden_state, gain_rows[2]))
    up_rows = low_back(product(mlp_norm, up_matrix))
    activated = low(jax.nn.gelu(up_rows, approximate=True))
    return hidden_state + low_back(product(activated, down_matrix))

def two_layers(latent_tokens_in, skip_row, caption_token_row, condition_vector_row, all_weights, key_validity_mask):
    leading_layer = tuple((weight[0] for weight in all_weights[:9]))
    trailing_layer = tuple((weight[1] for weight in all_weights[:9]))
    hidden_state = diffusion_transformer_block(latent_tokens_in, condition_vector_row, caption_token_row, key_validity_mask, leading_layer)
    joined = low(layer_norm(jnp.concatenate([hidden_state, skip_row], axis=-1), all_weights[9]))
    hidden_state = low_back(product(joined, all_weights[10]))
    return diffusion_transformer_block(hidden_state, condition_vector_row, caption_token_row, key_validity_mask, trailing_layer)

def reference(latents, skip_input, text_tokens, text_lengths, condition, cotangent, mod_weight, norm_gains, qkv_weight, query_weight, text_kv_weight, self_out_weight, cross_out_weight, up_weight, down_weight, skip_gain, skip_weight):
    all_weights = tuple((weight.astype(jnp.float32) for weight in (mod_weight, norm_gains, qkv_weight, query_weight, text_kv_weight, self_out_weight, cross_out_weight, up_weight, down_weight, skip_gain, skip_weight)))

    def per_latent(totals, items):
        latent_tokens_in, skip_row, caption_token_row, length, condition_vector_row, cot_row = items
        key_validity_mask = jnp.arange(TXT) < length

        def forward(latent_in, skip_in, text_in, cond_in, weights_in):
            return two_layers(latent_in, skip_in, text_in, cond_in, weights_in, key_validity_mask)
        result, pullback = jax.vjp(forward, latent_tokens_in, skip_row, caption_token_row, condition_vector_row, all_weights)
        grad_latent, grad_skip_row, grad_text_row, grad_cond_row, grad_weights = pullback(cot_row)
        totals = jax.tree.map(jnp.add, totals, grad_weights)
        return (totals, (result.astype(jnp.bfloat16), grad_latent, grad_skip_row, grad_text_row, grad_cond_row))
    zero_totals = jax.tree.map(jnp.zeros_like, all_weights)
    scanned = (latents.astype(jnp.float32), skip_input.astype(jnp.float32), text_tokens.astype(jnp.float32), text_lengths, condition.astype(jnp.float32), cotangent.astype(jnp.float32))
    totals, per_rows = lax.scan(per_latent, zero_totals, scanned)
    output, grad_latents, grad_skip, grad_text, grad_condition = per_rows
    return (output, grad_latents, grad_skip, grad_text, grad_condition, totals[0], totals[1], totals[2], totals[3], totals[4], totals[5], totals[6], totals[7], totals[8], totals[9], totals[10])
```

```python
import math

import jax
import jax.numpy as jnp
from jax import lax
from jax.sharding import PartitionSpec as P

H = 16

NORM_EPSILON = 1e-06
EXACT = lax.Precision.HIGHEST
BF16 = jnp.bfloat16
F32 = jnp.float32


def layer_norm(values, gain_vec):
    row_mean = jnp.mean(values, axis=-1, keepdims=True)
    centered = values - row_mean
    row_var = jnp.mean(centered * centered, axis=-1, keepdims=True)
    return centered * lax.rsqrt(row_var + NORM_EPSILON) * gain_vec


def norm_shift(values, gain_vec, shift_vec):
    return layer_norm(values, gain_vec) + shift_vec


def gelu_tanh(values):
    return jax.nn.gelu(values, approximate=True)


def product(left_in, right_in):
    return jnp.dot(left_in, right_in, preferred_element_type=F32)


def product_tn(left_in, right_in):
    return lax.dot_general(
        left_in, right_in, (((0,), (0,)), ((), ())), preferred_element_type=F32
    )


def product_nt(left_in, right_in):
    return lax.dot_general(
        left_in, right_in, (((1,), (1,)), ((), ())), preferred_element_type=F32
    )


def masked_scores(queries, key_rows, key_mask, score_scale):
    scores = (
        jnp.einsum("qhd,khd->hqk", queries, key_rows, preferred_element_type=F32) * score_scale
    )
    if key_mask is None:
        return scores
    return jnp.where(key_mask[None, None, :], scores, -1e30)


def attend_forward(queries, key_rows, values, key_mask, score_scale):
    scores = masked_scores(queries, key_rows, key_mask, score_scale)
    top_score = jnp.max(scores, axis=-1, keepdims=True)
    exponent = jnp.exp(scores - top_score)
    row_total = jnp.sum(exponent, axis=-1, keepdims=True)
    weights = (exponent / row_total).astype(BF16)
    attended = jnp.einsum("hqk,khd->qhd", weights, values, preferred_element_type=F32)
    return (attended.astype(BF16), (top_score + jnp.log(row_total))[..., 0])


def attend_backward(queries, key_rows, values, key_mask, grad_mixed, log_total, score_scale):
    scores = masked_scores(queries, key_rows, key_mask, score_scale)
    probability = jnp.exp(scores - log_total[..., None])
    weights = probability.astype(BF16)
    grad_values = jnp.einsum("hqk,qhd->khd", weights, grad_mixed, preferred_element_type=F32)
    grad_probs = jnp.einsum("qhd,khd->hqk", grad_mixed, values, preferred_element_type=F32)
    row_delta = jnp.sum(grad_probs * probability, axis=-1, keepdims=True)
    grad_scores = (probability * (grad_probs - row_delta)).astype(BF16)
    grad_queries = (
        jnp.einsum("hqk,khd->qhd", grad_scores, key_rows, preferred_element_type=F32) * score_scale
    )
    grad_keys = (
        jnp.einsum("hqk,qhd->khd", grad_scores, queries, preferred_element_type=F32) * score_scale
    )
    return (grad_queries.astype(BF16), grad_keys.astype(BF16), grad_values.astype(BF16))


def swap_seq(block, bits):
    seq_count = lax.axis_size("seq")
    return lax.ppermute(block, "seq", [(i, i ^ bits) for i in range(seq_count)])


def swap_core(block):
    fsdp_count = lax.axis_size("fsdp")
    return lax.ppermute(block, "fsdp", [(i, i ^ 1) for i in range(fsdp_count)])


def swap_by_core(block, even_bits, odd_bits):
    seq_count, fsdp_count = lax.axis_size("seq"), lax.axis_size("fsdp")
    pairs = []
    for s in range(seq_count):
        for f in range(fsdp_count):
            other = s ^ (odd_bits if f % 2 else even_bits)
            pairs.append((s * fsdp_count + f, other * fsdp_count + f))
    return lax.ppermute(block, ("seq", "fsdp"), pairs)


def gather_rel(block):
    seq_count = lax.axis_size("seq")
    if seq_count != 4:
        return [block] + [swap_seq(block, j) for j in range(1, seq_count)]
    half = block.shape[0] // 2
    from_x, from_y = swap_seq(block, 1), swap_seq(block, 2)
    corner = jnp.concatenate([swap_seq(from_y[:half], 1), swap_seq(from_x[half:], 2)], axis=0)
    return [block, from_x, from_y, corner]


def scatter_rel(blocks):
    seq_count = lax.axis_size("seq")
    if seq_count != 4:
        total = blocks[0].astype(F32)
        for j in range(1, seq_count):
            total = total + swap_seq(blocks[j].astype(BF16), j).astype(F32)
        return total
    half = blocks[0].shape[0] // 2
    corner = blocks[3].astype(BF16)
    by_x, by_y = swap_seq(corner[:half], 1), swap_seq(corner[half:], 2)
    to_y = jnp.concatenate(
        [(blocks[2][:half].astype(F32) + by_x.astype(F32)).astype(BF16), blocks[2][half:].astype(BF16)]
    )
    to_x = jnp.concatenate(
        [blocks[1][:half].astype(BF16), (blocks[1][half:].astype(F32) + by_y.astype(F32)).astype(BF16)]
    )
    return blocks[0].astype(F32) + swap_seq(to_x, 1).astype(F32) + swap_seq(to_y, 2).astype(F32)


def exchange_rel(blocks):
    return [blocks[0]] + [swap_seq(blocks[j], j) for j in range(1, len(blocks))]


def list_order():
    s, seq_count = lax.axis_index("seq"), lax.axis_size("seq")
    if seq_count != 4:
        return [s ^ j for j in range(seq_count)]
    odd = lax.axis_index("fsdp") % 2
    return [s, s ^ (1 + odd), s ^ (2 - odd), s ^ 3]


def spread(block):
    seq_count = lax.axis_size("seq")
    if seq_count != 4:
        return [block] + [swap_seq(block, j) for j in range(1, seq_count)]
    odd = lax.axis_index("fsdp") % 2
    half = block.shape[0] // 2
    first = swap_by_core(block, 1, 2)
    part = swap_by_core(lax.dynamic_slice_in_dim(first, odd * half, half, 0), 2, 1)
    second, other_part = swap_core(first), swap_core(part)
    corner = jnp.where(
        odd == 0,
        jnp.concatenate([part, other_part], axis=0),
        jnp.concatenate([other_part, part], axis=0),
    )
    return [block, first, second, corner]


def add_bf16(left_in, right_in):
    return (left_in.astype(F32) + right_in.astype(F32)).astype(BF16)


def unspread(blocks):
    seq_count = lax.axis_size("seq")
    if seq_count != 4:
        return scatter_rel(blocks).astype(BF16)
    odd = lax.axis_index("fsdp") % 2
    half = blocks[0].shape[0] // 2
    to_send = add_bf16(blocks[1], swap_core(blocks[2].astype(BF16)))
    corner = blocks[3].astype(BF16)
    mine = lax.dynamic_slice_in_dim(corner, odd * half, half, 0)
    others = lax.dynamic_slice_in_dim(corner, (1 - odd) * half, half, 0)
    passed = swap_by_core(add_bf16(mine, swap_core(others)), 2, 1)
    part = lax.dynamic_slice_in_dim(to_send, odd * half, half, 0)
    to_send = lax.dynamic_update_slice_in_dim(to_send, add_bf16(part, passed), odd * half, 0)
    return add_bf16(blocks[0], swap_by_core(to_send, 1, 2))


def place(blocks, order):
    seq_count = lax.axis_size("seq")
    stacked = jnp.stack(blocks)
    inverse = sum(
        (jnp.arange(seq_count) == order[i]).astype(jnp.int32) * i for i in range(seq_count)
    )
    picked = [lax.dynamic_index_in_dim(stacked, inverse[a], 0, False) for a in range(seq_count)]
    return jnp.concatenate(picked, axis=-1)


def split(rows, order):
    seq_count = lax.axis_size("seq")
    width = rows.shape[-1] // seq_count
    stacked = jnp.stack([rows[:, a * width : (a + 1) * width] for a in range(seq_count)])
    return [lax.dynamic_index_in_dim(stacked, order[i], 0, False) for i in range(seq_count)]


def own_part(matrix, groups):
    s, seq_count = lax.axis_index("seq"), lax.axis_size("seq")
    width = matrix.shape[1] // (groups * seq_count)
    parts = [
        lax.dynamic_slice_in_dim(matrix, (g * seq_count + s) * width, width, 1)
        for g in range(groups)
    ]
    return jnp.concatenate(parts, axis=1)


def gather_fsdp(shard):
    return lax.all_gather(shard, "fsdp", axis=0, tiled=True)


def scatter_fsdp(full):
    return lax.psum_scatter(full.astype(BF16), "fsdp", scatter_dimension=0, tiled=True)


def weighted_nt(parts, matrices):
    total = product_nt(parts[0], matrices[0])
    for part, matrix in zip(parts[1:], matrices[1:]):
        total = total + product_nt(part, matrix)
    return total


def layer_forward(hidden, shift_vec, gain_rows, text_rows, key_mask, weights, score_scale):
    qkv_part, square_parts, kv_part, up_part, down_part = weights
    seq_count = lax.axis_size("seq")
    tok_rows, model_width = hidden.shape
    width = model_width // seq_count
    head_count = H // seq_count
    order = list_order()
    relative = [lax.axis_index("seq") ^ j for j in range(seq_count)]
    self_parts = [m[:, :width] for m in square_parts]
    query_parts = [m[:, width : 2 * width] for m in square_parts]
    cross_parts = [m[:, 2 * width :] for m in square_parts]

    first_norm = norm_shift(hidden, gain_rows[0], shift_vec).astype(BF16)
    first_all = jnp.concatenate(gather_rel(first_norm), axis=0)
    triples = product(first_all, qkv_part).astype(BF16)
    heads = triples.reshape(triples.shape[0], 3, head_count, -1)
    self_mixed, self_log = attend_forward(
        heads[:, 0], heads[:, 1], heads[:, 2], None, score_scale
    )
    self_blocks = self_mixed.reshape(seq_count, tok_rows, width)
    self_tokens = place(exchange_rel([self_blocks[j] for j in range(seq_count)]), relative)
    after_self = hidden + place([product(self_tokens, m) for m in self_parts], order)

    cross_norm = layer_norm(after_self, gain_rows[1]).astype(BF16)
    queries = place([product(cross_norm, m).astype(BF16) for m in query_parts], order)
    pairs = gather_text(product(text_rows, kv_part).astype(BF16))
    pairs = place_pairs(pairs, relative)
    cross_mixed, cross_log = attend_forward(
        queries.reshape(tok_rows, H, -1), pairs[:, 0], pairs[:, 1], key_mask, score_scale
    )
    cross_tokens = cross_mixed.reshape(tok_rows, model_width)
    after_cross = after_self + place([product(cross_tokens, m) for m in cross_parts], order)

    mlp_norm = layer_norm(after_cross, gain_rows[2]).astype(BF16)
    mlp_all = jnp.concatenate(gather_rel(mlp_norm), axis=0)
    up_rows = product(mlp_all, up_part)
    activated = gelu_tanh(up_rows).astype(BF16)
    down_rows = product(activated, down_part).reshape(seq_count, tok_rows, model_width)
    result = after_cross + scatter_rel([down_rows[j] for j in range(seq_count)])
    saved = (
        hidden,
        first_all,
        heads,
        self_log,
        self_tokens,
        after_self,
        cross_norm,
        queries,
        pairs,
        cross_log,
        cross_tokens,
        after_cross,
        mlp_all,
        up_rows,
        activated,
    )
    return (result, saved)


def gather_text(pairs):
    return gather_rel(jnp.pad(pairs, ((0, pairs.shape[0] % 2), (0, 0))))


def place_pairs(blocks, order):
    head_count = H // len(blocks)
    stacked = [m.reshape(m.shape[0], 2 * head_count, -1) for m in blocks]
    halves = [place([m[:, k * m.shape[1] // 2 : (k + 1) * m.shape[1] // 2] for m in blocks], order) for k in range(2)]
    del stacked
    return jnp.stack([m.reshape(m.shape[0], H, -1) for m in halves], axis=1)


def layer_backward(
    grad_out, saved, shift_vec, gain_rows, text_rows, key_mask, weights, score_scale
):
    qkv_part, square_parts, kv_part, up_part, down_part = weights
    (
        hidden,
        first_all,
        heads,
        self_log,
        self_tokens,
        after_self,
        cross_norm,
        queries,
        pairs,
        cross_log,
        cross_tokens,
        after_cross,
        mlp_all,
        up_rows,
        activated,
    ) = saved
    seq_count = lax.axis_size("seq")
    tok_rows, model_width = hidden.shape
    width = model_width // seq_count
    head_count = H // seq_count
    order = list_order()
    relative = [lax.axis_index("seq") ^ j for j in range(seq_count)]
    self_parts = [m[:, :width] for m in square_parts]
    query_parts = [m[:, width : 2 * width] for m in square_parts]
    cross_parts = [m[:, 2 * width :] for m in square_parts]

    out_all = jnp.concatenate(gather_rel(grad_out.astype(BF16)), axis=0)
    grad_activated = product_nt(out_all, down_part)
    _, gelu_pull = jax.vjp(gelu_tanh, up_rows)
    grad_up_rows = gelu_pull(grad_activated)[0].astype(BF16)
    grad_mlp = product_nt(grad_up_rows, up_part).reshape(seq_count, tok_rows, model_width)
    grad_mlp_norm = scatter_rel([grad_mlp[j] for j in range(seq_count)])
    down_shard = scatter_fsdp(product_tn(activated, out_all))
    up_shard = scatter_fsdp(product_tn(mlp_all, grad_up_rows))

    _, mlp_pull = jax.vjp(layer_norm, after_cross, gain_rows[2])
    grad_cross_res, grad_gain_mlp = mlp_pull(grad_mlp_norm)
    grad_cross_res = grad_cross_res + grad_out
    branch = split(grad_cross_res.astype(BF16), order)
    grad_cross_w = [product_tn(cross_tokens, m) for m in branch]
    grad_cross_tok = weighted_nt(branch, cross_parts).astype(BF16)
    grad_queries, grad_keys, grad_values = attend_backward(
        queries.reshape(tok_rows, H, -1),
        pairs[:, 0],
        pairs[:, 1],
        key_mask,
        grad_cross_tok.reshape(tok_rows, H, -1),
        cross_log,
        score_scale,
    )
    text_count = grad_keys.shape[0]
    keys_split = split(grad_keys.reshape(text_count, model_width), relative)
    values_split = split(grad_values.reshape(text_count, model_width), relative)
    grad_pairs = scatter_rel(
        [jnp.concatenate(m, axis=1) for m in zip(keys_split, values_split)]
    ).astype(BF16)
    grad_pairs = grad_pairs[: text_rows.shape[0]]
    grad_text = product_nt(grad_pairs, kv_part)
    kv_shard = scatter_fsdp(product_tn(text_rows, grad_pairs))
    query_split = split(grad_queries.reshape(tok_rows, model_width), order)
    grad_query_w = [product_tn(cross_norm, m) for m in query_split]
    grad_cross_norm = weighted_nt(query_split, query_parts)

    _, cross_pull = jax.vjp(layer_norm, after_self, gain_rows[1])
    grad_self_res, grad_gain_cross = cross_pull(grad_cross_norm)
    grad_self_res = grad_self_res + grad_cross_res
    branch = split(grad_self_res.astype(BF16), order)
    grad_self_w = [product_tn(self_tokens, m) for m in branch]
    grad_self_tok = split(weighted_nt(branch, self_parts).astype(BF16), relative)
    grad_mixed = jnp.concatenate(exchange_rel(grad_self_tok), axis=0)
    grad_triples = jnp.stack(
        attend_backward(
            heads[:, 0],
            heads[:, 1],
            heads[:, 2],
            None,
            grad_mixed.reshape(grad_mixed.shape[0], head_count, -1),
            self_log,
            score_scale,
        ),
        axis=1,
    ).reshape(grad_mixed.shape[0], -1)
    square_shard = scatter_fsdp(
        unspread(
            [
                jnp.concatenate(m, axis=1).astype(BF16)
                for m in zip(grad_self_w, grad_query_w, grad_cross_w)
            ]
        )
    )
    grad_first = product_nt(grad_triples, qkv_part).reshape(seq_count, tok_rows, model_width)
    grad_first_norm = scatter_rel([grad_first[j] for j in range(seq_count)])
    qkv_shard = scatter_fsdp(product_tn(first_all, grad_triples))
    _, shift_pull = jax.vjp(norm_shift, hidden, gain_rows[0], shift_vec)
    grad_hidden, grad_gain_self, grad_shift = shift_pull(grad_first_norm)
    grad_hidden = grad_hidden + grad_self_res
    vectors = jnp.stack([grad_shift, grad_gain_self, grad_gain_cross, grad_gain_mlp])
    shards = (qkv_shard, square_shard, kv_shard, up_shard, down_shard)
    return (grad_hidden, grad_text, vectors, shards)


def gather_block(layer, qkv, query, text_kv, self_out, cross_out, up, down):
    s, seq_count = lax.axis_index("seq"), lax.axis_size("seq")
    fsdp_count = lax.axis_size("fsdp")
    squares = jnp.concatenate(
        [own_part(self_out[layer], 1), own_part(query[layer], 1), own_part(cross_out[layer], 1)],
        axis=1,
    )
    rows = down.shape[1] // seq_count
    return (
        gather_fsdp(own_part(qkv[layer], 3)),
        spread(gather_fsdp(squares)),
        gather_fsdp(own_part(text_kv[layer], 2)),
        gather_fsdp(own_part(up[layer], fsdp_count)),
        gather_fsdp(lax.dynamic_slice_in_dim(down[layer], s * rows, rows, 0)),
    )


def unpart(blocks, groups):
    seq_count = lax.axis_size("seq")
    s = lax.axis_index("seq")
    stacked = jnp.stack(blocks)
    picked = [lax.dynamic_index_in_dim(stacked, a ^ s, 0, False) for a in range(seq_count)]
    width = picked[0].shape[1] // groups
    return jnp.concatenate(
        [picked[a][:, g * width : (g + 1) * width] for g in range(groups) for a in range(seq_count)],
        axis=1,
    ).astype(F32)


def finish_block(shards):
    qkv_shard, square_shard, kv_shard, up_shard, down_shard = shards
    s, seq_count, fsdp_count = lax.axis_index("seq"), lax.axis_size("seq"), lax.axis_size("fsdp")
    qkv_blocks, square_blocks = gather_rel(qkv_shard), gather_rel(square_shard)
    kv_blocks, up_blocks, down_blocks = (
        gather_rel(kv_shard),
        gather_rel(up_shard),
        gather_rel(down_shard),
    )
    width = square_shard.shape[1] // 3
    stacked = jnp.stack(down_blocks)
    down_full = jnp.concatenate(
        [lax.dynamic_index_in_dim(stacked, a ^ s, 0, False) for a in range(seq_count)], axis=0
    ).astype(F32)
    return (
        unpart(qkv_blocks, 3),
        unpart([m[:, width : 2 * width] for m in square_blocks], 1),
        unpart(kv_blocks, 2),
        unpart([m[:, :width] for m in square_blocks], 1),
        unpart([m[:, 2 * width :] for m in square_blocks], 1),
        unpart(up_blocks, fsdp_count),
        down_full,
    )


def body(
    latents,
    skip_input,
    text_tokens,
    text_lengths,
    condition,
    cotangent,
    mod_weight,
    norm_gains,
    qkv_weight,
    query_weight,
    text_kv_weight,
    self_out_weight,
    cross_out_weight,
    up_weight,
    down_weight,
    skip_gain,
    skip_weight,
):
    seq_count, fsdp_count = lax.axis_size("seq"), lax.axis_size("fsdp")
    f = lax.axis_index("fsdp")
    _, tok_rows, model_width = latents.shape
    shard_rows = mod_weight.shape[1]
    score_scale = 1.0 / math.sqrt(model_width // H)
    text_rows = text_tokens[0]
    padded = text_rows.shape[0] + text_rows.shape[0] % 2
    key_mask = jnp.arange(padded) < text_lengths[0]
    order = list_order()

    gain_columns = jnp.concatenate(
        [norm_gains.reshape(-1, shard_rows), skip_gain.reshape(-1, shard_rows)], axis=0
    )
    gains_all = lax.all_gather(gain_columns, "fsdp", axis=0).astype(F32)
    gains = jnp.swapaxes(gains_all[:, :6], 0, 1).reshape(2, 3, model_width)
    skip_gains = gains_all[:, 6:].reshape(-1)

    cond_part = lax.all_to_all(
        condition.astype(F32).reshape(fsdp_count, shard_rows), "fsdp", 0, 0, tiled=True
    )
    silu_part = jax.nn.silu(cond_part)
    shift_terms = jnp.einsum(
        "br,lrd->bld", silu_part, mod_weight.astype(F32), precision=EXACT
    )
    shifts = jnp.sum(lax.all_to_all(shift_terms, "fsdp", 0, 0, tiled=True), axis=0)

    stacks = (
        qkv_weight,
        query_weight,
        text_kv_weight,
        self_out_weight,
        cross_out_weight,
        up_weight,
        down_weight,
    )
    first_weights = gather_block(0, *stacks)
    first_out, first_saved = layer_forward(
        latents[0].astype(F32), shifts[0], gains[0], text_rows, key_mask, first_weights, score_scale
    )
    skip_parts = spread(gather_fsdp(own_part(skip_weight, 1)))
    joined = jnp.concatenate([first_out, skip_input[0].astype(F32)], axis=-1)
    joined_norm = layer_norm(joined, skip_gains).astype(BF16)
    skip_out = place([product(joined_norm, m) for m in skip_parts], order)
    second_weights = gather_block(1, *stacks)
    final_out, second_saved = layer_forward(
        skip_out, shifts[1], gains[1], text_rows, key_mask, second_weights, score_scale
    )
    output = final_out.astype(BF16)

    grad_skip_out, text_second, vectors_second, shards_second = layer_backward(
        cotangent[0].astype(F32),
        second_saved,
        shifts[1],
        gains[1],
        text_rows,
        key_mask,
        second_weights,
        score_scale,
    )
    branch = split(grad_skip_out.astype(BF16), order)
    grad_joined_norm = weighted_nt(branch, skip_parts)
    _, joined_pull = jax.vjp(layer_norm, joined, skip_gains)
    grad_joined, grad_skip_gains = joined_pull(grad_joined_norm)
    skip_shard = scatter_fsdp(
        unspread([product_tn(joined_norm, m).astype(BF16) for m in branch])
    )
    grad_latents, text_first, vectors_first, shards_first = layer_backward(
        grad_joined[:, :model_width],
        first_saved,
        shifts[0],
        gains[0],
        text_rows,
        key_mask,
        first_weights,
        score_scale,
    )
    grad_skip = grad_joined[:, model_width:]

    vectors = jnp.concatenate(
        [vectors_first, vectors_second, grad_skip_gains.reshape(-1, model_width)], axis=0
    )
    vectors_all = lax.all_gather(vectors, ("fsdp", "seq"), axis=0)
    vectors_all = vectors_all.reshape(fsdp_count, seq_count, -1, model_width).sum(axis=1)
    shift_grads = jnp.stack([vectors_all[:, 0], vectors_all[:, 4]], axis=1)
    gain_sums = vectors_all.sum(axis=0)
    grad_norm_gains = lax.dynamic_slice_in_dim(
        jnp.stack([gain_sums[1:4], gain_sums[5:8]]), f * shard_rows, shard_rows, 2
    )
    grad_skip_gain = lax.dynamic_slice_in_dim(
        gain_sums[8:].reshape(-1), f * skip_gain.shape[0], skip_gain.shape[0], 0
    )
    grad_mod = jnp.einsum("br,bld->lrd", silu_part, shift_grads, precision=EXACT)
    grad_silu = jnp.einsum("bld,lrd->br", shift_grads, mod_weight.astype(F32), precision=EXACT)
    _, silu_pull = jax.vjp(jax.nn.silu, cond_part)
    grad_cond_part = silu_pull(grad_silu)[0]
    grad_condition = lax.all_to_all(grad_cond_part, "fsdp", 0, 0, tiled=True).reshape(1, -1)

    grad_text = lax.psum((text_first + text_second).astype(BF16), "seq").astype(F32)[None]
    first_done, second_done = finish_block(shards_first), finish_block(shards_second)
    stacked = [jnp.stack(pair) for pair in zip(first_done, second_done)]
    grad_skip_weight = unpart(gather_rel(skip_shard), 1)
    return (
        output[None],
        grad_latents[None],
        grad_skip[None],
        grad_text,
        grad_condition,
        grad_mod,
        grad_norm_gains,
        *stacked,
        grad_skip_gain,
        grad_skip_weight,
    )


def solution(mesh):
    in_specs = (
        P("fsdp", "seq", None),
        P("fsdp", "seq", None),
        P("fsdp", None, None),
        P("fsdp"),
        P("fsdp", None),
        P("fsdp", "seq", None),
        P(None, "fsdp", None),
        P(None, None, "fsdp"),
        P(None, "fsdp", None),
        P(None, "fsdp", None),
        P(None, "fsdp", None),
        P(None, "fsdp", None),
        P(None, "fsdp", None),
        P(None, "fsdp", None),
        P(None, "fsdp", None),
        P("fsdp"),
        P("fsdp", None),
    )
    out_specs = (
        P("fsdp", "seq", None),
        P("fsdp", "seq", None),
        P("fsdp", "seq", None),
        P("fsdp", None, None),
        P("fsdp", None),
        P(None, "fsdp", None),
        P(None, None, "fsdp"),
        P(None, "fsdp", None),
        P(None, "fsdp", None),
        P(None, "fsdp", None),
        P(None, "fsdp", None),
        P(None, "fsdp", None),
        P(None, "fsdp", None),
        P(None, "fsdp", None),
        P("fsdp"),
        P("fsdp", None),
    )
    return jax.shard_map(body, mesh=mesh, in_specs=in_specs, out_specs=out_specs, check_vma=False)
```

```python
import functools
import math

import jax
import jax.numpy as jnp
from jax import lax
from jax.experimental import pallas as pl
from jax.experimental.pallas import tpu as pltpu
from jax.sharding import PartitionSpec as P

H = 16
NORM_EPSILON = 1e-06
BF16 = jnp.bfloat16
F32 = jnp.float32
LOG2_E = 1.4426950408889634
VMEM_LIMIT = 56 * 1024 * 1024


def dot_nn(a, b):
    return lax.dot_general(a, b, (((1,), (0,)), ((), ())), preferred_element_type=F32)


def dot_nt(a, b):
    return lax.dot_general(a, b, (((1,), (1,)), ((), ())), preferred_element_type=F32)


def dot_tn(a, b):
    return lax.dot_general(a, b, (((0,), (0,)), ((), ())), preferred_element_type=F32)


def whole(count):
    return [pl.BlockSpec(memory_space=pltpu.VMEM)] * count


def call(kernel, outs, scratch, cost, *operands, scalars=None):
    specs = whole(len(operands))
    if scalars is not None:
        specs = [pl.BlockSpec(memory_space=pltpu.SMEM)] + specs
        operands = (scalars,) + operands
    return pl.pallas_call(
        kernel,
        out_shape=tuple(jax.ShapeDtypeStruct(s, d) for s, d in outs),
        in_specs=specs,
        out_specs=tuple(whole(len(outs))),
        scratch_shapes=scratch,
        compiler_params=pltpu.CompilerParams(vmem_limit_bytes=VMEM_LIMIT),
        cost_estimate=pl.CostEstimate(flops=cost[0], bytes_accessed=cost[1], transcendentals=0),
    )(*operands)


def self_forward_kernel(width, head_size, step, triples_ref, mixed_ref):
    rows = triples_ref.shape[0]
    head_count = width // head_size
    factor = LOG2_E / math.sqrt(head_size)

    def block(i, carry):
        at = pl.ds(pl.multiple_of(i * step, step), step)
        for h in range(head_count):
            low = h * head_size
            q = triples_ref[at, low : low + head_size]
            k = triples_ref[:, width + low : width + low + head_size]
            v = triples_ref[:, 2 * width + low : 2 * width + low + head_size]
            scores = dot_nt(q, k)
            top = jnp.max(scores, axis=1, keepdims=True)
            weights = jnp.exp2((scores - top) * factor)
            total = jnp.sum(weights, axis=1, keepdims=True)
            mixed = dot_nn(weights.astype(BF16), v) * (1.0 / total)
            mixed_ref[at, low : low + head_size] = mixed.astype(BF16)
        return carry

    lax.fori_loop(0, rows // step, block, 0)


def self_forward(triples, head_size):
    rows, width = triples.shape[0], triples.shape[1] // 3
    (mixed,) = call(
        functools.partial(self_forward_kernel, width, head_size, 256),
        [((rows, width), BF16)],
        [],
        (4 * rows * rows * width, 8 * rows * width),
        triples,
    )
    return mixed


def attention_back(q, k, v, grad, valid, head_size):
    factor = LOG2_E / math.sqrt(head_size)
    scores = dot_nt(k, q)
    if valid is not None:
        scores = jnp.where(valid, scores, -1e30)
    top = jnp.max(scores, axis=0, keepdims=True)
    weights = jnp.exp2((scores - top) * factor)
    weights = weights * (1.0 / jnp.sum(weights, axis=0, keepdims=True))
    grad_weights = dot_nt(v, grad)
    delta = jnp.sum(grad_weights * weights, axis=0, keepdims=True)
    grad_scores = (weights * (grad_weights - delta)).astype(BF16)
    scale = 1.0 / math.sqrt(head_size)
    return (
        dot_tn(grad_scores, k) * scale,
        dot_nn(grad_scores, q) * scale,
        dot_nn(weights.astype(BF16), grad),
    )


def self_backward_kernel(width, head_size, step, triples_ref, *refs):
    grad_refs, (out_ref, keys_ref, values_ref) = refs[:-3], refs[-3:]
    rows = triples_ref.shape[0]
    part = grad_refs[0].shape[0]
    for h in range(width // head_size):
        low = h * head_size
        k = triples_ref[:, width + low : width + low + head_size]
        v = triples_ref[:, 2 * width + low : 2 * width + low + head_size]
        for i in range(rows // step):
            at = slice(i * step, (i + 1) * step)
            inside = (i * step) % part
            q = triples_ref[at, low : low + head_size]
            grad = grad_refs[i * step // part][inside : inside + step, low : low + head_size]
            grad_q, grad_k, grad_v = attention_back(q, k, v, grad, None, head_size)
            out_ref[at, low : low + head_size] = grad_q.astype(BF16)
            if i == 0:
                keys_ref[...] = grad_k
                values_ref[...] = grad_v
            else:
                keys_ref[...] += grad_k
                values_ref[...] += grad_v
        out_ref[:, width + low : width + low + head_size] = keys_ref[...].astype(BF16)
        out_ref[:, 2 * width + low : 2 * width + low + head_size] = values_ref[...].astype(BF16)


def self_backward(triples, grads, head_size):
    rows, width = triples.shape[0], triples.shape[1] // 3
    step = min(256, grads[0].shape[0])
    (out,) = call(
        functools.partial(self_backward_kernel, width, head_size, step),
        [((rows, 3 * width), BF16)],
        [pltpu.VMEM((rows, head_size), F32), pltpu.VMEM((rows, head_size), F32)],
        (10 * rows * rows * width, 16 * rows * width),
        triples,
        *grads,
    )
    return out


def norm_stats(values):
    mean = jnp.mean(values, axis=1, keepdims=True)
    centered = values - mean
    var = jnp.mean(centered * centered, axis=1, keepdims=True)
    scale = lax.rsqrt(var + NORM_EPSILON)
    return centered * scale, scale


def norm_back(values, gain, grad):
    unit, scale = norm_stats(values)
    grad_unit = grad * gain
    inner = jnp.mean(grad_unit * unit, axis=1, keepdims=True)
    grad_values = scale * (grad_unit - jnp.mean(grad_unit, axis=1, keepdims=True) - unit * inner)
    return grad_values, jnp.sum(grad * unit, axis=0, keepdims=True)


def fill_corner(count, matrix_refs, scalars_ref, corner_ref):
    if len(matrix_refs) == count:
        return list(matrix_refs)
    odd = scalars_ref[2 * count]
    half = matrix_refs[-1].shape[0]
    corner_ref[pl.ds(pl.multiple_of(odd * half, half), half), :] = matrix_refs[-2][...]
    corner_ref[pl.ds(pl.multiple_of((1 - odd) * half, half), half), :] = matrix_refs[-1][...]
    return list(matrix_refs[:-2]) + [corner_ref]


def middle_forward_kernel(count, parts, head_size, scalars_ref, *refs):
    mixed_refs, refs = refs[:count], refs[count:]
    matrix_refs, refs = refs[:parts], refs[parts:]
    pair_refs, refs = refs[:count], refs[count:]
    hidden_ref, gains_ref = refs[:2]
    (self_ref, after_self_ref, norm_ref, queries_ref, cross_ref, after_cross_ref, mlp_ref) = refs[2:9]
    wide_ref, narrow_ref, corner_ref = refs[9:]
    width = mixed_refs[0].shape[1]
    matrices = fill_corner(count, matrix_refs, scalars_ref, corner_ref)
    order = [scalars_ref[i] for i in range(count)]
    relative = [scalars_ref[count + j] for j in range(count)]
    length = scalars_ref[2 * count + 1]
    spans = [slice(a * width, (a + 1) * width) for a in range(count)]

    for j in range(count):
        narrow_ref[relative[j]] = mixed_refs[j][...]
    for a in range(count):
        self_ref[:, spans[a]] = narrow_ref[a]
    tokens = self_ref[...]
    for i in range(count):
        wide_ref[order[i]] = dot_nn(tokens, matrices[i][:, :width])
    for a in range(count):
        after_self_ref[:, spans[a]] = hidden_ref[:, spans[a]] + wide_ref[a]
    normed = (norm_stats(after_self_ref[...])[0] * gains_ref[1:2, :]).astype(BF16)
    norm_ref[...] = normed
    for i in range(count):
        found = dot_nn(normed, matrices[i][:, width : 2 * width])
        queries_ref[order[i] ^ relative[0]] = found.astype(BF16)

    factor = LOG2_E / math.sqrt(head_size)
    valid = lax.broadcasted_iota(jnp.int32, (1, pair_refs[0].shape[0]), 1) < length
    for j in range(count):
        for h in range(width // head_size):
            at = slice(h * head_size, (h + 1) * head_size)
            values_at = slice(width + h * head_size, width + (h + 1) * head_size)
            scores = dot_nt(queries_ref[j, :, at], pair_refs[j][:, at])
            scores = jnp.where(valid, scores, -1e30)
            top = jnp.max(scores, axis=1, keepdims=True)
            weights = jnp.exp2((scores - top) * factor)
            total = jnp.sum(weights, axis=1, keepdims=True)
            mixed = dot_nn(weights.astype(BF16), pair_refs[j][:, values_at]) * (1.0 / total)
            narrow_ref[relative[j], :, at] = mixed.astype(BF16)
    for a in range(count):
        cross_ref[:, spans[a]] = narrow_ref[a]
    tokens = cross_ref[...]
    for i in range(count):
        wide_ref[order[i]] = dot_nn(tokens, matrices[i][:, 2 * width :])
    for a in range(count):
        after_cross_ref[:, spans[a]] = after_self_ref[:, spans[a]] + wide_ref[a]
    mlp_ref[...] = (norm_stats(after_cross_ref[...])[0] * gains_ref[2:3, :]).astype(BF16)


def corner_scratch(count, matrices):
    rows, columns = matrices[0].shape
    return pltpu.VMEM((rows, columns) if len(matrices) > count else (16, 128), BF16)


def middle_forward(scalars, mixed, matrices, pairs, hidden, gains, head_size):
    count = len(mixed)
    rows, columns = hidden.shape
    width = columns // count
    return call(
        functools.partial(middle_forward_kernel, count, len(matrices), head_size),
        [
            ((rows, columns), BF16),
            ((rows, columns), F32),
            ((rows, columns), BF16),
            ((count, rows, width), BF16),
            ((rows, columns), BF16),
            ((rows, columns), F32),
            ((rows, columns), BF16),
        ],
        [
            pltpu.VMEM((count, rows, width), F32),
            pltpu.VMEM((count, rows, width), BF16),
            corner_scratch(count, matrices),
        ],
        (6 * rows * columns * columns, 6 * columns * columns + 24 * rows * columns),
        *mixed,
        *matrices,
        *pairs,
        hidden,
        gains,
        scalars=scalars,
    )


def middle_backward_kernel(count, parts, head_size, scalars_ref, *refs):
    matrix_refs, refs = refs[:parts], refs[parts:]
    pair_refs, refs = refs[:count], refs[count:]
    grad_norm_ref, grad_out_ref, after_cross_ref, after_self_ref, queries_ref, gains_ref = refs[:6]
    out_ref, self_branch_ref, query_branch_ref, cross_branch_ref, gain_ref = refs[6:11]
    pair_grad_refs, refs = refs[11 : 11 + count], refs[11 + count :]
    mixed_grad_refs, refs = refs[:count], refs[count:]
    wide_ref, narrow_ref, query_ref, corner_ref = refs
    width = queries_ref.shape[2]
    matrices = fill_corner(count, matrix_refs, scalars_ref, corner_ref)
    order = [scalars_ref[i] for i in range(count)]
    relative = [scalars_ref[count + j] for j in range(count)]
    length = scalars_ref[2 * count + 1]
    spans = [slice(a * width, (a + 1) * width) for a in range(count)]

    def back(branch_ref, columns):
        total = dot_nt(branch_ref[0], matrices[0][:, columns])
        for i in range(1, count):
            total = total + dot_nt(branch_ref[i], matrices[i][:, columns])
        return total

    def divide(values):
        for a in range(count):
            narrow_ref[a] = values[:, spans[a]].astype(BF16)

    grad, grad_gain = norm_back(after_cross_ref[...], gains_ref[2:3, :], grad_norm_ref[...])
    gain_ref[1:2, :] = grad_gain
    wide_ref[...] = grad + grad_out_ref[...]
    divide(wide_ref[...])
    for i in range(count):
        cross_branch_ref[i] = narrow_ref[order[i]]
    divide(back(cross_branch_ref, slice(2 * width, 3 * width)))

    valid = lax.broadcasted_iota(jnp.int32, (pair_refs[0].shape[0], 1), 0) < length
    for j in range(count):
        for h in range(width // head_size):
            at = slice(h * head_size, (h + 1) * head_size)
            values_at = slice(width + h * head_size, width + (h + 1) * head_size)
            grad_q, grad_k, grad_v = attention_back(
                queries_ref[j, :, at],
                pair_refs[j][:, at],
                pair_refs[j][:, values_at],
                narrow_ref[relative[j], :, at],
                valid,
                head_size,
            )
            query_ref[j, :, at] = grad_q.astype(BF16)
            pair_grad_refs[j][:, at] = grad_k.astype(BF16)
            pair_grad_refs[j][:, values_at] = grad_v.astype(BF16)
    for i in range(count):
        query_branch_ref[i] = query_ref[order[i] ^ relative[0]]
    grad, grad_gain = norm_back(
        after_self_ref[...], gains_ref[1:2, :], back(query_branch_ref, slice(width, 2 * width))
    )
    gain_ref[0:1, :] = grad_gain
    out_ref[...] = grad + wide_ref[...]
    divide(out_ref[...])
    for i in range(count):
        self_branch_ref[i] = narrow_ref[order[i]]
    divide(back(self_branch_ref, slice(0, width)))
    for j in range(count):
        mixed_grad_refs[j][...] = narrow_ref[relative[j]]


def middle_backward(
    scalars, matrices, pairs, grad_norm, grad_out, after_cross, after_self, queries, gains, head_size
):
    count = len(pairs)
    rows, columns = grad_out.shape
    width = columns // count
    branch = ((count, rows, width), BF16)
    found = call(
        functools.partial(middle_backward_kernel, count, len(matrices), head_size),
        [((rows, columns), F32), branch, branch, branch, ((2, columns), F32)]
        + [(m.shape, BF16) for m in pairs]
        + [((rows, width), BF16)] * count,
        [
            pltpu.VMEM((rows, columns), F32),
            pltpu.VMEM((count, rows, width), BF16),
            pltpu.VMEM((count, rows, width), BF16),
            corner_scratch(count, matrices),
        ],
        (10 * rows * columns * columns, 6 * columns * columns + 36 * rows * columns),
        *matrices,
        *pairs,
        grad_norm,
        grad_out,
        after_cross,
        after_self,
        queries,
        gains,
        scalars=scalars,
    )
    return found[:5] + (found[5 : 5 + count], found[5 + count :])


def outer_kernel(groups, *refs):
    rows_refs, branch_refs, out_refs = refs[:groups], refs[groups : 2 * groups], refs[2 * groups :]
    width = branch_refs[0].shape[2]
    for g in range(groups):
        turned = rows_refs[g][...].T
        for i, out_ref in enumerate(out_refs):
            out_ref[:, g * width : (g + 1) * width] = dot_nn(turned, branch_refs[g][i]).astype(BF16)


def outer(rows, branches):
    count, tokens, width = branches[0].shape
    groups, columns = len(rows), rows[0].shape[1]
    return call(
        functools.partial(outer_kernel, groups),
        [((columns, groups * width), BF16)] * count,
        [],
        (2 * groups * count * tokens * columns * width, 2 * groups * count * columns * width),
        *rows,
        *branches,
    )


def joined_stats(first, second):
    count = first.shape[1] + second.shape[1]
    mean = (jnp.sum(first, axis=1, keepdims=True) + jnp.sum(second, axis=1, keepdims=True)) / count
    first, second = first - mean, second - mean
    var = (
        jnp.sum(first * first, axis=1, keepdims=True)
        + jnp.sum(second * second, axis=1, keepdims=True)
    ) / count
    scale = lax.rsqrt(var + NORM_EPSILON)
    return first * scale, second * scale, scale


def skip_forward_kernel(count, parts, scalars_ref, *refs):
    matrix_refs, refs = refs[:parts], refs[parts:]
    first_ref, second_ref, gains_ref, joined_ref, out_ref, wide_ref, corner_ref = refs
    columns = first_ref.shape[1]
    width = columns // count
    matrices = fill_corner(count, matrix_refs, scalars_ref, corner_ref)
    first, second, _ = joined_stats(first_ref[...], second_ref[...].astype(F32))
    joined_ref[:, :columns] = (first * gains_ref[0:1, :]).astype(BF16)
    joined_ref[:, columns:] = (second * gains_ref[1:2, :]).astype(BF16)
    joined = joined_ref[...]
    for i in range(count):
        wide_ref[scalars_ref[i]] = dot_nn(joined, matrices[i][...])
    for a in range(count):
        out_ref[:, a * width : (a + 1) * width] = wide_ref[a]


def skip_forward(scalars, matrices, first, second, gains):
    rows, columns = first.shape
    count = columns // matrices[0].shape[1]
    return call(
        functools.partial(skip_forward_kernel, count, len(matrices)),
        [((rows, 2 * columns), BF16), ((rows, columns), F32)],
        [pltpu.VMEM((count, rows, columns // count), F32), corner_scratch(count, matrices)],
        (4 * rows * columns * columns, 4 * columns * columns + 16 * rows * columns),
        *matrices,
        first,
        second,
        gains,
        scalars=scalars,
    )


def skip_backward_kernel(count, parts, scalars_ref, *refs):
    matrix_refs, refs = refs[:parts], refs[parts:]
    first_ref, second_ref, gains_ref, grad_ref = refs[:4]
    branch_ref, grad_first_ref, grad_second_ref, gain_ref, narrow_ref, corner_ref = refs[4:]
    columns = first_ref.shape[1]
    width = columns // count
    matrices = fill_corner(count, matrix_refs, scalars_ref, corner_ref)
    for a in range(count):
        narrow_ref[a] = grad_ref[:, a * width : (a + 1) * width].astype(BF16)
    for i in range(count):
        branch_ref[i] = narrow_ref[scalars_ref[i]]

    def back(at):
        total = dot_nt(branch_ref[0], matrices[0][at, :])
        for i in range(1, count):
            total = total + dot_nt(branch_ref[i], matrices[i][at, :])
        return total

    grad_first_ref[...] = back(slice(0, columns))
    grad_second_ref[...] = back(slice(columns, 2 * columns))
    first, second, scale = joined_stats(first_ref[...], second_ref[...].astype(F32))
    gain_ref[0:1, :] = jnp.sum(grad_first_ref[...] * first, axis=0, keepdims=True)
    gain_ref[1:2, :] = jnp.sum(grad_second_ref[...] * second, axis=0, keepdims=True)
    grad_first = grad_first_ref[...] * gains_ref[0:1, :]
    grad_second = grad_second_ref[...] * gains_ref[1:2, :]
    mean = (
        jnp.sum(grad_first, axis=1, keepdims=True) + jnp.sum(grad_second, axis=1, keepdims=True)
    ) / (2 * columns)
    inner = (
        jnp.sum(grad_first * first, axis=1, keepdims=True)
        + jnp.sum(grad_second * second, axis=1, keepdims=True)
    ) / (2 * columns)
    grad_first_ref[...] = scale * (grad_first - mean - first * inner)
    grad_second_ref[...] = scale * (grad_second - mean - second * inner)


def skip_backward(scalars, matrices, first, second, gains, grad):
    rows, columns = first.shape
    count = columns // matrices[0].shape[1]
    narrow = (count, rows, columns // count)
    return call(
        functools.partial(skip_backward_kernel, count, len(matrices)),
        [
            (narrow, BF16),
            ((rows, columns), F32),
            ((rows, columns), F32),
            ((2, columns), F32),
        ],
        [pltpu.VMEM(narrow, BF16), corner_scratch(count, matrices)],
        (4 * rows * columns * columns, 4 * columns * columns + 20 * rows * columns),
        *matrices,
        first,
        second,
        gains,
        grad,
        scalars=scalars,
    )


def settle_kernel(count, parts, groups, pieces, scalars_ref, *refs):
    block_refs, refs = refs[:parts], refs[parts:]
    out_refs, stack_ref = refs[-pieces - 1 : -1], refs[-1]
    columns = stack_ref.shape[2] // pieces
    width = columns // groups
    for j in range(count):
        owner = scalars_ref[count + j]
        if j == count - 1 and parts > count:
            cut = block_refs[j].shape[0]
            stack_ref[owner, :cut] = block_refs[j][...]
            stack_ref[owner, cut:] = block_refs[j + 1][...]
        else:
            stack_ref[owner] = block_refs[j][...]
    for p in range(pieces):
        for g in range(groups):
            for a in range(count):
                low = p * columns + g * width
                at = (g * count + a) * width
                out_refs[p][0, :, at : at + width] = stack_ref[a, :, low : low + width].astype(F32)


def settle_rows_kernel(count, parts, scalars_ref, *refs):
    block_refs, out_ref = refs[:parts], refs[-1]
    rows = block_refs[0].shape[0]
    for j in range(count):
        low = pl.multiple_of(scalars_ref[count + j] * rows, rows)
        if j == count - 1 and parts > count:
            cut = block_refs[j].shape[0]
            out_ref[0, pl.ds(low, cut), :] = block_refs[j][...].astype(F32)
            out_ref[0, pl.ds(low + cut, rows - cut), :] = block_refs[j + 1][...].astype(F32)
        else:
            out_ref[0, pl.ds(low, rows), :] = block_refs[j][...].astype(F32)


def settle_call(kernel, scalars, blocks, shape, pieces, layer, layer_count, before, scratch):
    held = [] if before is None else list(before)
    inputs = whole(len(blocks)) + [pl.BlockSpec(memory_space=pl.ANY)] * len(held)
    found = pl.pallas_call(
        kernel,
        grid=(1,),
        out_shape=[jax.ShapeDtypeStruct((layer_count,) + shape, F32)] * pieces,
        in_specs=[pl.BlockSpec(memory_space=pltpu.SMEM)] + inputs,
        out_specs=[pl.BlockSpec((1,) + shape, lambda i: (layer, 0, 0))] * pieces,
        scratch_shapes=scratch,
        input_output_aliases={1 + len(blocks) + i: i for i in range(len(held))},
        compiler_params=pltpu.CompilerParams(vmem_limit_bytes=VMEM_LIMIT),
        cost_estimate=pl.CostEstimate(
            flops=0, bytes_accessed=6 * pieces * shape[0] * shape[1], transcendentals=0
        ),
    )(scalars, *blocks, *held)
    return list(found)


def settle(scalars, blocks, groups, pieces, layer, layer_count, before=None):
    count = lax.axis_size("seq")
    rows, columns = blocks[0].shape
    return settle_call(
        functools.partial(settle_kernel, count, len(blocks), groups, pieces),
        scalars,
        blocks,
        (rows, count * columns // pieces),
        pieces,
        layer,
        layer_count,
        before,
        [pltpu.VMEM((count, rows, columns), BF16)],
    )


def settle_rows(scalars, blocks, layer, layer_count, before=None):
    count = lax.axis_size("seq")
    rows, columns = blocks[0].shape
    return settle_call(
        functools.partial(settle_rows_kernel, count, len(blocks)),
        scalars,
        blocks,
        (count * rows, columns),
        1,
        layer,
        layer_count,
        before,
        [],
    )


EXACT = lax.Precision.HIGHEST


def layer_norm(values, gain_vec):
    row_mean = jnp.mean(values, axis=-1, keepdims=True)
    centered = values - row_mean
    row_var = jnp.mean(centered * centered, axis=-1, keepdims=True)
    return centered * lax.rsqrt(row_var + NORM_EPSILON) * gain_vec


def norm_shift(values, gain_vec, shift_vec):
    return layer_norm(values, gain_vec) + shift_vec


def gelu_tanh(values):
    return jax.nn.gelu(values, approximate=True)


def swap_seq(block, bits):
    seq_count = lax.axis_size("seq")
    return lax.ppermute(block, "seq", [(i, i ^ bits) for i in range(seq_count)])


def swap_fsdp(block, bits):
    fsdp_count = lax.axis_size("fsdp")
    return lax.ppermute(block, "fsdp", [(i, i ^ bits) for i in range(fsdp_count)])


def swap_core(block):
    return swap_fsdp(block, 1)


def swap_by_core(block, even_bits, odd_bits):
    seq_count, fsdp_count = lax.axis_size("seq"), lax.axis_size("fsdp")
    pairs = []
    for s in range(seq_count):
        for f in range(fsdp_count):
            other = s ^ (odd_bits if f % 2 else even_bits)
            pairs.append((s * fsdp_count + f, other * fsdp_count + f))
    return lax.ppermute(block, ("seq", "fsdp"), pairs)


def gather_parts(block):
    seq_count = lax.axis_size("seq")
    if seq_count != 4:
        return [block] + [swap_seq(block, j) for j in range(1, seq_count)]
    cut = block.shape[0] // 32 * 16
    from_x, from_y = swap_seq(block, 1), swap_seq(block, 2)
    return [block, from_x, from_y, swap_seq(from_y[:cut], 1), swap_seq(from_x[cut:], 2)]


def gather_rel(block):
    parts = gather_parts(block)
    if len(parts) == 5:
        parts = parts[:3] + [jnp.concatenate(parts[3:], axis=0)]
    return parts


def add_bf16(left_in, right_in):
    return (left_in.astype(F32) + right_in.astype(F32)).astype(BF16)


def scatter_rel(blocks):
    seq_count = lax.axis_size("seq")
    if seq_count != 4:
        total = blocks[0].astype(F32)
        for j in range(1, seq_count):
            total = total + swap_seq(blocks[j].astype(BF16), j).astype(F32)
        return total
    cut = blocks[0].shape[0] // 32 * 16
    corner = blocks[3].astype(BF16)
    by_x, by_y = swap_seq(corner[:cut], 1), swap_seq(corner[cut:], 2)
    to_y = jnp.concatenate([add_bf16(blocks[2][:cut], by_x), blocks[2][cut:].astype(BF16)])
    to_x = jnp.concatenate([blocks[1][:cut].astype(BF16), add_bf16(blocks[1][cut:], by_y)])
    return blocks[0].astype(F32) + swap_seq(to_x, 1).astype(F32) + swap_seq(to_y, 2).astype(F32)


def exchange_rel(blocks):
    return [blocks[0]] + [swap_seq(blocks[j], j) for j in range(1, len(blocks))]


def list_order():
    s, seq_count = lax.axis_index("seq"), lax.axis_size("seq")
    if seq_count != 4:
        return [s ^ j for j in range(seq_count)]
    odd = lax.axis_index("fsdp") % 2
    return [s, s ^ (1 + odd), s ^ (2 - odd), s ^ 3]


def spread(block):
    seq_count = lax.axis_size("seq")
    if seq_count != 4:
        return [block] + [swap_seq(block, j) for j in range(1, seq_count)]
    odd = lax.axis_index("fsdp") % 2
    half = block.shape[0] // 2
    first = swap_by_core(block, 1, 2)
    part = swap_by_core(lax.dynamic_slice_in_dim(first, odd * half, half, 0), 2, 1)
    return [block, first, swap_core(first), part, swap_core(part)]


def unspread(blocks):
    seq_count = lax.axis_size("seq")
    if seq_count != 4:
        return scatter_rel(blocks).astype(BF16)
    odd = lax.axis_index("fsdp") % 2
    half = blocks[0].shape[0] // 2
    mine = lax.dynamic_slice_in_dim(blocks[3], odd * half, half, 0)
    others = lax.dynamic_slice_in_dim(blocks[3], (1 - odd) * half, half, 0)
    passed = swap_by_core(add_bf16(mine, swap_core(others)), 2, 1).astype(F32)
    from_core = swap_core(blocks[2])
    to_send = jnp.concatenate(
        [
            (
                blocks[1][k * half : (k + 1) * half].astype(F32)
                + from_core[k * half : (k + 1) * half].astype(F32)
                + jnp.where(odd == k, passed, 0.0)
            ).astype(BF16)
            for k in range(2)
        ]
    )
    return add_bf16(blocks[0], swap_by_core(to_send, 1, 2))


def own_part(matrix, groups):
    s, seq_count = lax.axis_index("seq"), lax.axis_size("seq")
    width = matrix.shape[1] // (groups * seq_count)
    parts = [
        lax.dynamic_slice_in_dim(matrix, (g * seq_count + s) * width, width, 1)
        for g in range(groups)
    ]
    return jnp.concatenate(parts, axis=1)


def gather_fsdp(shard):
    return lax.all_gather(shard, "fsdp", axis=0, tiled=True)


def scatter_fsdp(full):
    return lax.psum_scatter(full.astype(BF16), "fsdp", scatter_dimension=0, tiled=True)


def after(values, *others):
    for other in others:
        values = values + 0.0 * other[(slice(0, 1),) * other.ndim].reshape(()).astype(F32)
    return values


def layer_forward(first_all, hidden, scalars, gain_rows, pairs, weights):
    qkv_part, square_parts, _, up_part, down_part = weights
    seq_count = lax.axis_size("seq")
    tok_rows, model_width = hidden.shape
    head_size = model_width // H
    triples = dot_nn(first_all, qkv_part).astype(BF16)
    mixed = self_forward(triples, head_size).reshape(seq_count, tok_rows, -1)
    mixed = exchange_rel([mixed[j] for j in range(seq_count)])
    self_tokens, after_self, cross_norm, queries, cross_tokens, after_cross, mlp_norm = (
        middle_forward(scalars, mixed, square_parts, pairs, hidden, gain_rows, head_size)
    )
    mlp_all = jnp.concatenate(gather_rel(mlp_norm), axis=0)
    up_rows = dot_nn(mlp_all, up_part)
    activated = gelu_tanh(up_rows).astype(BF16)
    down_rows = [
        dot_nn(activated[j * tok_rows : (j + 1) * tok_rows], down_part) for j in range(seq_count)
    ]
    result = after_cross + scatter_rel(down_rows)
    saved = (
        first_all,
        triples,
        self_tokens,
        after_self,
        cross_norm,
        queries,
        cross_tokens,
        after_cross,
        mlp_all,
        up_rows,
        activated,
    )
    return (result, saved)


def layer_backward(grad_out, saved, hidden, shift_vec, scalars, gain_rows, text_rows, pairs, weights, earlier):
    qkv_part, square_parts, kv_part, up_part, down_part = weights
    (
        first_all,
        triples,
        self_tokens,
        after_self,
        cross_norm,
        queries,
        cross_tokens,
        after_cross,
        mlp_all,
        up_rows,
        activated,
    ) = saved
    seq_count = lax.axis_size("seq")
    tok_rows, model_width = grad_out.shape
    head_size = model_width // H

    out_all = jnp.concatenate(gather_rel(grad_out.astype(BF16)), axis=0)
    grad_activated = dot_nt(out_all, down_part)
    _, gelu_pull = jax.vjp(gelu_tanh, up_rows)
    grad_up_rows = gelu_pull(grad_activated)[0].astype(BF16)
    grad_mlp_norm = scatter_rel(
        [
            dot_nt(grad_up_rows[j * tok_rows : (j + 1) * tok_rows], up_part)
            for j in range(seq_count)
        ]
    )
    down_shard = scatter_fsdp(dot_tn(activated, out_all))
    up_shard = scatter_fsdp(dot_tn(mlp_all, grad_up_rows))

    grad_self_res, self_branch, query_branch, cross_branch, gain_grads, pair_grads, mixed_grads = (
        middle_backward(
            scalars,
            square_parts,
            pairs,
            grad_mlp_norm,
            grad_out,
            after_cross,
            after_self,
            queries,
            after(gain_rows, *earlier[0]),
            head_size,
        )
    )
    grad_triples = self_backward(triples, exchange_rel(mixed_grads), head_size)
    grad_first = [
        dot_nt(grad_triples[j * tok_rows : (j + 1) * tok_rows], qkv_part) for j in range(seq_count)
    ]
    grad_first_norm = scatter_rel(grad_first)
    grad_pairs = scatter_rel(pair_grads).astype(BF16)
    grad_text = dot_nt(grad_pairs, kv_part)
    kv_shard = scatter_fsdp(dot_tn(text_rows, grad_pairs))
    square_shard = scatter_fsdp(
        unspread(
            outer([self_tokens, cross_norm, cross_tokens], [self_branch, query_branch, cross_branch])
        )
    )
    qkv_shard = scatter_fsdp(dot_tn(first_all, grad_triples))
    _, shift_pull = jax.vjp(norm_shift, hidden, after(gain_rows[0], *earlier[1], down_shard), shift_vec)
    grad_hidden, grad_gain_self, grad_shift = shift_pull(grad_first_norm)
    grad_hidden = grad_hidden + grad_self_res
    vectors = jnp.concatenate([jnp.stack([grad_shift, grad_gain_self]), gain_grads])
    return (grad_hidden, grad_text, vectors, (qkv_shard, square_shard, kv_shard, up_shard, down_shard))


def gather_block(layer, qkv, query, text_kv, self_out, cross_out, up, down):
    s, seq_count = lax.axis_index("seq"), lax.axis_size("seq")
    fsdp_count = lax.axis_size("fsdp")
    squares = jnp.concatenate(
        [own_part(self_out[layer], 1), own_part(query[layer], 1), own_part(cross_out[layer], 1)],
        axis=1,
    )
    rows = down.shape[1] // seq_count
    return (
        gather_fsdp(own_part(qkv[layer], 3)),
        spread(gather_fsdp(squares)),
        gather_fsdp(own_part(text_kv[layer], 2)),
        gather_fsdp(own_part(up[layer], fsdp_count)),
        gather_fsdp(lax.dynamic_slice_in_dim(down[layer], s * rows, rows, 0)),
    )


def finish_block(scalars, shards, layer, before):
    qkv_shard, square_shard, kv_shard, up_shard, down_shard = shards
    fsdp_count = lax.axis_size("fsdp")
    if before is None:
        before = [None] * 5
    return [
        settle(scalars, gather_parts(qkv_shard), 3, 1, layer, 2, before[0]),
        settle(scalars, gather_parts(square_shard), 1, 3, layer, 2, before[1]),
        settle(scalars, gather_parts(kv_shard), 2, 1, layer, 2, before[2]),
        settle(scalars, gather_parts(up_shard), fsdp_count, 1, layer, 2, before[3]),
        settle_rows(scalars, gather_parts(down_shard), layer, 2, before[4]),
    ]


def sum_vectors(vectors):
    bits = 1
    while bits < lax.axis_size("seq"):
        vectors = vectors + swap_seq(vectors, bits)
        bits *= 2
    found, bits = vectors[None], 1
    while bits < lax.axis_size("fsdp"):
        found = jnp.concatenate([found, swap_fsdp(found, bits)], axis=0)
        bits *= 2
    return found


def body(
    latents,
    skip_input,
    text_tokens,
    text_lengths,
    condition,
    cotangent,
    mod_weight,
    norm_gains,
    qkv_weight,
    query_weight,
    text_kv_weight,
    self_out_weight,
    cross_out_weight,
    up_weight,
    down_weight,
    skip_gain,
    skip_weight,
):
    seq_count, fsdp_count = lax.axis_size("seq"), lax.axis_size("fsdp")
    s, f = lax.axis_index("seq"), lax.axis_index("fsdp")
    _, tok_rows, model_width = latents.shape
    shard_rows = mod_weight.shape[1]
    text_count = text_tokens.shape[1]
    padded = -(-text_count // 32) * 32
    text_rows = jnp.pad(text_tokens[0], ((0, padded - text_count), (0, 0)))
    scalars = jnp.stack(
        [*list_order(), *[s ^ j for j in range(seq_count)], f % 2, text_lengths[0]]
    ).astype(jnp.int32)

    gain_rows = jnp.concatenate(
        [norm_gains.reshape(-1, shard_rows), skip_gain.reshape(-1, shard_rows)], axis=0
    )
    small = jnp.concatenate(
        [
            condition.reshape(fsdp_count, 1, shard_rows),
            jnp.broadcast_to(gain_rows[None], (fsdp_count,) + gain_rows.shape),
        ],
        axis=1,
    ).astype(F32)
    small = lax.all_to_all(small, "fsdp", 0, 0, tiled=True)
    cond_part = small[:, 0]
    gains = jnp.swapaxes(small[:, 1:7], 0, 1).reshape(2, 3, model_width)
    skip_gains = small[:, 7:].reshape(2, model_width)
    silu_part = jax.nn.silu(cond_part)
    shift_terms = jnp.einsum("br,lrd->bld", silu_part, mod_weight.astype(F32), precision=EXACT)
    shifts = jnp.sum(lax.all_to_all(shift_terms, "fsdp", 0, 0, tiled=True), axis=0)

    stacks = (
        qkv_weight,
        query_weight,
        text_kv_weight,
        self_out_weight,
        cross_out_weight,
        up_weight,
        down_weight,
    )
    hidden = latents[0].astype(F32)
    all_hidden = jnp.concatenate(gather_rel(latents[0]), axis=0).astype(F32)
    first_weights = gather_block(0, *stacks)
    first_pairs = gather_rel(dot_nn(text_rows, first_weights[2]).astype(BF16))
    first_norm = norm_shift(all_hidden, gains[0, 0], shifts[0]).astype(BF16)
    first_out, first_saved = layer_forward(
        first_norm, hidden, scalars, gains[0], first_pairs, first_weights
    )
    skip_parts = spread(gather_fsdp(own_part(skip_weight, 1)))
    joined_norm, skip_out = skip_forward(scalars, skip_parts, first_out, skip_input[0], skip_gains)
    second_weights = gather_block(1, *stacks)
    second_pairs = gather_rel(dot_nn(text_rows, second_weights[2]).astype(BF16))
    second_norm = norm_shift(skip_out, gains[1, 0], shifts[1]).astype(BF16)
    second_norm = jnp.concatenate(gather_rel(second_norm), axis=0)
    final_out, second_saved = layer_forward(
        second_norm, skip_out, scalars, gains[1], second_pairs, second_weights
    )
    output = final_out.astype(BF16)

    grad_skip_out, text_second, vectors_second, shards_second = layer_backward(
        cotangent[0].astype(F32),
        second_saved,
        skip_out,
        shifts[1],
        scalars,
        gains[1],
        text_rows,
        second_pairs,
        second_weights,
        ((), ()),
    )
    skip_branch, grad_first_out, grad_skip, skip_gain_grads = skip_backward(
        scalars,
        skip_parts,
        first_out,
        skip_input[0],
        after(skip_gains, shards_second[3]),
        grad_skip_out,
    )
    skip_shard = scatter_fsdp(unspread(outer([joined_norm], [skip_branch])))
    second_done = finish_block(scalars, shards_second, 1, None)
    grad_latents, text_first, vectors_first, shards_first = layer_backward(
        grad_first_out,
        first_saved,
        hidden,
        shifts[0],
        scalars,
        gains[0],
        text_rows,
        first_pairs,
        first_weights,
        (
            (shards_second[2], shards_second[1]),
            (skip_shard, second_done[4][0], second_done[3][0], second_done[0][0]),
        ),
    )
    first_done = finish_block(scalars, shards_first, 0, second_done)
    (grad_qkv,), (grad_self_out, grad_query, grad_cross_out), (grad_kv,), (grad_up,), (grad_down,) = (
        first_done
    )
    (grad_skip_weight,) = settle(scalars, gather_parts(skip_shard), 1, 1, 0, 1)

    second_sums = sum_vectors(jnp.concatenate([vectors_second, skip_gain_grads]))
    first_sums = sum_vectors(vectors_first)
    shift_grads = jnp.stack([first_sums[:, 0], second_sums[:, 0]], axis=1)
    gain_sums = jnp.stack([first_sums[:, 1:4].sum(axis=0), second_sums[:, 1:4].sum(axis=0)])
    grad_norm_gains = lax.dynamic_slice_in_dim(gain_sums, f * shard_rows, shard_rows, 2)
    grad_skip_gain = lax.dynamic_slice_in_dim(
        second_sums[:, 4:].sum(axis=0).reshape(-1), f * skip_gain.shape[0], skip_gain.shape[0], 0
    )
    turned = jnp.stack(
        [lax.dynamic_index_in_dim(silu_part, f ^ j, 0, False) for j in range(fsdp_count)]
    )
    grad_mod = jnp.einsum("br,bld->lrd", turned, shift_grads, precision=EXACT)
    grad_silu = jnp.einsum("bld,lrd->br", shift_grads, mod_weight.astype(F32), precision=EXACT)
    grad_silu = jnp.stack(
        [lax.dynamic_index_in_dim(grad_silu, f ^ j, 0, False) for j in range(fsdp_count)]
    )
    _, silu_pull = jax.vjp(jax.nn.silu, cond_part)
    grad_cond_part = silu_pull(grad_silu)[0]
    grad_condition = lax.all_to_all(grad_cond_part, "fsdp", 0, 0, tiled=True).reshape(1, -1)

    text_sum = text_first + text_second
    width = text_sum.shape[1] // seq_count
    text_blocks = [
        lax.dynamic_slice_in_dim(text_sum, (s ^ j) * width, width, 1) for j in range(seq_count)
    ]
    (grad_text,) = settle(
        scalars, gather_parts(scatter_rel(text_blocks).astype(BF16)), 1, 1, 0, 1
    )
    return (
        output[None],
        grad_latents[None],
        grad_skip[None],
        grad_text[:, :text_count],
        grad_condition,
        grad_mod,
        grad_norm_gains,
        grad_qkv,
        grad_query,
        grad_kv,
        grad_self_out,
        grad_cross_out,
        grad_up,
        grad_down,
        grad_skip_gain,
        grad_skip_weight[0],
    )


def solution(mesh):
    in_specs = (
        P("fsdp", "seq", None),
        P("fsdp", "seq", None),
        P("fsdp", None, None),
        P("fsdp"),
        P("fsdp", None),
        P("fsdp", "seq", None),
        P(None, "fsdp", None),
        P(None, None, "fsdp"),
        P(None, "fsdp", None),
        P(None, "fsdp", None),
        P(None, "fsdp", None),
        P(None, "fsdp", None),
        P(None, "fsdp", None),
        P(None, "fsdp", None),
        P(None, "fsdp", None),
        P("fsdp"),
        P("fsdp", None),
    )
    out_specs = (
        P("fsdp", "seq", None),
        P("fsdp", "seq", None),
        P("fsdp", "seq", None),
        P("fsdp", None, None),
        P("fsdp", None),
        P(None, "fsdp", None),
        P(None, None, "fsdp"),
        P(None, "fsdp", None),
        P(None, "fsdp", None),
        P(None, "fsdp", None),
        P(None, "fsdp", None),
        P(None, "fsdp", None),
        P(None, "fsdp", None),
        P(None, "fsdp", None),
        P("fsdp"),
        P("fsdp", None),
    )
    return jax.shard_map(body, mesh=mesh, in_specs=in_specs, out_specs=out_specs, check_vma=False)
```

```python
import functools
import math

import jax
import jax.numpy as jnp
from jax import lax
from jax.experimental import pallas as pl
from jax.experimental.pallas import tpu as pltpu
from jax.sharding import PartitionSpec as P

H = 16
NORM_EPSILON = 1e-06
EXACT = lax.Precision.HIGHEST
BF16 = jnp.bfloat16
F32 = jnp.float32
LOG2_E = 1.4426950408889634
GELU_SCALE = math.sqrt(2.0 / math.pi)
VMEM_LIMIT = 56 * 1024 * 1024


def dot_nn(a, b):
    return lax.dot_general(a, b, (((1,), (0,)), ((), ())), preferred_element_type=F32)


def dot_nt(a, b):
    return lax.dot_general(a, b, (((1,), (1,)), ((), ())), preferred_element_type=F32)


def dot_tn(a, b):
    return lax.dot_general(a, b, (((0,), (0,)), ((), ())), preferred_element_type=F32)


def padded_width(width):
    return -(-width // 128) * 128


def call(kernel, outs, scratch, micros, *operands, scalars=None, deps=()):
    specs = [pl.BlockSpec(memory_space=pltpu.VMEM)] * len(operands)
    if scalars is not None:
        specs = [pl.BlockSpec(memory_space=pltpu.SMEM)] + specs
        operands = (scalars,) + tuple(operands)
    used, held = len(operands), len(deps)

    def run(*refs):
        kernel(*refs[:used], *refs[used + held :])

    return pl.pallas_call(
        run,
        out_shape=tuple(jax.ShapeDtypeStruct(s, d) for s, d in outs),
        in_specs=specs + [pl.BlockSpec(memory_space=pl.ANY)] * held,
        out_specs=tuple([pl.BlockSpec(memory_space=pltpu.VMEM)] * len(outs)),
        scratch_shapes=scratch,
        compiler_params=pltpu.CompilerParams(vmem_limit_bytes=VMEM_LIMIT),
        cost_estimate=pl.CostEstimate(
            flops=int(micros * 1.0e9), bytes_accessed=1000, transcendentals=0
        ),
    )(*operands, *deps)


def cut_of(rows):
    return rows // 32 * 16


def cuts(count, rows):
    return [(0, cut_of(rows)), (cut_of(rows), rows)] if count == 4 else [(0, rows)]


def pieces_of(count, rows):
    return [(j, low, high) for j in range(1, count) for low, high in cuts(count, rows)]


def put_pieces(refs, count, block, values):
    for ref, (j, low, high) in zip(refs, pieces_of(count, values.shape[0])):
        if j == block:
            ref[...] = values[low:high].astype(BF16)


def piece_shapes(count, rows, columns):
    return [((high - low, columns), BF16) for _, low, high in pieces_of(count, rows)]


def add_terms(count, refs):
    total = refs[0][...].astype(F32)
    if count != 4:
        for ref in refs[1:]:
            total = total + ref[...].astype(F32)
        return total
    for low, high in ((1, 2), (3, 4)):
        total = total + jnp.concatenate([refs[low][...], refs[high][...]], axis=0).astype(F32)
    return total


def norm_stats(values):
    mean = jnp.mean(values, axis=1, keepdims=True)
    centered = values - mean
    var = jnp.mean(centered * centered, axis=1, keepdims=True)
    scale = lax.rsqrt(var + NORM_EPSILON)
    return centered * scale, scale


def norm_back(values, gain, grad):
    unit, scale = norm_stats(values)
    grad_unit = grad * gain
    inner = jnp.mean(grad_unit * unit, axis=1, keepdims=True)
    grad_values = scale * (grad_unit - jnp.mean(grad_unit, axis=1, keepdims=True) - unit * inner)
    return grad_values, jnp.sum(grad * unit, axis=0, keepdims=True)


def self_forward_kernel(count, parts, head_size, normed, *refs):
    part_refs, refs = refs[:parts], refs[parts:]
    weight_ref, gains_ref, shift_ref = refs[:3]
    rows_ref, triples_ref = refs[3:5]
    mixed_refs = refs[5:]
    stride = weight_ref.shape[1] // 3
    rows, width = mixed_refs[0].shape
    factor = LOG2_E / math.sqrt(head_size)
    start = 0
    for ref in part_refs:
        values = ref[...]
        if not normed:
            unit, _ = norm_stats(values.astype(F32))
            values = (unit * gains_ref[0:1, :] + shift_ref[...]).astype(BF16)
        rows_ref[start : start + ref.shape[0], :] = values
        start += ref.shape[0]
    for j in range(count):
        at = slice(j * rows, (j + 1) * rows)
        triples_ref[at, :] = dot_nn(rows_ref[at, :], weight_ref[...]).astype(BF16)
    for j in range(count):
        at = slice(j * rows, (j + 1) * rows)
        for h in range(width // head_size):
            low = h * head_size
            q = triples_ref[at, low : low + head_size]
            k = triples_ref[:, stride + low : stride + low + head_size]
            v = triples_ref[:, 2 * stride + low : 2 * stride + low + head_size]
            scores = dot_nt(q, k)
            top = jnp.max(scores, axis=1, keepdims=True)
            weights = jnp.exp2((scores - top) * factor)
            total = jnp.sum(weights, axis=1, keepdims=True)
            mixed = dot_nn(weights.astype(BF16), v) * (1.0 / total)
            mixed_refs[j][:, low : low + head_size] = mixed.astype(BF16)


def self_forward(parts, weight, gains, shift, head_size, count, width, normed, deps=()):
    total = sum(m.shape[0] for m in parts)
    columns = parts[0].shape[1]
    found = call(
        functools.partial(self_forward_kernel, count, len(parts), head_size, normed),
        [((total, columns), BF16), ((total, weight.shape[1]), BF16)]
        + [((total // count, width), BF16)] * count,
        [],
        24,
        *parts,
        weight,
        gains,
        shift[None],
        deps=deps,
    )
    return found[0], found[1], list(found[2:])


def attention_back(q, k, v, grad, valid, head_size):
    factor = LOG2_E / math.sqrt(head_size)
    scores = dot_nt(k, q)
    if valid is not None:
        scores = jnp.where(valid, scores, -1e30)
    top = jnp.max(scores, axis=0, keepdims=True)
    weights = jnp.exp2((scores - top) * factor)
    weights = weights * (1.0 / jnp.sum(weights, axis=0, keepdims=True))
    grad_weights = dot_nt(v, grad)
    delta = jnp.sum(grad_weights * weights, axis=0, keepdims=True)
    grad_scores = (weights * (grad_weights - delta)).astype(BF16)
    scale = 1.0 / math.sqrt(head_size)
    return (
        dot_tn(grad_scores, k) * scale,
        dot_nn(grad_scores, q) * scale,
        dot_nn(weights.astype(BF16), grad),
    )


def self_backward_kernel(count, head_size, step, triples_ref, *refs):
    grad_refs, (weight_ref, out_ref, own_ref) = refs[:count], refs[count : count + 3]
    piece_refs, (keys_ref, values_ref) = refs[count + 3 : -2], refs[-2:]
    total = triples_ref.shape[0]
    rows, width = grad_refs[0].shape
    stride = weight_ref.shape[1] // 3
    for h in range(width // head_size):
        low = h * head_size
        k = triples_ref[:, stride + low : stride + low + head_size]
        v = triples_ref[:, 2 * stride + low : 2 * stride + low + head_size]
        for i in range(total // step):
            at = slice(i * step, (i + 1) * step)
            inside = (i * step) % rows
            q = triples_ref[at, low : low + head_size]
            grad = grad_refs[i * step // rows][inside : inside + step, low : low + head_size]
            grad_q, grad_k, grad_v = attention_back(q, k, v, grad, None, head_size)
            out_ref[at, low : low + head_size] = grad_q.astype(BF16)
            if i == 0:
                keys_ref[...] = grad_k
                values_ref[...] = grad_v
            else:
                keys_ref[...] += grad_k
                values_ref[...] += grad_v
        out_ref[:, stride + low : stride + low + head_size] = keys_ref[...].astype(BF16)
        out_ref[:, 2 * stride + low : 2 * stride + low + head_size] = values_ref[...].astype(BF16)
    if stride > width:
        for g in range(3):
            out_ref[:, g * stride + width : (g + 1) * stride] = jnp.zeros((total, stride - width), BF16)
    for j in range(count):
        found = dot_nt(out_ref[j * rows : (j + 1) * rows, :], weight_ref[...])
        if j == 0:
            own_ref[...] = found
        else:
            put_pieces(piece_refs, count, j, found)


def self_backward(triples, grads, weight, head_size, deps=()):
    count = len(grads)
    total, rows, columns = triples.shape[0], grads[0].shape[0], weight.shape[0]
    step = min(256, rows)
    found = call(
        functools.partial(self_backward_kernel, count, head_size, step),
        [(triples.shape, BF16), ((rows, columns), F32)] + piece_shapes(count, rows, columns),
        [pltpu.VMEM((total, head_size), F32), pltpu.VMEM((total, head_size), F32)],
        32,
        triples,
        *grads,
        weight,
        deps=deps,
    )
    return found[0], found[1], list(found[2:])


def fill_corner(count, matrix_refs, scalars_ref, corner_ref):
    if len(matrix_refs) == count:
        return list(matrix_refs)
    odd = scalars_ref[2 * count]
    half = matrix_refs[-1].shape[0]
    corner_ref[pl.ds(pl.multiple_of(odd * half, half), half), :] = matrix_refs[-2][...]
    corner_ref[pl.ds(pl.multiple_of((1 - odd) * half, half), half), :] = matrix_refs[-1][...]
    return list(matrix_refs[:-2]) + [corner_ref]


def corner_scratch(count, matrices):
    rows, columns = matrices[0].shape
    return pltpu.VMEM((rows, columns) if len(matrices) > count else (16, 128), BF16)


def fill_pairs(count, pair_refs, pairs_ref):
    padded = pairs_ref.shape[1]
    place = 0
    for ref in pair_refs:
        j, low = divmod(place, padded)
        pairs_ref[j, low : low + ref.shape[0], :] = ref[...]
        place += ref.shape[0]


def middle_forward_kernel(count, matrix_parts, pair_parts, head_size, scalars_ref, *refs):
    mixed_refs, refs = refs[:count], refs[count:]
    matrix_refs, refs = refs[:matrix_parts], refs[matrix_parts:]
    pair_refs, refs = refs[:pair_parts], refs[pair_parts:]
    hidden_ref, gains_ref = refs[:2]
    (self_ref, after_self_ref, norm_ref, queries_ref, cross_ref, after_cross_ref) = refs[2:8]
    mlp_refs = refs[8:-4]
    wide_ref, narrow_ref, corner_ref, pairs_ref = refs[-4:]
    width = mixed_refs[0].shape[1]
    stride = matrix_refs[0].shape[1] // 3
    matrices = fill_corner(count, matrix_refs, scalars_ref, corner_ref)
    fill_pairs(count, pair_refs, pairs_ref)
    order = [scalars_ref[i] for i in range(count)]
    relative = [scalars_ref[count + j] for j in range(count)]
    length = scalars_ref[2 * count + 1]
    spans = [slice(a * width, (a + 1) * width) for a in range(count)]

    for j in range(count):
        narrow_ref[relative[j]] = mixed_refs[j][...]
    for a in range(count):
        self_ref[:, spans[a]] = narrow_ref[a]
    tokens = self_ref[...]
    for i in range(count):
        wide_ref[order[i]] = dot_nn(tokens, matrices[i][:, :width])
    for a in range(count):
        after_self_ref[:, spans[a]] = hidden_ref[:, spans[a]].astype(F32) + wide_ref[a]
    normed = (norm_stats(after_self_ref[...])[0] * gains_ref[1:2, :]).astype(BF16)
    norm_ref[...] = normed
    for i in range(count):
        found = dot_nn(normed, matrices[i][:, stride : stride + width])
        queries_ref[order[i] ^ relative[0]] = found.astype(BF16)

    factor = LOG2_E / math.sqrt(head_size)
    keys_rows = pairs_ref.shape[1]
    valid = lax.broadcasted_iota(jnp.int32, (1, keys_rows), 1) < length
    pair_stride = pairs_ref.shape[2] // 2
    for j in range(count):
        for h in range(width // head_size):
            at = slice(h * head_size, (h + 1) * head_size)
            values_at = slice(pair_stride + h * head_size, pair_stride + (h + 1) * head_size)
            scores = dot_nt(queries_ref[j, :, at], pairs_ref[j, :, at])
            scores = jnp.where(valid, scores, -1e30)
            top = jnp.max(scores, axis=1, keepdims=True)
            weights = jnp.exp2((scores - top) * factor)
            total = jnp.sum(weights, axis=1, keepdims=True)
            mixed = dot_nn(weights.astype(BF16), pairs_ref[j, :, values_at]) * (1.0 / total)
            narrow_ref[relative[j], :, at] = mixed.astype(BF16)
    for a in range(count):
        cross_ref[:, spans[a]] = narrow_ref[a]
    tokens = cross_ref[...]
    for i in range(count):
        wide_ref[order[i]] = dot_nn(tokens, matrices[i][:, 2 * stride : 2 * stride + width])
    for a in range(count):
        after_cross_ref[:, spans[a]] = after_self_ref[:, spans[a]] + wide_ref[a]
    mlp_norm = norm_stats(after_cross_ref[...])[0] * gains_ref[2:3, :]
    for ref, (low, high) in zip(mlp_refs, cuts(count, mlp_norm.shape[0])):
        ref[...] = mlp_norm[low:high].astype(BF16)


def pairs_scratch(count, pairs):
    return pltpu.VMEM((count, sum(m.shape[0] for m in pairs) // count, pairs[0].shape[1]), BF16)


def middle_forward(scalars, mixed, matrices, pairs, hidden, gains, head_size, deps=()):
    count = len(mixed)
    rows, columns = hidden.shape
    width = columns // count
    found = call(
        functools.partial(
            middle_forward_kernel, count, len(matrices), len(pairs), head_size
        ),
        [
            ((rows, columns), BF16),
            ((rows, columns), F32),
            ((rows, columns), BF16),
            ((count, rows, width), BF16),
            ((rows, columns), BF16),
            ((rows, columns), F32),
        ]
        + [((high - low, columns), BF16) for low, high in cuts(count, rows)],
        [
            pltpu.VMEM((count, rows, width), F32),
            pltpu.VMEM((count, rows, width), BF16),
            corner_scratch(count, matrices),
            pairs_scratch(count, pairs),
        ],
        23,
        *mixed,
        *matrices,
        *pairs,
        hidden,
        gains,
        scalars=scalars,
        deps=deps,
    )
    return list(found[:6]) + [list(found[6:])]


def middle_backward_kernel(count, matrix_parts, pair_parts, terms, head_size, scalars_ref, *refs):
    matrix_refs, refs = refs[:matrix_parts], refs[matrix_parts:]
    pair_refs, refs = refs[:pair_parts], refs[pair_parts:]
    term_refs, refs = refs[:terms], refs[terms:]
    grad_out_ref, after_cross_ref, after_self_ref, queries_ref, gains_ref = refs[:5]
    out_ref, self_branch_ref, query_branch_ref, cross_branch_ref, gain_ref = refs[5:10]
    mixed_grad_refs, refs = refs[10 : 10 + count], refs[10 + count :]
    own_pairs_ref, pair_grad_refs = refs[0], refs[1:-6]
    wide_ref, narrow_ref, query_ref, corner_ref, pairs_ref, pair_total_ref = refs[-6:]
    width = queries_ref.shape[2]
    stride = matrix_refs[0].shape[1] // 3
    matrices = fill_corner(count, matrix_refs, scalars_ref, corner_ref)
    fill_pairs(count, pair_refs, pairs_ref)
    order = [scalars_ref[i] for i in range(count)]
    relative = [scalars_ref[count + j] for j in range(count)]
    length = scalars_ref[2 * count + 1]
    spans = [slice(a * width, (a + 1) * width) for a in range(count)]

    def back(branch_ref, group):
        columns = slice(group * stride, group * stride + width)
        total = dot_nt(branch_ref[0], matrices[0][:, columns])
        for i in range(1, count):
            total = total + dot_nt(branch_ref[i], matrices[i][:, columns])
        return total

    def divide(values):
        for a in range(count):
            narrow_ref[a] = values[:, spans[a]].astype(BF16)

    grad, grad_gain = norm_back(
        after_cross_ref[...], gains_ref[2:3, :], add_terms(count, term_refs)
    )
    gain_ref[1:2, :] = grad_gain
    wide_ref[...] = grad + grad_out_ref[...].astype(F32)
    divide(wide_ref[...])
    for i in range(count):
        cross_branch_ref[i] = narrow_ref[order[i]]
    divide(back(cross_branch_ref, 2))

    keys_rows = pairs_ref.shape[1]
    valid = lax.broadcasted_iota(jnp.int32, (keys_rows, 1), 0) < length
    pair_stride = pairs_ref.shape[2] // 2
    if pair_stride > width:
        for g in range(2):
            pair_total_ref[:, g * pair_stride + width : (g + 1) * pair_stride] = jnp.zeros(
                (keys_rows, pair_stride - width), F32
            )
    for j in range(count):
        for h in range(width // head_size):
            at = slice(h * head_size, (h + 1) * head_size)
            values_at = slice(pair_stride + h * head_size, pair_stride + (h + 1) * head_size)
            grad_q, grad_k, grad_v = attention_back(
                queries_ref[j, :, at],
                pairs_ref[j, :, at],
                pairs_ref[j, :, values_at],
                narrow_ref[relative[j], :, at],
                valid,
                head_size,
            )
            query_ref[j, :, at] = grad_q.astype(BF16)
            pair_total_ref[:, at] = grad_k
            pair_total_ref[:, values_at] = grad_v
        if j == 0:
            own_pairs_ref[...] = pair_total_ref[...]
        else:
            put_pieces(pair_grad_refs, count, j, pair_total_ref[...])
    for i in range(count):
        query_branch_ref[i] = query_ref[order[i] ^ relative[0]]
    grad, grad_gain = norm_back(after_self_ref[...], gains_ref[1:2, :], back(query_branch_ref, 1))
    gain_ref[0:1, :] = grad_gain
    out_ref[...] = grad + wide_ref[...]
    divide(out_ref[...])
    for i in range(count):
        self_branch_ref[i] = narrow_ref[order[i]]
    divide(back(self_branch_ref, 0))
    for j in range(count):
        mixed_grad_refs[j][...] = narrow_ref[relative[j]]


def middle_backward(
    scalars, matrices, pairs, terms, grad_out, after_cross, after_self, queries, gains, head_size, deps=()
):
    count, rows, width = queries.shape
    columns = count * width
    branch = ((count, rows, width), BF16)
    text = pairs_scratch(count, pairs)
    keys_rows, pair_columns = text.shape[1:]
    found = call(
        functools.partial(
            middle_backward_kernel, count, len(matrices), len(pairs), len(terms), head_size
        ),
        [((rows, columns), F32), branch, branch, branch, ((2, columns), F32)]
        + [((rows, width), BF16)] * count
        + [((keys_rows, pair_columns), F32)]
        + piece_shapes(count, keys_rows, pair_columns),
        [
            pltpu.VMEM((rows, columns), F32),
            pltpu.VMEM((count, rows, width), BF16),
            pltpu.VMEM((count, rows, width), BF16),
            corner_scratch(count, matrices),
            text,
            pltpu.VMEM((keys_rows, pair_columns), F32),
        ],
        37,
        *matrices,
        *pairs,
        *terms,
        grad_out,
        after_cross,
        after_self,
        queries,
        gains,
        scalars=scalars,
        deps=deps,
    )
    found = list(found)
    return found[:5] + [found[5 : 5 + count], found[5 + count], found[6 + count :]]


def mlp_forward_kernel(count, parts, *refs):
    part_refs, refs = refs[:parts], refs[parts:]
    up_ref, down_ref, rows_ref, up_rows_ref, activated_ref, own_ref = refs[:6]
    piece_refs = refs[6:]
    start = 0
    for ref in part_refs:
        rows_ref[start : start + ref.shape[0], :] = ref[...]
        start += ref.shape[0]
    rows = start // count
    for j in range(count - 1, -1, -1):
        at = slice(j * rows, (j + 1) * rows)
        values = dot_nn(rows_ref[at, :], up_ref[...])
        up_rows_ref[at, :] = values
        inner = GELU_SCALE * (values + 0.044715 * (values * values * values))
        activated_ref[at, :] = (0.5 * values * (1.0 + jnp.tanh(inner))).astype(BF16)
        found = dot_nn(activated_ref[at, :], down_ref[...])
        if j == 0:
            own_ref[...] = found
        else:
            put_pieces(piece_refs, count, j, found)


def mlp_forward(parts, up, down, count, deps=()):
    total, columns, hidden = sum(m.shape[0] for m in parts), up.shape[0], up.shape[1]
    rows = total // count
    found = call(
        functools.partial(mlp_forward_kernel, count, len(parts)),
        [
            ((total, columns), BF16),
            ((total, hidden), F32),
            ((total, hidden), BF16),
            ((rows, columns), F32),
        ]
        + piece_shapes(count, rows, columns),
        [],
        22,
        *parts,
        up,
        down,
        deps=deps,
    )
    return list(found[:4]) + [list(found[4:])]


def mlp_backward_kernel(count, parts, *refs):
    part_refs, refs = refs[:parts], refs[parts:]
    up_rows_ref, up_ref, down_ref, rows_ref, grad_up_ref, own_ref = refs[:6]
    piece_refs = refs[6:]
    start = 0
    for ref in part_refs:
        rows_ref[start : start + ref.shape[0], :] = ref[...]
        start += ref.shape[0]
    rows = start // count
    for j in range(count - 1, -1, -1):
        at = slice(j * rows, (j + 1) * rows)
        grad = dot_nt(rows_ref[at, :], down_ref[...])
        values = up_rows_ref[at, :]
        square = values * values
        bent = jnp.tanh(GELU_SCALE * (values + 0.044715 * (values * square)))
        slope = 0.5 * (1.0 + bent) + 0.5 * values * (1.0 - bent * bent) * (
            GELU_SCALE * (1.0 + 3.0 * 0.044715 * square)
        )
        grad_up_ref[at, :] = (grad * slope).astype(BF16)
        found = dot_nt(grad_up_ref[at, :], up_ref[...])
        if j == 0:
            own_ref[...] = found
        else:
            put_pieces(piece_refs, count, j, found)


def mlp_backward(parts, up_rows, up, down, count, deps=()):
    total, columns, hidden = sum(m.shape[0] for m in parts), up.shape[0], up.shape[1]
    rows = total // count
    found = call(
        functools.partial(mlp_backward_kernel, count, len(parts)),
        [((total, columns), BF16), ((total, hidden), BF16), ((rows, columns), F32)]
        + piece_shapes(count, rows, columns),
        [],
        22,
        *parts,
        up_rows,
        up,
        down,
        deps=deps,
    )
    return list(found[:3]) + [list(found[3:])]


def outer_kernel(count, groups, half, scalars_ref, *refs):
    rows_refs, branch_refs, refs = refs[:groups], refs[groups : 2 * groups], refs[2 * groups :]
    out_refs, turned_ref = refs[:-1], refs[-1]
    width = branch_refs[0].shape[2]
    stride = padded_width(width)
    odd = scalars_ref[2 * count]
    for g in range(groups):
        at = slice(g * stride, g * stride + width)
        turned_ref[...] = rows_refs[g][...].T
        out_refs[0][:, at] = dot_nn(turned_ref[...], branch_refs[g][0]).astype(BF16)
        for i in range(1, count):
            if not half:
                out_refs[i][:, at] = dot_nn(turned_ref[...], branch_refs[g][i]).astype(BF16)
                continue
            for k in range(2):
                low = pl.multiple_of((odd if k == 0 else 1 - odd) * half, half)
                found = dot_nn(turned_ref[pl.ds(low, half), :], branch_refs[g][i])
                out_refs[2 * i - 1 + k][:, at] = found.astype(BF16)
    if stride > width:
        for ref in out_refs:
            for g in range(groups):
                ref[:, g * stride + width : (g + 1) * stride] = jnp.zeros(
                    (ref.shape[0], stride - width), BF16
                )


def outer(scalars, rows, branches, deps=()):
    count, tokens, width = branches[0].shape
    groups, columns = len(rows), rows[0].shape[1]
    stride = padded_width(width)
    half = columns // 2 if count == 4 else 0
    shapes = [((columns, groups * stride), BF16)]
    if half:
        shapes += [((half, groups * stride), BF16)] * (2 * (count - 1))
    else:
        shapes = shapes * count
    return list(
        call(
            functools.partial(outer_kernel, count, groups, half),
            shapes,
            [pltpu.VMEM((columns, tokens), BF16)],
            3.5 * groups,
            *rows,
            *branches,
            scalars=scalars,
            deps=deps,
        )
    )


def join_kernel(count, scalars_ref, own_ref, mine_ref, other_ref, out_ref):
    odd = scalars_ref[2 * count]
    half = mine_ref.shape[0]
    for ref, place in ((mine_ref, odd), (other_ref, 1 - odd)):
        at = pl.ds(pl.multiple_of(place * half, half), half)
        out_ref[at, :] = (own_ref[at, :].astype(F32) + ref[...].astype(F32)).astype(BF16)


def join_halves(scalars, own, mine, other):
    count = lax.axis_size("seq")
    (found,) = call(
        functools.partial(join_kernel, count),
        [(own.shape, BF16)],
        [],
        4,
        own,
        mine,
        other,
        scalars=scalars,
    )
    return found


def joined_stats(first, second):
    count = first.shape[1] + second.shape[1]
    mean = (jnp.sum(first, axis=1, keepdims=True) + jnp.sum(second, axis=1, keepdims=True)) / count
    first, second = first - mean, second - mean
    var = (
        jnp.sum(first * first, axis=1, keepdims=True)
        + jnp.sum(second * second, axis=1, keepdims=True)
    ) / count
    scale = lax.rsqrt(var + NORM_EPSILON)
    return first * scale, second * scale, scale


def skip_forward_kernel(count, matrix_parts, terms, scalars_ref, *refs):
    matrix_refs, refs = refs[:matrix_parts], refs[matrix_parts:]
    term_refs, refs = refs[:terms], refs[terms:]
    residual_ref, second_ref, gains_ref, next_ref, shift_ref = refs[:5]
    first_ref, joined_ref, out_ref = refs[5:8]
    norm_refs, (wide_ref, corner_ref) = refs[8:-2], refs[-2:]
    rows, columns = first_ref.shape
    width = columns // count
    matrices = fill_corner(count, matrix_refs, scalars_ref, corner_ref)
    first_ref[...] = residual_ref[...] + add_terms(count, term_refs)
    first, second, _ = joined_stats(first_ref[...], second_ref[...].astype(F32))
    joined_ref[:, :columns] = (first * gains_ref[0:1, :]).astype(BF16)
    joined_ref[:, columns:] = (second * gains_ref[1:2, :]).astype(BF16)
    joined = joined_ref[...]
    for i in range(count):
        wide_ref[scalars_ref[i]] = dot_nn(joined, matrices[i][:, :width])
    for a in range(count):
        out_ref[:, a * width : (a + 1) * width] = wide_ref[a]
    normed = norm_stats(out_ref[...])[0] * next_ref[0:1, :] + shift_ref[...]
    for ref, (low, high) in zip(norm_refs, cuts(count, rows)):
        ref[...] = normed[low:high].astype(BF16)


def skip_forward(scalars, matrices, terms, residual, second, gains, next_gains, shift, deps=()):
    rows, columns = residual.shape
    count = lax.axis_size("seq")
    found = call(
        functools.partial(skip_forward_kernel, count, len(matrices), len(terms)),
        [((rows, columns), F32), ((rows, 2 * columns), BF16), ((rows, columns), F32)]
        + [((high - low, columns), BF16) for low, high in cuts(count, rows)],
        [pltpu.VMEM((count, rows, columns // count), F32), corner_scratch(count, matrices)],
        11,
        *matrices,
        *terms,
        residual,
        second,
        gains,
        next_gains,
        shift[None],
        scalars=scalars,
        deps=deps,
    )
    return list(found[:3]) + [list(found[3:])]


def skip_backward_kernel(count, matrix_parts, terms, scalars_ref, *refs):
    matrix_refs, refs = refs[:matrix_parts], refs[matrix_parts:]
    term_refs, refs = refs[:terms], refs[terms:]
    hidden_ref, next_ref, residual_ref, first_ref, second_ref, gains_ref = refs[:6]
    branch_ref, grad_first_ref, grad_second_ref, vectors_ref = refs[6:10]
    half_refs, (narrow_ref, corner_ref) = refs[10:-2], refs[-2:]
    rows, columns = first_ref.shape
    width = columns // count
    matrices = fill_corner(count, matrix_refs, scalars_ref, corner_ref)
    grad_norm = add_terms(count, term_refs)
    vectors_ref[0:1, :] = jnp.sum(grad_norm, axis=0, keepdims=True)
    grad, grad_gain = norm_back(hidden_ref[...], next_ref[0:1, :], grad_norm)
    vectors_ref[1:2, :] = grad_gain
    grad = grad + residual_ref[...]
    for a in range(count):
        narrow_ref[a] = grad[:, a * width : (a + 1) * width].astype(BF16)
    for i in range(count):
        branch_ref[i] = narrow_ref[scalars_ref[i]]

    def back(at):
        total = dot_nt(branch_ref[0], matrices[0][at, :width])
        for i in range(1, count):
            total = total + dot_nt(branch_ref[i], matrices[i][at, :width])
        return total

    grad_first_ref[...] = back(slice(0, columns))
    grad_second_ref[...] = back(slice(columns, 2 * columns))
    first, second, scale = joined_stats(first_ref[...], second_ref[...].astype(F32))
    vectors_ref[2:3, :] = jnp.sum(grad_first_ref[...] * first, axis=0, keepdims=True)
    vectors_ref[3:4, :] = jnp.sum(grad_second_ref[...] * second, axis=0, keepdims=True)
    grad_first = grad_first_ref[...] * gains_ref[0:1, :]
    grad_second = grad_second_ref[...] * gains_ref[1:2, :]
    mean = (
        jnp.sum(grad_first, axis=1, keepdims=True) + jnp.sum(grad_second, axis=1, keepdims=True)
    ) / (2 * columns)
    inner = (
        jnp.sum(grad_first * first, axis=1, keepdims=True)
        + jnp.sum(grad_second * second, axis=1, keepdims=True)
    ) / (2 * columns)
    grad_first_ref[...] = scale * (grad_first - mean - first * inner)
    grad_second_ref[...] = scale * (grad_second - mean - second * inner)
    for ref, (low, high) in zip(half_refs, cuts(count, rows)):
        ref[...] = grad_first_ref[low:high, :].astype(BF16)


def skip_backward(
    scalars, matrices, terms, hidden, next_gains, residual, first, second, gains, deps=()
):
    rows, columns = first.shape
    count = lax.axis_size("seq")
    narrow = (count, rows, columns // count)
    found = call(
        functools.partial(skip_backward_kernel, count, len(matrices), len(terms)),
        [
            (narrow, BF16),
            ((rows, columns), F32),
            ((rows, columns), F32),
            ((4, columns), F32),
        ]
        + [((high - low, columns), BF16) for low, high in cuts(count, rows)],
        [pltpu.VMEM(narrow, BF16), corner_scratch(count, matrices)],
        15,
        *matrices,
        *terms,
        hidden,
        next_gains,
        residual,
        first,
        second,
        gains,
        scalars=scalars,
        deps=deps,
    )
    return list(found[:4]) + [list(found[4:])]


def open_backward_kernel(count, terms, *refs):
    term_refs, refs = refs[:terms], refs[terms:]
    hidden_ref, gains_ref, residual_ref, out_ref, vectors_ref = refs
    grad_norm = add_terms(count, term_refs)
    vectors_ref[0:1, :] = jnp.sum(grad_norm, axis=0, keepdims=True)
    grad, grad_gain = norm_back(hidden_ref[...].astype(F32), gains_ref[0:1, :], grad_norm)
    vectors_ref[1:2, :] = grad_gain
    out_ref[...] = grad + residual_ref[...]


def open_backward(terms, hidden, gains, residual, deps=()):
    count = lax.axis_size("seq")
    return call(
        functools.partial(open_backward_kernel, count, len(terms)),
        [(residual.shape, F32), ((2, residual.shape[1]), F32)],
        [],
        5,
        *terms,
        hidden,
        gains,
        residual,
        deps=deps,
    )


def close_kernel(count, terms, *refs):
    refs[terms + 1][...] = (refs[terms][...] + add_terms(count, refs[:terms])).astype(BF16)


def close_forward(terms, residual, deps=()):
    count = lax.axis_size("seq")
    (found,) = call(
        functools.partial(close_kernel, count, len(terms)),
        [(residual.shape, BF16)],
        [],
        3,
        *terms,
        residual,
        deps=deps,
    )
    return found


def settle_kernel(count, parts, groups, pieces, width, scalars_ref, *refs):
    block_refs, refs = refs[:parts], refs[parts:]
    out_refs, stack_ref = refs[-pieces - 1 : -1], refs[-1]
    stride = stack_ref.shape[2] // (pieces * groups)
    for j in range(count):
        owner = scalars_ref[count + j]
        if j == count - 1 and parts > count:
            cut = block_refs[j].shape[0]
            stack_ref[owner, :cut] = block_refs[j][...]
            stack_ref[owner, cut:] = block_refs[j + 1][...]
        else:
            stack_ref[owner] = block_refs[j][...]
    for p in range(pieces):
        for g in range(groups):
            for a in range(count):
                low = (p * groups + g) * stride
                at = (g * count + a) * width
                out_refs[p][0, :, at : at + width] = stack_ref[a, :, low : low + width].astype(F32)


def settle_rows_kernel(count, parts, scalars_ref, *refs):
    block_refs, out_ref = refs[:parts], refs[-1]
    rows = block_refs[0].shape[0]
    for j in range(count):
        low = pl.multiple_of(scalars_ref[count + j] * rows, rows)
        if j == count - 1 and parts > count:
            cut = block_refs[j].shape[0]
            out_ref[0, pl.ds(low, cut), :] = block_refs[j][...].astype(F32)
            out_ref[0, pl.ds(low + cut, rows - cut), :] = block_refs[j + 1][...].astype(F32)
        else:
            out_ref[0, pl.ds(low, rows), :] = block_refs[j][...].astype(F32)


def settle_call(kernel, scalars, blocks, shape, pieces, layer, layer_count, before, scratch):
    held = [] if before is None else list(before)
    inputs = [pl.BlockSpec(memory_space=pltpu.VMEM)] * len(blocks)
    inputs += [pl.BlockSpec(memory_space=pl.ANY)] * len(held)
    found = pl.pallas_call(
        kernel,
        grid=(1,),
        out_shape=[jax.ShapeDtypeStruct((layer_count,) + shape, F32)] * pieces,
        in_specs=[pl.BlockSpec(memory_space=pltpu.SMEM)] + inputs,
        out_specs=[pl.BlockSpec((1,) + shape, lambda i: (layer, 0, 0))] * pieces,
        scratch_shapes=scratch,
        input_output_aliases={1 + len(blocks) + i: i for i in range(len(held))},
        compiler_params=pltpu.CompilerParams(vmem_limit_bytes=VMEM_LIMIT),
        cost_estimate=pl.CostEstimate(flops=4_000_000_000, bytes_accessed=1000, transcendentals=0),
    )(scalars, *blocks, *held)
    return list(found)


def settle(scalars, blocks, groups, pieces, width, layer, layer_count, before=None):
    count = lax.axis_size("seq")
    rows, columns = blocks[0].shape
    return settle_call(
        functools.partial(settle_kernel, count, len(blocks), groups, pieces, width),
        scalars,
        blocks,
        (rows, count * groups * width),
        pieces,
        layer,
        layer_count,
        before,
        [pltpu.VMEM((count, rows, columns), BF16)],
    )


def settle_rows(scalars, blocks, layer, layer_count, before=None):
    count = lax.axis_size("seq")
    rows, columns = blocks[0].shape
    return settle_call(
        functools.partial(settle_rows_kernel, count, len(blocks)),
        scalars,
        blocks,
        (count * rows, columns),
        1,
        layer,
        layer_count,
        before,
        [],
    )


def swap_seq(block, bits):
    seq_count = lax.axis_size("seq")
    return lax.ppermute(block, "seq", [(i, i ^ bits) for i in range(seq_count)])


def swap_fsdp(block, bits):
    fsdp_count = lax.axis_size("fsdp")
    return lax.ppermute(block, "fsdp", [(i, i ^ bits) for i in range(fsdp_count)])


def swap_core(block):
    return swap_fsdp(block, 1)


def swap_by_core(block, even_bits, odd_bits):
    seq_count, fsdp_count = lax.axis_size("seq"), lax.axis_size("fsdp")
    pairs = []
    for s in range(seq_count):
        for f in range(fsdp_count):
            other = s ^ (odd_bits if f % 2 else even_bits)
            pairs.append((s * fsdp_count + f, other * fsdp_count + f))
    return lax.ppermute(block, ("seq", "fsdp"), pairs)


def add_bf16(*terms):
    total = terms[0].astype(F32)
    for term in terms[1:]:
        total = total + term.astype(F32)
    return total.astype(BF16)


def halves_of(block):
    return [block[low:high] for low, high in cuts(lax.axis_size("seq"), block.shape[0])]


def gather_halves(halves):
    seq_count = lax.axis_size("seq")
    if seq_count != 4:
        return [halves[0]] + [swap_seq(halves[0], j) for j in range(1, seq_count)]
    top, bottom = halves
    y_top, x_bottom = swap_seq(top, 2), swap_seq(bottom, 1)
    x_top, y_bottom = swap_seq(top, 1), swap_seq(bottom, 2)
    return [top, bottom, x_top, x_bottom, y_top, y_bottom, swap_seq(y_top, 1), swap_seq(x_bottom, 2)]


def scatter_parts(own, pieces):
    seq_count = lax.axis_size("seq")
    if seq_count != 4:
        return [own] + [swap_seq(m, j + 1) for j, m in enumerate(pieces)]
    x_top, x_bottom, y_top, y_bottom, corner_top, corner_bottom = pieces
    by_x, by_y = swap_seq(corner_top, 1), swap_seq(corner_bottom, 2)
    from_x_top, from_y_bottom = swap_seq(x_top, 1), swap_seq(y_bottom, 2)
    from_y_top = swap_seq(add_bf16(y_top, by_x), 2)
    from_x_bottom = swap_seq(add_bf16(x_bottom, by_y), 1)
    return [own, from_x_top, from_x_bottom, from_y_top, from_y_bottom]


def exchange_rel(blocks):
    return [blocks[0]] + [swap_seq(blocks[j], j) for j in range(1, len(blocks))]


def gather_parts(block):
    seq_count = lax.axis_size("seq")
    if seq_count != 4:
        return [block] + [swap_seq(block, j) for j in range(1, seq_count)]
    cut = cut_of(block.shape[0])
    from_x, from_y = swap_seq(block, 1), swap_seq(block, 2)
    return [block, from_x, from_y, swap_seq(from_y[:cut], 1), swap_seq(from_x[cut:], 2)]


def list_order():
    s, seq_count = lax.axis_index("seq"), lax.axis_size("seq")
    if seq_count != 4:
        return [s ^ j for j in range(seq_count)]
    odd = lax.axis_index("fsdp") % 2
    return [s, s ^ (1 + odd), s ^ (2 - odd), s ^ 3]


def spread(block):
    seq_count = lax.axis_size("seq")
    if seq_count != 4:
        return [block] + [swap_seq(block, j) for j in range(1, seq_count)]
    odd = lax.axis_index("fsdp") % 2
    half = block.shape[0] // 2
    first = swap_by_core(block, 1, 2)
    part = swap_by_core(lax.dynamic_slice_in_dim(first, odd * half, half, 0), 2, 1)
    return [block, first, swap_core(first), part, swap_core(part)]


def unspread(scalars, blocks):
    seq_count = lax.axis_size("seq")
    if seq_count != 4:
        return add_bf16(blocks[0], *[swap_seq(blocks[j], j) for j in range(1, seq_count)])
    own, first_mine, first_other, second_mine, second_other, corner_mine, corner_other = blocks
    passed = swap_by_core(add_bf16(corner_mine, swap_core(corner_other)), 2, 1)
    other = swap_by_core(add_bf16(first_other, swap_core(second_mine)), 1, 2)
    mine = swap_by_core(add_bf16(first_mine, swap_core(second_other), passed), 1, 2)
    return join_halves(scalars, own, mine, other)


def own_part(matrix, groups, padded):
    s, seq_count = lax.axis_index("seq"), lax.axis_size("seq")
    width = matrix.shape[1] // (groups * seq_count)
    parts = [
        jnp.pad(
            lax.dynamic_slice_in_dim(matrix, (g * seq_count + s) * width, width, 1),
            ((0, 0), (0, padded - width)),
        )
        for g in range(groups)
    ]
    return jnp.concatenate(parts, axis=1)


def gather_fsdp(shard):
    return lax.all_gather(shard, "fsdp", axis=0, tiled=True)


def scatter_fsdp(full):
    return lax.psum_scatter(full.astype(BF16), "fsdp", scatter_dimension=0, tiled=True)


def text_pairs(text_rows, kv_part):
    return gather_halves([dot_nn(m, kv_part).astype(BF16) for m in halves_of(text_rows)])


def layer_forward(parts, hidden, scalars, gains, shift, pairs, weights, normed, deps):
    qkv_part, square_parts, _, up_part, down_part = weights
    seq_count = lax.axis_size("seq")
    tok_rows, model_width = hidden.shape
    head_size, width = model_width // H, model_width // seq_count
    first_all, triples, mixed = self_forward(
        parts, qkv_part, gains, shift, head_size, seq_count, width, normed, deps[0]
    )
    self_tokens, after_self, cross_norm, queries, cross_tokens, after_cross, mlp_halves = (
        middle_forward(
            scalars, exchange_rel(mixed), square_parts, pairs, hidden, gains, head_size, deps[1]
        )
    )
    mlp_all, up_rows, activated, own, pieces = mlp_forward(
        gather_halves(mlp_halves), up_part, down_part, seq_count, deps[2]
    )
    saved = (
        first_all,
        triples,
        self_tokens,
        after_self,
        cross_norm,
        queries,
        cross_tokens,
        after_cross,
        mlp_all,
        up_rows,
        activated,
    )
    return (scatter_parts(own, pieces), saved)


def layer_backward(out_parts, grad_out, saved, scalars, gains, text_rows, pairs, weights, deps):
    qkv_part, square_parts, kv_part, up_part, down_part = weights
    (
        first_all,
        triples,
        self_tokens,
        after_self,
        cross_norm,
        queries,
        cross_tokens,
        after_cross,
        mlp_all,
        up_rows,
        activated,
    ) = saved
    seq_count = lax.axis_size("seq")
    head_size = after_self.shape[1] // H

    out_all, grad_up_rows, own, pieces = mlp_backward(
        out_parts, up_rows, up_part, down_part, seq_count, deps[0]
    )
    terms = scatter_parts(own, pieces)
    grad_down = dot_tn(activated, out_all).astype(BF16)
    grad_up = dot_tn(mlp_all, grad_up_rows).astype(BF16)
    (
        grad_after_self,
        self_branch,
        query_branch,
        cross_branch,
        gain_grads,
        mixed_grads,
        own_pairs,
        pair_pieces,
    ) = middle_backward(
        scalars,
        square_parts,
        pairs,
        terms,
        grad_out,
        after_cross,
        after_self,
        queries,
        gains,
        head_size,
        (grad_down, grad_up) + deps[1],
    )
    squares = outer(
        scalars,
        [self_tokens, cross_norm, cross_tokens],
        [self_branch, query_branch, cross_branch],
    )
    grad_triples, own, pieces = self_backward(
        triples, exchange_rel(mixed_grads), qkv_part, head_size, (squares[0],) + deps[2]
    )
    terms = scatter_parts(own, pieces)
    grad_qkv = dot_tn(first_all, grad_triples).astype(BF16)
    pair_terms = scatter_parts(own_pairs, pair_pieces)
    if seq_count == 4:
        grad_pairs = jnp.concatenate(
            [
                add_bf16(pair_terms[0][low:high], pair_terms[1 + k], pair_terms[3 + k])
                for k, (low, high) in enumerate(cuts(seq_count, text_rows.shape[0]))
            ]
        )
    else:
        grad_pairs = add_bf16(*pair_terms)
    grad_text = dot_nt(grad_pairs, kv_part)
    shards = (
        scatter_fsdp(grad_qkv),
        scatter_fsdp(unspread(scalars, squares)),
        scatter_fsdp(dot_tn(text_rows, grad_pairs)),
        scatter_fsdp(grad_up),
        scatter_fsdp(grad_down),
    )
    return (terms, grad_after_self, gain_grads, grad_text, shards, grad_qkv)


def gather_block(layer, qkv, query, text_kv, self_out, cross_out, up, down):
    s, seq_count = lax.axis_index("seq"), lax.axis_size("seq")
    fsdp_count = lax.axis_size("fsdp")
    padded = padded_width(query.shape[2] // seq_count)
    squares = jnp.concatenate(
        [own_part(m[layer], 1, padded) for m in (self_out, query, cross_out)], axis=1
    )
    rows = down.shape[1] // seq_count
    return (
        gather_fsdp(own_part(qkv[layer], 3, padded)),
        spread(gather_fsdp(squares)),
        gather_fsdp(own_part(text_kv[layer], 2, padded)),
        gather_fsdp(own_part(up[layer], fsdp_count, up.shape[2] // (fsdp_count * seq_count))),
        gather_fsdp(lax.dynamic_slice_in_dim(down[layer], s * rows, rows, 0)),
    )


def finish_block(scalars, shards, width, layer, before):
    qkv_shard, square_shard, kv_shard, up_shard, down_shard = shards
    fsdp_count = lax.axis_size("fsdp")
    if before is None:
        before = [None] * 5
    up_width = up_shard.shape[1] // fsdp_count
    return [
        settle(scalars, gather_parts(qkv_shard), 3, 1, width, layer, 2, before[0]),
        settle(scalars, gather_parts(square_shard), 1, 3, width, layer, 2, before[1]),
        settle(scalars, gather_parts(kv_shard), 2, 1, width, layer, 2, before[2]),
        settle(scalars, gather_parts(up_shard), fsdp_count, 1, up_width, layer, 2, before[3]),
        settle_rows(scalars, gather_parts(down_shard), layer, 2, before[4]),
    ]


def sum_vectors(vectors):
    bits = 1
    while bits < lax.axis_size("seq"):
        vectors = vectors + swap_seq(vectors, bits)
        bits *= 2
    found, bits = vectors[None], 1
    while bits < lax.axis_size("fsdp"):
        found = jnp.concatenate([found, swap_fsdp(found, bits)], axis=0)
        bits *= 2
    return found


def body(
    latents,
    skip_input,
    text_tokens,
    text_lengths,
    condition,
    cotangent,
    mod_weight,
    norm_gains,
    qkv_weight,
    query_weight,
    text_kv_weight,
    self_out_weight,
    cross_out_weight,
    up_weight,
    down_weight,
    skip_gain,
    skip_weight,
):
    seq_count, fsdp_count = lax.axis_size("seq"), lax.axis_size("fsdp")
    s, f = lax.axis_index("seq"), lax.axis_index("fsdp")
    _, tok_rows, model_width = latents.shape
    width = model_width // seq_count
    shard_rows = mod_weight.shape[1]
    text_count = text_tokens.shape[1]
    padded = -(-text_count // 32) * 32
    text_rows = jnp.pad(text_tokens[0], ((0, padded - text_count), (0, 0)))
    scalars = jnp.stack(
        [*list_order(), *[s ^ j for j in range(seq_count)], f % 2, text_lengths[0]]
    ).astype(jnp.int32)

    gain_rows = jnp.concatenate(
        [norm_gains.reshape(-1, shard_rows), skip_gain.reshape(-1, shard_rows)], axis=0
    )
    small = jnp.concatenate(
        [
            condition.reshape(fsdp_count, 1, shard_rows),
            jnp.broadcast_to(gain_rows[None], (fsdp_count,) + gain_rows.shape),
        ],
        axis=1,
    ).astype(F32)
    small = lax.all_to_all(small, "fsdp", 0, 0, tiled=True)
    cond_part = small[:, 0]
    gains = jnp.swapaxes(small[:, 1:7], 0, 1).reshape(2, 3, model_width)
    skip_gains = small[:, 7:].reshape(2, model_width)
    silu_part = jax.nn.silu(cond_part)
    shift_terms = jnp.einsum("br,lrd->bld", silu_part, mod_weight.astype(F32), precision=EXACT)
    shifts = jnp.sum(lax.all_to_all(shift_terms, "fsdp", 0, 0, tiled=True), axis=0)

    stacks = (
        qkv_weight,
        query_weight,
        text_kv_weight,
        self_out_weight,
        cross_out_weight,
        up_weight,
        down_weight,
    )
    first_weights = gather_block(0, *stacks)
    first_pairs = text_pairs(text_rows, first_weights[2])
    first_terms, first_saved = layer_forward(
        gather_halves(halves_of(latents[0])),
        latents[0],
        scalars,
        gains[0],
        shifts[0],
        first_pairs,
        first_weights,
        False,
        ((), (), ()),
    )
    out_parts = gather_halves(halves_of(cotangent[0]))
    skip_parts = spread(
        gather_fsdp(own_part(skip_weight, 1, padded_width(width)))
    )
    first_out, joined_norm, skip_out, second_halves = skip_forward(
        scalars,
        skip_parts,
        first_terms,
        first_saved[7],
        skip_input[0],
        skip_gains,
        gains[1],
        shifts[1],
        (out_parts[-1], out_parts[-2]),
    )
    second_weights = gather_block(1, *stacks)
    second_pairs = text_pairs(text_rows, second_weights[2])
    second_terms, second_saved = layer_forward(
        gather_halves(second_halves),
        skip_out,
        scalars,
        gains[1],
        shifts[1],
        second_pairs,
        second_weights,
        True,
        ((), (), ()),
    )
    output = close_forward(second_terms, second_saved[7])

    terms, grad_after_self, gain_grads, text_second, shards_second, grad_qkv = layer_backward(
        out_parts,
        cotangent[0],
        second_saved,
        scalars,
        gains[1],
        text_rows,
        second_pairs,
        second_weights,
        ((), (), ()),
    )
    skip_branch, grad_first_out, grad_skip, vectors, first_halves = skip_backward(
        scalars,
        skip_parts,
        terms,
        skip_out,
        gains[1],
        grad_after_self,
        first_out,
        skip_input[0],
        skip_gains,
        (grad_qkv,),
    )
    vectors_second = jnp.concatenate([vectors[:2], gain_grads, vectors[2:]], axis=0)
    skip_shard = scatter_fsdp(
        unspread(scalars, outer(scalars, [joined_norm], [skip_branch]))
    )
    second_done = finish_block(scalars, shards_second, width, 1, None)
    terms, grad_after_self, gain_grads, text_first, shards_first, grad_qkv = layer_backward(
        gather_halves(first_halves),
        grad_first_out,
        first_saved,
        scalars,
        gains[0],
        text_rows,
        first_pairs,
        first_weights,
        (
            (shards_second[4], shards_second[3]),
            (shards_second[2], shards_second[1]),
            (shards_second[0], second_done[4][0], second_done[3][0]),
        ),
    )
    grad_latents, vectors = open_backward(
        terms, latents[0], gains[0], grad_after_self, (grad_qkv, skip_shard, second_done[0][0])
    )
    vectors_first = jnp.concatenate([vectors, gain_grads], axis=0)
    first_done = finish_block(scalars, shards_first, width, 0, second_done)
    (grad_qkv,), (grad_self_out, grad_query, grad_cross_out), (grad_kv,), (grad_up,), (grad_down,) = (
        first_done
    )
    (grad_skip_weight,) = settle(scalars, gather_parts(skip_shard), 1, 1, width, 0, 1)

    second_sums = sum_vectors(vectors_second)
    first_sums = sum_vectors(vectors_first)
    shift_grads = jnp.stack([first_sums[:, 0], second_sums[:, 0]], axis=1)
    gain_sums = jnp.stack([first_sums[:, 1:4].sum(axis=0), second_sums[:, 1:4].sum(axis=0)])
    grad_norm_gains = lax.dynamic_slice_in_dim(gain_sums, f * shard_rows, shard_rows, 2)
    grad_skip_gain = lax.dynamic_slice_in_dim(
        second_sums[:, 4:].sum(axis=0).reshape(-1), f * skip_gain.shape[0], skip_gain.shape[0], 0
    )
    turned = jnp.stack(
        [lax.dynamic_index_in_dim(silu_part, f ^ j, 0, False) for j in range(fsdp_count)]
    )
    grad_mod = jnp.einsum("br,bld->lrd", turned, shift_grads, precision=EXACT)
    grad_silu = jnp.einsum("bld,lrd->br", shift_grads, mod_weight.astype(F32), precision=EXACT)
    grad_silu = jnp.stack(
        [lax.dynamic_index_in_dim(grad_silu, f ^ j, 0, False) for j in range(fsdp_count)]
    )
    _, silu_pull = jax.vjp(jax.nn.silu, cond_part)
    grad_cond_part = silu_pull(grad_silu)[0]
    grad_condition = lax.all_to_all(grad_cond_part, "fsdp", 0, 0, tiled=True).reshape(1, -1)

    text_sum, bits = text_first + text_second, 1
    while bits < seq_count:
        text_sum = text_sum + swap_seq(text_sum.astype(BF16), bits).astype(F32)
        bits *= 2
    return (
        output[None],
        grad_latents[None],
        grad_skip[None],
        text_sum[None, :text_count],
        grad_condition,
        grad_mod,
        grad_norm_gains,
        grad_qkv,
        grad_query,
        grad_kv,
        grad_self_out,
        grad_cross_out,
        grad_up,
        grad_down,
        grad_skip_gain,
        grad_skip_weight[0],
    )


def solution(mesh):
    in_specs = (
        P("fsdp", "seq", None),
        P("fsdp", "seq", None),
        P("fsdp", None, None),
        P("fsdp"),
        P("fsdp", None),
        P("fsdp", "seq", None),
        P(None, "fsdp", None),
        P(None, None, "fsdp"),
        P(None, "fsdp", None),
        P(None, "fsdp", None),
        P(None, "fsdp", None),
        P(None, "fsdp", None),
        P(None, "fsdp", None),
        P(None, "fsdp", None),
        P(None, "fsdp", None),
        P("fsdp"),
        P("fsdp", None),
    )
    out_specs = (
        P("fsdp", "seq", None),
        P("fsdp", "seq", None),
        P("fsdp", "seq", None),
        P("fsdp", None, None),
        P("fsdp", None),
        P(None, "fsdp", None),
        P(None, None, "fsdp"),
        P(None, "fsdp", None),
        P(None, "fsdp", None),
        P(None, "fsdp", None),
        P(None, "fsdp", None),
        P(None, "fsdp", None),
        P(None, "fsdp", None),
        P(None, "fsdp", None),
        P("fsdp"),
        P("fsdp", None),
    )
    return jax.shard_map(body, mesh=mesh, in_specs=in_specs, out_specs=out_specs, check_vma=False)
```

```python
import functools
import math

import jax
import jax.numpy as jnp
from jax import lax
from jax.experimental import pallas as pl
from jax.experimental.pallas import tpu as pltpu
from jax.sharding import PartitionSpec as P

H = 16
NORM_EPSILON = 1e-06
EXACT = lax.Precision.HIGHEST
BF16 = jnp.bfloat16
F32 = jnp.float32
LOG2_E = 1.4426950408889634
GELU_SCALE = math.sqrt(2.0 / math.pi)
VMEM_LIMIT = 56 * 1024 * 1024


def dot_nn(a, b):
    return lax.dot_general(a, b, (((1,), (0,)), ((), ())), preferred_element_type=F32)


def dot_nt(a, b):
    return lax.dot_general(a, b, (((1,), (1,)), ((), ())), preferred_element_type=F32)


def dot_tn(a, b):
    return lax.dot_general(a, b, (((0,), (0,)), ((), ())), preferred_element_type=F32)


def padded_width(width):
    return -(-width // 128) * 128


def call(kernel, outs, scratch, micros, *operands, scalars=None, deps=(), outside=()):
    specs = [
        pl.BlockSpec(memory_space=pl.ANY if i in outside else pltpu.VMEM)
        for i in range(len(operands))
    ]
    if scalars is not None:
        specs = [pl.BlockSpec(memory_space=pltpu.SMEM)] + specs
        operands = (scalars,) + tuple(operands)
    used, held = len(operands), len(deps)

    def run(*refs):
        kernel(*refs[:used], *refs[used + held :])

    return pl.pallas_call(
        run,
        out_shape=tuple(jax.ShapeDtypeStruct(s, d) for s, d in outs),
        in_specs=specs + [pl.BlockSpec(memory_space=pl.ANY)] * held,
        out_specs=tuple([pl.BlockSpec(memory_space=pltpu.VMEM)] * len(outs)),
        scratch_shapes=scratch,
        compiler_params=pltpu.CompilerParams(vmem_limit_bytes=VMEM_LIMIT),
        cost_estimate=pl.CostEstimate(
            flops=int(micros * 1.0e9), bytes_accessed=1000, transcendentals=0
        ),
    )(*operands, *deps)


def gate_kernel(*refs):
    del refs


def gate(values, deps):
    values, deps = list(values), list(deps)
    return list(
        pl.pallas_call(
            gate_kernel,
            out_shape=tuple(jax.ShapeDtypeStruct(m.shape, m.dtype) for m in values),
            in_specs=[pl.BlockSpec(memory_space=pl.ANY)] * (len(values) + len(deps)),
            out_specs=tuple([pl.BlockSpec(memory_space=pl.ANY)] * len(values)),
            input_output_aliases={i: i for i in range(len(values))},
            cost_estimate=pl.CostEstimate(flops=1000, bytes_accessed=1000, transcendentals=0),
        )(*values, *deps)
    )


def cut_of(rows):
    return rows // 32 * 16


def cuts(count, rows):
    return [(0, cut_of(rows)), (cut_of(rows), rows)] if count == 4 else [(0, rows)]


def pieces_of(count, rows):
    return [(j, low, high) for j in range(1, count) for low, high in cuts(count, rows)]


def put_pieces(refs, count, block, values):
    for ref, (j, low, high) in zip(refs, pieces_of(count, values.shape[0])):
        if j == block:
            ref[...] = values[low:high].astype(BF16)


def piece_shapes(count, rows, columns):
    return [((high - low, columns), BF16) for _, low, high in pieces_of(count, rows)]


def add_terms(count, refs):
    total = refs[0][...].astype(F32)
    if count != 4:
        for ref in refs[1:]:
            total = total + ref[...].astype(F32)
        return total
    for low, high in ((1, 2), (3, 4)):
        total = total + jnp.concatenate([refs[low][...], refs[high][...]], axis=0).astype(F32)
    return total


def norm_stats(values):
    mean = jnp.mean(values, axis=1, keepdims=True)
    centered = values - mean
    var = jnp.mean(centered * centered, axis=1, keepdims=True)
    scale = lax.rsqrt(var + NORM_EPSILON)
    return centered * scale, scale


def norm_back(values, gain, grad):
    unit, scale = norm_stats(values)
    grad_unit = grad * gain
    inner = jnp.mean(grad_unit * unit, axis=1, keepdims=True)
    grad_values = scale * (grad_unit - jnp.mean(grad_unit, axis=1, keepdims=True) - unit * inner)
    return grad_values, jnp.sum(grad * unit, axis=0, keepdims=True)


def self_forward_kernel(count, parts, head_size, normed, *refs):
    part_refs, refs = refs[:parts], refs[parts:]
    weight_ref, gains_ref, shift_ref = refs[:3]
    rows_ref, triples_ref = refs[3:5]
    mixed_refs, (held_ref, done) = refs[5:-2], refs[-2:]
    copy = pltpu.make_async_copy(weight_ref.at[:, : held_ref.shape[1]], held_ref, done)
    copy.start()
    stride = held_ref.shape[1] // 3
    rows, width = mixed_refs[0].shape
    factor = LOG2_E / math.sqrt(head_size)
    start = 0
    for ref in part_refs:
        values = ref[...]
        if not normed:
            unit, _ = norm_stats(values.astype(F32))
            values = (unit * gains_ref[0:1, :] + shift_ref[...]).astype(BF16)
        rows_ref[start : start + ref.shape[0], :] = values
        start += ref.shape[0]
    copy.wait()
    for j in range(count):
        at = slice(j * rows, (j + 1) * rows)
        triples_ref[at, :] = dot_nn(rows_ref[at, :], held_ref[...]).astype(BF16)
    for j in range(count):
        at = slice(j * rows, (j + 1) * rows)
        for h in range(width // head_size):
            low = h * head_size
            q = triples_ref[at, low : low + head_size]
            k = triples_ref[:, stride + low : stride + low + head_size]
            v = triples_ref[:, 2 * stride + low : 2 * stride + low + head_size]
            scores = dot_nt(q, k)
            top = jnp.max(scores, axis=1, keepdims=True)
            weights = jnp.exp2((scores - top) * factor)
            total = jnp.sum(weights, axis=1, keepdims=True)
            mixed = dot_nn(weights.astype(BF16), v) * (1.0 / total)
            mixed_refs[j][:, low : low + head_size] = mixed.astype(BF16)


def self_forward(parts, weight, gains, shift, head_size, count, width, normed, deps=()):
    total = sum(m.shape[0] for m in parts)
    columns = parts[0].shape[1]
    held = (columns, 3 * padded_width(width))
    found = call(
        functools.partial(self_forward_kernel, count, len(parts), head_size, normed),
        [((total, columns), BF16), ((total, held[1]), BF16)]
        + [((total // count, width), BF16)] * count,
        [pltpu.VMEM(held, BF16), pltpu.SemaphoreType.DMA],
        24,
        *parts,
        weight,
        gains,
        shift[None],
        deps=deps,
        outside=(len(parts),),
    )
    return found[0], found[1], list(found[2:])


def attention_back(q, k, v, grad, valid, head_size):
    factor = LOG2_E / math.sqrt(head_size)
    scores = dot_nt(k, q)
    if valid is not None:
        scores = jnp.where(valid, scores, -1e30)
    top = jnp.max(scores, axis=0, keepdims=True)
    weights = jnp.exp2((scores - top) * factor)
    weights = weights * (1.0 / jnp.sum(weights, axis=0, keepdims=True))
    grad_weights = dot_nt(v, grad)
    delta = jnp.sum(grad_weights * weights, axis=0, keepdims=True)
    grad_scores = (weights * (grad_weights - delta)).astype(BF16)
    scale = 1.0 / math.sqrt(head_size)
    return (
        dot_tn(grad_scores, k) * scale,
        dot_nn(grad_scores, q) * scale,
        dot_nn(weights.astype(BF16), grad),
    )


def self_backward_kernel(count, head_size, step, triples_ref, *refs):
    grad_refs, (weight_ref, out_ref, own_ref) = refs[:count], refs[count : count + 3]
    piece_refs, (keys_ref, values_ref, held_ref, done) = refs[count + 3 : -4], refs[-4:]
    copy = pltpu.make_async_copy(weight_ref.at[:, : held_ref.shape[1]], held_ref, done)
    copy.start()
    total = triples_ref.shape[0]
    rows, width = grad_refs[0].shape
    stride = held_ref.shape[1] // 3
    for h in range(width // head_size):
        low = h * head_size
        k = triples_ref[:, stride + low : stride + low + head_size]
        v = triples_ref[:, 2 * stride + low : 2 * stride + low + head_size]
        for i in range(total // step):
            at = slice(i * step, (i + 1) * step)
            inside = (i * step) % rows
            q = triples_ref[at, low : low + head_size]
            grad = grad_refs[i * step // rows][inside : inside + step, low : low + head_size]
            grad_q, grad_k, grad_v = attention_back(q, k, v, grad, None, head_size)
            out_ref[at, low : low + head_size] = grad_q.astype(BF16)
            if i == 0:
                keys_ref[...] = grad_k
                values_ref[...] = grad_v
            else:
                keys_ref[...] += grad_k
                values_ref[...] += grad_v
        out_ref[:, stride + low : stride + low + head_size] = keys_ref[...].astype(BF16)
        out_ref[:, 2 * stride + low : 2 * stride + low + head_size] = values_ref[...].astype(BF16)
    if stride > width:
        for g in range(3):
            out_ref[:, g * stride + width : (g + 1) * stride] = jnp.zeros((total, stride - width), BF16)
    copy.wait()
    for j in range(count):
        found = dot_nt(out_ref[j * rows : (j + 1) * rows, :], held_ref[...])
        if j == 0:
            own_ref[...] = found
        else:
            put_pieces(piece_refs, count, j, found)


def self_backward(triples, grads, weight, head_size, deps=()):
    count = len(grads)
    total, rows, columns = triples.shape[0], grads[0].shape[0], weight.shape[0]
    step = min(256, rows)
    found = call(
        functools.partial(self_backward_kernel, count, head_size, step),
        [(triples.shape, BF16), ((rows, columns), F32)] + piece_shapes(count, rows, columns),
        [
            pltpu.VMEM((total, head_size), F32),
            pltpu.VMEM((total, head_size), F32),
            pltpu.VMEM((columns, triples.shape[1]), BF16),
            pltpu.SemaphoreType.DMA,
        ],
        32,
        triples,
        *grads,
        weight,
        deps=deps,
        outside=(1 + count,),
    )
    return found[0], found[1], list(found[2:])


def fill_corner(count, matrix_refs, scalars_ref, corner_ref):
    if len(matrix_refs) == count:
        return list(matrix_refs)
    odd = scalars_ref[2 * count]
    half = matrix_refs[-1].shape[0]
    corner_ref[pl.ds(pl.multiple_of(odd * half, half), half), :] = matrix_refs[-2][...]
    corner_ref[pl.ds(pl.multiple_of((1 - odd) * half, half), half), :] = matrix_refs[-1][...]
    return list(matrix_refs[:-2]) + [corner_ref]


def corner_scratch(count, matrices):
    rows, columns = matrices[0].shape
    return pltpu.VMEM((rows, columns) if len(matrices) > count else (16, 128), BF16)


def fill_pairs(count, pair_refs, pairs_ref):
    padded = pairs_ref.shape[1]
    place = 0
    for ref in pair_refs:
        j, low = divmod(place, padded)
        pairs_ref[j, low : low + ref.shape[0], :] = ref[...]
        place += ref.shape[0]


def middle_forward_kernel(count, matrix_parts, pair_parts, head_size, scalars_ref, *refs):
    mixed_refs, refs = refs[:count], refs[count:]
    matrix_refs, refs = refs[:matrix_parts], refs[matrix_parts:]
    pair_refs, refs = refs[:pair_parts], refs[pair_parts:]
    hidden_ref, gains_ref = refs[:2]
    (self_ref, after_self_ref, norm_ref, queries_ref, cross_ref, after_cross_ref) = refs[2:8]
    mlp_refs = refs[8:-4]
    wide_ref, narrow_ref, corner_ref, pairs_ref = refs[-4:]
    width = mixed_refs[0].shape[1]
    stride = matrix_refs[0].shape[1] // 3
    matrices = fill_corner(count, matrix_refs, scalars_ref, corner_ref)
    fill_pairs(count, pair_refs, pairs_ref)
    order = [scalars_ref[i] for i in range(count)]
    relative = [scalars_ref[count + j] for j in range(count)]
    length = scalars_ref[2 * count + 1]
    spans = [slice(a * width, (a + 1) * width) for a in range(count)]

    for j in range(count):
        narrow_ref[relative[j]] = mixed_refs[j][...]
    for a in range(count):
        self_ref[:, spans[a]] = narrow_ref[a]
    tokens = self_ref[...]
    for i in range(count):
        wide_ref[order[i]] = dot_nn(tokens, matrices[i][:, :width])
    for a in range(count):
        after_self_ref[:, spans[a]] = hidden_ref[:, spans[a]].astype(F32) + wide_ref[a]
    normed = (norm_stats(after_self_ref[...])[0] * gains_ref[1:2, :]).astype(BF16)
    norm_ref[...] = normed
    for i in range(count):
        found = dot_nn(normed, matrices[i][:, stride : stride + width])
        queries_ref[order[i] ^ relative[0]] = found.astype(BF16)

    factor = LOG2_E / math.sqrt(head_size)
    keys_rows = pairs_ref.shape[1]
    valid = lax.broadcasted_iota(jnp.int32, (1, keys_rows), 1) < length
    pair_stride = pairs_ref.shape[2] // 2
    for j in range(count):
        for h in range(width // head_size):
            at = slice(h * head_size, (h + 1) * head_size)
            values_at = slice(pair_stride + h * head_size, pair_stride + (h + 1) * head_size)
            scores = dot_nt(queries_ref[j, :, at], pairs_ref[j, :, at])
            scores = jnp.where(valid, scores, -1e30)
            top = jnp.max(scores, axis=1, keepdims=True)
            weights = jnp.exp2((scores - top) * factor)
            total = jnp.sum(weights, axis=1, keepdims=True)
            mixed = dot_nn(weights.astype(BF16), pairs_ref[j, :, values_at]) * (1.0 / total)
            narrow_ref[relative[j], :, at] = mixed.astype(BF16)
    for a in range(count):
        cross_ref[:, spans[a]] = narrow_ref[a]
    tokens = cross_ref[...]
    for i in range(count):
        wide_ref[order[i]] = dot_nn(tokens, matrices[i][:, 2 * stride : 2 * stride + width])
    for a in range(count):
        after_cross_ref[:, spans[a]] = after_self_ref[:, spans[a]] + wide_ref[a]
    mlp_norm = norm_stats(after_cross_ref[...])[0] * gains_ref[2:3, :]
    for ref, (low, high) in zip(mlp_refs, cuts(count, mlp_norm.shape[0])):
        ref[...] = mlp_norm[low:high].astype(BF16)


def pairs_scratch(count, pairs):
    return pltpu.VMEM((count, sum(m.shape[0] for m in pairs) // count, pairs[0].shape[1]), BF16)


def middle_forward(scalars, mixed, matrices, pairs, hidden, gains, head_size, deps=()):
    count = len(mixed)
    rows, columns = hidden.shape
    width = columns // count
    found = call(
        functools.partial(
            middle_forward_kernel, count, len(matrices), len(pairs), head_size
        ),
        [
            ((rows, columns), BF16),
            ((rows, columns), F32),
            ((rows, columns), BF16),
            ((count, rows, width), BF16),
            ((rows, columns), BF16),
            ((rows, columns), F32),
        ]
        + [((high - low, columns), BF16) for low, high in cuts(count, rows)],
        [
            pltpu.VMEM((count, rows, width), F32),
            pltpu.VMEM((count, rows, width), BF16),
            corner_scratch(count, matrices),
            pairs_scratch(count, pairs),
        ],
        23,
        *mixed,
        *matrices,
        *pairs,
        hidden,
        gains,
        scalars=scalars,
        deps=deps,
    )
    return list(found[:6]) + [list(found[6:])]


def middle_backward_kernel(count, matrix_parts, pair_parts, terms, head_size, scalars_ref, *refs):
    matrix_refs, refs = refs[:matrix_parts], refs[matrix_parts:]
    pair_refs, refs = refs[:pair_parts], refs[pair_parts:]
    term_refs, refs = refs[:terms], refs[terms:]
    grad_out_ref, after_cross_ref, after_self_ref, queries_ref, gains_ref = refs[:5]
    out_ref, self_branch_ref, query_branch_ref, cross_branch_ref, gain_ref = refs[5:10]
    mixed_grad_refs, refs = refs[10 : 10 + count], refs[10 + count :]
    own_pairs_ref, pair_grad_refs = refs[0], refs[1:-6]
    wide_ref, narrow_ref, query_ref, corner_ref, pairs_ref, pair_total_ref = refs[-6:]
    width = queries_ref.shape[2]
    stride = matrix_refs[0].shape[1] // 3
    matrices = fill_corner(count, matrix_refs, scalars_ref, corner_ref)
    fill_pairs(count, pair_refs, pairs_ref)
    order = [scalars_ref[i] for i in range(count)]
    relative = [scalars_ref[count + j] for j in range(count)]
    length = scalars_ref[2 * count + 1]
    spans = [slice(a * width, (a + 1) * width) for a in range(count)]

    def back(branch_ref, group):
        columns = slice(group * stride, group * stride + width)
        total = dot_nt(branch_ref[0], matrices[0][:, columns])
        for i in range(1, count):
            total = total + dot_nt(branch_ref[i], matrices[i][:, columns])
        return total

    def divide(values):
        for a in range(count):
            narrow_ref[a] = values[:, spans[a]].astype(BF16)

    grad, grad_gain = norm_back(
        after_cross_ref[...], gains_ref[2:3, :], add_terms(count, term_refs)
    )
    gain_ref[1:2, :] = grad_gain
    wide_ref[...] = grad + grad_out_ref[...].astype(F32)
    divide(wide_ref[...])
    for i in range(count):
        cross_branch_ref[i] = narrow_ref[order[i]]
    divide(back(cross_branch_ref, 2))

    keys_rows = pairs_ref.shape[1]
    valid = lax.broadcasted_iota(jnp.int32, (keys_rows, 1), 0) < length
    pair_stride = pairs_ref.shape[2] // 2
    if pair_stride > width:
        for g in range(2):
            pair_total_ref[:, g * pair_stride + width : (g + 1) * pair_stride] = jnp.zeros(
                (keys_rows, pair_stride - width), F32
            )
    for j in range(count):
        for h in range(width // head_size):
            at = slice(h * head_size, (h + 1) * head_size)
            values_at = slice(pair_stride + h * head_size, pair_stride + (h + 1) * head_size)
            grad_q, grad_k, grad_v = attention_back(
                queries_ref[j, :, at],
                pairs_ref[j, :, at],
                pairs_ref[j, :, values_at],
                narrow_ref[relative[j], :, at],
                valid,
                head_size,
            )
            query_ref[j, :, at] = grad_q.astype(BF16)
            pair_total_ref[:, at] = grad_k
            pair_total_ref[:, values_at] = grad_v
        if j == 0:
            own_pairs_ref[...] = pair_total_ref[...]
        else:
            put_pieces(pair_grad_refs, count, j, pair_total_ref[...])
    for i in range(count):
        query_branch_ref[i] = query_ref[order[i] ^ relative[0]]
    grad, grad_gain = norm_back(after_self_ref[...], gains_ref[1:2, :], back(query_branch_ref, 1))
    gain_ref[0:1, :] = grad_gain
    out_ref[...] = grad + wide_ref[...]
    divide(out_ref[...])
    for i in range(count):
        self_branch_ref[i] = narrow_ref[order[i]]
    divide(back(self_branch_ref, 0))
    for j in range(count):
        mixed_grad_refs[j][...] = narrow_ref[relative[j]]


def middle_backward(
    scalars, matrices, pairs, terms, grad_out, after_cross, after_self, queries, gains, head_size, deps=()
):
    count, rows, width = queries.shape
    columns = count * width
    branch = ((count, rows, width), BF16)
    text = pairs_scratch(count, pairs)
    keys_rows, pair_columns = text.shape[1:]
    found = call(
        functools.partial(
            middle_backward_kernel, count, len(matrices), len(pairs), len(terms), head_size
        ),
        [((rows, columns), F32), branch, branch, branch, ((2, columns), F32)]
        + [((rows, width), BF16)] * count
        + [((keys_rows, pair_columns), F32)]
        + piece_shapes(count, keys_rows, pair_columns),
        [
            pltpu.VMEM((rows, columns), F32),
            pltpu.VMEM((count, rows, width), BF16),
            pltpu.VMEM((count, rows, width), BF16),
            corner_scratch(count, matrices),
            text,
            pltpu.VMEM((keys_rows, pair_columns), F32),
        ],
        37,
        *matrices,
        *pairs,
        *terms,
        grad_out,
        after_cross,
        after_self,
        queries,
        gains,
        scalars=scalars,
        deps=deps,
    )
    found = list(found)
    return found[:5] + [found[5 : 5 + count], found[5 + count], found[6 + count :]]


def mlp_up_kernel(count, parts, *refs):
    part_refs, (up_ref, rows_ref, up_rows_ref, activated_ref) = refs[:parts], refs[parts:]
    start = 0
    for ref in part_refs:
        rows_ref[start : start + ref.shape[0], :] = ref[...]
        start += ref.shape[0]
    rows = start // count
    for j in range(count):
        at = slice(j * rows, (j + 1) * rows)
        values = dot_nn(rows_ref[at, :], up_ref[...])
        up_rows_ref[at, :] = values
        inner = GELU_SCALE * (values + 0.044715 * (values * values * values))
        activated_ref[at, :] = (0.5 * values * (1.0 + jnp.tanh(inner))).astype(BF16)


def mlp_up(parts, up, count, deps=()):
    total, columns, hidden = sum(m.shape[0] for m in parts), up.shape[0], up.shape[1]
    return call(
        functools.partial(mlp_up_kernel, count, len(parts)),
        [((total, columns), BF16), ((total, hidden), F32), ((total, hidden), BF16)],
        [],
        15,
        *parts,
        up,
        deps=deps,
    )


def mlp_down_kernel(count, activated_ref, down_ref, own_ref, *piece_refs):
    rows = own_ref.shape[0]
    for j in range(count - 1, -1, -1):
        found = dot_nn(activated_ref[j * rows : (j + 1) * rows, :], down_ref[...])
        if j == 0:
            own_ref[...] = found
        else:
            put_pieces(piece_refs, count, j, found)


def mlp_down(activated, down, count, deps=()):
    rows, columns = activated.shape[0] // count, down.shape[1]
    found = call(
        functools.partial(mlp_down_kernel, count),
        [((rows, columns), F32)] + piece_shapes(count, rows, columns),
        [],
        11,
        activated,
        down,
        deps=deps,
    )
    return found[0], list(found[1:])


def stack_kernel(*refs):
    start = 0
    for ref in refs[:-1]:
        refs[-1][start : start + ref.shape[0], :] = ref[...]
        start += ref.shape[0]


def stack_rows(parts, deps=()):
    shape = (sum(m.shape[0] for m in parts), parts[0].shape[1])
    return call(stack_kernel, [(shape, parts[0].dtype)], [], 3, *parts, deps=deps)[0]


def mlp_backward_kernel(count, parts, *refs):
    part_refs, refs = refs[:parts], refs[parts:]
    up_rows_ref, up_ref, down_ref, rows_ref, grad_up_ref, own_ref = refs[:6]
    piece_refs = refs[6:]
    start = 0
    for ref in part_refs:
        rows_ref[start : start + ref.shape[0], :] = ref[...]
        start += ref.shape[0]
    rows = start // count
    for j in range(count - 1, -1, -1):
        at = slice(j * rows, (j + 1) * rows)
        grad = dot_nt(rows_ref[at, :], down_ref[...])
        values = up_rows_ref[at, :]
        square = values * values
        bent = jnp.tanh(GELU_SCALE * (values + 0.044715 * (values * square)))
        slope = 0.5 * (1.0 + bent) + 0.5 * values * (1.0 - bent * bent) * (
            GELU_SCALE * (1.0 + 3.0 * 0.044715 * square)
        )
        grad_up_ref[at, :] = (grad * slope).astype(BF16)
        found = dot_nt(grad_up_ref[at, :], up_ref[...])
        if j == 0:
            own_ref[...] = found
        else:
            put_pieces(piece_refs, count, j, found)


def mlp_backward(parts, up_rows, up, down, count, deps=()):
    total, columns, hidden = sum(m.shape[0] for m in parts), up.shape[0], up.shape[1]
    rows = total // count
    found = call(
        functools.partial(mlp_backward_kernel, count, len(parts)),
        [((total, columns), BF16), ((total, hidden), BF16), ((rows, columns), F32)]
        + piece_shapes(count, rows, columns),
        [],
        22,
        *parts,
        up_rows,
        up,
        down,
        deps=deps,
    )
    return list(found[:3]) + [list(found[3:])]


def outer_kernel(count, groups, half, scalars_ref, *refs):
    rows_refs, branch_refs, refs = refs[:groups], refs[groups : 2 * groups], refs[2 * groups :]
    out_refs, turned_ref = refs[:-1], refs[-1]
    width = branch_refs[0].shape[2]
    stride = padded_width(width)
    odd = scalars_ref[2 * count]
    for g in range(groups):
        at = slice(g * stride, g * stride + width)
        turned_ref[...] = rows_refs[g][...].T
        out_refs[0][:, at] = dot_nn(turned_ref[...], branch_refs[g][0]).astype(BF16)
        for i in range(1, count):
            if not half:
                out_refs[i][:, at] = dot_nn(turned_ref[...], branch_refs[g][i]).astype(BF16)
                continue
            for k in range(2):
                low = pl.multiple_of((odd if k == 0 else 1 - odd) * half, half)
                found = dot_nn(turned_ref[pl.ds(low, half), :], branch_refs[g][i])
                out_refs[2 * i - 1 + k][:, at] = found.astype(BF16)
    if stride > width:
        for ref in out_refs:
            for g in range(groups):
                ref[:, g * stride + width : (g + 1) * stride] = jnp.zeros(
                    (ref.shape[0], stride - width), BF16
                )


def outer(scalars, rows, branches, deps=()):
    count, tokens, width = branches[0].shape
    groups, columns = len(rows), rows[0].shape[1]
    stride = padded_width(width)
    half = columns // 2 if count == 4 else 0
    shapes = [((columns, groups * stride), BF16)]
    if half:
        shapes += [((half, groups * stride), BF16)] * (2 * (count - 1))
    else:
        shapes = shapes * count
    return list(
        call(
            functools.partial(outer_kernel, count, groups, half),
            shapes,
            [pltpu.VMEM((columns, tokens), BF16)],
            3.5 * groups,
            *rows,
            *branches,
            scalars=scalars,
            deps=deps,
        )
    )


def join_kernel(count, scalars_ref, own_ref, mine_ref, other_ref, out_ref):
    odd = scalars_ref[2 * count]
    half = mine_ref.shape[0]
    for ref, place in ((mine_ref, odd), (other_ref, 1 - odd)):
        at = pl.ds(pl.multiple_of(place * half, half), half)
        out_ref[at, :] = (own_ref[at, :].astype(F32) + ref[...].astype(F32)).astype(BF16)


def join_halves(scalars, own, mine, other):
    count = lax.axis_size("seq")
    (found,) = call(
        functools.partial(join_kernel, count),
        [(own.shape, BF16)],
        [],
        4,
        own,
        mine,
        other,
        scalars=scalars,
    )
    return found


def joined_stats(first, second):
    count = first.shape[1] + second.shape[1]
    mean = (jnp.sum(first, axis=1, keepdims=True) + jnp.sum(second, axis=1, keepdims=True)) / count
    first, second = first - mean, second - mean
    var = (
        jnp.sum(first * first, axis=1, keepdims=True)
        + jnp.sum(second * second, axis=1, keepdims=True)
    ) / count
    scale = lax.rsqrt(var + NORM_EPSILON)
    return first * scale, second * scale, scale


def skip_forward_kernel(count, matrix_parts, terms, scalars_ref, *refs):
    matrix_refs, refs = refs[:matrix_parts], refs[matrix_parts:]
    term_refs, refs = refs[:terms], refs[terms:]
    residual_ref, second_ref, gains_ref, next_ref, shift_ref = refs[:5]
    first_ref, joined_ref, out_ref = refs[5:8]
    norm_refs, (wide_ref, corner_ref) = refs[8:-2], refs[-2:]
    rows, columns = first_ref.shape
    width = columns // count
    matrices = fill_corner(count, matrix_refs, scalars_ref, corner_ref)
    first_ref[...] = residual_ref[...] + add_terms(count, term_refs)
    first, second, _ = joined_stats(first_ref[...], second_ref[...].astype(F32))
    joined_ref[:, :columns] = (first * gains_ref[0:1, :]).astype(BF16)
    joined_ref[:, columns:] = (second * gains_ref[1:2, :]).astype(BF16)
    joined = joined_ref[...]
    for i in range(count):
        wide_ref[scalars_ref[i]] = dot_nn(joined, matrices[i][:, :width])
    for a in range(count):
        out_ref[:, a * width : (a + 1) * width] = wide_ref[a]
    normed = norm_stats(out_ref[...])[0] * next_ref[0:1, :] + shift_ref[...]
    for ref, (low, high) in zip(norm_refs, cuts(count, rows)):
        ref[...] = normed[low:high].astype(BF16)


def skip_forward(scalars, matrices, terms, residual, second, gains, next_gains, shift, deps=()):
    rows, columns = residual.shape
    count = lax.axis_size("seq")
    found = call(
        functools.partial(skip_forward_kernel, count, len(matrices), len(terms)),
        [((rows, columns), F32), ((rows, 2 * columns), BF16), ((rows, columns), F32)]
        + [((high - low, columns), BF16) for low, high in cuts(count, rows)],
        [pltpu.VMEM((count, rows, columns // count), F32), corner_scratch(count, matrices)],
        11,
        *matrices,
        *terms,
        residual,
        second,
        gains,
        next_gains,
        shift[None],
        scalars=scalars,
        deps=deps,
    )
    return list(found[:3]) + [list(found[3:])]


def skip_backward_kernel(count, matrix_parts, terms, scalars_ref, *refs):
    matrix_refs, refs = refs[:matrix_parts], refs[matrix_parts:]
    term_refs, refs = refs[:terms], refs[terms:]
    hidden_ref, next_ref, residual_ref, first_ref, second_ref, gains_ref = refs[:6]
    branch_ref, grad_first_ref, grad_second_ref, vectors_ref = refs[6:10]
    half_refs, (narrow_ref, corner_ref) = refs[10:-2], refs[-2:]
    rows, columns = first_ref.shape
    width = columns // count
    matrices = fill_corner(count, matrix_refs, scalars_ref, corner_ref)
    grad_norm = add_terms(count, term_refs)
    vectors_ref[0:1, :] = jnp.sum(grad_norm, axis=0, keepdims=True)
    grad, grad_gain = norm_back(hidden_ref[...], next_ref[0:1, :], grad_norm)
    vectors_ref[1:2, :] = grad_gain
    grad = grad + residual_ref[...]
    for a in range(count):
        narrow_ref[a] = grad[:, a * width : (a + 1) * width].astype(BF16)
    for i in range(count):
        branch_ref[i] = narrow_ref[scalars_ref[i]]

    def back(at):
        total = dot_nt(branch_ref[0], matrices[0][at, :width])
        for i in range(1, count):
            total = total + dot_nt(branch_ref[i], matrices[i][at, :width])
        return total

    grad_first_ref[...] = back(slice(0, columns))
    grad_second_ref[...] = back(slice(columns, 2 * columns))
    first, second, scale = joined_stats(first_ref[...], second_ref[...].astype(F32))
    vectors_ref[2:3, :] = jnp.sum(grad_first_ref[...] * first, axis=0, keepdims=True)
    vectors_ref[3:4, :] = jnp.sum(grad_second_ref[...] * second, axis=0, keepdims=True)
    grad_first = grad_first_ref[...] * gains_ref[0:1, :]
    grad_second = grad_second_ref[...] * gains_ref[1:2, :]
    mean = (
        jnp.sum(grad_first, axis=1, keepdims=True) + jnp.sum(grad_second, axis=1, keepdims=True)
    ) / (2 * columns)
    inner = (
        jnp.sum(grad_first * first, axis=1, keepdims=True)
        + jnp.sum(grad_second * second, axis=1, keepdims=True)
    ) / (2 * columns)
    grad_first_ref[...] = scale * (grad_first - mean - first * inner)
    grad_second_ref[...] = scale * (grad_second - mean - second * inner)
    for ref, (low, high) in zip(half_refs, cuts(count, rows)):
        ref[...] = grad_first_ref[low:high, :].astype(BF16)


def skip_backward(
    scalars, matrices, terms, hidden, next_gains, residual, first, second, gains, deps=()
):
    rows, columns = first.shape
    count = lax.axis_size("seq")
    narrow = (count, rows, columns // count)
    found = call(
        functools.partial(skip_backward_kernel, count, len(matrices), len(terms)),
        [
            (narrow, BF16),
            ((rows, columns), F32),
            ((rows, columns), F32),
            ((4, columns), F32),
        ]
        + [((high - low, columns), BF16) for low, high in cuts(count, rows)],
        [pltpu.VMEM(narrow, BF16), corner_scratch(count, matrices)],
        15,
        *matrices,
        *terms,
        hidden,
        next_gains,
        residual,
        first,
        second,
        gains,
        scalars=scalars,
        deps=deps,
    )
    return list(found[:4]) + [list(found[4:])]


def open_backward_kernel(count, terms, *refs):
    term_refs, refs = refs[:terms], refs[terms:]
    hidden_ref, gains_ref, residual_ref, out_ref, vectors_ref = refs
    grad_norm = add_terms(count, term_refs)
    vectors_ref[0:1, :] = jnp.sum(grad_norm, axis=0, keepdims=True)
    grad, grad_gain = norm_back(hidden_ref[...].astype(F32), gains_ref[0:1, :], grad_norm)
    vectors_ref[1:2, :] = grad_gain
    out_ref[...] = grad + residual_ref[...]


def open_backward(terms, hidden, gains, residual, deps=()):
    count = lax.axis_size("seq")
    return call(
        functools.partial(open_backward_kernel, count, len(terms)),
        [(residual.shape, F32), ((2, residual.shape[1]), F32)],
        [],
        5,
        *terms,
        hidden,
        gains,
        residual,
        deps=deps,
    )


def close_kernel(count, terms, *refs):
    refs[terms + 1][...] = (refs[terms][...] + add_terms(count, refs[:terms])).astype(BF16)


def close_forward(terms, residual, deps=()):
    count = lax.axis_size("seq")
    (found,) = call(
        functools.partial(close_kernel, count, len(terms)),
        [(residual.shape, BF16)],
        [],
        3,
        *terms,
        residual,
        deps=deps,
    )
    return found


def pack_kernel(count, *refs):
    start = 0
    for ref in refs[:count]:
        refs[count][: ref.shape[0], start : start + ref.shape[1]] = ref[...]
        start += ref.shape[1]


def pack(shards):
    rows = -(-max(m.shape[0] for m in shards) // 32) * 32
    shape = (rows, sum(m.shape[1] for m in shards))
    return call(functools.partial(pack_kernel, len(shards)), [(shape, BF16)], [], 3, *shards)[0]


def settle_kernel(count, parts, plan, scalars_ref, *refs):
    block_refs, refs = refs[:parts], refs[parts:]
    outs = sum(entry[3] for entry in plan)
    out_refs, stack_ref = refs[-outs - 1 : -1], refs[-1]
    for j in range(count):
        owner = scalars_ref[count + j]
        if j == count - 1 and parts > count:
            cut = block_refs[j].shape[0]
            stack_ref[owner, :cut] = block_refs[j][...]
            stack_ref[owner, cut:] = block_refs[j + 1][...]
        else:
            stack_ref[owner] = block_refs[j][...]
    place = 0
    for first, rows, groups, pieces, width, stride in plan:
        if not groups:
            for a in range(count):
                found = stack_ref[a, :rows, first : first + width]
                out_refs[place][0, a * rows : (a + 1) * rows, :] = found.astype(F32)
        for p in range(pieces):
            for g in range(groups):
                for a in range(count):
                    low = first + (p * groups + g) * stride
                    at = (g * count + a) * width
                    found = stack_ref[a, :rows, low : low + width]
                    out_refs[place + p][0, :, at : at + width] = found.astype(F32)
        place += pieces


def settle(scalars, blocks, plan, layer, layer_count, before):
    count = lax.axis_size("seq")
    shapes = []
    for _, rows, groups, pieces, width, _ in plan:
        shapes += [(rows, groups * count * width) if groups else (count * rows, width)] * pieces
    held = [] if before is None else list(before)
    inputs = [pl.BlockSpec(memory_space=pltpu.VMEM)] * len(blocks)
    inputs += [pl.BlockSpec(memory_space=pl.ANY)] * len(held)
    found = pl.pallas_call(
        functools.partial(settle_kernel, count, len(blocks), plan),
        grid=(1,),
        out_shape=[jax.ShapeDtypeStruct((layer_count,) + shape, F32) for shape in shapes],
        in_specs=[pl.BlockSpec(memory_space=pltpu.SMEM)] + inputs,
        out_specs=[pl.BlockSpec((1,) + shape, lambda i: (layer, 0, 0)) for shape in shapes],
        scratch_shapes=[pltpu.VMEM((count,) + blocks[0].shape, BF16)],
        input_output_aliases={1 + len(blocks) + i: i for i in range(len(held))},
        compiler_params=pltpu.CompilerParams(vmem_limit_bytes=VMEM_LIMIT),
        cost_estimate=pl.CostEstimate(flops=8_000_000_000, bytes_accessed=1000, transcendentals=0),
    )(scalars, *blocks, *held)
    return list(found)


def finish(scalars, entries, layer, layer_count, before=None):
    plan, first = [], 0
    for shard, groups, pieces, width in entries:
        rows, columns = shard.shape
        stride = columns // (groups * pieces) if groups else columns
        plan.append((first, rows, groups, pieces, width, stride))
        first += columns
    blocks = gather_parts(pack([entry[0] for entry in entries]))
    return settle(scalars, blocks, tuple(plan), layer, layer_count, before)


def swap_seq(block, bits):
    seq_count = lax.axis_size("seq")
    return lax.ppermute(block, "seq", [(i, i ^ bits) for i in range(seq_count)])


def swap_fsdp(block, bits):
    fsdp_count = lax.axis_size("fsdp")
    return lax.ppermute(block, "fsdp", [(i, i ^ bits) for i in range(fsdp_count)])


def swap_core(block):
    return swap_fsdp(block, 1)


def swap_by_core(block, even_bits, odd_bits):
    seq_count, fsdp_count = lax.axis_size("seq"), lax.axis_size("fsdp")
    pairs = []
    for s in range(seq_count):
        for f in range(fsdp_count):
            other = s ^ (odd_bits if f % 2 else even_bits)
            pairs.append((s * fsdp_count + f, other * fsdp_count + f))
    return lax.ppermute(block, ("seq", "fsdp"), pairs)


def add_bf16(*terms):
    total = terms[0].astype(F32)
    for term in terms[1:]:
        total = total + term.astype(F32)
    return total.astype(BF16)


def halves_of(block):
    return [block[low:high] for low, high in cuts(lax.axis_size("seq"), block.shape[0])]


def gather_halves(halves):
    seq_count = lax.axis_size("seq")
    if seq_count != 4:
        return [halves[0]] + [swap_seq(halves[0], j) for j in range(1, seq_count)]
    top, bottom = halves
    y_top, x_bottom = swap_seq(top, 2), swap_seq(bottom, 1)
    x_top, y_bottom = swap_seq(top, 1), swap_seq(bottom, 2)
    return [top, bottom, x_top, x_bottom, y_top, y_bottom, swap_seq(y_top, 1), swap_seq(x_bottom, 2)]


def scatter_parts(own, pieces):
    seq_count = lax.axis_size("seq")
    if seq_count != 4:
        return [own] + [swap_seq(m, j + 1) for j, m in enumerate(pieces)]
    x_top, x_bottom, y_top, y_bottom, corner_top, corner_bottom = pieces
    by_x, by_y = swap_seq(corner_top, 1), swap_seq(corner_bottom, 2)
    from_x_top, from_y_bottom = swap_seq(x_top, 1), swap_seq(y_bottom, 2)
    from_y_top = swap_seq(add_bf16(y_top, by_x), 2)
    from_x_bottom = swap_seq(add_bf16(x_bottom, by_y), 1)
    return [own, from_x_top, from_x_bottom, from_y_top, from_y_bottom]


def exchange_rel(blocks):
    return [blocks[0]] + [swap_seq(blocks[j], j) for j in range(1, len(blocks))]


def gather_parts(block):
    seq_count = lax.axis_size("seq")
    if seq_count != 4:
        return [block] + [swap_seq(block, j) for j in range(1, seq_count)]
    cut = cut_of(block.shape[0])
    from_x, from_y = swap_seq(block, 1), swap_seq(block, 2)
    return [block, from_x, from_y, swap_seq(from_y[:cut], 1), swap_seq(from_x[cut:], 2)]


def list_order():
    s, seq_count = lax.axis_index("seq"), lax.axis_size("seq")
    if seq_count != 4:
        return [s ^ j for j in range(seq_count)]
    odd = lax.axis_index("fsdp") % 2
    return [s, s ^ (1 + odd), s ^ (2 - odd), s ^ 3]


def spread(block):
    seq_count = lax.axis_size("seq")
    if seq_count != 4:
        return [block] + [swap_seq(block, j) for j in range(1, seq_count)]
    odd = lax.axis_index("fsdp") % 2
    half = block.shape[0] // 2
    first = swap_by_core(block, 1, 2)
    part = swap_by_core(lax.dynamic_slice_in_dim(first, odd * half, half, 0), 2, 1)
    return [block, first, swap_core(first), part, swap_core(part)]


def unspread(scalars, blocks):
    seq_count = lax.axis_size("seq")
    if seq_count != 4:
        return add_bf16(blocks[0], *[swap_seq(blocks[j], j) for j in range(1, seq_count)])
    own, first_mine, first_other, second_mine, second_other, corner_mine, corner_other = blocks
    passed = swap_by_core(add_bf16(corner_mine, swap_core(corner_other)), 2, 1)
    other = swap_by_core(add_bf16(first_other, swap_core(second_mine)), 1, 2)
    mine = swap_by_core(add_bf16(first_mine, swap_core(second_other), passed), 1, 2)
    return join_halves(scalars, own, mine, other)


def own_part(matrix, groups, padded):
    s, seq_count = lax.axis_index("seq"), lax.axis_size("seq")
    width = matrix.shape[1] // (groups * seq_count)
    parts = [
        jnp.pad(
            lax.dynamic_slice_in_dim(matrix, (g * seq_count + s) * width, width, 1),
            ((0, 0), (0, padded - width)),
        )
        for g in range(groups)
    ]
    return jnp.concatenate(parts, axis=1)


def gather_fsdp(shard):
    return lax.all_gather(shard, "fsdp", axis=0, tiled=True)


def scatter_fsdp(full):
    return lax.psum_scatter(full.astype(BF16), "fsdp", scatter_dimension=0, tiled=True)


def text_pairs(text_rows, kv_part):
    return gather_halves([dot_nn(m, kv_part).astype(BF16) for m in halves_of(text_rows)])


def layer_forward(parts, hidden, scalars, gains, shift, kv_part, text_rows, weights, normed, cross_deps):
    lead_part, square_parts, up_part = weights
    seq_count = lax.axis_size("seq")
    tok_rows, model_width = hidden.shape
    head_size, width = model_width // H, model_width // seq_count
    first_all, triples, mixed = self_forward(
        parts, lead_part, gains, shift, head_size, seq_count, width, normed
    )
    (kv_part,) = gate([kv_part], [mixed[0]])
    pairs = text_pairs(text_rows, kv_part)
    self_tokens, after_self, cross_norm, queries, cross_tokens, after_cross, mlp_halves = (
        middle_forward(
            scalars, exchange_rel(mixed), square_parts, pairs, hidden, gains, head_size, cross_deps
        )
    )
    mlp_parts = gather_halves(mlp_halves)
    mlp_all, up_rows, activated = mlp_up(mlp_parts, up_part, seq_count)
    saved = (
        first_all,
        triples,
        self_tokens,
        after_self,
        cross_norm,
        queries,
        cross_tokens,
        after_cross,
        mlp_all,
        up_rows,
        activated,
    )
    return (saved, kv_part, pairs, mlp_parts)


def unspread_first(blocks, ready):
    own, first_mine, first_other, second_mine, second_other, corner_mine, corner_other = blocks
    swapped = [swap_core(corner_other), swap_core(second_mine), swap_core(second_other)]
    from_corner, to_other, to_mine = gate(swapped, ready)
    passed = swap_by_core(add_bf16(corner_mine, from_corner), 2, 1)
    other = swap_by_core(add_bf16(first_other, to_other), 1, 2)
    return own, other, passed, [first_mine, to_mine]


def unspread_last(scalars, first, ready):
    own, other, passed, terms = first
    (passed,) = gate([passed], ready)
    mine = swap_by_core(add_bf16(*terms, passed), 1, 2)
    return join_halves(scalars, own, mine, other)


def unspread_any(blocks):
    return add_bf16(blocks[0], *[swap_seq(m, j + 1) for j, m in enumerate(blocks[1:])])


def gather_lead(layer, qkv, query, self_out, cross_out):
    padded = padded_width(query.shape[2] // lax.axis_size("seq"))
    return gather_fsdp(
        jnp.concatenate(
            [own_part(qkv[layer], 3, padded)]
            + [own_part(m[layer], 1, padded) for m in (self_out, query, cross_out)],
            axis=1,
        )
    )


def gather_rest(layer, text_kv, up, down):
    s, seq_count, fsdp_count = lax.axis_index("seq"), lax.axis_size("seq"), lax.axis_size("fsdp")
    padded = padded_width(text_kv.shape[2] // (2 * seq_count))
    rows = down.shape[1] // seq_count
    return (
        gather_fsdp(own_part(text_kv[layer], 2, padded)),
        gather_fsdp(own_part(up[layer], fsdp_count, up.shape[2] // (fsdp_count * seq_count))),
        gather_fsdp(lax.dynamic_slice_in_dim(down[layer], s * rows, rows, 0)),
    )


def sum_vectors(vectors):
    bits = 1
    while bits < lax.axis_size("seq"):
        vectors = vectors + swap_seq(vectors, bits)
        bits *= 2
    found, bits = vectors[None], 1
    while bits < lax.axis_size("fsdp"):
        found = jnp.concatenate([found, swap_fsdp(found, bits)], axis=0)
        bits *= 2
    return found


def body(
    latents,
    skip_input,
    text_tokens,
    text_lengths,
    condition,
    cotangent,
    mod_weight,
    norm_gains,
    qkv_weight,
    query_weight,
    text_kv_weight,
    self_out_weight,
    cross_out_weight,
    up_weight,
    down_weight,
    skip_gain,
    skip_weight,
):
    seq_count, fsdp_count = lax.axis_size("seq"), lax.axis_size("fsdp")
    s, f = lax.axis_index("seq"), lax.axis_index("fsdp")
    _, tok_rows, model_width = latents.shape
    width = model_width // seq_count
    shard_rows = mod_weight.shape[1]
    text_count = text_tokens.shape[1]
    padded = -(-text_count // 32) * 32
    text_rows = jnp.pad(text_tokens[0], ((0, padded - text_count), (0, 0)))
    scalars = jnp.stack(
        [*list_order(), *[s ^ j for j in range(seq_count)], f % 2, text_lengths[0]]
    ).astype(jnp.int32)

    gain_rows = jnp.concatenate(
        [norm_gains.reshape(-1, shard_rows), skip_gain.reshape(-1, shard_rows)], axis=0
    )
    small = jnp.concatenate(
        [
            condition.reshape(fsdp_count, 1, shard_rows),
            jnp.broadcast_to(gain_rows[None], (fsdp_count,) + gain_rows.shape),
        ],
        axis=1,
    ).astype(F32)
    small = lax.all_to_all(small, "fsdp", 0, 0, tiled=True)
    cond_part = small[:, 0]
    gains = jnp.swapaxes(small[:, 1:7], 0, 1).reshape(2, 3, model_width)
    skip_gains = small[:, 7:].reshape(2, model_width)
    silu_part = jax.nn.silu(cond_part)
    shift_terms = jnp.einsum("br,lrd->bld", silu_part, mod_weight.astype(F32), precision=EXACT)
    shifts = jnp.sum(lax.all_to_all(shift_terms, "fsdp", 0, 0, tiled=True), axis=0)

    lead_stacks = (qkv_weight, query_weight, self_out_weight, cross_out_weight)
    rest_stacks = (text_kv_weight, up_weight, down_weight)
    lead_columns = 3 * padded_width(width)
    head_size = model_width // H
    fours = seq_count == 4

    lead_first = gather_lead(0, *lead_stacks)
    kv_first, up_first, down_first = gather_rest(0, *rest_stacks)
    (square_first,) = gate([lead_first[:, lead_columns:]], [shifts])
    squares_first = spread(square_first)
    saved_first, kv_first, pairs_first, mlp_parts = layer_forward(
        gather_halves(halves_of(latents[0])),
        latents[0],
        scalars,
        gains[0],
        shifts[0],
        kv_first,
        text_rows,
        (lead_first, squares_first, up_first),
        False,
        (),
    )
    out_halves = gate(halves_of(cotangent[0]), mlp_parts[-2:])
    out_parts = gather_halves(out_halves)
    own, pieces = mlp_down(saved_first[10], down_first, seq_count)
    terms = scatter_parts(own, pieces)

    (skip_matrix,) = gate(
        [gather_fsdp(own_part(skip_weight, 1, padded_width(width)))], [own]
    )
    skip_parts = spread(skip_matrix)
    first_out, joined_norm, skip_out, second_halves = skip_forward(
        scalars,
        skip_parts,
        terms,
        saved_first[7],
        skip_input[0],
        skip_gains,
        gains[1],
        shifts[1],
        out_parts[-2:],
    )

    lead_second = gather_lead(1, *lead_stacks)
    kv_second, up_second, down_second = gather_rest(1, *rest_stacks)
    second_parts = gather_halves(second_halves)
    (square_second,) = gate([lead_second[:, lead_columns:]], second_parts[-2:])
    squares_second = spread(square_second)
    saved_second, kv_second, pairs_second, _ = layer_forward(
        second_parts,
        skip_out,
        scalars,
        gains[1],
        shifts[1],
        kv_second,
        text_rows,
        (lead_second, squares_second, up_second),
        True,
        (),
    )
    out_all = stack_rows(out_parts, (saved_second[7],))

    def block_backward(rows, grad_out, saved, block, weights, early, mlp_deps, middle_deps, self_deps):
        lead_part, square_parts, kv_part, up_part, down_part = weights
        grad_down = dot_tn(saved[10], early).astype(BF16) if early is not None else None
        found_all, grad_up_rows, own, pieces = mlp_backward(
            rows,
            saved[9],
            up_part,
            down_part,
            seq_count,
            mlp_deps + ((grad_down,) if early is not None else ()),
        )
        terms = scatter_parts(own, pieces)
        if early is None:
            grad_down = dot_tn(saved[10], found_all).astype(BF16)
        grad_up = dot_tn(saved[8], grad_up_rows).astype(BF16)
        down_shard, up_shard = scatter_fsdp(grad_down), scatter_fsdp(grad_up)
        (
            grad_after_self,
            self_branch,
            query_branch,
            cross_branch,
            gain_grads,
            mixed_grads,
            own_pairs,
            pair_pieces,
        ) = middle_backward(
            scalars,
            square_parts,
            pairs_first if block == 0 else pairs_second,
            terms,
            grad_out,
            saved[7],
            saved[3],
            saved[5],
            gains[block],
            head_size,
            (grad_down, grad_up) + middle_deps(grad_up_rows),
        )
        squares = outer(
            scalars,
            [saved[2], saved[4], saved[6]],
            [self_branch, query_branch, cross_branch],
        )
        grad_triples, own, pieces = self_backward(
            saved[1],
            exchange_rel(mixed_grads),
            lead_part,
            head_size,
            (squares[0], down_shard) + self_deps(grad_after_self),
        )
        terms = scatter_parts(own, pieces)
        grad_qkv = dot_tn(saved[0], grad_triples).astype(BF16)
        pair_pieces = gate(pair_pieces, [grad_triples])
        pair_terms = scatter_parts(own_pairs, pair_pieces)
        if fours:
            grad_pairs = jnp.concatenate(
                [
                    add_bf16(pair_terms[0][low:high], pair_terms[1 + k], pair_terms[3 + k])
                    for k, (low, high) in enumerate(cuts(seq_count, text_rows.shape[0]))
                ]
            )
        else:
            grad_pairs = add_bf16(*pair_terms)
        grad_text = dot_nt(grad_pairs, kv_part)
        kv_shard = scatter_fsdp(dot_tn(text_rows, grad_pairs))
        if fours:
            squares = unspread_first(squares, [grad_triples])
        return (
            terms,
            grad_after_self,
            gain_grads,
            grad_text,
            squares,
            grad_qkv,
            scatter_fsdp(grad_qkv),
            kv_shard,
            up_shard,
            down_shard,
        )

    def squares_done(squares, ready):
        joined = unspread_last(scalars, squares, ready) if fours else unspread_any(squares)
        return joined, scatter_fsdp(joined)

    (
        terms,
        grad_after_self,
        gain_grads,
        text_second,
        squares,
        grad_qkv,
        qkv_shard,
        kv_shard,
        up_shard,
        down_shard,
    ) = block_backward(
        [out_all],
        cotangent[0],
        saved_second,
        1,
        (lead_second, squares_second, kv_second, up_second, down_second),
        out_all,
        (),
        lambda done: (),
        lambda done: (),
    )
    skip_branch, grad_first_out, grad_skip, vectors, first_halves = skip_backward(
        scalars,
        skip_parts,
        terms,
        skip_out,
        gains[1],
        grad_after_self,
        first_out,
        skip_input[0],
        skip_gains,
        (grad_qkv, up_shard),
    )
    vectors_second = jnp.concatenate([vectors[:2], gain_grads, vectors[2:]], axis=0)
    square_joined, square_shard = squares_done(squares, [grad_first_out])
    skip_outer = outer(scalars, [joined_norm], [skip_branch])
    held = {}

    def skip_first(done):
        if fours:
            held["first"] = unspread_first(skip_outer, [done])
        else:
            held["joined"] = unspread_any(skip_outer)
        return (kv_shard,)

    def skip_last(done):
        if fours:
            held["joined"] = unspread_last(scalars, held["first"], [done])
        held["shard"] = scatter_fsdp(held["joined"])
        return (qkv_shard,)

    second_layer = (qkv_shard, square_shard, kv_shard, up_shard, down_shard)
    (
        terms,
        grad_after_self,
        gain_grads,
        text_first,
        squares,
        grad_qkv,
        qkv_shard,
        kv_shard,
        up_shard,
        down_shard,
    ) = block_backward(
        gather_halves(first_halves),
        grad_first_out,
        saved_first,
        0,
        (lead_first, squares_first, kv_first, up_first, down_first),
        None,
        (skip_outer[0], square_joined),
        skip_first,
        skip_last,
    )
    skip_shard = held["shard"]
    grad_latents, vectors = open_backward(
        terms, latents[0], gains[0], grad_after_self, (grad_qkv, skip_shard, square_shard)
    )
    vectors_first = jnp.concatenate([vectors, gain_grads], axis=0)
    _, square_shard = squares_done(squares, [grad_latents])
    first_layer = (qkv_shard, square_shard, kv_shard, up_shard, down_shard)

    own, pieces = mlp_down(saved_second[10], down_second, seq_count, (grad_latents,))
    output = close_forward(scatter_parts(own, pieces), saved_second[7])

    def entries(layer):
        qkv, square, kv, up, down = layer
        return (
            [
                (up, fsdp_count, 1, up.shape[1] // fsdp_count),
                (kv, 2, 1, width),
                (down, 0, 1, down.shape[1]),
            ],
            [(qkv, 3, 1, width), (square, 1, 3, width)],
        )

    early, late = entries(second_layer)
    early_done, late_done = finish(scalars, early, 1, 2), finish(scalars, late, 1, 2)
    early, late = entries(first_layer)
    grad_up, grad_kv, grad_down = finish(scalars, early, 0, 2, early_done)
    grad_qkv, grad_self_out, grad_query, grad_cross_out = finish(scalars, late, 0, 2, late_done)
    (grad_skip_weight,) = finish(scalars, [(skip_shard, 1, 1, width)], 0, 1)

    sums = sum_vectors(jnp.concatenate([vectors_first, vectors_second], axis=0))
    first_sums, second_sums = sums[:, :4], sums[:, 4:]
    shift_grads = jnp.stack([first_sums[:, 0], second_sums[:, 0]], axis=1)
    gain_sums = jnp.stack([first_sums[:, 1:4].sum(axis=0), second_sums[:, 1:4].sum(axis=0)])
    grad_norm_gains = lax.dynamic_slice_in_dim(gain_sums, f * shard_rows, shard_rows, 2)
    grad_skip_gain = lax.dynamic_slice_in_dim(
        second_sums[:, 4:].sum(axis=0).reshape(-1), f * skip_gain.shape[0], skip_gain.shape[0], 0
    )
    turned = jnp.stack(
        [lax.dynamic_index_in_dim(silu_part, f ^ j, 0, False) for j in range(fsdp_count)]
    )
    grad_mod = jnp.einsum("br,bld->lrd", turned, shift_grads, precision=EXACT)
    grad_silu = jnp.einsum("bld,lrd->br", shift_grads, mod_weight.astype(F32), precision=EXACT)
    grad_silu = jnp.stack(
        [lax.dynamic_index_in_dim(grad_silu, f ^ j, 0, False) for j in range(fsdp_count)]
    )
    _, silu_pull = jax.vjp(jax.nn.silu, cond_part)
    grad_cond_part = silu_pull(grad_silu)[0]
    grad_condition = lax.all_to_all(grad_cond_part, "fsdp", 0, 0, tiled=True).reshape(1, -1)

    text_sum, bits = text_first + text_second, 1
    while bits < seq_count:
        text_sum = text_sum + swap_seq(text_sum.astype(BF16), bits).astype(F32)
        bits *= 2
    return (
        output[None],
        grad_latents[None],
        grad_skip[None],
        text_sum[None, :text_count],
        grad_condition,
        grad_mod,
        grad_norm_gains,
        grad_qkv,
        grad_query,
        grad_kv,
        grad_self_out,
        grad_cross_out,
        grad_up,
        grad_down,
        grad_skip_gain,
        grad_skip_weight[0],
    )


def solution(mesh):
    in_specs = (
        P("fsdp", "seq", None),
        P("fsdp", "seq", None),
        P("fsdp", None, None),
        P("fsdp"),
        P("fsdp", None),
        P("fsdp", "seq", None),
        P(None, "fsdp", None),
        P(None, None, "fsdp"),
        P(None, "fsdp", None),
        P(None, "fsdp", None),
        P(None, "fsdp", None),
        P(None, "fsdp", None),
        P(None, "fsdp", None),
        P(None, "fsdp", None),
        P(None, "fsdp", None),
        P("fsdp"),
        P("fsdp", None),
    )
    out_specs = (
        P("fsdp", "seq", None),
        P("fsdp", "seq", None),
        P("fsdp", "seq", None),
        P("fsdp", None, None),
        P("fsdp", None),
        P(None, "fsdp", None),
        P(None, None, "fsdp"),
        P(None, "fsdp", None),
        P(None, "fsdp", None),
        P(None, "fsdp", None),
        P(None, "fsdp", None),
        P(None, "fsdp", None),
        P(None, "fsdp", None),
        P(None, "fsdp", None),
        P("fsdp"),
        P("fsdp", None),
    )
    return jax.shard_map(body, mesh=mesh, in_specs=in_specs, out_specs=out_specs, check_vma=False)
```

```python
import functools
import math

import jax
import jax.numpy as jnp
from jax import lax
from jax.experimental import pallas as pl
from jax.experimental.pallas import tpu as pltpu
from jax.sharding import PartitionSpec as P

H = 16
NORM_EPSILON = 1e-06
EXACT = lax.Precision.HIGHEST
BF16 = jnp.bfloat16
F32 = jnp.float32
LOG2_E = 1.4426950408889634
GELU_SCALE = math.sqrt(2.0 / math.pi)
VMEM_LIMIT = 56 * 1024 * 1024


def dot_nn(a, b):
    return lax.dot_general(a, b, (((1,), (0,)), ((), ())), preferred_element_type=F32)


def dot_nt(a, b):
    return lax.dot_general(a, b, (((1,), (1,)), ((), ())), preferred_element_type=F32)


def dot_tn(a, b):
    return lax.dot_general(a, b, (((0,), (0,)), ((), ())), preferred_element_type=F32)


def padded_width(width):
    return -(-width // 128) * 128


def call(kernel, outs, scratch, micros, *operands, scalars=None, deps=(), outside=()):
    specs = [
        pl.BlockSpec(memory_space=pl.ANY if i in outside else pltpu.VMEM)
        for i in range(len(operands))
    ]
    if scalars is not None:
        specs = [pl.BlockSpec(memory_space=pltpu.SMEM)] + specs
        operands = (scalars,) + tuple(operands)
    used, held = len(operands), len(deps)

    def run(*refs):
        kernel(*refs[:used], *refs[used + held :])

    return pl.pallas_call(
        run,
        name=getattr(kernel, "func", kernel).__name__,
        out_shape=tuple(jax.ShapeDtypeStruct(s, d) for s, d in outs),
        in_specs=specs + [pl.BlockSpec(memory_space=pl.ANY)] * held,
        out_specs=tuple([pl.BlockSpec(memory_space=pltpu.VMEM)] * len(outs)),
        scratch_shapes=scratch,
        compiler_params=pltpu.CompilerParams(vmem_limit_bytes=VMEM_LIMIT),
        cost_estimate=pl.CostEstimate(
            flops=int(micros * 1000), bytes_accessed=1000, transcendentals=0
        ),
    )(*operands, *deps)


def gate_kernel(*refs):
    del refs


def gate(values, deps):
    values, deps = list(values), list(deps)
    return list(
        pl.pallas_call(
            gate_kernel,
            out_shape=tuple(jax.ShapeDtypeStruct(m.shape, m.dtype) for m in values),
            in_specs=[pl.BlockSpec(memory_space=pl.ANY)] * (len(values) + len(deps)),
            out_specs=tuple([pl.BlockSpec(memory_space=pl.ANY)] * len(values)),
            input_output_aliases={i: i for i in range(len(values))},
            cost_estimate=pl.CostEstimate(flops=1000, bytes_accessed=1000, transcendentals=0),
        )(*values, *deps)
    )


def cut_of(rows):
    return rows // 32 * 16


def piece_shapes(count, rows, columns):
    if count != 4:
        return [((rows, columns), BF16)] * (count - 1)
    cut = cut_of(rows)
    return [((m, columns), BF16) for m in (2 * cut, 2 * (rows - cut), rows - cut, cut)]


def put_pieces(refs, count, block, values):
    if count != 4:
        refs[block - 1][...] = values.astype(BF16)
        return
    to_x, to_y, x_bottom, y_top = refs
    rows = values.shape[0]
    cut = cut_of(rows)
    top, bottom = values[:cut].astype(BF16), values[cut:].astype(BF16)
    if block == 1:
        to_x[cut:, :] = top
        x_bottom[...] = bottom
    elif block == 2:
        y_top[...] = top
        to_y[rows - cut :, :] = bottom
    else:
        to_x[:cut, :] = top
        to_y[: rows - cut, :] = bottom


def add_terms(count, refs):
    total = refs[0][...].astype(F32)
    if count != 4:
        for ref in refs[1:]:
            total = total + ref[...].astype(F32)
        return total
    from_x, from_y, x_bottom, y_top = [ref[...] for ref in refs[1:]]
    cut, rest = y_top.shape[0], x_bottom.shape[0]
    by_x = jnp.concatenate([from_x[cut:], x_bottom], axis=0)
    by_y = jnp.concatenate([y_top, from_y[rest:]], axis=0)
    return total + by_x.astype(F32) + by_y.astype(F32)


def norm_stats(values):
    mean = jnp.mean(values, axis=1, keepdims=True)
    centered = values - mean
    var = jnp.mean(centered * centered, axis=1, keepdims=True)
    scale = lax.rsqrt(var + NORM_EPSILON)
    return centered * scale, scale


def norm_back(values, gain, grad):
    unit, scale = norm_stats(values)
    grad_unit = grad * gain
    inner = jnp.mean(grad_unit * unit, axis=1, keepdims=True)
    grad_values = scale * (grad_unit - jnp.mean(grad_unit, axis=1, keepdims=True) - unit * inner)
    return grad_values, jnp.sum(grad * unit, axis=0, keepdims=True)


def self_forward_kernel(count, parts, head_size, normed, *refs):
    part_refs, refs = refs[:parts], refs[parts:]
    weight_ref, gains_ref, shift_ref = refs[:3]
    rows_ref, triples_ref = refs[3:5]
    mixed_refs, (held_ref, done) = refs[5:-2], refs[-2:]
    copy = pltpu.make_async_copy(weight_ref.at[:, : held_ref.shape[1]], held_ref, done)
    copy.start()
    stride = held_ref.shape[1] // 3
    rows, width = mixed_refs[0].shape
    factor = LOG2_E / math.sqrt(head_size)
    start = 0
    for ref in part_refs:
        values = ref[...]
        if not normed:
            unit, _ = norm_stats(values.astype(F32))
            values = (unit * gains_ref[0:1, :] + shift_ref[...]).astype(BF16)
        rows_ref[start : start + ref.shape[0], :] = values
        start += ref.shape[0]
    copy.wait()
    for j in range(count):
        at = slice(j * rows, (j + 1) * rows)
        triples_ref[at, :] = dot_nn(rows_ref[at, :], held_ref[...]).astype(BF16)
    for j in range(count):
        at = slice(j * rows, (j + 1) * rows)
        for h in range(width // head_size):
            low = h * head_size
            q = triples_ref[at, low : low + head_size]
            k = triples_ref[:, stride + low : stride + low + head_size]
            v = triples_ref[:, 2 * stride + low : 2 * stride + low + head_size]
            scores = dot_nt(q, k)
            top = jnp.max(scores, axis=1, keepdims=True)
            weights = jnp.exp2((scores - top) * factor)
            total = jnp.sum(weights, axis=1, keepdims=True)
            mixed = dot_nn(weights.astype(BF16), v) * (1.0 / total)
            mixed_refs[j][:, low : low + head_size] = mixed.astype(BF16)


def self_forward(parts, weight, gains, shift, head_size, count, width, normed, deps=()):
    total = sum(m.shape[0] for m in parts)
    columns = parts[0].shape[1]
    held = (columns, 3 * padded_width(width))
    found = call(
        functools.partial(self_forward_kernel, count, len(parts), head_size, normed),
        [((total, columns), BF16), ((total, held[1]), BF16)]
        + [((total // count, width), BF16)] * count,
        [pltpu.VMEM(held, BF16), pltpu.SemaphoreType.DMA],
        24,
        *parts,
        weight,
        gains,
        shift[None],
        deps=deps,
        outside=(len(parts),),
    )
    return found[0], found[1], list(found[2:])


def attention_back(q, k, v, grad, valid, head_size):
    factor = LOG2_E / math.sqrt(head_size)
    scores = dot_nt(k, q)
    if valid is not None:
        scores = jnp.where(valid, scores, -1e30)
    top = jnp.max(scores, axis=0, keepdims=True)
    weights = jnp.exp2((scores - top) * factor)
    weights = weights * (1.0 / jnp.sum(weights, axis=0, keepdims=True))
    grad_weights = dot_nt(v, grad)
    delta = jnp.sum(grad_weights * weights, axis=0, keepdims=True)
    grad_scores = (weights * (grad_weights - delta)).astype(BF16)
    scale = 1.0 / math.sqrt(head_size)
    return (
        dot_tn(grad_scores, k) * scale,
        dot_nn(grad_scores, q) * scale,
        dot_nn(weights.astype(BF16), grad),
    )


def self_backward_kernel(count, head_size, step, triples_ref, *refs):
    grad_refs, (weight_ref, out_ref, own_ref) = refs[:count], refs[count : count + 3]
    piece_refs, (keys_ref, values_ref, held_ref, done) = refs[count + 3 : -4], refs[-4:]
    copy = pltpu.make_async_copy(weight_ref.at[:, : held_ref.shape[1]], held_ref, done)
    copy.start()
    total = triples_ref.shape[0]
    rows, width = grad_refs[0].shape
    stride = held_ref.shape[1] // 3
    for h in range(width // head_size):
        low = h * head_size
        k = triples_ref[:, stride + low : stride + low + head_size]
        v = triples_ref[:, 2 * stride + low : 2 * stride + low + head_size]
        for i in range(total // step):
            at = slice(i * step, (i + 1) * step)
            inside = (i * step) % rows
            q = triples_ref[at, low : low + head_size]
            grad = grad_refs[i * step // rows][inside : inside + step, low : low + head_size]
            grad_q, grad_k, grad_v = attention_back(q, k, v, grad, None, head_size)
            out_ref[at, low : low + head_size] = grad_q.astype(BF16)
            if i == 0:
                keys_ref[...] = grad_k
                values_ref[...] = grad_v
            else:
                keys_ref[...] += grad_k
                values_ref[...] += grad_v
        out_ref[:, stride + low : stride + low + head_size] = keys_ref[...].astype(BF16)
        out_ref[:, 2 * stride + low : 2 * stride + low + head_size] = values_ref[...].astype(BF16)
    if stride > width:
        for g in range(3):
            out_ref[:, g * stride + width : (g + 1) * stride] = jnp.zeros((total, stride - width), BF16)
    copy.wait()
    for j in range(count):
        found = dot_nt(out_ref[j * rows : (j + 1) * rows, :], held_ref[...])
        if j == 0:
            own_ref[...] = found
        else:
            put_pieces(piece_refs, count, j, found)


def self_backward(triples, grads, weight, head_size, deps=()):
    count = len(grads)
    total, rows, columns = triples.shape[0], grads[0].shape[0], weight.shape[0]
    step = min(256, rows)
    found = call(
        functools.partial(self_backward_kernel, count, head_size, step),
        [(triples.shape, BF16), ((rows, columns), F32)] + piece_shapes(count, rows, columns),
        [
            pltpu.VMEM((total, head_size), F32),
            pltpu.VMEM((total, head_size), F32),
            pltpu.VMEM((columns, triples.shape[1]), BF16),
            pltpu.SemaphoreType.DMA,
        ],
        32,
        triples,
        *grads,
        weight,
        deps=deps,
        outside=(1 + count,),
    )
    return found[0], found[1], list(found[2:])


def fill_corner(count, matrix_refs, scalars_ref, corner_ref):
    if len(matrix_refs) == count:
        return list(matrix_refs)
    odd = scalars_ref[2 * count]
    half = matrix_refs[-1].shape[0]
    corner_ref[pl.ds(pl.multiple_of(odd * half, half), half), :] = matrix_refs[-2][...]
    corner_ref[pl.ds(pl.multiple_of((1 - odd) * half, half), half), :] = matrix_refs[-1][...]
    return list(matrix_refs[:-2]) + [corner_ref]


def corner_scratch(count, matrices):
    rows, columns = matrices[0].shape
    return pltpu.VMEM((rows, columns) if len(matrices) > count else (16, 128), BF16)


def fill_pairs(count, block, pair_refs, pairs_ref):
    padded, columns = pairs_ref.shape[1:]
    place = 0
    for ref in pair_refs:
        j, low = divmod(place, padded)
        pairs_ref[j, low : low + ref.shape[0], :] = ref[:, block * columns : (block + 1) * columns]
        place += ref.shape[0]


def middle_forward_kernel(block, count, matrix_parts, pair_parts, head_size, scalars_ref, *refs):
    mixed_refs, refs = refs[:count], refs[count:]
    matrix_refs, refs = refs[:matrix_parts], refs[matrix_parts:]
    pair_refs, refs = refs[:pair_parts], refs[pair_parts:]
    hidden_ref, gains_ref = refs[:2]
    (self_ref, after_self_ref, norm_ref, queries_ref, cross_ref, after_cross_ref) = refs[2:8]
    mlp_ref = refs[8]
    wide_ref, narrow_ref, corner_ref, pairs_ref = refs[-4:]
    width = mixed_refs[0].shape[1]
    stride = matrix_refs[0].shape[1] // 3
    matrices = fill_corner(count, matrix_refs, scalars_ref, corner_ref)
    fill_pairs(count, block, pair_refs, pairs_ref)
    order = [scalars_ref[i] for i in range(count)]
    relative = [scalars_ref[count + j] for j in range(count)]
    length = scalars_ref[2 * count + 1]
    spans = [slice(a * width, (a + 1) * width) for a in range(count)]

    for j in range(count):
        narrow_ref[relative[j]] = mixed_refs[j][...]
    for a in range(count):
        self_ref[:, spans[a]] = narrow_ref[a]
    tokens = self_ref[...]
    for i in range(count):
        wide_ref[order[i]] = dot_nn(tokens, matrices[i][:, :width])
    for a in range(count):
        after_self_ref[:, spans[a]] = hidden_ref[:, spans[a]].astype(F32) + wide_ref[a]
    normed = (norm_stats(after_self_ref[...])[0] * gains_ref[1:2, :]).astype(BF16)
    norm_ref[...] = normed
    for i in range(count):
        found = dot_nn(normed, matrices[i][:, stride : stride + width])
        queries_ref[order[i] ^ relative[0]] = found.astype(BF16)

    factor = LOG2_E / math.sqrt(head_size)
    keys_rows = pairs_ref.shape[1]
    valid = lax.broadcasted_iota(jnp.int32, (1, keys_rows), 1) < length
    pair_stride = pairs_ref.shape[2] // 2
    for j in range(count):
        for h in range(width // head_size):
            at = slice(h * head_size, (h + 1) * head_size)
            values_at = slice(pair_stride + h * head_size, pair_stride + (h + 1) * head_size)
            scores = dot_nt(queries_ref[j, :, at], pairs_ref[j, :, at])
            scores = jnp.where(valid, scores, -1e30)
            top = jnp.max(scores, axis=1, keepdims=True)
            weights = jnp.exp2((scores - top) * factor)
            total = jnp.sum(weights, axis=1, keepdims=True)
            mixed = dot_nn(weights.astype(BF16), pairs_ref[j, :, values_at]) * (1.0 / total)
            narrow_ref[relative[j], :, at] = mixed.astype(BF16)
    for a in range(count):
        cross_ref[:, spans[a]] = narrow_ref[a]
    tokens = cross_ref[...]
    for i in range(count):
        wide_ref[order[i]] = dot_nn(tokens, matrices[i][:, 2 * stride : 2 * stride + width])
    for a in range(count):
        after_cross_ref[:, spans[a]] = after_self_ref[:, spans[a]] + wide_ref[a]
    mlp_ref[...] = (norm_stats(after_cross_ref[...])[0] * gains_ref[2:3, :]).astype(BF16)


def pairs_scratch(count, pairs):
    return pltpu.VMEM(
        (count, sum(m.shape[0] for m in pairs) // count, pairs[0].shape[1] // 2), BF16
    )


def middle_forward(block, scalars, mixed, matrices, pairs, hidden, gains, head_size, deps=()):
    count = len(mixed)
    rows, columns = hidden.shape
    width = columns // count
    return call(
        functools.partial(
            middle_forward_kernel, block, count, len(matrices), len(pairs), head_size
        ),
        [
            ((rows, columns), BF16),
            ((rows, columns), F32),
            ((rows, columns), BF16),
            ((count, rows, width), BF16),
            ((rows, columns), BF16),
            ((rows, columns), F32),
            ((rows, columns), BF16),
        ],
        [
            pltpu.VMEM((count, rows, width), F32),
            pltpu.VMEM((count, rows, width), BF16),
            corner_scratch(count, matrices),
            pairs_scratch(count, pairs),
        ],
        23,
        *mixed,
        *matrices,
        *pairs,
        hidden,
        gains,
        scalars=scalars,
        deps=deps,
    )


def middle_backward_kernel(block, count, matrix_parts, pair_parts, terms, head_size, scalars_ref, *refs):
    matrix_refs, refs = refs[:matrix_parts], refs[matrix_parts:]
    pair_refs, refs = refs[:pair_parts], refs[pair_parts:]
    term_refs, refs = refs[:terms], refs[terms:]
    grad_out_ref, after_cross_ref, after_self_ref, queries_ref, gains_ref = refs[:5]
    out_ref, self_branch_ref, query_branch_ref, cross_branch_ref, gain_ref = refs[5:10]
    mixed_grad_refs, refs = refs[10 : 10 + count], refs[10 + count :]
    own_pairs_ref, pair_grad_refs = refs[0], refs[1:-6]
    wide_ref, narrow_ref, query_ref, corner_ref, pairs_ref, pair_total_ref = refs[-6:]
    width = queries_ref.shape[2]
    stride = matrix_refs[0].shape[1] // 3
    matrices = fill_corner(count, matrix_refs, scalars_ref, corner_ref)
    fill_pairs(count, block, pair_refs, pairs_ref)
    order = [scalars_ref[i] for i in range(count)]
    relative = [scalars_ref[count + j] for j in range(count)]
    length = scalars_ref[2 * count + 1]
    spans = [slice(a * width, (a + 1) * width) for a in range(count)]

    def back(branch_ref, group):
        columns = slice(group * stride, group * stride + width)
        total = dot_nt(branch_ref[0], matrices[0][:, columns])
        for i in range(1, count):
            total = total + dot_nt(branch_ref[i], matrices[i][:, columns])
        return total

    def divide(values):
        for a in range(count):
            narrow_ref[a] = values[:, spans[a]].astype(BF16)

    grad, grad_gain = norm_back(
        after_cross_ref[...], gains_ref[2:3, :], add_terms(count, term_refs)
    )
    gain_ref[1:2, :] = grad_gain
    wide_ref[...] = grad + grad_out_ref[...].astype(F32)
    divide(wide_ref[...])
    for i in range(count):
        cross_branch_ref[i] = narrow_ref[order[i]]
    divide(back(cross_branch_ref, 2))

    keys_rows = pairs_ref.shape[1]
    valid = lax.broadcasted_iota(jnp.int32, (keys_rows, 1), 0) < length
    pair_stride = pairs_ref.shape[2] // 2
    if pair_stride > width:
        for g in range(2):
            pair_total_ref[:, g * pair_stride + width : (g + 1) * pair_stride] = jnp.zeros(
                (keys_rows, pair_stride - width), F32
            )
    for j in range(count):
        for h in range(width // head_size):
            at = slice(h * head_size, (h + 1) * head_size)
            values_at = slice(pair_stride + h * head_size, pair_stride + (h + 1) * head_size)
            grad_q, grad_k, grad_v = attention_back(
                queries_ref[j, :, at],
                pairs_ref[j, :, at],
                pairs_ref[j, :, values_at],
                narrow_ref[relative[j], :, at],
                valid,
                head_size,
            )
            query_ref[j, :, at] = grad_q.astype(BF16)
            pair_total_ref[:, at] = grad_k
            pair_total_ref[:, values_at] = grad_v
        if j == 0:
            own_pairs_ref[...] = pair_total_ref[...]
        else:
            pair_grad_refs[j - 1][...] = pair_total_ref[...].astype(BF16)
    for i in range(count):
        query_branch_ref[i] = query_ref[order[i] ^ relative[0]]
    grad, grad_gain = norm_back(after_self_ref[...], gains_ref[1:2, :], back(query_branch_ref, 1))
    gain_ref[0:1, :] = grad_gain
    out_ref[...] = grad + wide_ref[...]
    divide(out_ref[...])
    for i in range(count):
        self_branch_ref[i] = narrow_ref[order[i]]
    divide(back(self_branch_ref, 0))
    for j in range(count):
        mixed_grad_refs[j][...] = narrow_ref[relative[j]]


def middle_backward(
    block, scalars, matrices, pairs, terms, grad_out, after_cross, after_self, queries, gains, head_size, deps=()
):
    count, rows, width = queries.shape
    columns = count * width
    branch = ((count, rows, width), BF16)
    text = pairs_scratch(count, pairs)
    keys_rows, pair_columns = text.shape[1:]
    found = call(
        functools.partial(
            middle_backward_kernel, block, count, len(matrices), len(pairs), len(terms), head_size
        ),
        [((rows, columns), F32), branch, branch, branch, ((2, columns), F32)]
        + [((rows, width), BF16)] * count
        + [((keys_rows, pair_columns), F32)]
        + [((keys_rows, pair_columns), BF16)] * (count - 1),
        [
            pltpu.VMEM((rows, columns), F32),
            pltpu.VMEM((count, rows, width), BF16),
            pltpu.VMEM((count, rows, width), BF16),
            corner_scratch(count, matrices),
            text,
            pltpu.VMEM((keys_rows, pair_columns), F32),
        ],
        37,
        *matrices,
        *pairs,
        *terms,
        grad_out,
        after_cross,
        after_self,
        queries,
        gains,
        scalars=scalars,
        deps=deps,
    )
    found = list(found)
    return found[:5] + [found[5 : 5 + count], found[5 + count], found[6 + count :]]


def mlp_up_kernel(count, parts, *refs):
    part_refs, (up_ref, rows_ref, up_rows_ref, activated_ref) = refs[:parts], refs[parts:]
    start = 0
    for ref in part_refs:
        rows_ref[start : start + ref.shape[0], :] = ref[...]
        start += ref.shape[0]
    rows = start // count
    for j in range(count):
        at = slice(j * rows, (j + 1) * rows)
        values = dot_nn(rows_ref[at, :], up_ref[...])
        up_rows_ref[at, :] = values
        inner = GELU_SCALE * (values + 0.044715 * (values * values * values))
        activated_ref[at, :] = (0.5 * values * (1.0 + jnp.tanh(inner))).astype(BF16)


def mlp_up(parts, up, count, deps=()):
    total, columns, hidden = sum(m.shape[0] for m in parts), up.shape[0], up.shape[1]
    return call(
        functools.partial(mlp_up_kernel, count, len(parts)),
        [((total, columns), BF16), ((total, hidden), F32), ((total, hidden), BF16)],
        [],
        15,
        *parts,
        up,
        deps=deps,
    )


def mlp_down_kernel(count, activated_ref, down_ref, own_ref, *piece_refs):
    rows = own_ref.shape[0]
    for j in range(count - 1, -1, -1):
        found = dot_nn(activated_ref[j * rows : (j + 1) * rows, :], down_ref[...])
        if j == 0:
            own_ref[...] = found
        else:
            put_pieces(piece_refs, count, j, found)


def mlp_down(activated, down, count, deps=()):
    rows, columns = activated.shape[0] // count, down.shape[1]
    found = call(
        functools.partial(mlp_down_kernel, count),
        [((rows, columns), F32)] + piece_shapes(count, rows, columns),
        [],
        11,
        activated,
        down,
        deps=deps,
    )
    return found[0], list(found[1:])


def stack_kernel(*refs):
    start = 0
    for ref in refs[:-1]:
        refs[-1][start : start + ref.shape[0], :] = ref[...]
        start += ref.shape[0]


def stack_rows(parts, deps=()):
    shape = (sum(m.shape[0] for m in parts), parts[0].shape[1])
    return call(stack_kernel, [(shape, parts[0].dtype)], [], 3, *parts, deps=deps)[0]


def mlp_backward_kernel(count, parts, *refs):
    part_refs, refs = refs[:parts], refs[parts:]
    up_rows_ref, up_ref, down_ref, rows_ref, grad_up_ref, own_ref = refs[:6]
    piece_refs = refs[6:]
    start = 0
    for ref in part_refs:
        rows_ref[start : start + ref.shape[0], :] = ref[...]
        start += ref.shape[0]
    rows = start // count
    for j in range(count - 1, -1, -1):
        at = slice(j * rows, (j + 1) * rows)
        grad = dot_nt(rows_ref[at, :], down_ref[...])
        values = up_rows_ref[at, :]
        square = values * values
        bent = jnp.tanh(GELU_SCALE * (values + 0.044715 * (values * square)))
        slope = 0.5 * (1.0 + bent) + 0.5 * values * (1.0 - bent * bent) * (
            GELU_SCALE * (1.0 + 3.0 * 0.044715 * square)
        )
        grad_up_ref[at, :] = (grad * slope).astype(BF16)
        found = dot_nt(grad_up_ref[at, :], up_ref[...])
        if j == 0:
            own_ref[...] = found
        else:
            put_pieces(piece_refs, count, j, found)


def mlp_backward(parts, up_rows, up, down, count, deps=()):
    total, columns, hidden = sum(m.shape[0] for m in parts), up.shape[0], up.shape[1]
    rows = total // count
    found = call(
        functools.partial(mlp_backward_kernel, count, len(parts)),
        [((total, columns), BF16), ((total, hidden), BF16), ((rows, columns), F32)]
        + piece_shapes(count, rows, columns),
        [],
        22,
        *parts,
        up_rows,
        up,
        down,
        deps=deps,
    )
    return list(found[:3]) + [list(found[3:])]


def outer_kernel(count, groups, half, scalars_ref, *refs):
    rows_refs, branch_refs, refs = refs[:groups], refs[groups : 2 * groups], refs[2 * groups :]
    out_refs, turned_ref = refs[:-1], refs[-1]
    width = branch_refs[0].shape[2]
    stride = padded_width(width)
    odd = scalars_ref[2 * count]
    for g in range(groups):
        at = slice(g * stride, g * stride + width)
        turned_ref[...] = rows_refs[g][...].T
        out_refs[0][:, at] = dot_nn(turned_ref[...], branch_refs[g][0]).astype(BF16)
        for i in range(1, count):
            if not half:
                out_refs[i][:, at] = dot_nn(turned_ref[...], branch_refs[g][i]).astype(BF16)
                continue
            for k in range(2):
                low = pl.multiple_of((odd if k == 0 else 1 - odd) * half, half)
                found = dot_nn(turned_ref[pl.ds(low, half), :], branch_refs[g][i])
                out_refs[2 * i - 1 + k][:, at] = found.astype(BF16)
    if stride > width:
        for ref in out_refs:
            for g in range(groups):
                ref[:, g * stride + width : (g + 1) * stride] = jnp.zeros(
                    (ref.shape[0], stride - width), BF16
                )


def outer(scalars, rows, branches, deps=()):
    count, tokens, width = branches[0].shape
    groups, columns = len(rows), rows[0].shape[1]
    stride = padded_width(width)
    half = columns // 2 if count == 4 else 0
    shapes = [((columns, groups * stride), BF16)]
    if half:
        shapes += [((half, groups * stride), BF16)] * (2 * (count - 1))
    else:
        shapes = shapes * count
    return list(
        call(
            functools.partial(outer_kernel, count, groups, half),
            shapes,
            [pltpu.VMEM((columns, tokens), BF16)],
            3.5 * groups,
            *rows,
            *branches,
            scalars=scalars,
            deps=deps,
        )
    )


def join_kernel(count, scalars_ref, own_ref, mine_ref, other_ref, out_ref):
    odd = scalars_ref[2 * count]
    half = mine_ref.shape[0]
    for ref, place in ((mine_ref, odd), (other_ref, 1 - odd)):
        at = pl.ds(pl.multiple_of(place * half, half), half)
        out_ref[at, :] = (own_ref[at, :].astype(F32) + ref[...].astype(F32)).astype(BF16)


def join_halves(scalars, own, mine, other):
    count = lax.axis_size("seq")
    (found,) = call(
        functools.partial(join_kernel, count),
        [(own.shape, BF16)],
        [],
        4,
        own,
        mine,
        other,
        scalars=scalars,
    )
    return found


def joined_stats(first, second):
    count = first.shape[1] + second.shape[1]
    mean = (jnp.sum(first, axis=1, keepdims=True) + jnp.sum(second, axis=1, keepdims=True)) / count
    first, second = first - mean, second - mean
    var = (
        jnp.sum(first * first, axis=1, keepdims=True)
        + jnp.sum(second * second, axis=1, keepdims=True)
    ) / count
    scale = lax.rsqrt(var + NORM_EPSILON)
    return first * scale, second * scale, scale


def skip_forward_kernel(count, matrix_parts, terms, scalars_ref, *refs):
    matrix_refs, refs = refs[:matrix_parts], refs[matrix_parts:]
    term_refs, refs = refs[:terms], refs[terms:]
    residual_ref, second_ref, gains_ref, next_ref, shift_ref = refs[:5]
    first_ref, joined_ref, out_ref, norm_ref, wide_ref, corner_ref = refs[5:]
    rows, columns = first_ref.shape
    width = columns // count
    matrices = fill_corner(count, matrix_refs, scalars_ref, corner_ref)
    first_ref[...] = residual_ref[...] + add_terms(count, term_refs)
    first, second, _ = joined_stats(first_ref[...], second_ref[...].astype(F32))
    joined_ref[:, :columns] = (first * gains_ref[0:1, :]).astype(BF16)
    joined_ref[:, columns:] = (second * gains_ref[1:2, :]).astype(BF16)
    joined = joined_ref[...]
    for i in range(count):
        wide_ref[scalars_ref[i]] = dot_nn(joined, matrices[i][:, :width])
    for a in range(count):
        out_ref[:, a * width : (a + 1) * width] = wide_ref[a]
    normed = norm_stats(out_ref[...])[0] * next_ref[0:1, :] + shift_ref[...]
    norm_ref[...] = normed.astype(BF16)


def skip_forward(scalars, matrices, terms, residual, second, gains, next_gains, shift, deps=()):
    rows, columns = residual.shape
    count = lax.axis_size("seq")
    return call(
        functools.partial(skip_forward_kernel, count, len(matrices), len(terms)),
        [
            ((rows, columns), F32),
            ((rows, 2 * columns), BF16),
            ((rows, columns), F32),
            ((rows, columns), BF16),
        ],
        [pltpu.VMEM((count, rows, columns // count), F32), corner_scratch(count, matrices)],
        11,
        *matrices,
        *terms,
        residual,
        second,
        gains,
        next_gains,
        shift[None],
        scalars=scalars,
        deps=deps,
    )


def skip_backward_kernel(count, matrix_parts, terms, scalars_ref, *refs):
    matrix_refs, refs = refs[:matrix_parts], refs[matrix_parts:]
    term_refs, refs = refs[:terms], refs[terms:]
    hidden_ref, next_ref, residual_ref, first_ref, second_ref, gains_ref = refs[:6]
    branch_ref, grad_first_ref, grad_second_ref, vectors_ref, round_ref = refs[6:11]
    narrow_ref, corner_ref = refs[11:]
    rows, columns = first_ref.shape
    width = columns // count
    matrices = fill_corner(count, matrix_refs, scalars_ref, corner_ref)
    grad_norm = add_terms(count, term_refs)
    vectors_ref[0:1, :] = jnp.sum(grad_norm, axis=0, keepdims=True)
    grad, grad_gain = norm_back(hidden_ref[...], next_ref[0:1, :], grad_norm)
    vectors_ref[1:2, :] = grad_gain
    grad = grad + residual_ref[...]
    for a in range(count):
        narrow_ref[a] = grad[:, a * width : (a + 1) * width].astype(BF16)
    for i in range(count):
        branch_ref[i] = narrow_ref[scalars_ref[i]]

    def back(at):
        total = dot_nt(branch_ref[0], matrices[0][at, :width])
        for i in range(1, count):
            total = total + dot_nt(branch_ref[i], matrices[i][at, :width])
        return total

    grad_first_ref[...] = back(slice(0, columns))
    grad_second_ref[...] = back(slice(columns, 2 * columns))
    first, second, scale = joined_stats(first_ref[...], second_ref[...].astype(F32))
    vectors_ref[2:3, :] = jnp.sum(grad_first_ref[...] * first, axis=0, keepdims=True)
    vectors_ref[3:4, :] = jnp.sum(grad_second_ref[...] * second, axis=0, keepdims=True)
    grad_first = grad_first_ref[...] * gains_ref[0:1, :]
    grad_second = grad_second_ref[...] * gains_ref[1:2, :]
    mean = (
        jnp.sum(grad_first, axis=1, keepdims=True) + jnp.sum(grad_second, axis=1, keepdims=True)
    ) / (2 * columns)
    inner = (
        jnp.sum(grad_first * first, axis=1, keepdims=True)
        + jnp.sum(grad_second * second, axis=1, keepdims=True)
    ) / (2 * columns)
    grad_first_ref[...] = scale * (grad_first - mean - first * inner)
    grad_second_ref[...] = scale * (grad_second - mean - second * inner)
    round_ref[...] = grad_first_ref[...].astype(BF16)


def skip_backward(
    scalars, matrices, terms, hidden, next_gains, residual, first, second, gains, deps=()
):
    rows, columns = first.shape
    count = lax.axis_size("seq")
    narrow = (count, rows, columns // count)
    return call(
        functools.partial(skip_backward_kernel, count, len(matrices), len(terms)),
        [
            (narrow, BF16),
            ((rows, columns), F32),
            ((rows, columns), F32),
            ((4, columns), F32),
            ((rows, columns), BF16),
        ],
        [pltpu.VMEM(narrow, BF16), corner_scratch(count, matrices)],
        15,
        *matrices,
        *terms,
        hidden,
        next_gains,
        residual,
        first,
        second,
        gains,
        scalars=scalars,
        deps=deps,
    )


def open_backward_kernel(count, terms, *refs):
    term_refs, refs = refs[:terms], refs[terms:]
    hidden_ref, gains_ref, residual_ref, out_ref, vectors_ref = refs
    grad_norm = add_terms(count, term_refs)
    vectors_ref[0:1, :] = jnp.sum(grad_norm, axis=0, keepdims=True)
    grad, grad_gain = norm_back(hidden_ref[...].astype(F32), gains_ref[0:1, :], grad_norm)
    vectors_ref[1:2, :] = grad_gain
    out_ref[...] = grad + residual_ref[...]


def open_backward(terms, hidden, gains, residual, deps=()):
    count = lax.axis_size("seq")
    return call(
        functools.partial(open_backward_kernel, count, len(terms)),
        [(residual.shape, F32), ((2, residual.shape[1]), F32)],
        [],
        5,
        *terms,
        hidden,
        gains,
        residual,
        deps=deps,
    )


def close_kernel(count, terms, *refs):
    refs[terms + 1][...] = (refs[terms][...] + add_terms(count, refs[:terms])).astype(BF16)


def close_forward(terms, residual, deps=()):
    count = lax.axis_size("seq")
    (found,) = call(
        functools.partial(close_kernel, count, len(terms)),
        [(residual.shape, BF16)],
        [],
        3,
        *terms,
        residual,
        deps=deps,
    )
    return found


def pack_kernel(count, *refs):
    start = 0
    for ref in refs[:count]:
        refs[count][: ref.shape[0], start : start + ref.shape[1]] = ref[...]
        start += ref.shape[1]


def pack(shards, deps=()):
    rows = -(-max(m.shape[0] for m in shards) // 32) * 32
    shape = (rows, sum(m.shape[1] for m in shards))
    return call(functools.partial(pack_kernel, len(shards)), [(shape, BF16)], [], 3, *shards, deps=deps)[0]


def settle_kernel(count, parts, plan, scalars_ref, *refs):
    block_refs, refs = refs[:parts], refs[parts:]
    outs = sum(entry[3] for entry in plan)
    out_refs, stack_ref = refs[-outs - 1 : -1], refs[-1]
    for j in range(count):
        owner = scalars_ref[count + j]
        if j == count - 1 and parts > count:
            cut = block_refs[j].shape[0]
            stack_ref[owner, :cut] = block_refs[j][...]
            stack_ref[owner, cut:] = block_refs[j + 1][...]
        else:
            stack_ref[owner] = block_refs[j][...]
    place = 0
    for first, rows, groups, pieces, width, stride in plan:
        if not groups:
            for a in range(count):
                found = stack_ref[a, :rows, first : first + width]
                out_refs[place][0, a * rows : (a + 1) * rows, :] = found.astype(F32)
        for p in range(pieces):
            for g in range(groups):
                for a in range(count):
                    low = first + (p * groups + g) * stride
                    at = (g * count + a) * width
                    found = stack_ref[a, :rows, low : low + width]
                    out_refs[place + p][0, :, at : at + width] = found.astype(F32)
        place += pieces


def settle(scalars, blocks, plan, layer, layer_count, before):
    count = lax.axis_size("seq")
    shapes = []
    for _, rows, groups, pieces, width, _ in plan:
        shapes += [(rows, groups * count * width) if groups else (count * rows, width)] * pieces
    held = [] if before is None else list(before)
    inputs = [pl.BlockSpec(memory_space=pltpu.VMEM)] * len(blocks)
    inputs += [pl.BlockSpec(memory_space=pl.ANY)] * len(held)
    found = pl.pallas_call(
        functools.partial(settle_kernel, count, len(blocks), plan),
        grid=(1,),
        out_shape=[jax.ShapeDtypeStruct((layer_count,) + shape, F32) for shape in shapes],
        in_specs=[pl.BlockSpec(memory_space=pltpu.SMEM)] + inputs,
        out_specs=[pl.BlockSpec((1,) + shape, lambda i: (layer, 0, 0)) for shape in shapes],
        scratch_shapes=[pltpu.VMEM((count,) + blocks[0].shape, BF16)],
        input_output_aliases={1 + len(blocks) + i: i for i in range(len(held))},
        compiler_params=pltpu.CompilerParams(vmem_limit_bytes=VMEM_LIMIT),
        cost_estimate=pl.CostEstimate(flops=8_000_000_000, bytes_accessed=1000, transcendentals=0),
    )(scalars, *blocks, *held)
    return list(found)


def plan_of(entries):
    plan, first = [], 0
    for shard, groups, pieces, width in entries:
        rows, columns = shard.shape
        stride = columns // (groups * pieces) if groups else columns
        plan.append((first, rows, groups, pieces, width, stride))
        first += columns
    return tuple(plan)


def finish(scalars, entries, layer, layer_count, before=None, deps=()):
    blocks = gather_parts(pack([entry[0] for entry in entries], deps))
    return settle(scalars, blocks, plan_of(entries), layer, layer_count, before)


def swap_seq(block, bits):
    seq_count = lax.axis_size("seq")
    return lax.ppermute(block, "seq", [(i, i ^ bits) for i in range(seq_count)])


def swap_fsdp(block, bits):
    fsdp_count = lax.axis_size("fsdp")
    return lax.ppermute(block, "fsdp", [(i, i ^ bits) for i in range(fsdp_count)])


def swap_core(block):
    return swap_fsdp(block, 1)


def swap_by_core(block, even_bits, odd_bits):
    seq_count, fsdp_count = lax.axis_size("seq"), lax.axis_size("fsdp")
    pairs = []
    for s in range(seq_count):
        for f in range(fsdp_count):
            other = s ^ (odd_bits if f % 2 else even_bits)
            pairs.append((s * fsdp_count + f, other * fsdp_count + f))
    return lax.ppermute(block, ("seq", "fsdp"), pairs)


def add_bf16(*terms):
    total = terms[0].astype(F32)
    for term in terms[1:]:
        total = total + term.astype(F32)
    return total.astype(BF16)


def scatter_first(pieces):
    seq_count = lax.axis_size("seq")
    if seq_count != 4:
        return [swap_seq(m, j + 1) for j, m in enumerate(pieces)]
    return [swap_seq(pieces[0], 1), swap_seq(pieces[1], 2), pieces[2], pieces[3]]


def scatter_last(own, first, ready=None):
    seq_count = lax.axis_size("seq")
    if seq_count != 4:
        return [own] + first
    from_x, from_y, x_bottom, y_top = first
    if ready is not None:
        from_x, from_y = gate([from_x, from_y], ready)
    cut, rest = y_top.shape[0], x_bottom.shape[0]
    to_y, to_x = add_bf16(y_top, from_x[:cut]), add_bf16(x_bottom, from_y[:rest])
    return [own, from_x, from_y, swap_seq(to_x, 1), swap_seq(to_y, 2)]


def exchange_rel(blocks):
    return [blocks[0]] + [swap_seq(blocks[j], j) for j in range(1, len(blocks))]


def gather_first(block):
    seq_count = lax.axis_size("seq")
    if seq_count != 4:
        return [block] + [swap_seq(block, j) for j in range(1, seq_count)]
    return [block, swap_seq(block, 1), swap_seq(block, 2)]


def gather_last(first, ready=None):
    seq_count = lax.axis_size("seq")
    if seq_count != 4:
        return first
    block, from_x, from_y = first
    if ready is not None:
        from_x, from_y = gate([from_x, from_y], ready)
    cut = cut_of(block.shape[0])
    return [block, from_x, from_y, swap_seq(from_y[:cut], 1), swap_seq(from_x[cut:], 2)]


def gather_parts(block):
    return gather_last(gather_first(block))


def list_order():
    s, seq_count = lax.axis_index("seq"), lax.axis_size("seq")
    if seq_count != 4:
        return [s ^ j for j in range(seq_count)]
    odd = lax.axis_index("fsdp") % 2
    return [s, s ^ (1 + odd), s ^ (2 - odd), s ^ 3]


def spread_first(block):
    seq_count = lax.axis_size("seq")
    if seq_count != 4:
        return [block] + [swap_seq(block, j) for j in range(1, seq_count)]
    return [block, swap_by_core(block, 1, 2)]


def spread_last(blocks, ready, part_ready=None):
    seq_count = lax.axis_size("seq")
    if seq_count != 4:
        return blocks
    odd = lax.axis_index("fsdp") % 2
    block, first = blocks
    half = block.shape[0] // 2
    if ready is not None:
        (first,) = gate([first], ready)
    part = swap_by_core(lax.dynamic_slice_in_dim(first, odd * half, half, 0), 2, 1)
    other = swap_core(first)
    if part_ready is not None:
        (part,) = gate([part], part_ready)
    return [block, first, other, part, swap_core(part)]


def unspread(scalars, blocks):
    seq_count = lax.axis_size("seq")
    if seq_count != 4:
        return add_bf16(blocks[0], *[swap_seq(blocks[j], j) for j in range(1, seq_count)])
    own, first_mine, first_other, second_mine, second_other, corner_mine, corner_other = blocks
    passed = swap_by_core(add_bf16(corner_mine, swap_core(corner_other)), 2, 1)
    other = swap_by_core(add_bf16(first_other, swap_core(second_mine)), 1, 2)
    mine = swap_by_core(add_bf16(first_mine, swap_core(second_other), passed), 1, 2)
    return join_halves(scalars, own, mine, other)


def own_part(matrix, groups, padded):
    s, seq_count = lax.axis_index("seq"), lax.axis_size("seq")
    width = matrix.shape[1] // (groups * seq_count)
    parts = [
        jnp.pad(
            lax.dynamic_slice_in_dim(matrix, (g * seq_count + s) * width, width, 1),
            ((0, 0), (0, padded - width)),
        )
        for g in range(groups)
    ]
    return jnp.concatenate(parts, axis=1)


def gather_fsdp(shard):
    return lax.all_gather(shard, "fsdp", axis=0, tiled=True)


def scatter_fsdp(full):
    return lax.psum_scatter(full.astype(BF16), "fsdp", scatter_dimension=0, tiled=True)


def layer_forward(parts, hidden, scalars, gains, shift, pairs, weights, normed, deps):
    lead_part, square_parts, up_part = weights
    seq_count = lax.axis_size("seq")
    tok_rows, model_width = hidden.shape
    head_size, width = model_width // H, model_width // seq_count
    first_all, triples, mixed = self_forward(
        parts,
        lead_part,
        gains,
        shift,
        head_size,
        seq_count,
        width,
        normed,
        (square_parts[0],) + deps,
    )
    mixed_rel = exchange_rel(mixed)
    square_parts = spread_last(square_parts, [mixed[0]], mixed_rel[1:])
    self_tokens, after_self, cross_norm, queries, cross_tokens, after_cross, mlp_norm = (
        middle_forward(
            int(normed), scalars, mixed_rel, square_parts, pairs, hidden, gains, head_size
        )
    )
    mlp_parts = gather_parts(mlp_norm)
    mlp_all, up_rows, activated = mlp_up(mlp_parts, up_part, seq_count)
    saved = (
        first_all,
        triples,
        self_tokens,
        after_self,
        cross_norm,
        queries,
        cross_tokens,
        after_cross,
        mlp_all,
        up_rows,
        activated,
    )
    return (saved, square_parts, mlp_parts)


def unspread_first(blocks, ready):
    own, first_mine, first_other, second_mine, second_other, corner_mine, corner_other = blocks
    from_corner, to_other = swap_core(corner_other), swap_core(second_mine)
    to_mine = swap_core(second_other)
    sums = [add_bf16(corner_mine, from_corner), add_bf16(first_other, to_other)]
    sums = gate(sums, ready)
    hops = [swap_by_core(sums[0], 2, 1), swap_by_core(sums[1], 1, 2)]
    return own, hops, [first_mine, to_mine], sums


def unspread_last(scalars, first, hops_ready, joined_ready):
    own, hops, terms, _ = first
    passed, other = gate(hops, hops_ready)
    mine = swap_by_core(add_bf16(*terms, passed), 1, 2)
    (mine,) = gate([mine], joined_ready)
    return join_halves(scalars, own, mine, other)


def unspread_any(blocks):
    return add_bf16(blocks[0], *[swap_seq(m, j + 1) for j, m in enumerate(blocks[1:])])


def lead_part(layer, qkv, query, self_out, cross_out):
    padded = padded_width(query.shape[2] // lax.axis_size("seq"))
    return jnp.concatenate(
        [own_part(qkv[layer], 3, padded)]
        + [own_part(m[layer], 1, padded) for m in (self_out, query, cross_out)],
        axis=1,
    )


def gather_rest(layer, up, down):
    s, seq_count, fsdp_count = lax.axis_index("seq"), lax.axis_size("seq"), lax.axis_size("fsdp")
    rows = down.shape[1] // seq_count
    return (
        gather_fsdp(own_part(up[layer], fsdp_count, up.shape[2] // (fsdp_count * seq_count))),
        gather_fsdp(lax.dynamic_slice_in_dim(down[layer], s * rows, rows, 0)),
    )


def sum_vectors(vectors):
    bits = 1
    while bits < lax.axis_size("seq"):
        vectors = vectors + swap_seq(vectors, bits)
        bits *= 2
    found, bits = vectors[None], 1
    while bits < lax.axis_size("fsdp"):
        found = jnp.concatenate([found, swap_fsdp(found, bits)], axis=0)
        bits *= 2
    return found


def body(
    latents,
    skip_input,
    text_tokens,
    text_lengths,
    condition,
    cotangent,
    mod_weight,
    norm_gains,
    qkv_weight,
    query_weight,
    text_kv_weight,
    self_out_weight,
    cross_out_weight,
    up_weight,
    down_weight,
    skip_gain,
    skip_weight,
):
    seq_count, fsdp_count = lax.axis_size("seq"), lax.axis_size("fsdp")
    s, f = lax.axis_index("seq"), lax.axis_index("fsdp")
    _, tok_rows, model_width = latents.shape
    width = model_width // seq_count
    shard_rows = mod_weight.shape[1]
    text_count = text_tokens.shape[1]
    padded = -(-text_count // 32) * 32
    text_rows = jnp.pad(text_tokens[0], ((0, padded - text_count), (0, 0)))
    scalars = jnp.stack(
        [*list_order(), *[s ^ j for j in range(seq_count)], f % 2, text_lengths[0]]
    ).astype(jnp.int32)

    gain_rows = jnp.concatenate(
        [norm_gains.reshape(-1, shard_rows), skip_gain.reshape(-1, shard_rows)], axis=0
    )
    small = jnp.concatenate(
        [
            condition.reshape(fsdp_count, 1, shard_rows),
            jnp.broadcast_to(gain_rows[None], (fsdp_count,) + gain_rows.shape),
        ],
        axis=1,
    ).astype(F32)
    latent_hops = gather_first(latents[0])
    (small,) = gate([small], latent_hops[1:])
    small = lax.all_to_all(small, "fsdp", 0, 0, tiled=True)
    cond_part = small[:, 0]
    gains = jnp.swapaxes(small[:, 1:7], 0, 1).reshape(2, 3, model_width)
    skip_gains = small[:, 7:].reshape(2, model_width)
    silu_part = jax.nn.silu(cond_part)
    shift_terms = jnp.einsum("br,lrd->bld", silu_part, mod_weight.astype(F32), precision=EXACT)
    latent_parts = gather_last(latent_hops)
    (shift_terms,) = gate([shift_terms], latent_parts[-2:])
    out_hops = gather_first(gate([cotangent[0]], latent_parts[-2:])[0])
    shifts = jnp.sum(lax.all_to_all(shift_terms, "fsdp", 0, 0, tiled=True), axis=0)

    lead_stacks = (qkv_weight, query_weight, self_out_weight, cross_out_weight)
    rest_stacks = (up_weight, down_weight)
    lead_columns = 3 * padded_width(width)
    head_size = model_width // H
    fours = seq_count == 4

    padded_columns = padded_width(width)
    kv_both = gather_fsdp(
        jnp.concatenate([own_part(text_kv_weight[l], 2, padded_columns) for l in range(2)], axis=1)
    )
    lead_first = gather_fsdp(
        gate([lead_part(0, *lead_stacks)], [kv_both] + latent_hops[1:])[0]
    )
    up_first, down_first = gather_rest(0, *rest_stacks)
    pairs_all = gather_parts(dot_nn(text_rows, kv_both).astype(BF16))
    (lead_first,) = gate([lead_first], [shifts] + pairs_all[-2:])
    square_first = lead_first[:, lead_columns:]
    pairs_first, pairs_second = pairs_all, pairs_all
    saved_first, squares_first, mlp_parts = layer_forward(
        latent_parts,
        latents[0],
        scalars,
        gains[0],
        shifts[0],
        pairs_first,
        (lead_first, spread_first(square_first), up_first),
        False,
        (),
    )
    own, pieces = mlp_down(saved_first[10], down_first, seq_count)
    terms = scatter_last(own, scatter_first(pieces))

    (skip_matrix,) = gate(
        [gather_fsdp(own_part(skip_weight, 1, padded_width(width)))], mlp_parts[-2:]
    )
    skip_parts = spread_last(spread_first(skip_matrix), [own], terms[-2:])
    lead_second = gather_fsdp(lead_part(1, *lead_stacks))
    (square_second,) = gate([lead_second[:, lead_columns:]], terms[-2:])
    squares_second = spread_first(square_second)
    first_out, joined_norm, skip_out, second_norm = skip_forward(
        scalars,
        skip_parts,
        terms,
        saved_first[7],
        skip_input[0],
        skip_gains,
        gains[1],
        shifts[1],
        (square_second,),
    )

    up_second, down_second = gather_rest(1, *rest_stacks)
    saved_second, squares_second, mlp_parts = layer_forward(
        gather_parts(second_norm),
        skip_out,
        scalars,
        gains[1],
        shifts[1],
        pairs_second,
        (lead_second, squares_second, up_second),
        True,
        (),
    )
    out_parts = gather_last(out_hops, [squares_second[-1]])
    out_all = stack_rows(out_parts, (mlp_parts[1],))

    held = {}

    def block_backward(rows, grad_out, saved, block, weights, early, hooks):
        lead_matrix, square_parts, pairs, up_part, down_part = weights
        grad_down = dot_tn(saved[10], early).astype(BF16) if early is not None else None
        found_all, grad_up_rows, own, pieces = mlp_backward(
            rows,
            saved[9],
            up_part,
            down_part,
            seq_count,
            hooks[0] + ((grad_down,) if early is not None else ()),
        )
        first = scatter_first(gate(pieces, hooks[3]) if hooks[3] else pieces)
        terms = scatter_last(own, first)
        held["hops"] = first[:2]
        if early is None:
            grad_down = dot_tn(saved[10], found_all).astype(BF16)
            (grad_down,) = gate([grad_down], first[:2])
        grad_up = dot_tn(saved[8], grad_up_rows).astype(BF16)
        (grad_up,) = gate([grad_up], first[:2])
        down_shard, up_shard = scatter_fsdp(grad_down), scatter_fsdp(grad_up)
        (
            grad_after_self,
            self_branch,
            query_branch,
            cross_branch,
            gain_grads,
            mixed_grads,
            own_pairs,
            pair_blocks,
        ) = middle_backward(
            block,
            scalars,
            square_parts,
            pairs,
            terms,
            grad_out,
            saved[7],
            saved[3],
            saved[5],
            gains[block],
            head_size,
            (grad_down, grad_up) + hooks[1](grad_up_rows, terms),
        )
        mixed_rel = exchange_rel(mixed_grads)
        pair_blocks = gate(pair_blocks, mixed_rel[1:])
        pair_terms = [swap_seq(m, j + 1) for j, m in enumerate(pair_blocks)]
        grad_triples, own, pieces = self_backward(
            saved[1],
            mixed_rel,
            lead_matrix,
            head_size,
            (down_shard,) + hooks[2](mixed_grads[0]),
        )
        pair_terms = gate(pair_terms, [grad_triples])
        first = scatter_first(gate(pieces, pair_terms))
        terms = scatter_last(own, first)
        grad_qkv = dot_tn(saved[0], grad_triples).astype(BF16)
        (grad_qkv,) = gate([grad_qkv], first[:2])
        held["last"] = first[:2]
        squares = outer(
            scalars,
            [saved[2], saved[4], saved[6]],
            [self_branch, query_branch, cross_branch],
            (grad_triples,),
        )
        squares = gate(squares, first[:2])
        pair_terms = gate(pair_terms, first[:2])
        grad_pairs = add_bf16(own_pairs, *pair_terms)
        kv_part = kv_both[:, 2 * block * padded_columns : 2 * (block + 1) * padded_columns]
        grad_text = dot_nt(grad_pairs, kv_part)
        kv_shard = scatter_fsdp(dot_tn(text_rows, grad_pairs))
        return (
            terms,
            grad_after_self,
            gain_grads,
            grad_text,
            squares,
            grad_qkv,
            grad_triples,
            (scatter_fsdp(grad_qkv), kv_shard, up_shard, down_shard),
        )

    def second_own(grad_up_rows, terms):
        own, pieces = mlp_down(saved_second[10], down_second, seq_count, (grad_up_rows,))
        pieces = gate(pieces, terms[-2:])
        held["own"], held["own_hops"] = own, scatter_first(pieces)
        return tuple(pieces)

    def second_sum(ready):
        held["ready"] = ready
        return tuple(held["own_hops"][:2])

    (
        terms,
        grad_after_self,
        gain_grads,
        text_second,
        squares,
        grad_qkv,
        grad_triples,
        (qkv_shard, kv_shard, up_shard, down_shard),
    ) = block_backward(
        [out_all],
        cotangent[0],
        saved_second,
        1,
        (lead_second, squares_second, pairs_second, up_second, down_second),
        out_all,
        ((), second_own, second_sum, ()),
    )
    skip_branch, grad_first_out, grad_skip, vectors, first_round = skip_backward(
        scalars,
        skip_parts,
        terms,
        skip_out,
        gains[1],
        grad_after_self,
        first_out,
        skip_input[0],
        skip_gains,
        (grad_qkv, up_shard),
    )
    vectors_second = jnp.concatenate([vectors[:2], gain_grads, vectors[2:]], axis=0)
    first_hops = gather_first(first_round)
    first_parts = gather_last(first_hops)
    if fours:
        squares = unspread_first(squares, first_parts[-2:])
    output = close_forward(
        scatter_last(held["own"], held["own_hops"], first_hops[1:]), saved_second[7]
    )
    skip_outer = outer(scalars, [joined_norm], [skip_branch], tuple(first_hops[1:]))

    def entries(layer):
        qkv, square, kv, up, down = layer
        return (
            [
                (up, fsdp_count, 1, up.shape[1] // fsdp_count),
                (kv, 2, 1, width),
                (down, 0, 1, down.shape[1]),
            ],
            [(qkv, 3, 1, width), (square, 1, 3, width)],
        )

    early, _ = entries((qkv_shard, qkv_shard, kv_shard, up_shard, down_shard))

    def first_middle(grad_up_rows, terms):
        if fours:
            held["skip"] = unspread_first(skip_outer, terms[-2:])
        held["up"], held["terms"] = grad_up_rows, terms
        held["packed"] = pack([entry[0] for entry in early], (grad_up_rows,))
        return (held["packed"],)

    def first_self(ready):
        held["blocks"] = gather_first(gate([held["packed"]], [ready])[0])
        held["middle"] = ready
        return (qkv_shard,)

    (
        terms,
        grad_after_self,
        gain_grads,
        text_first,
        first_squares,
        grad_qkv,
        grad_triples,
        (first_qkv_shard, first_kv_shard, first_up_shard, first_down_shard),
    ) = block_backward(
        first_parts,
        grad_first_out,
        saved_first,
        0,
        (lead_first, squares_first, pairs_first, up_first, down_first),
        None,
        (
            (skip_outer[0],) + (tuple(squares[3]) if fours else ()),
            first_middle,
            first_self,
            squares[1] if fours else (),
        ),
    )
    if fours:
        joined = unspread_last(scalars, squares, held["hops"], held["last"])
        skip_joined = unspread_last(scalars, held["skip"], held["last"], terms[-2:])
        first_squares = unspread_first(first_squares, terms[-2:])
    else:
        joined, skip_joined = unspread_any(squares), unspread_any(skip_outer)
    square_shard, skip_shard = scatter_fsdp(joined), scatter_fsdp(skip_joined)
    grad_latents, vectors = open_backward(
        terms, latents[0], gains[0], grad_after_self, (grad_qkv,)
    )
    vectors_first = jnp.concatenate([vectors, gain_grads], axis=0)
    if fours:
        first_joined = unspread_last(scalars, first_squares, [grad_latents], [grad_latents])
    else:
        first_joined = unspread_any(first_squares)
    first_layer = (
        first_qkv_shard,
        scatter_fsdp(first_joined),
        first_kv_shard,
        first_up_shard,
        first_down_shard,
    )

    early_done = settle(
        scalars, gather_last(held["blocks"], terms[-2:]), plan_of(early), 1, 2, None
    )
    _, late = entries((qkv_shard, square_shard, kv_shard, up_shard, down_shard))
    late_done = finish(scalars, late, 1, 2, None, (terms[-1],))
    early, late = entries(first_layer)
    grad_up, grad_kv, grad_down = finish(scalars, early, 0, 2, early_done)
    grad_qkv, grad_self_out, grad_query, grad_cross_out = finish(scalars, late, 0, 2, late_done)
    (grad_skip_weight,) = finish(scalars, [(skip_shard, 1, 1, width)], 0, 1)

    sums = sum_vectors(jnp.concatenate([vectors_first, vectors_second], axis=0))
    first_sums, second_sums = sums[:, :4], sums[:, 4:]
    shift_grads = jnp.stack([first_sums[:, 0], second_sums[:, 0]], axis=1)
    gain_sums = jnp.stack([first_sums[:, 1:4].sum(axis=0), second_sums[:, 1:4].sum(axis=0)])
    grad_norm_gains = lax.dynamic_slice_in_dim(gain_sums, f * shard_rows, shard_rows, 2)
    grad_skip_gain = lax.dynamic_slice_in_dim(
        second_sums[:, 4:].sum(axis=0).reshape(-1), f * skip_gain.shape[0], skip_gain.shape[0], 0
    )
    turned = jnp.stack(
        [lax.dynamic_index_in_dim(silu_part, f ^ j, 0, False) for j in range(fsdp_count)]
    )
    grad_mod = jnp.einsum("br,bld->lrd", turned, shift_grads, precision=EXACT)
    grad_silu = jnp.einsum("bld,lrd->br", shift_grads, mod_weight.astype(F32), precision=EXACT)
    grad_silu = jnp.stack(
        [lax.dynamic_index_in_dim(grad_silu, f ^ j, 0, False) for j in range(fsdp_count)]
    )
    _, silu_pull = jax.vjp(jax.nn.silu, cond_part)
    grad_cond_part = silu_pull(grad_silu)[0]
    grad_condition = lax.all_to_all(grad_cond_part, "fsdp", 0, 0, tiled=True).reshape(1, -1)

    text_sum, bits = text_first + text_second, 1
    while bits < seq_count:
        text_sum = text_sum + swap_seq(text_sum.astype(BF16), bits).astype(F32)
        bits *= 2
    return (
        output[None],
        grad_latents[None],
        grad_skip[None],
        text_sum[None, :text_count],
        grad_condition,
        grad_mod,
        grad_norm_gains,
        grad_qkv,
        grad_query,
        grad_kv,
        grad_self_out,
        grad_cross_out,
        grad_up,
        grad_down,
        grad_skip_gain,
        grad_skip_weight[0],
    )


def solution(mesh):
    in_specs = (
        P("fsdp", "seq", None),
        P("fsdp", "seq", None),
        P("fsdp", None, None),
        P("fsdp"),
        P("fsdp", None),
        P("fsdp", "seq", None),
        P(None, "fsdp", None),
        P(None, None, "fsdp"),
        P(None, "fsdp", None),
        P(None, "fsdp", None),
        P(None, "fsdp", None),
        P(None, "fsdp", None),
        P(None, "fsdp", None),
        P(None, "fsdp", None),
        P(None, "fsdp", None),
        P("fsdp"),
        P("fsdp", None),
    )
    out_specs = (
        P("fsdp", "seq", None),
        P("fsdp", "seq", None),
        P("fsdp", "seq", None),
        P("fsdp", None, None),
        P("fsdp", None),
        P(None, "fsdp", None),
        P(None, None, "fsdp"),
        P(None, "fsdp", None),
        P(None, "fsdp", None),
        P(None, "fsdp", None),
        P(None, "fsdp", None),
        P(None, "fsdp", None),
        P(None, "fsdp", None),
        P(None, "fsdp", None),
        P("fsdp"),
        P("fsdp", None),
    )
    return jax.shard_map(body, mesh=mesh, in_specs=in_specs, out_specs=out_specs, check_vma=False)
```

```python
import functools
import math

import jax
import jax.numpy as jnp
from jax import lax
from jax.experimental import pallas as pl
from jax.experimental.pallas import tpu as pltpu
from jax.sharding import PartitionSpec as P

H = 16
NORM_EPSILON = 1e-06
EXACT = lax.Precision.HIGHEST
BF16 = jnp.bfloat16
F32 = jnp.float32
LOG2_E = 1.4426950408889634
GELU_SCALE = math.sqrt(2.0 / math.pi)
VMEM_LIMIT = 56 * 1024 * 1024


def dot_nn(a, b):
    return lax.dot_general(a, b, (((1,), (0,)), ((), ())), preferred_element_type=F32)


def dot_nt(a, b):
    return lax.dot_general(a, b, (((1,), (1,)), ((), ())), preferred_element_type=F32)


def dot_tn(a, b):
    return lax.dot_general(a, b, (((0,), (0,)), ((), ())), preferred_element_type=F32)


def padded_width(width):
    return -(-width // 128) * 128


def call(kernel, outs, scratch, micros, *operands, scalars=None, deps=(), outside=()):
    specs = [
        pl.BlockSpec(memory_space=pl.ANY if i in outside else pltpu.VMEM)
        for i in range(len(operands))
    ]
    if scalars is not None:
        specs = [pl.BlockSpec(memory_space=pltpu.SMEM)] + specs
        operands = (scalars,) + tuple(operands)
    used, held = len(operands), len(deps)

    def run(*refs):
        kernel(*refs[:used], *refs[used + held :])

    return pl.pallas_call(
        run,
        name=getattr(kernel, "func", kernel).__name__,
        out_shape=tuple(jax.ShapeDtypeStruct(s, d) for s, d in outs),
        in_specs=specs + [pl.BlockSpec(memory_space=pl.ANY)] * held,
        out_specs=tuple([pl.BlockSpec(memory_space=pltpu.VMEM)] * len(outs)),
        scratch_shapes=scratch,
        compiler_params=pltpu.CompilerParams(vmem_limit_bytes=VMEM_LIMIT),
        cost_estimate=pl.CostEstimate(
            flops=int(micros * 1000), bytes_accessed=1000, transcendentals=0
        ),
    )(*operands, *deps)


def gate_kernel(*refs):
    del refs


def gate(values, deps):
    values, deps = list(values), list(deps)
    return list(
        pl.pallas_call(
            gate_kernel,
            out_shape=tuple(jax.ShapeDtypeStruct(m.shape, m.dtype) for m in values),
            in_specs=[pl.BlockSpec(memory_space=pl.ANY)] * (len(values) + len(deps)),
            out_specs=tuple([pl.BlockSpec(memory_space=pl.ANY)] * len(values)),
            input_output_aliases={i: i for i in range(len(values))},
            cost_estimate=pl.CostEstimate(flops=1000, bytes_accessed=1000, transcendentals=0),
        )(*values, *deps)
    )


def cut_of(rows):
    return rows // 32 * 16


def piece_shapes(count, rows, columns):
    if count != 4:
        return [((rows, columns), BF16)] * (count - 1)
    cut = cut_of(rows)
    return [((m, columns), BF16) for m in (2 * cut, 2 * (rows - cut), rows - cut, cut)]


def put_pieces(refs, count, block, values):
    if count != 4:
        refs[block - 1][...] = values.astype(BF16)
        return
    to_x, to_y, x_bottom, y_top = refs
    rows = values.shape[0]
    cut = cut_of(rows)
    top, bottom = values[:cut].astype(BF16), values[cut:].astype(BF16)
    if block == 1:
        to_x[cut:, :] = top
        x_bottom[...] = bottom
    elif block == 2:
        y_top[...] = top
        to_y[rows - cut :, :] = bottom
    else:
        to_x[:cut, :] = top
        to_y[: rows - cut, :] = bottom


def add_terms(count, refs):
    total = refs[0][...].astype(F32)
    if count != 4:
        for ref in refs[1:]:
            total = total + ref[...].astype(F32)
        return total
    from_x, from_y, x_bottom, y_top = [ref[...] for ref in refs[1:]]
    cut, rest = y_top.shape[0], x_bottom.shape[0]
    by_x = jnp.concatenate([from_x[cut:], x_bottom], axis=0)
    by_y = jnp.concatenate([y_top, from_y[rest:]], axis=0)
    return total + by_x.astype(F32) + by_y.astype(F32)


def norm_stats(values):
    mean = jnp.mean(values, axis=1, keepdims=True)
    centered = values - mean
    var = jnp.mean(centered * centered, axis=1, keepdims=True)
    scale = lax.rsqrt(var + NORM_EPSILON)
    return centered * scale, scale


def norm_back(values, gain, grad):
    unit, scale = norm_stats(values)
    grad_unit = grad * gain
    inner = jnp.mean(grad_unit * unit, axis=1, keepdims=True)
    grad_values = scale * (grad_unit - jnp.mean(grad_unit, axis=1, keepdims=True) - unit * inner)
    return grad_values, jnp.sum(grad * unit, axis=0, keepdims=True)


def self_forward_kernel(count, parts, head_size, normed, *refs):
    part_refs, refs = refs[:parts], refs[parts:]
    weight_ref, gains_ref, shift_ref = refs[:3]
    rows_ref, triples_ref = refs[3:5]
    mixed_refs, (held_ref, done) = refs[5:-2], refs[-2:]
    copy = pltpu.make_async_copy(weight_ref.at[:, : held_ref.shape[1]], held_ref, done)
    copy.start()
    stride = held_ref.shape[1] // 3
    rows, width = mixed_refs[0].shape
    factor = LOG2_E / math.sqrt(head_size)
    start = 0
    for ref in part_refs:
        values = ref[...]
        if not normed:
            unit, _ = norm_stats(values.astype(F32))
            values = (unit * gains_ref[0:1, :] + shift_ref[...]).astype(BF16)
        rows_ref[start : start + ref.shape[0], :] = values
        start += ref.shape[0]
    copy.wait()
    for j in range(count):
        at = slice(j * rows, (j + 1) * rows)
        triples_ref[at, :] = dot_nn(rows_ref[at, :], held_ref[...]).astype(BF16)
    for j in range(count):
        at = slice(j * rows, (j + 1) * rows)
        for h in range(width // head_size):
            low = h * head_size
            q = triples_ref[at, low : low + head_size]
            k = triples_ref[:, stride + low : stride + low + head_size]
            v = triples_ref[:, 2 * stride + low : 2 * stride + low + head_size]
            scores = dot_nt(q, k)
            top = jnp.max(scores, axis=1, keepdims=True)
            weights = jnp.exp2((scores - top) * factor)
            total = jnp.sum(weights, axis=1, keepdims=True)
            mixed = dot_nn(weights.astype(BF16), v) * (1.0 / total)
            mixed_refs[j][:, low : low + head_size] = mixed.astype(BF16)


def self_forward(parts, weight, gains, shift, head_size, count, width, normed, deps=()):
    total = sum(m.shape[0] for m in parts)
    columns = parts[0].shape[1]
    held = (columns, 3 * padded_width(width))
    found = call(
        functools.partial(self_forward_kernel, count, len(parts), head_size, normed),
        [((total, columns), BF16), ((total, held[1]), BF16)]
        + [((total // count, width), BF16)] * count,
        [pltpu.VMEM(held, BF16), pltpu.SemaphoreType.DMA],
        24,
        *parts,
        weight,
        gains,
        shift[None],
        deps=deps,
        outside=(len(parts),),
    )
    return found[0], found[1], list(found[2:])


def attention_back(q, k, v, grad, valid, head_size):
    factor = LOG2_E / math.sqrt(head_size)
    scores = dot_nt(k, q)
    if valid is not None:
        scores = jnp.where(valid, scores, -1e30)
    top = jnp.max(scores, axis=0, keepdims=True)
    weights = jnp.exp2((scores - top) * factor)
    weights = weights * (1.0 / jnp.sum(weights, axis=0, keepdims=True))
    grad_weights = dot_nt(v, grad)
    delta = jnp.sum(grad_weights * weights, axis=0, keepdims=True)
    grad_scores = (weights * (grad_weights - delta)).astype(BF16)
    scale = 1.0 / math.sqrt(head_size)
    return (
        dot_tn(grad_scores, k) * scale,
        dot_nn(grad_scores, q) * scale,
        dot_nn(weights.astype(BF16), grad),
    )


def self_backward_kernel(count, head_size, step, triples_ref, *refs):
    grad_refs, (weight_ref, out_ref, own_ref) = refs[:count], refs[count : count + 3]
    piece_refs, (keys_ref, values_ref, held_ref, done) = refs[count + 3 : -4], refs[-4:]
    copy = pltpu.make_async_copy(weight_ref.at[:, : held_ref.shape[1]], held_ref, done)
    copy.start()
    total = triples_ref.shape[0]
    rows, width = grad_refs[0].shape
    stride = held_ref.shape[1] // 3
    for h in range(width // head_size):
        low = h * head_size
        k = triples_ref[:, stride + low : stride + low + head_size]
        v = triples_ref[:, 2 * stride + low : 2 * stride + low + head_size]
        for i in range(total // step):
            at = slice(i * step, (i + 1) * step)
            inside = (i * step) % rows
            q = triples_ref[at, low : low + head_size]
            grad = grad_refs[i * step // rows][inside : inside + step, low : low + head_size]
            grad_q, grad_k, grad_v = attention_back(q, k, v, grad, None, head_size)
            out_ref[at, low : low + head_size] = grad_q.astype(BF16)
            if i == 0:
                keys_ref[...] = grad_k
                values_ref[...] = grad_v
            else:
                keys_ref[...] += grad_k
                values_ref[...] += grad_v
        out_ref[:, stride + low : stride + low + head_size] = keys_ref[...].astype(BF16)
        out_ref[:, 2 * stride + low : 2 * stride + low + head_size] = values_ref[...].astype(BF16)
    if stride > width:
        for g in range(3):
            out_ref[:, g * stride + width : (g + 1) * stride] = jnp.zeros((total, stride - width), BF16)
    copy.wait()
    for j in range(count):
        found = dot_nt(out_ref[j * rows : (j + 1) * rows, :], held_ref[...])
        if j == 0:
            own_ref[...] = found
        else:
            put_pieces(piece_refs, count, j, found)


def self_backward(triples, grads, weight, head_size, deps=()):
    count = len(grads)
    total, rows, columns = triples.shape[0], grads[0].shape[0], weight.shape[0]
    step = min(256, rows)
    found = call(
        functools.partial(self_backward_kernel, count, head_size, step),
        [(triples.shape, BF16), ((rows, columns), F32)] + piece_shapes(count, rows, columns),
        [
            pltpu.VMEM((total, head_size), F32),
            pltpu.VMEM((total, head_size), F32),
            pltpu.VMEM((columns, triples.shape[1]), BF16),
            pltpu.SemaphoreType.DMA,
        ],
        32,
        triples,
        *grads,
        weight,
        deps=deps,
        outside=(1 + count,),
    )
    return found[0], found[1], list(found[2:])


def fill_corner(count, matrix_refs, scalars_ref, corner_ref):
    if len(matrix_refs) == count:
        return list(matrix_refs)
    odd = scalars_ref[2 * count]
    half = matrix_refs[-1].shape[0]
    corner_ref[pl.ds(pl.multiple_of(odd * half, half), half), :] = matrix_refs[-2][...]
    corner_ref[pl.ds(pl.multiple_of((1 - odd) * half, half), half), :] = matrix_refs[-1][...]
    return list(matrix_refs[:-2]) + [corner_ref]


def corner_scratch(count, matrices):
    rows, columns = matrices[0].shape
    return pltpu.VMEM((rows, columns) if len(matrices) > count else (16, 128), BF16)


def fill_pairs(count, block, pair_refs, pairs_ref):
    padded, columns = pairs_ref.shape[1:]
    place = 0
    for ref in pair_refs:
        j, low = divmod(place, padded)
        pairs_ref[j, low : low + ref.shape[0], :] = ref[:, block * columns : (block + 1) * columns]
        place += ref.shape[0]


def middle_forward_kernel(block, count, matrix_parts, pair_parts, head_size, scalars_ref, *refs):
    mixed_refs, refs = refs[:count], refs[count:]
    matrix_refs, refs = refs[:matrix_parts], refs[matrix_parts:]
    pair_refs, refs = refs[:pair_parts], refs[pair_parts:]
    hidden_ref, gains_ref = refs[:2]
    (self_ref, after_self_ref, norm_ref, queries_ref, cross_ref, after_cross_ref) = refs[2:8]
    mlp_ref = refs[8]
    wide_ref, narrow_ref, corner_ref, pairs_ref = refs[-4:]
    width = mixed_refs[0].shape[1]
    stride = matrix_refs[0].shape[1] // 3
    matrices = fill_corner(count, matrix_refs, scalars_ref, corner_ref)
    fill_pairs(count, block, pair_refs, pairs_ref)
    order = [scalars_ref[i] for i in range(count)]
    relative = [scalars_ref[count + j] for j in range(count)]
    length = scalars_ref[2 * count + 1]
    spans = [slice(a * width, (a + 1) * width) for a in range(count)]

    for j in range(count):
        narrow_ref[relative[j]] = mixed_refs[j][...]
    for a in range(count):
        self_ref[:, spans[a]] = narrow_ref[a]
    tokens = self_ref[...]
    for i in range(count):
        wide_ref[order[i]] = dot_nn(tokens, matrices[i][:, :width])
    for a in range(count):
        after_self_ref[:, spans[a]] = hidden_ref[:, spans[a]].astype(F32) + wide_ref[a]
    normed = (norm_stats(after_self_ref[...])[0] * gains_ref[1:2, :]).astype(BF16)
    norm_ref[...] = normed
    for i in range(count):
        found = dot_nn(normed, matrices[i][:, stride : stride + width])
        queries_ref[order[i] ^ relative[0]] = found.astype(BF16)

    factor = LOG2_E / math.sqrt(head_size)
    keys_rows = pairs_ref.shape[1]
    valid = lax.broadcasted_iota(jnp.int32, (1, keys_rows), 1) < length
    pair_stride = pairs_ref.shape[2] // 2
    for j in range(count):
        for h in range(width // head_size):
            at = slice(h * head_size, (h + 1) * head_size)
            values_at = slice(pair_stride + h * head_size, pair_stride + (h + 1) * head_size)
            scores = dot_nt(queries_ref[j, :, at], pairs_ref[j, :, at])
            scores = jnp.where(valid, scores, -1e30)
            top = jnp.max(scores, axis=1, keepdims=True)
            weights = jnp.exp2((scores - top) * factor)
            total = jnp.sum(weights, axis=1, keepdims=True)
            mixed = dot_nn(weights.astype(BF16), pairs_ref[j, :, values_at]) * (1.0 / total)
            narrow_ref[relative[j], :, at] = mixed.astype(BF16)
    for a in range(count):
        cross_ref[:, spans[a]] = narrow_ref[a]
    tokens = cross_ref[...]
    for i in range(count):
        wide_ref[order[i]] = dot_nn(tokens, matrices[i][:, 2 * stride : 2 * stride + width])
    for a in range(count):
        after_cross_ref[:, spans[a]] = after_self_ref[:, spans[a]] + wide_ref[a]
    mlp_ref[...] = (norm_stats(after_cross_ref[...])[0] * gains_ref[2:3, :]).astype(BF16)


def pairs_scratch(count, pairs):
    return pltpu.VMEM(
        (count, sum(m.shape[0] for m in pairs) // count, pairs[0].shape[1] // 2), BF16
    )


def middle_forward(block, scalars, mixed, matrices, pairs, hidden, gains, head_size, deps=()):
    count = len(mixed)
    rows, columns = hidden.shape
    width = columns // count
    return call(
        functools.partial(
            middle_forward_kernel, block, count, len(matrices), len(pairs), head_size
        ),
        [
            ((rows, columns), BF16),
            ((rows, columns), F32),
            ((rows, columns), BF16),
            ((count, rows, width), BF16),
            ((rows, columns), BF16),
            ((rows, columns), F32),
            ((rows, columns), BF16),
        ],
        [
            pltpu.VMEM((count, rows, width), F32),
            pltpu.VMEM((count, rows, width), BF16),
            corner_scratch(count, matrices),
            pairs_scratch(count, pairs),
        ],
        23,
        *mixed,
        *matrices,
        *pairs,
        hidden,
        gains,
        scalars=scalars,
        deps=deps,
    )


def middle_backward_kernel(block, count, matrix_parts, pair_parts, terms, head_size, scalars_ref, *refs):
    matrix_refs, refs = refs[:matrix_parts], refs[matrix_parts:]
    pair_refs, refs = refs[:pair_parts], refs[pair_parts:]
    term_refs, refs = refs[:terms], refs[terms:]
    grad_out_ref, after_cross_ref, after_self_ref, queries_ref, gains_ref = refs[:5]
    out_ref, self_branch_ref, query_branch_ref, cross_branch_ref, gain_ref = refs[5:10]
    mixed_grad_refs, refs = refs[10 : 10 + count], refs[10 + count :]
    own_pairs_ref, pair_grad_refs = refs[0], refs[1:-6]
    wide_ref, narrow_ref, query_ref, corner_ref, pairs_ref, pair_total_ref = refs[-6:]
    width = queries_ref.shape[2]
    stride = matrix_refs[0].shape[1] // 3
    matrices = fill_corner(count, matrix_refs, scalars_ref, corner_ref)
    fill_pairs(count, block, pair_refs, pairs_ref)
    order = [scalars_ref[i] for i in range(count)]
    relative = [scalars_ref[count + j] for j in range(count)]
    length = scalars_ref[2 * count + 1]
    spans = [slice(a * width, (a + 1) * width) for a in range(count)]

    def back(branch_ref, group):
        columns = slice(group * stride, group * stride + width)
        total = dot_nt(branch_ref[0], matrices[0][:, columns])
        for i in range(1, count):
            total = total + dot_nt(branch_ref[i], matrices[i][:, columns])
        return total

    def divide(values):
        for a in range(count):
            narrow_ref[a] = values[:, spans[a]].astype(BF16)

    grad, grad_gain = norm_back(
        after_cross_ref[...], gains_ref[2:3, :], add_terms(count, term_refs)
    )
    gain_ref[1:2, :] = grad_gain
    wide_ref[...] = grad + grad_out_ref[...].astype(F32)
    divide(wide_ref[...])
    for i in range(count):
        cross_branch_ref[i] = narrow_ref[order[i]]
    divide(back(cross_branch_ref, 2))

    keys_rows = pairs_ref.shape[1]
    valid = lax.broadcasted_iota(jnp.int32, (keys_rows, 1), 0) < length
    pair_stride = pairs_ref.shape[2] // 2
    if pair_stride > width:
        for g in range(2):
            pair_total_ref[:, g * pair_stride + width : (g + 1) * pair_stride] = jnp.zeros(
                (keys_rows, pair_stride - width), F32
            )
    for j in range(count):
        for h in range(width // head_size):
            at = slice(h * head_size, (h + 1) * head_size)
            values_at = slice(pair_stride + h * head_size, pair_stride + (h + 1) * head_size)
            grad_q, grad_k, grad_v = attention_back(
                queries_ref[j, :, at],
                pairs_ref[j, :, at],
                pairs_ref[j, :, values_at],
                narrow_ref[relative[j], :, at],
                valid,
                head_size,
            )
            query_ref[j, :, at] = grad_q.astype(BF16)
            pair_total_ref[:, at] = grad_k
            pair_total_ref[:, values_at] = grad_v
        if j == 0:
            own_pairs_ref[...] = pair_total_ref[...]
        else:
            pair_grad_refs[j - 1][...] = pair_total_ref[...].astype(BF16)
    for i in range(count):
        query_branch_ref[i] = query_ref[order[i] ^ relative[0]]
    grad, grad_gain = norm_back(after_self_ref[...], gains_ref[1:2, :], back(query_branch_ref, 1))
    gain_ref[0:1, :] = grad_gain
    out_ref[...] = grad + wide_ref[...]
    divide(out_ref[...])
    for i in range(count):
        self_branch_ref[i] = narrow_ref[order[i]]
    divide(back(self_branch_ref, 0))
    for j in range(count):
        mixed_grad_refs[j][...] = narrow_ref[relative[j]]


def middle_backward(
    block, scalars, matrices, pairs, terms, grad_out, after_cross, after_self, queries, gains, head_size, deps=()
):
    count, rows, width = queries.shape
    columns = count * width
    branch = ((count, rows, width), BF16)
    text = pairs_scratch(count, pairs)
    keys_rows, pair_columns = text.shape[1:]
    found = call(
        functools.partial(
            middle_backward_kernel, block, count, len(matrices), len(pairs), len(terms), head_size
        ),
        [((rows, columns), F32), branch, branch, branch, ((2, columns), F32)]
        + [((rows, width), BF16)] * count
        + [((keys_rows, pair_columns), F32)]
        + [((keys_rows, pair_columns), BF16)] * (count - 1),
        [
            pltpu.VMEM((rows, columns), F32),
            pltpu.VMEM((count, rows, width), BF16),
            pltpu.VMEM((count, rows, width), BF16),
            corner_scratch(count, matrices),
            text,
            pltpu.VMEM((keys_rows, pair_columns), F32),
        ],
        37,
        *matrices,
        *pairs,
        *terms,
        grad_out,
        after_cross,
        after_self,
        queries,
        gains,
        scalars=scalars,
        deps=deps,
    )
    found = list(found)
    return found[:5] + [found[5 : 5 + count], found[5 + count], found[6 + count :]]


def mlp_up_kernel(count, parts, *refs):
    part_refs, (up_ref, rows_ref, up_rows_ref, activated_ref) = refs[:parts], refs[parts:]
    start = 0
    for ref in part_refs:
        rows_ref[start : start + ref.shape[0], :] = ref[...]
        start += ref.shape[0]
    rows = start // count
    for j in range(count):
        at = slice(j * rows, (j + 1) * rows)
        values = dot_nn(rows_ref[at, :], up_ref[...])
        up_rows_ref[at, :] = values
        inner = GELU_SCALE * (values + 0.044715 * (values * values * values))
        activated_ref[at, :] = (0.5 * values * (1.0 + jnp.tanh(inner))).astype(BF16)


def mlp_up(parts, up, count, deps=()):
    total, columns, hidden = sum(m.shape[0] for m in parts), up.shape[0], up.shape[1]
    return call(
        functools.partial(mlp_up_kernel, count, len(parts)),
        [((total, columns), BF16), ((total, hidden), F32), ((total, hidden), BF16)],
        [],
        15,
        *parts,
        up,
        deps=deps,
    )


def mlp_down_kernel(count, activated_ref, down_ref, own_ref, *piece_refs):
    rows = own_ref.shape[0]
    for j in range(count - 1, -1, -1):
        found = dot_nn(activated_ref[j * rows : (j + 1) * rows, :], down_ref[...])
        if j == 0:
            own_ref[...] = found
        else:
            put_pieces(piece_refs, count, j, found)


def mlp_down(activated, down, count, deps=()):
    rows, columns = activated.shape[0] // count, down.shape[1]
    found = call(
        functools.partial(mlp_down_kernel, count),
        [((rows, columns), F32)] + piece_shapes(count, rows, columns),
        [],
        11,
        activated,
        down,
        deps=deps,
    )
    return found[0], list(found[1:])


def stack_kernel(*refs):
    start = 0
    for ref in refs[:-1]:
        refs[-1][start : start + ref.shape[0], :] = ref[...]
        start += ref.shape[0]


def stack_rows(parts, deps=()):
    shape = (sum(m.shape[0] for m in parts), parts[0].shape[1])
    return call(stack_kernel, [(shape, parts[0].dtype)], [], 3, *parts, deps=deps)[0]


def mlp_backward_kernel(count, parts, *refs):
    part_refs, refs = refs[:parts], refs[parts:]
    up_rows_ref, up_ref, down_ref, rows_ref, grad_up_ref, own_ref = refs[:6]
    piece_refs = refs[6:]
    start = 0
    for ref in part_refs:
        rows_ref[start : start + ref.shape[0], :] = ref[...]
        start += ref.shape[0]
    rows = start // count
    for j in range(count - 1, -1, -1):
        at = slice(j * rows, (j + 1) * rows)
        grad = dot_nt(rows_ref[at, :], down_ref[...])
        values = up_rows_ref[at, :]
        square = values * values
        bent = jnp.tanh(GELU_SCALE * (values + 0.044715 * (values * square)))
        slope = 0.5 * (1.0 + bent) + 0.5 * values * (1.0 - bent * bent) * (
            GELU_SCALE * (1.0 + 3.0 * 0.044715 * square)
        )
        grad_up_ref[at, :] = (grad * slope).astype(BF16)
        found = dot_nt(grad_up_ref[at, :], up_ref[...])
        if j == 0:
            own_ref[...] = found
        else:
            put_pieces(piece_refs, count, j, found)


def mlp_backward(parts, up_rows, up, down, count, deps=()):
    total, columns, hidden = sum(m.shape[0] for m in parts), up.shape[0], up.shape[1]
    rows = total // count
    found = call(
        functools.partial(mlp_backward_kernel, count, len(parts)),
        [((total, columns), BF16), ((total, hidden), BF16), ((rows, columns), F32)]
        + piece_shapes(count, rows, columns),
        [],
        22,
        *parts,
        up_rows,
        up,
        down,
        deps=deps,
    )
    return list(found[:3]) + [list(found[3:])]


def outer_kernel(count, groups, half, scalars_ref, *refs):
    rows_refs, branch_refs, refs = refs[:groups], refs[groups : 2 * groups], refs[2 * groups :]
    out_refs, turned_ref = refs[:-1], refs[-1]
    width = branch_refs[0].shape[2]
    stride = padded_width(width)
    odd = scalars_ref[2 * count]
    for g in range(groups):
        at = slice(g * stride, g * stride + width)
        turned_ref[...] = rows_refs[g][...].T
        out_refs[0][:, at] = dot_nn(turned_ref[...], branch_refs[g][0]).astype(BF16)
        for i in range(1, count):
            if not half:
                out_refs[i][:, at] = dot_nn(turned_ref[...], branch_refs[g][i]).astype(BF16)
                continue
            for k in range(2):
                low = pl.multiple_of((odd if k == 0 else 1 - odd) * half, half)
                found = dot_nn(turned_ref[pl.ds(low, half), :], branch_refs[g][i])
                out_refs[2 * i - 1 + k][:, at] = found.astype(BF16)
    if stride > width:
        for ref in out_refs:
            for g in range(groups):
                ref[:, g * stride + width : (g + 1) * stride] = jnp.zeros(
                    (ref.shape[0], stride - width), BF16
                )


def outer(scalars, rows, branches, deps=()):
    count, tokens, width = branches[0].shape
    groups, columns = len(rows), rows[0].shape[1]
    stride = padded_width(width)
    half = columns // 2 if count == 4 else 0
    shapes = [((columns, groups * stride), BF16)]
    if half:
        shapes += [((half, groups * stride), BF16)] * (2 * (count - 1))
    else:
        shapes = shapes * count
    return list(
        call(
            functools.partial(outer_kernel, count, groups, half),
            shapes,
            [pltpu.VMEM((columns, tokens), BF16)],
            3.5 * groups,
            *rows,
            *branches,
            scalars=scalars,
            deps=deps,
        )
    )


def join_kernel(count, scalars_ref, own_ref, mine_ref, other_ref, out_ref):
    odd = scalars_ref[2 * count]
    half = mine_ref.shape[0]
    for ref, place in ((mine_ref, odd), (other_ref, 1 - odd)):
        at = pl.ds(pl.multiple_of(place * half, half), half)
        out_ref[at, :] = (own_ref[at, :].astype(F32) + ref[...].astype(F32)).astype(BF16)


def join_halves(scalars, own, mine, other):
    count = lax.axis_size("seq")
    (found,) = call(
        functools.partial(join_kernel, count),
        [(own.shape, BF16)],
        [],
        4,
        own,
        mine,
        other,
        scalars=scalars,
    )
    return found


def joined_stats(first, second):
    count = first.shape[1] + second.shape[1]
    mean = (jnp.sum(first, axis=1, keepdims=True) + jnp.sum(second, axis=1, keepdims=True)) / count
    first, second = first - mean, second - mean
    var = (
        jnp.sum(first * first, axis=1, keepdims=True)
        + jnp.sum(second * second, axis=1, keepdims=True)
    ) / count
    scale = lax.rsqrt(var + NORM_EPSILON)
    return first * scale, second * scale, scale


def skip_forward_kernel(count, matrix_parts, terms, scalars_ref, *refs):
    matrix_refs, refs = refs[:matrix_parts], refs[matrix_parts:]
    term_refs, refs = refs[:terms], refs[terms:]
    residual_ref, second_ref, gains_ref, next_ref, shift_ref = refs[:5]
    first_ref, joined_ref, out_ref, norm_ref, wide_ref, corner_ref = refs[5:]
    rows, columns = first_ref.shape
    width = columns // count
    matrices = fill_corner(count, matrix_refs, scalars_ref, corner_ref)
    first_ref[...] = residual_ref[...] + add_terms(count, term_refs)
    first, second, _ = joined_stats(first_ref[...], second_ref[...].astype(F32))
    joined_ref[:, :columns] = (first * gains_ref[0:1, :]).astype(BF16)
    joined_ref[:, columns:] = (second * gains_ref[1:2, :]).astype(BF16)
    joined = joined_ref[...]
    for i in range(count):
        wide_ref[scalars_ref[i]] = dot_nn(joined, matrices[i][:, :width])
    for a in range(count):
        out_ref[:, a * width : (a + 1) * width] = wide_ref[a]
    normed = norm_stats(out_ref[...])[0] * next_ref[0:1, :] + shift_ref[...]
    norm_ref[...] = normed.astype(BF16)


def skip_forward(scalars, matrices, terms, residual, second, gains, next_gains, shift, deps=()):
    rows, columns = residual.shape
    count = lax.axis_size("seq")
    return call(
        functools.partial(skip_forward_kernel, count, len(matrices), len(terms)),
        [
            ((rows, columns), F32),
            ((rows, 2 * columns), BF16),
            ((rows, columns), F32),
            ((rows, columns), BF16),
        ],
        [pltpu.VMEM((count, rows, columns // count), F32), corner_scratch(count, matrices)],
        11,
        *matrices,
        *terms,
        residual,
        second,
        gains,
        next_gains,
        shift[None],
        scalars=scalars,
        deps=deps,
    )


def skip_backward_kernel(count, matrix_parts, terms, scalars_ref, *refs):
    matrix_refs, refs = refs[:matrix_parts], refs[matrix_parts:]
    term_refs, refs = refs[:terms], refs[terms:]
    hidden_ref, next_ref, residual_ref, first_ref, second_ref, gains_ref = refs[:6]
    branch_ref, grad_first_ref, grad_second_ref, vectors_ref, round_ref = refs[6:11]
    narrow_ref, corner_ref = refs[11:]
    rows, columns = first_ref.shape
    width = columns // count
    matrices = fill_corner(count, matrix_refs, scalars_ref, corner_ref)
    grad_norm = add_terms(count, term_refs)
    vectors_ref[0:1, :] = jnp.sum(grad_norm, axis=0, keepdims=True)
    grad, grad_gain = norm_back(hidden_ref[...], next_ref[0:1, :], grad_norm)
    vectors_ref[1:2, :] = grad_gain
    grad = grad + residual_ref[...]
    for a in range(count):
        narrow_ref[a] = grad[:, a * width : (a + 1) * width].astype(BF16)
    for i in range(count):
        branch_ref[i] = narrow_ref[scalars_ref[i]]

    def back(at):
        total = dot_nt(branch_ref[0], matrices[0][at, :width])
        for i in range(1, count):
            total = total + dot_nt(branch_ref[i], matrices[i][at, :width])
        return total

    grad_first_ref[...] = back(slice(0, columns))
    grad_second_ref[...] = back(slice(columns, 2 * columns))
    first, second, scale = joined_stats(first_ref[...], second_ref[...].astype(F32))
    vectors_ref[2:3, :] = jnp.sum(grad_first_ref[...] * first, axis=0, keepdims=True)
    vectors_ref[3:4, :] = jnp.sum(grad_second_ref[...] * second, axis=0, keepdims=True)
    grad_first = grad_first_ref[...] * gains_ref[0:1, :]
    grad_second = grad_second_ref[...] * gains_ref[1:2, :]
    mean = (
        jnp.sum(grad_first, axis=1, keepdims=True) + jnp.sum(grad_second, axis=1, keepdims=True)
    ) / (2 * columns)
    inner = (
        jnp.sum(grad_first * first, axis=1, keepdims=True)
        + jnp.sum(grad_second * second, axis=1, keepdims=True)
    ) / (2 * columns)
    grad_first_ref[...] = scale * (grad_first - mean - first * inner)
    grad_second_ref[...] = scale * (grad_second - mean - second * inner)
    round_ref[...] = grad_first_ref[...].astype(BF16)


def skip_backward(
    scalars, matrices, terms, hidden, next_gains, residual, first, second, gains, deps=()
):
    rows, columns = first.shape
    count = lax.axis_size("seq")
    narrow = (count, rows, columns // count)
    return call(
        functools.partial(skip_backward_kernel, count, len(matrices), len(terms)),
        [
            (narrow, BF16),
            ((rows, columns), F32),
            ((rows, columns), F32),
            ((4, columns), F32),
            ((rows, columns), BF16),
        ],
        [pltpu.VMEM(narrow, BF16), corner_scratch(count, matrices)],
        15,
        *matrices,
        *terms,
        hidden,
        next_gains,
        residual,
        first,
        second,
        gains,
        scalars=scalars,
        deps=deps,
    )


def open_backward_kernel(count, terms, *refs):
    term_refs, refs = refs[:terms], refs[terms:]
    hidden_ref, gains_ref, residual_ref, out_ref, vectors_ref = refs
    grad_norm = add_terms(count, term_refs)
    vectors_ref[0:1, :] = jnp.sum(grad_norm, axis=0, keepdims=True)
    grad, grad_gain = norm_back(hidden_ref[...].astype(F32), gains_ref[0:1, :], grad_norm)
    vectors_ref[1:2, :] = grad_gain
    out_ref[...] = grad + residual_ref[...]


def open_backward(terms, hidden, gains, residual, deps=()):
    count = lax.axis_size("seq")
    return call(
        functools.partial(open_backward_kernel, count, len(terms)),
        [(residual.shape, F32), ((2, residual.shape[1]), F32)],
        [],
        5,
        *terms,
        hidden,
        gains,
        residual,
        deps=deps,
    )


def close_kernel(count, terms, *refs):
    refs[terms + 1][...] = (refs[terms][...] + add_terms(count, refs[:terms])).astype(BF16)


def close_forward(terms, residual, deps=()):
    count = lax.axis_size("seq")
    (found,) = call(
        functools.partial(close_kernel, count, len(terms)),
        [(residual.shape, BF16)],
        [],
        3,
        *terms,
        residual,
        deps=deps,
    )
    return found


def pack_kernel(count, *refs):
    start = 0
    for ref in refs[:count]:
        refs[count][: ref.shape[0], start : start + ref.shape[1]] = ref[...]
        start += ref.shape[1]


def pack(shards, deps=()):
    rows = -(-max(m.shape[0] for m in shards) // 16) * 16
    shape = (rows, sum(m.shape[1] for m in shards))
    return call(functools.partial(pack_kernel, len(shards)), [(shape, BF16)], [], 3, *shards, deps=deps)[0]


def settle_kernel(count, parts, plan, scalars_ref, *refs):
    block_refs, refs = refs[:parts], refs[parts:]
    outs = sum(entry[3] for entry in plan)
    out_refs, stack_ref = refs[-outs - 1 : -1], refs[-1]
    for j in range(count):
        owner = scalars_ref[count + j]
        if j == count - 1 and parts > count:
            cut = block_refs[j].shape[0]
            stack_ref[owner, :cut] = block_refs[j][...]
            stack_ref[owner, cut:] = block_refs[j + 1][...]
        else:
            stack_ref[owner] = block_refs[j][...]
    place = 0
    for first, rows, groups, pieces, width, stride in plan:
        if not groups:
            for a in range(count):
                found = stack_ref[a, :rows, first : first + width]
                out_refs[place][0, a * rows : (a + 1) * rows, :] = found.astype(F32)
        for p in range(pieces):
            for g in range(groups):
                for a in range(count):
                    low = first + (p * groups + g) * stride
                    at = (g * count + a) * width
                    found = stack_ref[a, :rows, low : low + width]
                    out_refs[place + p][0, :, at : at + width] = found.astype(F32)
        place += pieces


def settle(scalars, blocks, plan, layer, layer_count, before):
    count = lax.axis_size("seq")
    shapes = []
    for _, rows, groups, pieces, width, _ in plan:
        shapes += [(rows, groups * count * width) if groups else (count * rows, width)] * pieces
    held = [] if before is None else list(before)
    inputs = [pl.BlockSpec(memory_space=pltpu.VMEM)] * len(blocks)
    inputs += [pl.BlockSpec(memory_space=pl.ANY)] * len(held)
    found = pl.pallas_call(
        functools.partial(settle_kernel, count, len(blocks), plan),
        grid=(1,),
        out_shape=[jax.ShapeDtypeStruct((layer_count,) + shape, F32) for shape in shapes],
        in_specs=[pl.BlockSpec(memory_space=pltpu.SMEM)] + inputs,
        out_specs=[pl.BlockSpec((1,) + shape, lambda i: (layer, 0, 0)) for shape in shapes],
        scratch_shapes=[pltpu.VMEM((count,) + blocks[0].shape, BF16)],
        input_output_aliases={1 + len(blocks) + i: i for i in range(len(held))},
        compiler_params=pltpu.CompilerParams(vmem_limit_bytes=VMEM_LIMIT),
        cost_estimate=pl.CostEstimate(flops=8_000_000_000, bytes_accessed=1000, transcendentals=0),
    )(scalars, *blocks, *held)
    return list(found)


def plan_of(entries):
    plan, first = [], 0
    for shard, groups, pieces, width in entries:
        rows, columns = shard.shape
        stride = columns // (groups * pieces) if groups else columns
        plan.append((first, rows, groups, pieces, width, stride))
        first += columns
    return tuple(plan)


def finish(scalars, entries, layer, layer_count, before=None, deps=()):
    blocks = gather_parts(pack([entry[0] for entry in entries], deps))
    return settle(scalars, blocks, plan_of(entries), layer, layer_count, before)


def swap_seq(block, bits):
    seq_count = lax.axis_size("seq")
    return lax.ppermute(block, "seq", [(i, i ^ bits) for i in range(seq_count)])


def swap_fsdp(block, bits):
    fsdp_count = lax.axis_size("fsdp")
    return lax.ppermute(block, "fsdp", [(i, i ^ bits) for i in range(fsdp_count)])


def swap_core(block):
    return swap_fsdp(block, 1)


def swap_by_core(block, even_bits, odd_bits):
    seq_count, fsdp_count = lax.axis_size("seq"), lax.axis_size("fsdp")
    pairs = []
    for s in range(seq_count):
        for f in range(fsdp_count):
            other = s ^ (odd_bits if f % 2 else even_bits)
            pairs.append((s * fsdp_count + f, other * fsdp_count + f))
    return lax.ppermute(block, ("seq", "fsdp"), pairs)


def add_bf16(*terms):
    total = terms[0].astype(F32)
    for term in terms[1:]:
        total = total + term.astype(F32)
    return total.astype(BF16)


def scatter_first(pieces):
    seq_count = lax.axis_size("seq")
    if seq_count != 4:
        return [swap_seq(m, j + 1) for j, m in enumerate(pieces)]
    return [swap_seq(pieces[0], 1), swap_seq(pieces[1], 2), pieces[2], pieces[3]]


def scatter_last(own, first, ready=None):
    seq_count = lax.axis_size("seq")
    if seq_count != 4:
        return [own] + first
    from_x, from_y, x_bottom, y_top = first
    if ready is not None:
        from_x, from_y = gate([from_x, from_y], ready)
    cut, rest = y_top.shape[0], x_bottom.shape[0]
    to_y, to_x = add_bf16(y_top, from_x[:cut]), add_bf16(x_bottom, from_y[:rest])
    return [own, from_x, from_y, swap_seq(to_x, 1), swap_seq(to_y, 2)]


def exchange_rel(blocks):
    return [blocks[0]] + [swap_seq(blocks[j], j) for j in range(1, len(blocks))]


def gather_first(block):
    seq_count = lax.axis_size("seq")
    if seq_count != 4:
        return [block] + [swap_seq(block, j) for j in range(1, seq_count)]
    return [block, swap_seq(block, 1), swap_seq(block, 2)]


def gather_last(first, ready=None):
    seq_count = lax.axis_size("seq")
    if seq_count != 4:
        return first
    block, from_x, from_y = first
    if ready is not None:
        from_x, from_y = gate([from_x, from_y], ready)
    cut = cut_of(block.shape[0])
    return [block, from_x, from_y, swap_seq(from_y[:cut], 1), swap_seq(from_x[cut:], 2)]


def gather_parts(block):
    return gather_last(gather_first(block))


def list_order():
    s, seq_count = lax.axis_index("seq"), lax.axis_size("seq")
    if seq_count != 4:
        return [s ^ j for j in range(seq_count)]
    odd = lax.axis_index("fsdp") % 2
    return [s, s ^ (1 + odd), s ^ (2 - odd), s ^ 3]


def spread_first(block):
    seq_count = lax.axis_size("seq")
    if seq_count != 4:
        return [block] + [swap_seq(block, j) for j in range(1, seq_count)]
    return [block, swap_by_core(block, 1, 2)]


def spread_last(blocks, ready, part_ready=None):
    seq_count = lax.axis_size("seq")
    if seq_count != 4:
        return blocks
    odd = lax.axis_index("fsdp") % 2
    block, first = blocks
    half = block.shape[0] // 2
    if ready is not None:
        (first,) = gate([first], ready)
    part = swap_by_core(lax.dynamic_slice_in_dim(first, odd * half, half, 0), 2, 1)
    other = swap_core(first)
    if part_ready is not None:
        (part,) = gate([part], part_ready)
    return [block, first, other, part, swap_core(part)]


def unspread(scalars, blocks):
    seq_count = lax.axis_size("seq")
    if seq_count != 4:
        return add_bf16(blocks[0], *[swap_seq(blocks[j], j) for j in range(1, seq_count)])
    own, first_mine, first_other, second_mine, second_other, corner_mine, corner_other = blocks
    passed = swap_by_core(add_bf16(corner_mine, swap_core(corner_other)), 2, 1)
    other = swap_by_core(add_bf16(first_other, swap_core(second_mine)), 1, 2)
    mine = swap_by_core(add_bf16(first_mine, swap_core(second_other), passed), 1, 2)
    return join_halves(scalars, own, mine, other)


def own_part(matrix, groups, padded):
    s, seq_count = lax.axis_index("seq"), lax.axis_size("seq")
    width = matrix.shape[1] // (groups * seq_count)
    parts = [
        jnp.pad(
            lax.dynamic_slice_in_dim(matrix, (g * seq_count + s) * width, width, 1),
            ((0, 0), (0, padded - width)),
        )
        for g in range(groups)
    ]
    return jnp.concatenate(parts, axis=1)


def gather_fsdp(shard):
    return lax.all_gather(shard, "fsdp", axis=0, tiled=True)


def scatter_fsdp(full):
    return lax.psum_scatter(full.astype(BF16), "fsdp", scatter_dimension=0, tiled=True)


def layer_forward(parts, hidden, scalars, gains, shift, pairs, weights, normed, deps):
    lead_part, square_parts, up_part = weights
    seq_count = lax.axis_size("seq")
    tok_rows, model_width = hidden.shape
    head_size, width = model_width // H, model_width // seq_count
    first_all, triples, mixed = self_forward(
        parts,
        lead_part,
        gains,
        shift,
        head_size,
        seq_count,
        width,
        normed,
        (square_parts[0],) + deps,
    )
    mixed_rel = exchange_rel(mixed)
    square_parts = spread_last(square_parts, [mixed[0]], mixed_rel[1:])
    self_tokens, after_self, cross_norm, queries, cross_tokens, after_cross, mlp_norm = (
        middle_forward(
            int(normed), scalars, mixed_rel, square_parts, pairs, hidden, gains, head_size
        )
    )
    mlp_parts = gather_parts(mlp_norm)
    mlp_all, up_rows, activated = mlp_up(mlp_parts, up_part, seq_count)
    saved = (
        first_all,
        triples,
        self_tokens,
        after_self,
        cross_norm,
        queries,
        cross_tokens,
        after_cross,
        mlp_all,
        up_rows,
        activated,
    )
    return (saved, square_parts, mlp_parts, mixed_rel)


def unspread_first(blocks, ready):
    own, first_mine, first_other, second_mine, second_other, corner_mine, corner_other = blocks
    from_corner, to_other = swap_core(corner_other), swap_core(second_mine)
    to_mine = swap_core(second_other)
    sums = [add_bf16(corner_mine, from_corner), add_bf16(first_other, to_other)]
    sums = gate(sums, ready)
    hops = [swap_by_core(sums[0], 2, 1), swap_by_core(sums[1], 1, 2)]
    return own, hops, [first_mine, to_mine], sums


def unspread_next(first, ready):
    own, hops, terms, _ = first
    passed, other = gate(hops, ready)
    return own, swap_by_core(add_bf16(*terms, passed), 1, 2), other


def unspread_last(scalars, second, ready):
    own, mine, other = second
    (mine,) = gate([mine], ready)
    return join_halves(scalars, own, mine, other)


def unspread_any(blocks):
    return add_bf16(blocks[0], *[swap_seq(m, j + 1) for j, m in enumerate(blocks[1:])])


def qkv_own(layer, qkv):
    return own_part(qkv[layer], 3, padded_width(qkv.shape[2] // (3 * lax.axis_size("seq"))))


def squares_own(layer, *stacks):
    padded = padded_width(stacks[0].shape[2] // lax.axis_size("seq"))
    return jnp.concatenate([own_part(m[layer], 1, padded) for m in stacks], axis=1)


def gather_rest(layer, up, down):
    s, seq_count, fsdp_count = lax.axis_index("seq"), lax.axis_size("seq"), lax.axis_size("fsdp")
    rows = down.shape[1] // seq_count
    return (
        gather_fsdp(own_part(up[layer], fsdp_count, up.shape[2] // (fsdp_count * seq_count))),
        gather_fsdp(lax.dynamic_slice_in_dim(down[layer], s * rows, rows, 0)),
    )


def sum_vectors(vectors):
    bits = 1
    while bits < lax.axis_size("seq"):
        vectors = vectors + swap_seq(vectors, bits)
        bits *= 2
    found, bits = vectors[None], 1
    while bits < lax.axis_size("fsdp"):
        found = jnp.concatenate([found, swap_fsdp(found, bits)], axis=0)
        bits *= 2
    return found


def body(
    latents,
    skip_input,
    text_tokens,
    text_lengths,
    condition,
    cotangent,
    mod_weight,
    norm_gains,
    qkv_weight,
    query_weight,
    text_kv_weight,
    self_out_weight,
    cross_out_weight,
    up_weight,
    down_weight,
    skip_gain,
    skip_weight,
):
    seq_count, fsdp_count = lax.axis_size("seq"), lax.axis_size("fsdp")
    s, f = lax.axis_index("seq"), lax.axis_index("fsdp")
    _, tok_rows, model_width = latents.shape
    width = model_width // seq_count
    shard_rows = mod_weight.shape[1]
    text_count = text_tokens.shape[1]
    padded = -(-text_count // 32) * 32
    text_rows = jnp.pad(text_tokens[0], ((0, padded - text_count), (0, 0)))
    scalars = jnp.stack(
        [*list_order(), *[s ^ j for j in range(seq_count)], f % 2, text_lengths[0]]
    ).astype(jnp.int32)

    gain_rows = jnp.concatenate(
        [norm_gains.reshape(-1, shard_rows), skip_gain.reshape(-1, shard_rows)], axis=0
    )
    small = jnp.concatenate(
        [
            condition.reshape(fsdp_count, 1, shard_rows),
            jnp.broadcast_to(gain_rows[None], (fsdp_count,) + gain_rows.shape),
        ],
        axis=1,
    ).astype(F32)
    latent_hops = gather_first(latents[0])
    (small,) = gate([small], latent_hops[1:])
    small = lax.all_to_all(small, "fsdp", 0, 0, tiled=True)
    cond_part = small[:, 0]
    gains = jnp.swapaxes(small[:, 1:7], 0, 1).reshape(2, 3, model_width)
    skip_gains = small[:, 7:].reshape(2, model_width)
    silu_part = jax.nn.silu(cond_part)
    shift_terms = jnp.einsum("br,lrd->bld", silu_part, mod_weight.astype(F32), precision=EXACT)
    latent_parts = gather_last(latent_hops)
    (shift_terms,) = gate([shift_terms], latent_parts[-2:])
    out_hops = gather_first(gate([cotangent[0]], latent_parts[-2:])[0])
    shifts = jnp.sum(lax.all_to_all(shift_terms, "fsdp", 0, 0, tiled=True), axis=0)

    square_stacks = (self_out_weight, query_weight, cross_out_weight)
    rest_stacks = (up_weight, down_weight)
    head_size = model_width // H
    fours = seq_count == 4

    padded_columns = padded_width(width)
    kv_both = gather_fsdp(
        jnp.concatenate([own_part(text_kv_weight[l], 2, padded_columns) for l in range(2)], axis=1)
    )
    square_shard, qkv_shard = gate(
        [squares_own(0, *square_stacks), qkv_own(0, qkv_weight)], [kv_both] + latent_hops[1:]
    )
    square_first, lead_first = gather_fsdp(square_shard), gather_fsdp(qkv_shard)
    up_first, down_first = gather_rest(0, *rest_stacks)
    pairs_all = gather_parts(dot_nn(text_rows, kv_both).astype(BF16))
    spread_squares = spread_first(gate([square_first], pairs_all[-2:])[0])
    (lead_first,) = gate([lead_first], [shifts])
    pairs_first, pairs_second = pairs_all, pairs_all
    saved_first, squares_first, mlp_parts, mixed_rel = layer_forward(
        latent_parts,
        latents[0],
        scalars,
        gains[0],
        shifts[0],
        pairs_first,
        (lead_first, spread_squares, up_first),
        False,
        (),
    )
    own, pieces = mlp_down(saved_first[10], down_first, seq_count)
    terms = scatter_last(own, scatter_first(pieces))

    (skip_matrix,) = gate(
        [gather_fsdp(own_part(skip_weight, 1, padded_width(width)))], mixed_rel[1:]
    )
    skip_parts = spread_last(spread_first(skip_matrix), mlp_parts[-2:], [own])
    square_second = gather_fsdp(squares_own(1, *square_stacks))
    lead_second = gather_fsdp(qkv_own(1, qkv_weight))
    (square_second,) = gate([square_second], terms[-2:])
    squares_second = spread_first(square_second)
    first_out, joined_norm, skip_out, second_norm = skip_forward(
        scalars,
        skip_parts,
        terms,
        saved_first[7],
        skip_input[0],
        skip_gains,
        gains[1],
        shifts[1],
        (square_second,),
    )

    up_second, down_second = gather_rest(1, *rest_stacks)
    saved_second, squares_second, mlp_parts, _ = layer_forward(
        gather_parts(second_norm),
        skip_out,
        scalars,
        gains[1],
        shifts[1],
        pairs_second,
        (lead_second, squares_second, up_second),
        True,
        (),
    )
    out_parts = gather_last(out_hops, [squares_second[-1]])
    out_all = stack_rows(out_parts, (mlp_parts[1],))

    held = {}

    def block_backward(rows, grad_out, saved, block, weights, early, hooks):
        lead_matrix, square_parts, pairs, up_part, down_part = weights
        grad_down = dot_tn(saved[10], early).astype(BF16) if early is not None else None
        found_all, grad_up_rows, own, pieces = mlp_backward(
            rows,
            saved[9],
            up_part,
            down_part,
            seq_count,
            hooks[0] + ((grad_down,) if early is not None else ()),
        )
        first = scatter_first(gate(pieces, hooks[3]) if hooks[3] else pieces)
        terms = scatter_last(own, first)
        held["hops"] = first[:2]
        if early is None:
            grad_down = dot_tn(saved[10], found_all).astype(BF16)
            (grad_down,) = gate([grad_down], first[:2])
        grad_up = dot_tn(saved[8], grad_up_rows).astype(BF16)
        (grad_up,) = gate([grad_up], first[:2])
        down_shard, up_shard = scatter_fsdp(grad_down), scatter_fsdp(grad_up)
        (
            grad_after_self,
            self_branch,
            query_branch,
            cross_branch,
            gain_grads,
            mixed_grads,
            own_pairs,
            pair_blocks,
        ) = middle_backward(
            block,
            scalars,
            square_parts,
            pairs,
            terms,
            grad_out,
            saved[7],
            saved[3],
            saved[5],
            gains[block],
            head_size,
            (grad_down, grad_up) + hooks[1](grad_up_rows, terms),
        )
        mixed_rel = exchange_rel(mixed_grads)
        pair_blocks = gate(pair_blocks, mixed_rel[1:])
        pair_terms = [swap_seq(m, j + 1) for j, m in enumerate(pair_blocks)]
        grad_triples, own, pieces = self_backward(
            saved[1],
            mixed_rel,
            lead_matrix,
            head_size,
            (down_shard,) + hooks[2](mixed_grads[0]),
        )
        pair_terms = gate(pair_terms, [grad_triples])
        first = scatter_first(gate(pieces, pair_terms))
        terms = scatter_last(own, first)
        grad_qkv = dot_tn(saved[0], grad_triples).astype(BF16)
        (grad_qkv,) = gate([grad_qkv], first[:2])
        held["last"] = first[:2]
        squares = outer(
            scalars,
            [saved[2], saved[4], saved[6]],
            [self_branch, query_branch, cross_branch],
            (grad_triples,),
        )
        squares = gate(squares, first[:2])
        pair_terms = gate(pair_terms, first[:2])
        grad_pairs = add_bf16(own_pairs, *pair_terms)
        kv_part = kv_both[:, 2 * block * padded_columns : 2 * (block + 1) * padded_columns]
        grad_text = dot_nt(grad_pairs, kv_part)
        kv_shard = scatter_fsdp(dot_tn(text_rows, grad_pairs))
        return (
            terms,
            grad_after_self,
            gain_grads,
            grad_text,
            squares,
            grad_qkv,
            grad_triples,
            (scatter_fsdp(grad_qkv), kv_shard, up_shard, down_shard),
        )

    def second_own(grad_up_rows, terms):
        own, pieces = mlp_down(saved_second[10], down_second, seq_count, (grad_up_rows,))
        pieces = gate(pieces, terms[-2:])
        held["own"], held["own_hops"] = own, scatter_first(pieces)
        return tuple(pieces)

    def second_sum(ready):
        held["ready"] = ready
        return tuple(held["own_hops"][:2])

    (
        terms,
        grad_after_self,
        gain_grads,
        text_second,
        squares,
        grad_qkv,
        grad_triples,
        (qkv_shard, kv_shard, up_shard, down_shard),
    ) = block_backward(
        [out_all],
        cotangent[0],
        saved_second,
        1,
        (lead_second, squares_second, pairs_second, up_second, down_second),
        out_all,
        ((), second_own, second_sum, ()),
    )
    skip_branch, grad_first_out, grad_skip, vectors, first_round = skip_backward(
        scalars,
        skip_parts,
        terms,
        skip_out,
        gains[1],
        grad_after_self,
        first_out,
        skip_input[0],
        skip_gains,
        (grad_qkv, up_shard),
    )
    vectors_second = jnp.concatenate([vectors[:2], gain_grads, vectors[2:]], axis=0)
    first_hops = gather_first(first_round)
    first_parts = gather_last(first_hops)
    if fours:
        squares = unspread_first(squares, first_parts[-2:])
    output = close_forward(
        scatter_last(held["own"], held["own_hops"], terms[-2:]), saved_second[7]
    )
    skip_outer = outer(scalars, [joined_norm], [skip_branch], tuple(first_hops[1:]))

    def entries(layer):
        qkv, square, kv, up, down = layer
        return (
            [
                (up, fsdp_count, 1, up.shape[1] // fsdp_count),
                (kv, 2, 1, width),
                (down, 0, 1, down.shape[1]),
            ],
            [(qkv, 3, 1, width), (square, 1, 3, width)],
        )

    early, _ = entries((qkv_shard, qkv_shard, kv_shard, up_shard, down_shard))

    def first_middle(grad_up_rows, terms):
        if fours:
            held["skip"] = unspread_first(skip_outer, terms[-2:])
        held["up"], held["terms"] = grad_up_rows, terms
        held["packed"] = pack([entry[0] for entry in early], (grad_up_rows,))
        return (held["packed"],) + (tuple(held["skip"][3]) if fours else ())

    def first_self(ready):
        if not fours:
            return (qkv_shard,)
        held["squares"] = unspread_next(squares, held["hops"])
        return (qkv_shard, held["squares"][1], *held["skip"][1])

    (
        terms,
        grad_after_self,
        gain_grads,
        text_first,
        first_squares,
        grad_qkv,
        grad_triples,
        (first_qkv_shard, first_kv_shard, first_up_shard, first_down_shard),
    ) = block_backward(
        first_parts,
        grad_first_out,
        saved_first,
        0,
        (lead_first, squares_first, pairs_first, up_first, down_first),
        None,
        (
            (skip_outer[0],) + (tuple(squares[3]) if fours else ()),
            first_middle,
            first_self,
            squares[1] if fours else (),
        ),
    )
    if fours:
        outer_done = [first_squares[1]]
        joined = unspread_last(scalars, held["squares"], outer_done)
        skip_second = unspread_next(held["skip"], outer_done)
        skip_joined = unspread_last(scalars, skip_second, [joined])
        first_squares = unspread_next(unspread_first(first_squares, terms[3:4]), terms[-2:])
    else:
        joined, skip_joined = unspread_any(squares), unspread_any(skip_outer)
        outer_done = [joined]
    square_shard, skip_shard = scatter_fsdp(joined), scatter_fsdp(skip_joined)
    early_hops = gather_first(gate([held["packed"]], outer_done)[0])
    grad_latents, vectors = open_backward(
        terms, latents[0], gains[0], grad_after_self, (grad_qkv, *early_hops[1:])
    )
    vectors_first = jnp.concatenate([vectors, gain_grads], axis=0)
    if fours:
        first_joined = unspread_last(scalars, first_squares, [grad_latents])
    else:
        first_joined = unspread_any(first_squares)
    first_layer = (
        first_qkv_shard,
        scatter_fsdp(first_joined),
        first_kv_shard,
        first_up_shard,
        first_down_shard,
    )

    early_done = settle(
        scalars,
        gather_last(early_hops),
        plan_of(early),
        1,
        2,
        None,
    )
    _, late = entries((qkv_shard, square_shard, kv_shard, up_shard, down_shard))
    late_done = finish(scalars, late, 1, 2, None)
    early, late = entries(first_layer)
    grad_up, grad_kv, grad_down = finish(scalars, early, 0, 2, early_done)
    grad_qkv, grad_self_out, grad_query, grad_cross_out = finish(scalars, late, 0, 2, late_done)
    (grad_skip_weight,) = finish(scalars, [(skip_shard, 1, 1, width)], 0, 1)

    sums = sum_vectors(jnp.concatenate([vectors_first, vectors_second], axis=0))
    first_sums, second_sums = sums[:, :4], sums[:, 4:]
    shift_grads = jnp.stack([first_sums[:, 0], second_sums[:, 0]], axis=1)
    gain_sums = jnp.stack([first_sums[:, 1:4].sum(axis=0), second_sums[:, 1:4].sum(axis=0)])
    grad_norm_gains = lax.dynamic_slice_in_dim(gain_sums, f * shard_rows, shard_rows, 2)
    grad_skip_gain = lax.dynamic_slice_in_dim(
        second_sums[:, 4:].sum(axis=0).reshape(-1), f * skip_gain.shape[0], skip_gain.shape[0], 0
    )
    turned = jnp.stack(
        [lax.dynamic_index_in_dim(silu_part, f ^ j, 0, False) for j in range(fsdp_count)]
    )
    grad_mod = jnp.einsum("br,bld->lrd", turned, shift_grads, precision=EXACT)
    grad_silu = jnp.einsum("bld,lrd->br", shift_grads, mod_weight.astype(F32), precision=EXACT)
    grad_silu = jnp.stack(
        [lax.dynamic_index_in_dim(grad_silu, f ^ j, 0, False) for j in range(fsdp_count)]
    )
    _, silu_pull = jax.vjp(jax.nn.silu, cond_part)
    grad_cond_part = silu_pull(grad_silu)[0]
    grad_condition = lax.all_to_all(grad_cond_part, "fsdp", 0, 0, tiled=True).reshape(1, -1)

    text_sum, bits = text_first + text_second, 1
    while bits < seq_count:
        text_sum = text_sum + swap_seq(text_sum.astype(BF16), bits).astype(F32)
        bits *= 2
    return (
        output[None],
        grad_latents[None],
        grad_skip[None],
        text_sum[None, :text_count],
        grad_condition,
        grad_mod,
        grad_norm_gains,
        grad_qkv,
        grad_query,
        grad_kv,
        grad_self_out,
        grad_cross_out,
        grad_up,
        grad_down,
        grad_skip_gain,
        grad_skip_weight[0],
    )


def solution(mesh):
    in_specs = (
        P("fsdp", "seq", None),
        P("fsdp", "seq", None),
        P("fsdp", None, None),
        P("fsdp"),
        P("fsdp", None),
        P("fsdp", "seq", None),
        P(None, "fsdp", None),
        P(None, None, "fsdp"),
        P(None, "fsdp", None),
        P(None, "fsdp", None),
        P(None, "fsdp", None),
        P(None, "fsdp", None),
        P(None, "fsdp", None),
        P(None, "fsdp", None),
        P(None, "fsdp", None),
        P("fsdp"),
        P("fsdp", None),
    )
    out_specs = (
        P("fsdp", "seq", None),
        P("fsdp", "seq", None),
        P("fsdp", "seq", None),
        P("fsdp", None, None),
        P("fsdp", None),
        P(None, "fsdp", None),
        P(None, None, "fsdp"),
        P(None, "fsdp", None),
        P(None, "fsdp", None),
        P(None, "fsdp", None),
        P(None, "fsdp", None),
        P(None, "fsdp", None),
        P(None, "fsdp", None),
        P(None, "fsdp", None),
        P("fsdp"),
        P("fsdp", None),
    )
    return jax.shard_map(body, mesh=mesh, in_specs=in_specs, out_specs=out_specs, check_vma=False)
```

```python
import functools
import math

import jax
import jax.numpy as jnp
from jax import lax
from jax.experimental import pallas as pl
from jax.experimental.pallas import tpu as pltpu
from jax.sharding import PartitionSpec as P

H = 16
NORM_EPSILON = 1e-06
EXACT = lax.Precision.HIGHEST
BF16 = jnp.bfloat16
F32 = jnp.float32
LOG2_E = 1.4426950408889634
GELU_SCALE = math.sqrt(2.0 / math.pi)
VMEM_LIMIT = 56 * 1024 * 1024


def dot_nn(a, b):
    return lax.dot_general(a, b, (((1,), (0,)), ((), ())), preferred_element_type=F32)


def dot_nt(a, b):
    return lax.dot_general(a, b, (((1,), (1,)), ((), ())), preferred_element_type=F32)


def dot_tn(a, b):
    return lax.dot_general(a, b, (((0,), (0,)), ((), ())), preferred_element_type=F32)


def padded_width(width):
    return -(-width // 128) * 128


def call(kernel, outs, scratch, micros, *operands, scalars=None, deps=(), outside=()):
    specs = [
        pl.BlockSpec(memory_space=pl.ANY if i in outside else pltpu.VMEM)
        for i in range(len(operands))
    ]
    if scalars is not None:
        specs = [pl.BlockSpec(memory_space=pltpu.SMEM)] + specs
        operands = (scalars,) + tuple(operands)
    used, held = len(operands), len(deps)

    def run(*refs):
        kernel(*refs[:used], *refs[used + held :])

    return pl.pallas_call(
        run,
        name=getattr(kernel, "func", kernel).__name__,
        out_shape=tuple(jax.ShapeDtypeStruct(s, d) for s, d in outs),
        in_specs=specs + [pl.BlockSpec(memory_space=pl.ANY)] * held,
        out_specs=tuple([pl.BlockSpec(memory_space=pltpu.VMEM)] * len(outs)),
        scratch_shapes=scratch,
        compiler_params=pltpu.CompilerParams(vmem_limit_bytes=VMEM_LIMIT),
        cost_estimate=pl.CostEstimate(
            flops=int(micros * 1000), bytes_accessed=1000, transcendentals=0
        ),
    )(*operands, *deps)


def gate_kernel(*refs):
    del refs


def gate(values, deps):
    values, deps = list(values), list(deps)
    return list(
        pl.pallas_call(
            gate_kernel,
            out_shape=tuple(jax.ShapeDtypeStruct(m.shape, m.dtype) for m in values),
            in_specs=[pl.BlockSpec(memory_space=pl.ANY)] * (len(values) + len(deps)),
            out_specs=tuple([pl.BlockSpec(memory_space=pl.ANY)] * len(values)),
            input_output_aliases={i: i for i in range(len(values))},
            cost_estimate=pl.CostEstimate(flops=1000, bytes_accessed=1000, transcendentals=0),
        )(*values, *deps)
    )


def cut_of(rows):
    return rows // 32 * 16


def piece_shapes(count, rows, columns):
    if count != 4:
        return [((rows, columns), BF16)] * (count - 1)
    cut = cut_of(rows)
    return [((m, columns), BF16) for m in (2 * cut, 2 * (rows - cut), rows - cut, cut)]


def put_pieces(refs, count, block, values):
    if count != 4:
        refs[block - 1][...] = values.astype(BF16)
        return
    to_x, to_y, x_bottom, y_top = refs
    rows = values.shape[0]
    cut = cut_of(rows)
    top, bottom = values[:cut].astype(BF16), values[cut:].astype(BF16)
    if block == 1:
        to_x[cut:, :] = top
        x_bottom[...] = bottom
    elif block == 2:
        y_top[...] = top
        to_y[rows - cut :, :] = bottom
    else:
        to_x[:cut, :] = top
        to_y[: rows - cut, :] = bottom


def add_terms(count, refs):
    total = refs[0][...].astype(F32)
    if count != 4:
        for ref in refs[1:]:
            total = total + ref[...].astype(F32)
        return total
    from_x, from_y, x_bottom, y_top = [ref[...] for ref in refs[1:]]
    cut, rest = y_top.shape[0], x_bottom.shape[0]
    by_x = jnp.concatenate([from_x[cut:], x_bottom], axis=0)
    by_y = jnp.concatenate([y_top, from_y[rest:]], axis=0)
    return total + by_x.astype(F32) + by_y.astype(F32)


def norm_stats(values):
    mean = jnp.mean(values, axis=1, keepdims=True)
    centered = values - mean
    var = jnp.mean(centered * centered, axis=1, keepdims=True)
    scale = lax.rsqrt(var + NORM_EPSILON)
    return centered * scale, scale


def norm_back(values, gain, grad):
    unit, scale = norm_stats(values)
    grad_unit = grad * gain
    inner = jnp.mean(grad_unit * unit, axis=1, keepdims=True)
    grad_values = scale * (grad_unit - jnp.mean(grad_unit, axis=1, keepdims=True) - unit * inner)
    return grad_values, jnp.sum(grad * unit, axis=0, keepdims=True)


def self_forward_kernel(count, parts, head_size, normed, *refs):
    part_refs, refs = refs[:parts], refs[parts:]
    weight_ref, gains_ref, shift_ref = refs[:3]
    rows_ref, triples_ref = refs[3:5]
    mixed_refs, (held_ref, done) = refs[5:-2], refs[-2:]
    copy = pltpu.make_async_copy(weight_ref.at[:, : held_ref.shape[1]], held_ref, done)
    copy.start()
    stride = held_ref.shape[1] // 3
    rows, width = mixed_refs[0].shape
    factor = LOG2_E / math.sqrt(head_size)
    start = 0
    for ref in part_refs:
        values = ref[...]
        if not normed:
            unit, _ = norm_stats(values.astype(F32))
            values = (unit * gains_ref[0:1, :] + shift_ref[...]).astype(BF16)
        rows_ref[start : start + ref.shape[0], :] = values
        start += ref.shape[0]
    copy.wait()
    for j in range(count):
        at = slice(j * rows, (j + 1) * rows)
        triples_ref[at, :] = dot_nn(rows_ref[at, :], held_ref[...]).astype(BF16)
    for j in range(count):
        at = slice(j * rows, (j + 1) * rows)
        for h in range(width // head_size):
            low = h * head_size
            q = triples_ref[at, low : low + head_size]
            k = triples_ref[:, stride + low : stride + low + head_size]
            v = triples_ref[:, 2 * stride + low : 2 * stride + low + head_size]
            scores = dot_nt(q, k)
            top = jnp.max(scores, axis=1, keepdims=True)
            weights = jnp.exp2((scores - top) * factor)
            total = jnp.sum(weights, axis=1, keepdims=True)
            mixed = dot_nn(weights.astype(BF16), v) * (1.0 / total)
            mixed_refs[j][:, low : low + head_size] = mixed.astype(BF16)


def self_forward(parts, weight, gains, shift, head_size, count, width, normed, deps=()):
    total = sum(m.shape[0] for m in parts)
    columns = parts[0].shape[1]
    held = (columns, 3 * padded_width(width))
    found = call(
        functools.partial(self_forward_kernel, count, len(parts), head_size, normed),
        [((total, columns), BF16), ((total, held[1]), BF16)]
        + [((total // count, width), BF16)] * count,
        [pltpu.VMEM(held, BF16), pltpu.SemaphoreType.DMA],
        24,
        *parts,
        weight,
        gains,
        shift[None],
        deps=deps,
        outside=(len(parts),),
    )
    return found[0], found[1], list(found[2:])


def attention_back(q, k, v, grad, valid, head_size):
    factor = LOG2_E / math.sqrt(head_size)
    scores = dot_nt(k, q)
    if valid is not None:
        scores = jnp.where(valid, scores, -1e30)
    top = jnp.max(scores, axis=0, keepdims=True)
    weights = jnp.exp2((scores - top) * factor)
    weights = weights * (1.0 / jnp.sum(weights, axis=0, keepdims=True))
    grad_weights = dot_nt(v, grad)
    delta = jnp.sum(grad_weights * weights, axis=0, keepdims=True)
    grad_scores = (weights * (grad_weights - delta)).astype(BF16)
    scale = 1.0 / math.sqrt(head_size)
    return (
        dot_tn(grad_scores, k) * scale,
        dot_nn(grad_scores, q) * scale,
        dot_nn(weights.astype(BF16), grad),
    )


def self_backward_kernel(count, head_size, step, triples_ref, *refs):
    grad_refs, (weight_ref, out_ref, own_ref) = refs[:count], refs[count : count + 3]
    piece_refs, (keys_ref, values_ref, held_ref, done) = refs[count + 3 : -4], refs[-4:]
    copy = pltpu.make_async_copy(weight_ref.at[:, : held_ref.shape[1]], held_ref, done)
    copy.start()
    total = triples_ref.shape[0]
    rows, width = grad_refs[0].shape
    stride = held_ref.shape[1] // 3
    for h in range(width // head_size):
        low = h * head_size
        k = triples_ref[:, stride + low : stride + low + head_size]
        v = triples_ref[:, 2 * stride + low : 2 * stride + low + head_size]
        for i in range(total // step):
            at = slice(i * step, (i + 1) * step)
            inside = (i * step) % rows
            q = triples_ref[at, low : low + head_size]
            grad = grad_refs[i * step // rows][inside : inside + step, low : low + head_size]
            grad_q, grad_k, grad_v = attention_back(q, k, v, grad, None, head_size)
            out_ref[at, low : low + head_size] = grad_q.astype(BF16)
            if i == 0:
                keys_ref[...] = grad_k
                values_ref[...] = grad_v
            else:
                keys_ref[...] += grad_k
                values_ref[...] += grad_v
        out_ref[:, stride + low : stride + low + head_size] = keys_ref[...].astype(BF16)
        out_ref[:, 2 * stride + low : 2 * stride + low + head_size] = values_ref[...].astype(BF16)
    if stride > width:
        for g in range(3):
            out_ref[:, g * stride + width : (g + 1) * stride] = jnp.zeros((total, stride - width), BF16)
    copy.wait()
    for j in range(count):
        found = dot_nt(out_ref[j * rows : (j + 1) * rows, :], held_ref[...])
        if j == 0:
            own_ref[...] = found
        else:
            put_pieces(piece_refs, count, j, found)


def self_backward(triples, grads, weight, head_size, deps=()):
    count = len(grads)
    total, rows, columns = triples.shape[0], grads[0].shape[0], weight.shape[0]
    step = min(256, rows)
    found = call(
        functools.partial(self_backward_kernel, count, head_size, step),
        [(triples.shape, BF16), ((rows, columns), F32)] + piece_shapes(count, rows, columns),
        [
            pltpu.VMEM((total, head_size), F32),
            pltpu.VMEM((total, head_size), F32),
            pltpu.VMEM((columns, triples.shape[1]), BF16),
            pltpu.SemaphoreType.DMA,
        ],
        32,
        triples,
        *grads,
        weight,
        deps=deps,
        outside=(1 + count,),
    )
    return found[0], found[1], list(found[2:])


def fill_corner(count, matrix_refs, scalars_ref, corner_ref):
    if len(matrix_refs) == count:
        return list(matrix_refs)
    odd = scalars_ref[2 * count]
    half = matrix_refs[-1].shape[0]
    corner_ref[pl.ds(pl.multiple_of(odd * half, half), half), :] = matrix_refs[-2][...]
    corner_ref[pl.ds(pl.multiple_of((1 - odd) * half, half), half), :] = matrix_refs[-1][...]
    return list(matrix_refs[:-2]) + [corner_ref]


def corner_scratch(count, matrices):
    rows, columns = matrices[0].shape
    return pltpu.VMEM((rows, columns) if len(matrices) > count else (16, 128), BF16)


def fill_pairs(count, block, pair_refs, pairs_ref):
    padded, columns = pairs_ref.shape[1:]
    place = 0
    for ref in pair_refs:
        j, low = divmod(place, padded)
        pairs_ref[j, low : low + ref.shape[0], :] = ref[:, block * columns : (block + 1) * columns]
        place += ref.shape[0]


def middle_forward_kernel(block, count, matrix_parts, pair_parts, head_size, scalars_ref, *refs):
    mixed_refs, refs = refs[:count], refs[count:]
    matrix_refs, refs = refs[:matrix_parts], refs[matrix_parts:]
    pair_refs, refs = refs[:pair_parts], refs[pair_parts:]
    hidden_ref, gains_ref = refs[:2]
    (self_ref, after_self_ref, norm_ref, queries_ref, cross_ref, after_cross_ref) = refs[2:8]
    mlp_ref = refs[8]
    wide_ref, narrow_ref, corner_ref, pairs_ref = refs[-4:]
    width = mixed_refs[0].shape[1]
    stride = matrix_refs[0].shape[1] // 3
    matrices = fill_corner(count, matrix_refs, scalars_ref, corner_ref)
    fill_pairs(count, block, pair_refs, pairs_ref)
    order = [scalars_ref[i] for i in range(count)]
    relative = [scalars_ref[count + j] for j in range(count)]
    length = scalars_ref[2 * count + 1]
    spans = [slice(a * width, (a + 1) * width) for a in range(count)]

    for j in range(count):
        narrow_ref[relative[j]] = mixed_refs[j][...]
    for a in range(count):
        self_ref[:, spans[a]] = narrow_ref[a]
    tokens = self_ref[...]
    for i in range(count):
        wide_ref[order[i]] = dot_nn(tokens, matrices[i][:, :width])
    for a in range(count):
        after_self_ref[:, spans[a]] = hidden_ref[:, spans[a]].astype(F32) + wide_ref[a]
    normed = (norm_stats(after_self_ref[...])[0] * gains_ref[1:2, :]).astype(BF16)
    norm_ref[...] = normed
    for i in range(count):
        found = dot_nn(normed, matrices[i][:, stride : stride + width])
        queries_ref[order[i] ^ relative[0]] = found.astype(BF16)

    factor = LOG2_E / math.sqrt(head_size)
    keys_rows = pairs_ref.shape[1]
    valid = lax.broadcasted_iota(jnp.int32, (1, keys_rows), 1) < length
    pair_stride = pairs_ref.shape[2] // 2
    for j in range(count):
        for h in range(width // head_size):
            at = slice(h * head_size, (h + 1) * head_size)
            values_at = slice(pair_stride + h * head_size, pair_stride + (h + 1) * head_size)
            scores = dot_nt(queries_ref[j, :, at], pairs_ref[j, :, at])
            scores = jnp.where(valid, scores, -1e30)
            top = jnp.max(scores, axis=1, keepdims=True)
            weights = jnp.exp2((scores - top) * factor)
            total = jnp.sum(weights, axis=1, keepdims=True)
            mixed = dot_nn(weights.astype(BF16), pairs_ref[j, :, values_at]) * (1.0 / total)
            narrow_ref[relative[j], :, at] = mixed.astype(BF16)
    for a in range(count):
        cross_ref[:, spans[a]] = narrow_ref[a]
    tokens = cross_ref[...]
    for i in range(count):
        wide_ref[order[i]] = dot_nn(tokens, matrices[i][:, 2 * stride : 2 * stride + width])
    for a in range(count):
        after_cross_ref[:, spans[a]] = after_self_ref[:, spans[a]] + wide_ref[a]
    mlp_ref[...] = (norm_stats(after_cross_ref[...])[0] * gains_ref[2:3, :]).astype(BF16)


def pairs_scratch(count, pairs):
    return pltpu.VMEM(
        (count, sum(m.shape[0] for m in pairs) // count, pairs[0].shape[1] // 2), BF16
    )


def middle_forward(block, scalars, mixed, matrices, pairs, hidden, gains, head_size, deps=()):
    count = len(mixed)
    rows, columns = hidden.shape
    width = columns // count
    return call(
        functools.partial(
            middle_forward_kernel, block, count, len(matrices), len(pairs), head_size
        ),
        [
            ((rows, columns), BF16),
            ((rows, columns), F32),
            ((rows, columns), BF16),
            ((count, rows, width), BF16),
            ((rows, columns), BF16),
            ((rows, columns), F32),
            ((rows, columns), BF16),
        ],
        [
            pltpu.VMEM((count, rows, width), F32),
            pltpu.VMEM((count, rows, width), BF16),
            corner_scratch(count, matrices),
            pairs_scratch(count, pairs),
        ],
        23,
        *mixed,
        *matrices,
        *pairs,
        hidden,
        gains,
        scalars=scalars,
        deps=deps,
    )


def middle_backward_kernel(block, count, matrix_parts, pair_parts, terms, head_size, scalars_ref, *refs):
    matrix_refs, refs = refs[:matrix_parts], refs[matrix_parts:]
    pair_refs, refs = refs[:pair_parts], refs[pair_parts:]
    term_refs, refs = refs[:terms], refs[terms:]
    grad_out_ref, after_cross_ref, after_self_ref, queries_ref, gains_ref = refs[:5]
    out_ref, self_branch_ref, query_branch_ref, cross_branch_ref, gain_ref = refs[5:10]
    mixed_grad_refs, refs = refs[10 : 10 + count], refs[10 + count :]
    own_pairs_ref, pair_grad_refs = refs[0], refs[1:-6]
    wide_ref, narrow_ref, query_ref, corner_ref, pairs_ref, pair_total_ref = refs[-6:]
    width = queries_ref.shape[2]
    stride = matrix_refs[0].shape[1] // 3
    matrices = fill_corner(count, matrix_refs, scalars_ref, corner_ref)
    fill_pairs(count, block, pair_refs, pairs_ref)
    order = [scalars_ref[i] for i in range(count)]
    relative = [scalars_ref[count + j] for j in range(count)]
    length = scalars_ref[2 * count + 1]
    spans = [slice(a * width, (a + 1) * width) for a in range(count)]

    def back(branch_ref, group):
        columns = slice(group * stride, group * stride + width)
        total = dot_nt(branch_ref[0], matrices[0][:, columns])
        for i in range(1, count):
            total = total + dot_nt(branch_ref[i], matrices[i][:, columns])
        return total

    def divide(values):
        for a in range(count):
            narrow_ref[a] = values[:, spans[a]].astype(BF16)

    grad, grad_gain = norm_back(
        after_cross_ref[...], gains_ref[2:3, :], add_terms(count, term_refs)
    )
    gain_ref[1:2, :] = grad_gain
    wide_ref[...] = grad + grad_out_ref[...].astype(F32)
    divide(wide_ref[...])
    for i in range(count):
        cross_branch_ref[i] = narrow_ref[order[i]]
    divide(back(cross_branch_ref, 2))

    keys_rows = pairs_ref.shape[1]
    valid = lax.broadcasted_iota(jnp.int32, (keys_rows, 1), 0) < length
    pair_stride = pairs_ref.shape[2] // 2
    if pair_stride > width:
        for g in range(2):
            pair_total_ref[:, g * pair_stride + width : (g + 1) * pair_stride] = jnp.zeros(
                (keys_rows, pair_stride - width), F32
            )
    for j in range(count):
        for h in range(width // head_size):
            at = slice(h * head_size, (h + 1) * head_size)
            values_at = slice(pair_stride + h * head_size, pair_stride + (h + 1) * head_size)
            grad_q, grad_k, grad_v = attention_back(
                queries_ref[j, :, at],
                pairs_ref[j, :, at],
                pairs_ref[j, :, values_at],
                narrow_ref[relative[j], :, at],
                valid,
                head_size,
            )
            query_ref[j, :, at] = grad_q.astype(BF16)
            pair_total_ref[:, at] = grad_k
            pair_total_ref[:, values_at] = grad_v
        if j == 0:
            own_pairs_ref[...] = pair_total_ref[...]
        else:
            pair_grad_refs[j - 1][...] = pair_total_ref[...].astype(BF16)
    for i in range(count):
        query_branch_ref[i] = query_ref[order[i] ^ relative[0]]
    grad, grad_gain = norm_back(after_self_ref[...], gains_ref[1:2, :], back(query_branch_ref, 1))
    gain_ref[0:1, :] = grad_gain
    out_ref[...] = grad + wide_ref[...]
    divide(out_ref[...])
    for i in range(count):
        self_branch_ref[i] = narrow_ref[order[i]]
    divide(back(self_branch_ref, 0))
    for j in range(count):
        mixed_grad_refs[j][...] = narrow_ref[relative[j]]


def middle_backward(
    block, scalars, matrices, pairs, terms, grad_out, after_cross, after_self, queries, gains, head_size, deps=()
):
    count, rows, width = queries.shape
    columns = count * width
    branch = ((count, rows, width), BF16)
    text = pairs_scratch(count, pairs)
    keys_rows, pair_columns = text.shape[1:]
    found = call(
        functools.partial(
            middle_backward_kernel, block, count, len(matrices), len(pairs), len(terms), head_size
        ),
        [((rows, columns), F32), branch, branch, branch, ((2, columns), F32)]
        + [((rows, width), BF16)] * count
        + [((keys_rows, pair_columns), F32)]
        + [((keys_rows, pair_columns), BF16)] * (count - 1),
        [
            pltpu.VMEM((rows, columns), F32),
            pltpu.VMEM((count, rows, width), BF16),
            pltpu.VMEM((count, rows, width), BF16),
            corner_scratch(count, matrices),
            text,
            pltpu.VMEM((keys_rows, pair_columns), F32),
        ],
        37,
        *matrices,
        *pairs,
        *terms,
        grad_out,
        after_cross,
        after_self,
        queries,
        gains,
        scalars=scalars,
        deps=deps,
    )
    found = list(found)
    return found[:5] + [found[5 : 5 + count], found[5 + count], found[6 + count :]]


def mlp_up_kernel(count, parts, *refs):
    part_refs, (up_ref, rows_ref, up_rows_ref, activated_ref) = refs[:parts], refs[parts:]
    start = 0
    for ref in part_refs:
        rows_ref[start : start + ref.shape[0], :] = ref[...]
        start += ref.shape[0]
    rows = start // count
    for j in range(count):
        at = slice(j * rows, (j + 1) * rows)
        values = dot_nn(rows_ref[at, :], up_ref[...])
        up_rows_ref[at, :] = values
        inner = GELU_SCALE * (values + 0.044715 * (values * values * values))
        activated_ref[at, :] = (0.5 * values * (1.0 + jnp.tanh(inner))).astype(BF16)


def mlp_up(parts, up, count, deps=()):
    total, columns, hidden = sum(m.shape[0] for m in parts), up.shape[0], up.shape[1]
    return call(
        functools.partial(mlp_up_kernel, count, len(parts)),
        [((total, columns), BF16), ((total, hidden), F32), ((total, hidden), BF16)],
        [],
        15,
        *parts,
        up,
        deps=deps,
    )


def mlp_down_kernel(count, activated_ref, down_ref, own_ref, *piece_refs):
    rows = own_ref.shape[0]
    for j in range(count - 1, -1, -1):
        found = dot_nn(activated_ref[j * rows : (j + 1) * rows, :], down_ref[...])
        if j == 0:
            own_ref[...] = found
        else:
            put_pieces(piece_refs, count, j, found)


def mlp_down(activated, down, count, deps=()):
    rows, columns = activated.shape[0] // count, down.shape[1]
    found = call(
        functools.partial(mlp_down_kernel, count),
        [((rows, columns), F32)] + piece_shapes(count, rows, columns),
        [],
        11,
        activated,
        down,
        deps=deps,
    )
    return found[0], list(found[1:])


def stack_kernel(*refs):
    start = 0
    for ref in refs[:-1]:
        refs[-1][start : start + ref.shape[0], :] = ref[...]
        start += ref.shape[0]


def stack_rows(parts, deps=()):
    shape = (sum(m.shape[0] for m in parts), parts[0].shape[1])
    return call(stack_kernel, [(shape, parts[0].dtype)], [], 3, *parts, deps=deps)[0]


def mlp_backward_kernel(count, parts, *refs):
    part_refs, refs = refs[:parts], refs[parts:]
    up_rows_ref, up_ref, down_ref, rows_ref, grad_up_ref, own_ref = refs[:6]
    piece_refs = refs[6:]
    start = 0
    for ref in part_refs:
        rows_ref[start : start + ref.shape[0], :] = ref[...]
        start += ref.shape[0]
    rows = start // count
    for j in range(count - 1, -1, -1):
        at = slice(j * rows, (j + 1) * rows)
        grad = dot_nt(rows_ref[at, :], down_ref[...])
        values = up_rows_ref[at, :]
        square = values * values
        bent = jnp.tanh(GELU_SCALE * (values + 0.044715 * (values * square)))
        slope = 0.5 * (1.0 + bent) + 0.5 * values * (1.0 - bent * bent) * (
            GELU_SCALE * (1.0 + 3.0 * 0.044715 * square)
        )
        grad_up_ref[at, :] = (grad * slope).astype(BF16)
        found = dot_nt(grad_up_ref[at, :], up_ref[...])
        if j == 0:
            own_ref[...] = found
        else:
            put_pieces(piece_refs, count, j, found)


def mlp_backward(parts, up_rows, up, down, count, deps=()):
    total, columns, hidden = sum(m.shape[0] for m in parts), up.shape[0], up.shape[1]
    rows = total // count
    found = call(
        functools.partial(mlp_backward_kernel, count, len(parts)),
        [((total, columns), BF16), ((total, hidden), BF16), ((rows, columns), F32)]
        + piece_shapes(count, rows, columns),
        [],
        22,
        *parts,
        up_rows,
        up,
        down,
        deps=deps,
    )
    return list(found[:3]) + [list(found[3:])]


def outer_kernel(count, groups, half, scalars_ref, *refs):
    rows_refs, branch_refs, refs = refs[:groups], refs[groups : 2 * groups], refs[2 * groups :]
    out_refs, turned_ref = refs[:-1], refs[-1]
    width = branch_refs[0].shape[2]
    stride = padded_width(width)
    odd = scalars_ref[2 * count]
    for g in range(groups):
        at = slice(g * stride, g * stride + width)
        turned_ref[...] = rows_refs[g][...].T
        out_refs[0][:, at] = dot_nn(turned_ref[...], branch_refs[g][0]).astype(BF16)
        for i in range(1, count):
            if not half:
                out_refs[i][:, at] = dot_nn(turned_ref[...], branch_refs[g][i]).astype(BF16)
                continue
            for k in range(2):
                low = pl.multiple_of((odd if k == 0 else 1 - odd) * half, half)
                found = dot_nn(turned_ref[pl.ds(low, half), :], branch_refs[g][i])
                out_refs[2 * i - 1 + k][:, at] = found.astype(BF16)
    if stride > width:
        for ref in out_refs:
            for g in range(groups):
                ref[:, g * stride + width : (g + 1) * stride] = jnp.zeros(
                    (ref.shape[0], stride - width), BF16
                )


def outer(scalars, rows, branches, deps=()):
    count, tokens, width = branches[0].shape
    groups, columns = len(rows), rows[0].shape[1]
    stride = padded_width(width)
    half = columns // 2 if count == 4 else 0
    shapes = [((columns, groups * stride), BF16)]
    if half:
        shapes += [((half, groups * stride), BF16)] * (2 * (count - 1))
    else:
        shapes = shapes * count
    return list(
        call(
            functools.partial(outer_kernel, count, groups, half),
            shapes,
            [pltpu.VMEM((columns, tokens), BF16)],
            3.5 * groups,
            *rows,
            *branches,
            scalars=scalars,
            deps=deps,
        )
    )


def join_kernel(count, scalars_ref, own_ref, mine_ref, other_ref, out_ref):
    odd = scalars_ref[2 * count]
    half = mine_ref.shape[0]
    for ref, place in ((mine_ref, odd), (other_ref, 1 - odd)):
        at = pl.ds(pl.multiple_of(place * half, half), half)
        out_ref[at, :] = (own_ref[at, :].astype(F32) + ref[...].astype(F32)).astype(BF16)


def join_halves(scalars, own, mine, other):
    count = lax.axis_size("seq")
    (found,) = call(
        functools.partial(join_kernel, count),
        [(own.shape, BF16)],
        [],
        4,
        own,
        mine,
        other,
        scalars=scalars,
    )
    return found


def joined_stats(first, second):
    count = first.shape[1] + second.shape[1]
    mean = (jnp.sum(first, axis=1, keepdims=True) + jnp.sum(second, axis=1, keepdims=True)) / count
    first, second = first - mean, second - mean
    var = (
        jnp.sum(first * first, axis=1, keepdims=True)
        + jnp.sum(second * second, axis=1, keepdims=True)
    ) / count
    scale = lax.rsqrt(var + NORM_EPSILON)
    return first * scale, second * scale, scale


def skip_forward_kernel(count, matrix_parts, terms, scalars_ref, *refs):
    matrix_refs, refs = refs[:matrix_parts], refs[matrix_parts:]
    term_refs, refs = refs[:terms], refs[terms:]
    residual_ref, second_ref, gains_ref, next_ref, shift_ref = refs[:5]
    first_ref, joined_ref, out_ref, norm_ref, wide_ref, corner_ref = refs[5:]
    rows, columns = first_ref.shape
    width = columns // count
    matrices = fill_corner(count, matrix_refs, scalars_ref, corner_ref)
    first_ref[...] = residual_ref[...] + add_terms(count, term_refs)
    first, second, _ = joined_stats(first_ref[...], second_ref[...].astype(F32))
    joined_ref[:, :columns] = (first * gains_ref[0:1, :]).astype(BF16)
    joined_ref[:, columns:] = (second * gains_ref[1:2, :]).astype(BF16)
    joined = joined_ref[...]
    for i in range(count):
        wide_ref[scalars_ref[i]] = dot_nn(joined, matrices[i][:, :width])
    for a in range(count):
        out_ref[:, a * width : (a + 1) * width] = wide_ref[a]
    normed = norm_stats(out_ref[...])[0] * next_ref[0:1, :] + shift_ref[...]
    norm_ref[...] = normed.astype(BF16)


def skip_forward(scalars, matrices, terms, residual, second, gains, next_gains, shift, deps=()):
    rows, columns = residual.shape
    count = lax.axis_size("seq")
    return call(
        functools.partial(skip_forward_kernel, count, len(matrices), len(terms)),
        [
            ((rows, columns), F32),
            ((rows, 2 * columns), BF16),
            ((rows, columns), F32),
            ((rows, columns), BF16),
        ],
        [pltpu.VMEM((count, rows, columns // count), F32), corner_scratch(count, matrices)],
        11,
        *matrices,
        *terms,
        residual,
        second,
        gains,
        next_gains,
        shift[None],
        scalars=scalars,
        deps=deps,
    )


def skip_backward_kernel(count, matrix_parts, terms, scalars_ref, *refs):
    matrix_refs, refs = refs[:matrix_parts], refs[matrix_parts:]
    term_refs, refs = refs[:terms], refs[terms:]
    hidden_ref, next_ref, residual_ref, first_ref, second_ref, gains_ref = refs[:6]
    branch_ref, grad_first_ref, grad_second_ref, vectors_ref, round_ref = refs[6:11]
    narrow_ref, corner_ref = refs[11:]
    rows, columns = first_ref.shape
    width = columns // count
    matrices = fill_corner(count, matrix_refs, scalars_ref, corner_ref)
    grad_norm = add_terms(count, term_refs)
    vectors_ref[0:1, :] = jnp.sum(grad_norm, axis=0, keepdims=True)
    grad, grad_gain = norm_back(hidden_ref[...], next_ref[0:1, :], grad_norm)
    vectors_ref[1:2, :] = grad_gain
    grad = grad + residual_ref[...]
    for a in range(count):
        narrow_ref[a] = grad[:, a * width : (a + 1) * width].astype(BF16)
    for i in range(count):
        branch_ref[i] = narrow_ref[scalars_ref[i]]

    def back(at):
        total = dot_nt(branch_ref[0], matrices[0][at, :width])
        for i in range(1, count):
            total = total + dot_nt(branch_ref[i], matrices[i][at, :width])
        return total

    grad_first_ref[...] = back(slice(0, columns))
    grad_second_ref[...] = back(slice(columns, 2 * columns))
    first, second, scale = joined_stats(first_ref[...], second_ref[...].astype(F32))
    vectors_ref[2:3, :] = jnp.sum(grad_first_ref[...] * first, axis=0, keepdims=True)
    vectors_ref[3:4, :] = jnp.sum(grad_second_ref[...] * second, axis=0, keepdims=True)
    grad_first = grad_first_ref[...] * gains_ref[0:1, :]
    grad_second = grad_second_ref[...] * gains_ref[1:2, :]
    mean = (
        jnp.sum(grad_first, axis=1, keepdims=True) + jnp.sum(grad_second, axis=1, keepdims=True)
    ) / (2 * columns)
    inner = (
        jnp.sum(grad_first * first, axis=1, keepdims=True)
        + jnp.sum(grad_second * second, axis=1, keepdims=True)
    ) / (2 * columns)
    grad_first_ref[...] = scale * (grad_first - mean - first * inner)
    grad_second_ref[...] = scale * (grad_second - mean - second * inner)
    round_ref[...] = grad_first_ref[...].astype(BF16)


def skip_backward(
    scalars, matrices, terms, hidden, next_gains, residual, first, second, gains, deps=()
):
    rows, columns = first.shape
    count = lax.axis_size("seq")
    narrow = (count, rows, columns // count)
    return call(
        functools.partial(skip_backward_kernel, count, len(matrices), len(terms)),
        [
            (narrow, BF16),
            ((rows, columns), F32),
            ((rows, columns), F32),
            ((4, columns), F32),
            ((rows, columns), BF16),
        ],
        [pltpu.VMEM(narrow, BF16), corner_scratch(count, matrices)],
        15,
        *matrices,
        *terms,
        hidden,
        next_gains,
        residual,
        first,
        second,
        gains,
        scalars=scalars,
        deps=deps,
    )


def open_backward_kernel(count, terms, *refs):
    term_refs, refs = refs[:terms], refs[terms:]
    hidden_ref, gains_ref, residual_ref, out_ref, vectors_ref = refs
    grad_norm = add_terms(count, term_refs)
    vectors_ref[0:1, :] = jnp.sum(grad_norm, axis=0, keepdims=True)
    grad, grad_gain = norm_back(hidden_ref[...].astype(F32), gains_ref[0:1, :], grad_norm)
    vectors_ref[1:2, :] = grad_gain
    out_ref[...] = grad + residual_ref[...]


def open_backward(terms, hidden, gains, residual, deps=()):
    count = lax.axis_size("seq")
    return call(
        functools.partial(open_backward_kernel, count, len(terms)),
        [(residual.shape, F32), ((2, residual.shape[1]), F32)],
        [],
        5,
        *terms,
        hidden,
        gains,
        residual,
        deps=deps,
    )


def close_kernel(count, terms, *refs):
    refs[terms + 1][...] = (refs[terms][...] + add_terms(count, refs[:terms])).astype(BF16)


def close_forward(terms, residual, deps=()):
    count = lax.axis_size("seq")
    (found,) = call(
        functools.partial(close_kernel, count, len(terms)),
        [(residual.shape, BF16)],
        [],
        3,
        *terms,
        residual,
        deps=deps,
    )
    return found


def pack_kernel(count, *refs):
    start = 0
    for ref in refs[:count]:
        refs[count][: ref.shape[0], start : start + ref.shape[1]] = ref[...]
        start += ref.shape[1]


def pack(shards, deps=()):
    rows = -(-max(m.shape[0] for m in shards) // 16) * 16
    shape = (rows, sum(m.shape[1] for m in shards))
    return call(functools.partial(pack_kernel, len(shards)), [(shape, BF16)], [], 3, *shards, deps=deps)[0]


def settle_kernel(count, parts, plan, scalars_ref, *refs):
    block_refs, refs = refs[:parts], refs[parts:]
    outs = sum(entry[3] for entry in plan)
    out_refs, stack_ref = refs[-outs - 1 : -1], refs[-1]
    for j in range(count):
        owner = scalars_ref[count + j]
        if j == count - 1 and parts > count:
            cut = block_refs[j].shape[0]
            stack_ref[owner, :cut] = block_refs[j][...]
            stack_ref[owner, cut:] = block_refs[j + 1][...]
        else:
            stack_ref[owner] = block_refs[j][...]
    place = 0
    for first, rows, groups, pieces, width, stride in plan:
        if not groups:
            for a in range(count):
                found = stack_ref[a, :rows, first : first + width]
                out_refs[place][0, a * rows : (a + 1) * rows, :] = found.astype(F32)
        for p in range(pieces):
            for g in range(groups):
                for a in range(count):
                    low = first + (p * groups + g) * stride
                    at = (g * count + a) * width
                    found = stack_ref[a, :rows, low : low + width]
                    out_refs[place + p][0, :, at : at + width] = found.astype(F32)
        place += pieces


def settle(scalars, blocks, plan, layer, layer_count, before):
    count = lax.axis_size("seq")
    shapes = []
    for _, rows, groups, pieces, width, _ in plan:
        shapes += [(rows, groups * count * width) if groups else (count * rows, width)] * pieces
    held = [] if before is None else list(before)
    inputs = [pl.BlockSpec(memory_space=pltpu.VMEM)] * len(blocks)
    inputs += [pl.BlockSpec(memory_space=pl.ANY)] * len(held)
    found = pl.pallas_call(
        functools.partial(settle_kernel, count, len(blocks), plan),
        grid=(1,),
        out_shape=[jax.ShapeDtypeStruct((layer_count,) + shape, F32) for shape in shapes],
        in_specs=[pl.BlockSpec(memory_space=pltpu.SMEM)] + inputs,
        out_specs=[pl.BlockSpec((1,) + shape, lambda i: (layer, 0, 0)) for shape in shapes],
        scratch_shapes=[pltpu.VMEM((count,) + blocks[0].shape, BF16)],
        input_output_aliases={1 + len(blocks) + i: i for i in range(len(held))},
        compiler_params=pltpu.CompilerParams(vmem_limit_bytes=VMEM_LIMIT),
        cost_estimate=pl.CostEstimate(flops=8_000_000_000, bytes_accessed=1000, transcendentals=0),
    )(scalars, *blocks, *held)
    return list(found)


def plan_of(entries):
    plan, first = [], 0
    for shard, groups, pieces, width in entries:
        rows, columns = shard.shape
        stride = columns // (groups * pieces) if groups else columns
        plan.append((first, rows, groups, pieces, width, stride))
        first += columns
    return tuple(plan)


def finish(scalars, entries, layer, layer_count, before=None, deps=()):
    blocks = gather_parts(pack([entry[0] for entry in entries], deps))
    return settle(scalars, blocks, plan_of(entries), layer, layer_count, before)


def swap_seq(block, bits):
    seq_count = lax.axis_size("seq")
    return lax.ppermute(block, "seq", [(i, i ^ bits) for i in range(seq_count)])


def swap_fsdp(block, bits):
    fsdp_count = lax.axis_size("fsdp")
    return lax.ppermute(block, "fsdp", [(i, i ^ bits) for i in range(fsdp_count)])


def swap_core(block):
    return swap_fsdp(block, 1)


def swap_by_core(block, even_bits, odd_bits):
    seq_count, fsdp_count = lax.axis_size("seq"), lax.axis_size("fsdp")
    pairs = []
    for s in range(seq_count):
        for f in range(fsdp_count):
            other = s ^ (odd_bits if f % 2 else even_bits)
            pairs.append((s * fsdp_count + f, other * fsdp_count + f))
    return lax.ppermute(block, ("seq", "fsdp"), pairs)


def add_bf16(*terms):
    total = terms[0].astype(F32)
    for term in terms[1:]:
        total = total + term.astype(F32)
    return total.astype(BF16)


def scatter_first(pieces):
    seq_count = lax.axis_size("seq")
    if seq_count != 4:
        return [swap_seq(m, j + 1) for j, m in enumerate(pieces)]
    return [swap_seq(pieces[0], 1), swap_seq(pieces[1], 2), pieces[2], pieces[3]]


def scatter_last(own, first, ready=None):
    seq_count = lax.axis_size("seq")
    if seq_count != 4:
        return [own] + first
    from_x, from_y, x_bottom, y_top = first
    if ready is not None:
        from_x, from_y = gate([from_x, from_y], ready)
    cut, rest = y_top.shape[0], x_bottom.shape[0]
    to_y, to_x = add_bf16(y_top, from_x[:cut]), add_bf16(x_bottom, from_y[:rest])
    return [own, from_x, from_y, swap_seq(to_x, 1), swap_seq(to_y, 2)]


def exchange_rel(blocks):
    return [blocks[0]] + [swap_seq(blocks[j], j) for j in range(1, len(blocks))]


def gather_first(block):
    seq_count = lax.axis_size("seq")
    if seq_count != 4:
        return [block] + [swap_seq(block, j) for j in range(1, seq_count)]
    return [block, swap_seq(block, 1), swap_seq(block, 2)]


def gather_last(first, ready=None):
    seq_count = lax.axis_size("seq")
    if seq_count != 4:
        return first
    block, from_x, from_y = first
    if ready is not None:
        from_x, from_y = gate([from_x, from_y], ready)
    cut = cut_of(block.shape[0])
    return [block, from_x, from_y, swap_seq(from_y[:cut], 1), swap_seq(from_x[cut:], 2)]


def gather_parts(block):
    return gather_last(gather_first(block))


def list_order():
    s, seq_count = lax.axis_index("seq"), lax.axis_size("seq")
    if seq_count != 4:
        return [s ^ j for j in range(seq_count)]
    odd = lax.axis_index("fsdp") % 2
    return [s, s ^ (1 + odd), s ^ (2 - odd), s ^ 3]


def spread_first(block):
    seq_count = lax.axis_size("seq")
    if seq_count != 4:
        return [block] + [swap_seq(block, j) for j in range(1, seq_count)]
    return [block, swap_by_core(block, 1, 2)]


def spread_last(blocks, ready, part_ready=None):
    seq_count = lax.axis_size("seq")
    if seq_count != 4:
        return blocks
    odd = lax.axis_index("fsdp") % 2
    block, first = blocks
    half = block.shape[0] // 2
    if ready is not None:
        (first,) = gate([first], ready)
    part = swap_by_core(lax.dynamic_slice_in_dim(first, odd * half, half, 0), 2, 1)
    other = swap_core(first)
    if part_ready is not None:
        (part,) = gate([part], part_ready)
    return [block, first, other, part, swap_core(part)]


def unspread(scalars, blocks):
    seq_count = lax.axis_size("seq")
    if seq_count != 4:
        return add_bf16(blocks[0], *[swap_seq(blocks[j], j) for j in range(1, seq_count)])
    own, first_mine, first_other, second_mine, second_other, corner_mine, corner_other = blocks
    passed = swap_by_core(add_bf16(corner_mine, swap_core(corner_other)), 2, 1)
    other = swap_by_core(add_bf16(first_other, swap_core(second_mine)), 1, 2)
    mine = swap_by_core(add_bf16(first_mine, swap_core(second_other), passed), 1, 2)
    return join_halves(scalars, own, mine, other)


def own_part(matrix, groups, padded):
    s, seq_count = lax.axis_index("seq"), lax.axis_size("seq")
    width = matrix.shape[1] // (groups * seq_count)
    parts = [
        jnp.pad(
            lax.dynamic_slice_in_dim(matrix, (g * seq_count + s) * width, width, 1),
            ((0, 0), (0, padded - width)),
        )
        for g in range(groups)
    ]
    return jnp.concatenate(parts, axis=1)


def gather_fsdp(shard):
    return lax.all_gather(shard, "fsdp", axis=0, tiled=True)


def scatter_fsdp(full):
    return lax.psum_scatter(full.astype(BF16), "fsdp", scatter_dimension=0, tiled=True)


def layer_forward(parts, hidden, scalars, gains, shift, pairs, weights, normed, deps):
    lead_part, square_parts, up_part = weights
    seq_count = lax.axis_size("seq")
    tok_rows, model_width = hidden.shape
    head_size, width = model_width // H, model_width // seq_count
    first_all, triples, mixed = self_forward(
        parts,
        lead_part,
        gains,
        shift,
        head_size,
        seq_count,
        width,
        normed,
        (square_parts[0],) + deps,
    )
    mixed_rel = exchange_rel(mixed)
    square_parts = spread_last(square_parts, [mixed[0]], mixed_rel[1:])
    self_tokens, after_self, cross_norm, queries, cross_tokens, after_cross, mlp_norm = (
        middle_forward(
            int(normed), scalars, mixed_rel, square_parts, pairs, hidden, gains, head_size
        )
    )
    mlp_parts = gather_parts(mlp_norm)
    mlp_all, up_rows, activated = mlp_up(mlp_parts, up_part, seq_count)
    saved = (
        first_all,
        triples,
        self_tokens,
        after_self,
        cross_norm,
        queries,
        cross_tokens,
        after_cross,
        mlp_all,
        up_rows,
        activated,
    )
    return (saved, square_parts, mlp_parts, mixed_rel)


def unspread_first(blocks, ready):
    own, first_mine, first_other, second_mine, second_other, corner_mine, corner_other = blocks
    from_corner, to_other = swap_core(corner_other), swap_core(second_mine)
    to_mine = swap_core(second_other)
    sums = [add_bf16(corner_mine, from_corner), add_bf16(first_other, to_other)]
    sums = gate(sums, ready)
    hops = [swap_by_core(sums[0], 2, 1), swap_by_core(sums[1], 1, 2)]
    return own, hops, [first_mine, to_mine], sums


def unspread_next(first, ready):
    own, hops, terms, _ = first
    passed, other = gate(hops, ready)
    return own, swap_by_core(add_bf16(*terms, passed), 1, 2), other


def unspread_last(scalars, second, ready):
    own, mine, other = second
    (mine,) = gate([mine], ready)
    return join_halves(scalars, own, mine, other)


def unspread_any(blocks):
    return add_bf16(blocks[0], *[swap_seq(m, j + 1) for j, m in enumerate(blocks[1:])])


def qkv_own(layer, qkv):
    return own_part(qkv[layer], 3, padded_width(qkv.shape[2] // (3 * lax.axis_size("seq"))))


def squares_own(layer, *stacks):
    padded = padded_width(stacks[0].shape[2] // lax.axis_size("seq"))
    return jnp.concatenate([own_part(m[layer], 1, padded) for m in stacks], axis=1)


def gather_rest(layer, up, down):
    s, seq_count, fsdp_count = lax.axis_index("seq"), lax.axis_size("seq"), lax.axis_size("fsdp")
    rows = down.shape[1] // seq_count
    return (
        gather_fsdp(own_part(up[layer], fsdp_count, up.shape[2] // (fsdp_count * seq_count))),
        gather_fsdp(lax.dynamic_slice_in_dim(down[layer], s * rows, rows, 0)),
    )


def sum_vectors(vectors):
    bits = 1
    while bits < lax.axis_size("seq"):
        vectors = vectors + swap_seq(vectors, bits)
        bits *= 2
    found, bits = vectors[None], 1
    while bits < lax.axis_size("fsdp"):
        found = jnp.concatenate([found, swap_fsdp(found, bits)], axis=0)
        bits *= 2
    return found


def body(
    latents,
    skip_input,
    text_tokens,
    text_lengths,
    condition,
    cotangent,
    mod_weight,
    norm_gains,
    qkv_weight,
    query_weight,
    text_kv_weight,
    self_out_weight,
    cross_out_weight,
    up_weight,
    down_weight,
    skip_gain,
    skip_weight,
):
    seq_count, fsdp_count = lax.axis_size("seq"), lax.axis_size("fsdp")
    s, f = lax.axis_index("seq"), lax.axis_index("fsdp")
    _, tok_rows, model_width = latents.shape
    width = model_width // seq_count
    shard_rows = mod_weight.shape[1]
    text_count = text_tokens.shape[1]
    padded = -(-text_count // 32) * 32
    text_rows = jnp.pad(text_tokens[0], ((0, padded - text_count), (0, 0)))
    scalars = jnp.stack(
        [*list_order(), *[s ^ j for j in range(seq_count)], f % 2, text_lengths[0]]
    ).astype(jnp.int32)

    gain_rows = jnp.concatenate(
        [norm_gains.reshape(-1, shard_rows), skip_gain.reshape(-1, shard_rows)], axis=0
    )
    small = jnp.concatenate(
        [
            condition.reshape(fsdp_count, 1, shard_rows),
            jnp.broadcast_to(gain_rows[None], (fsdp_count,) + gain_rows.shape),
        ],
        axis=1,
    ).astype(F32)
    latent_parts = gather_parts(latents[0])
    (small,) = gate([small], latent_parts[-2:])
    small = lax.all_to_all(small, "fsdp", 0, 0, tiled=True)
    cond_part = small[:, 0]
    gains = jnp.swapaxes(small[:, 1:7], 0, 1).reshape(2, 3, model_width)
    skip_gains = small[:, 7:].reshape(2, model_width)
    silu_part = jax.nn.silu(cond_part)
    shift_terms = jnp.einsum("br,lrd->bld", silu_part, mod_weight.astype(F32), precision=EXACT)
    padded_columns = padded_width(width)
    kv_both = gather_fsdp(
        jnp.concatenate([own_part(text_kv_weight[l], 2, padded_columns) for l in range(2)], axis=1)
    )
    pair_hops = gather_first(dot_nn(text_rows, kv_both).astype(BF16))
    pairs_all = gather_last(pair_hops)
    (shift_terms,) = gate([shift_terms], pair_hops[1:])
    shifts = jnp.sum(lax.all_to_all(shift_terms, "fsdp", 0, 0, tiled=True), axis=0)

    square_stacks = (self_out_weight, query_weight, cross_out_weight)
    rest_stacks = (up_weight, down_weight)
    head_size = model_width // H
    fours = seq_count == 4

    square_shard, qkv_shard = gate(
        [squares_own(0, *square_stacks), qkv_own(0, qkv_weight)], [kv_both] + latent_parts[-2:]
    )
    square_first, lead_first = gather_fsdp(square_shard), gather_fsdp(qkv_shard)
    up_first, down_first = gather_rest(0, *rest_stacks)
    spread_squares = spread_first(gate([square_first], [shifts])[0])
    (lead_first,) = gate([lead_first], [shifts])
    pairs_first, pairs_second = pairs_all, pairs_all
    saved_first, squares_first, mlp_parts, mixed_rel = layer_forward(
        latent_parts,
        latents[0],
        scalars,
        gains[0],
        shifts[0],
        pairs_first,
        (lead_first, spread_squares, up_first),
        False,
        (),
    )
    own, pieces = mlp_down(saved_first[10], down_first, seq_count)
    terms = scatter_last(own, scatter_first(pieces))

    (skip_matrix,) = gate(
        [gather_fsdp(own_part(skip_weight, 1, padded_width(width)))], mixed_rel[1:]
    )
    skip_parts = spread_last(spread_first(skip_matrix), mlp_parts[-2:], [own])
    square_second = gather_fsdp(squares_own(1, *square_stacks))
    lead_second = gather_fsdp(qkv_own(1, qkv_weight))
    (square_second,) = gate([square_second], terms[-2:])
    squares_second = spread_first(square_second)
    first_out, joined_norm, skip_out, second_norm = skip_forward(
        scalars,
        skip_parts,
        terms,
        saved_first[7],
        skip_input[0],
        skip_gains,
        gains[1],
        shifts[1],
        (square_second,),
    )

    up_second, down_second = gather_rest(1, *rest_stacks)
    out_hops = gather_first(gate([cotangent[0]], [skip_out])[0])
    saved_second, squares_second, mlp_parts, _ = layer_forward(
        gather_parts(second_norm),
        skip_out,
        scalars,
        gains[1],
        shifts[1],
        pairs_second,
        (lead_second, squares_second, up_second),
        True,
        (),
    )
    out_parts = gather_last(out_hops, [squares_second[-1]])
    out_all = stack_rows(out_parts, (mlp_parts[1],))

    held = {}

    def block_backward(rows, grad_out, saved, block, weights, early, hooks):
        lead_matrix, square_parts, pairs, up_part, down_part = weights
        grad_down = dot_tn(saved[10], early).astype(BF16) if early is not None else None
        found_all, grad_up_rows, own, pieces = mlp_backward(
            rows,
            saved[9],
            up_part,
            down_part,
            seq_count,
            hooks[0] + ((grad_down,) if early is not None else ()),
        )
        first = scatter_first(gate(pieces, hooks[3]) if hooks[3] else pieces)
        terms = scatter_last(own, first)
        held["hops"] = first[:2]
        if early is None:
            grad_down = dot_tn(saved[10], found_all).astype(BF16)
            (grad_down,) = gate([grad_down], first[:2])
        grad_up = dot_tn(saved[8], grad_up_rows).astype(BF16)
        (grad_up,) = gate([grad_up], first[:2])
        down_shard, up_shard = scatter_fsdp(grad_down), scatter_fsdp(grad_up)
        (
            grad_after_self,
            self_branch,
            query_branch,
            cross_branch,
            gain_grads,
            mixed_grads,
            own_pairs,
            pair_blocks,
        ) = middle_backward(
            block,
            scalars,
            square_parts,
            pairs,
            terms,
            grad_out,
            saved[7],
            saved[3],
            saved[5],
            gains[block],
            head_size,
            (grad_down, grad_up) + hooks[1](grad_up_rows, terms),
        )
        mixed_rel = exchange_rel(mixed_grads)
        pair_blocks = gate(pair_blocks, mixed_rel[1:])
        pair_terms = [swap_seq(m, j + 1) for j, m in enumerate(pair_blocks)]
        grad_triples, own, pieces = self_backward(
            saved[1],
            mixed_rel,
            lead_matrix,
            head_size,
            (down_shard,) + hooks[2](mixed_rel[1]),
        )
        pair_terms = gate(pair_terms, [grad_triples])
        first = scatter_first(gate(pieces, pair_terms))
        terms = scatter_last(own, first)
        grad_qkv = dot_tn(saved[0], grad_triples).astype(BF16)
        (grad_qkv,) = gate([grad_qkv], first[:2])
        held["last"] = first[:2]
        squares = outer(
            scalars,
            [saved[2], saved[4], saved[6]],
            [self_branch, query_branch, cross_branch],
            (grad_triples,),
        )
        squares = gate(squares, first[:2])
        pair_terms = gate(pair_terms, first[:2])
        grad_pairs = add_bf16(own_pairs, *pair_terms)
        kv_part = kv_both[:, 2 * block * padded_columns : 2 * (block + 1) * padded_columns]
        grad_text = dot_nt(grad_pairs, kv_part)
        kv_shard = scatter_fsdp(dot_tn(text_rows, grad_pairs))
        return (
            terms,
            grad_after_self,
            gain_grads,
            grad_text,
            squares,
            grad_qkv,
            grad_triples,
            (scatter_fsdp(grad_qkv), kv_shard, up_shard, down_shard),
        )

    def second_own(grad_up_rows, terms):
        own, pieces = mlp_down(saved_second[10], down_second, seq_count, (grad_up_rows,))
        pieces = gate(pieces, terms[-2:])
        held["own"], held["own_hops"] = own, scatter_first(pieces)
        return tuple(pieces)

    def second_sum(ready):
        held["ready"] = ready
        return tuple(held["own_hops"][:2])

    (
        terms,
        grad_after_self,
        gain_grads,
        text_second,
        squares,
        grad_qkv,
        grad_triples,
        (qkv_shard, kv_shard, up_shard, down_shard),
    ) = block_backward(
        [out_all],
        cotangent[0],
        saved_second,
        1,
        (lead_second, squares_second, pairs_second, up_second, down_second),
        out_all,
        ((), second_own, second_sum, ()),
    )
    skip_branch, grad_first_out, grad_skip, vectors, first_round = skip_backward(
        scalars,
        skip_parts,
        terms,
        skip_out,
        gains[1],
        grad_after_self,
        first_out,
        skip_input[0],
        skip_gains,
        (grad_qkv, up_shard),
    )
    vectors_second = jnp.concatenate([vectors[:2], gain_grads, vectors[2:]], axis=0)
    first_hops = gather_first(first_round)
    first_parts = gather_last(first_hops)
    if fours:
        squares = unspread_first(squares, first_parts[-2:])
    own_terms = scatter_last(held["own"], held["own_hops"], terms[-2:])
    output = close_forward(own_terms, saved_second[7])
    skip_outer = outer(scalars, [joined_norm], [skip_branch], tuple(first_hops[1:]))

    def entries(layer):
        qkv, square, kv, up, down = layer
        return (
            [
                (up, fsdp_count, 1, up.shape[1] // fsdp_count),
                (down, 0, 1, down.shape[1]),
            ],
            [(qkv, 3, 1, width), (square, 1, 3, width), (kv, 2, 1, width)],
        )

    early, _ = entries((qkv_shard, qkv_shard, kv_shard, up_shard, down_shard))

    def first_middle(grad_up_rows, terms):
        held["up"], held["terms"] = grad_up_rows, terms
        held["packed"] = pack([entry[0] for entry in early], (grad_up_rows,))
        held["early"] = gather_first(gate([held["packed"]], terms[-2:])[0])
        return (held["early"][0], kv_shard)

    def first_self(ready):
        if not fours:
            return (qkv_shard,)
        held["joined"] = unspread_last(scalars, unspread_next(squares, held["hops"]), [ready])
        return (qkv_shard, held["joined"], *held["early"][1:])

    (
        terms,
        grad_after_self,
        gain_grads,
        text_first,
        first_squares,
        grad_qkv,
        grad_triples,
        (first_qkv_shard, first_kv_shard, first_up_shard, first_down_shard),
    ) = block_backward(
        first_parts,
        grad_first_out,
        saved_first,
        0,
        (lead_first, squares_first, pairs_first, up_first, down_first),
        None,
        (
            (skip_outer[0], *own_terms[-2:]) + (tuple(squares[3]) if fours else ()),
            first_middle,
            first_self,
            squares[1] if fours else (),
        ),
    )
    if fours:
        outer_done = [first_squares[1]]
        joined = held["joined"]
        first_squares = unspread_first(first_squares, outer_done)
        skip_first = unspread_first(skip_outer, first_squares[3])
        first_squares = unspread_next(first_squares, terms[-2:])
        first_joined = unspread_last(scalars, first_squares, terms[-2:])
        skip_joined = unspread_last(
            scalars, unspread_next(skip_first, [first_squares[1]]), [first_joined]
        )
    else:
        joined, skip_joined = unspread_any(squares), unspread_any(skip_outer)
        first_joined = unspread_any(first_squares)
        outer_done = [joined]
    square_shard, skip_shard = scatter_fsdp(joined), scatter_fsdp(skip_joined)
    early, _ = entries(
        (first_qkv_shard, first_qkv_shard, first_kv_shard, first_up_shard, first_down_shard)
    )
    first_hops = gather_first(pack([entry[0] for entry in early], outer_done))
    grad_latents, vectors = open_backward(
        terms, latents[0], gains[0], grad_after_self, (grad_qkv, first_joined, *first_hops[1:])
    )
    vectors_first = jnp.concatenate([vectors, gain_grads], axis=0)
    first_layer = (
        first_qkv_shard,
        scatter_fsdp(first_joined),
        first_kv_shard,
        first_up_shard,
        first_down_shard,
    )

    early_done = settle(
        scalars,
        gather_last(held["early"], outer_done),
        plan_of(early),
        1,
        2,
        None,
    )
    _, late = entries((qkv_shard, square_shard, kv_shard, up_shard, down_shard))
    late_done = finish(scalars, late, 1, 2, None)
    early, late = entries(first_layer)
    grad_up, grad_down = settle(
        scalars, gather_last(first_hops), plan_of(early), 0, 2, early_done
    )
    grad_qkv, grad_self_out, grad_query, grad_cross_out, grad_kv = finish(
        scalars, late, 0, 2, late_done
    )
    (grad_skip_weight,) = finish(scalars, [(skip_shard, 1, 1, width)], 0, 1)

    sums = sum_vectors(jnp.concatenate([vectors_first, vectors_second], axis=0))
    first_sums, second_sums = sums[:, :4], sums[:, 4:]
    shift_grads = jnp.stack([first_sums[:, 0], second_sums[:, 0]], axis=1)
    gain_sums = jnp.stack([first_sums[:, 1:4].sum(axis=0), second_sums[:, 1:4].sum(axis=0)])
    grad_norm_gains = lax.dynamic_slice_in_dim(gain_sums, f * shard_rows, shard_rows, 2)
    grad_skip_gain = lax.dynamic_slice_in_dim(
        second_sums[:, 4:].sum(axis=0).reshape(-1), f * skip_gain.shape[0], skip_gain.shape[0], 0
    )
    turned = jnp.stack(
        [lax.dynamic_index_in_dim(silu_part, f ^ j, 0, False) for j in range(fsdp_count)]
    )
    grad_mod = jnp.einsum("br,bld->lrd", turned, shift_grads, precision=EXACT)
    grad_silu = jnp.einsum("bld,lrd->br", shift_grads, mod_weight.astype(F32), precision=EXACT)
    grad_silu = jnp.stack(
        [lax.dynamic_index_in_dim(grad_silu, f ^ j, 0, False) for j in range(fsdp_count)]
    )
    _, silu_pull = jax.vjp(jax.nn.silu, cond_part)
    grad_cond_part = silu_pull(grad_silu)[0]
    grad_condition = lax.all_to_all(grad_cond_part, "fsdp", 0, 0, tiled=True).reshape(1, -1)

    text_sum, bits = text_first + text_second, 1
    while bits < seq_count:
        text_sum = text_sum + swap_seq(text_sum.astype(BF16), bits).astype(F32)
        bits *= 2
    return (
        output[None],
        grad_latents[None],
        grad_skip[None],
        text_sum[None, :text_count],
        grad_condition,
        grad_mod,
        grad_norm_gains,
        grad_qkv,
        grad_query,
        grad_kv,
        grad_self_out,
        grad_cross_out,
        grad_up,
        grad_down,
        grad_skip_gain,
        grad_skip_weight[0],
    )


def solution(mesh):
    in_specs = (
        P("fsdp", "seq", None),
        P("fsdp", "seq", None),
        P("fsdp", None, None),
        P("fsdp"),
        P("fsdp", None),
        P("fsdp", "seq", None),
        P(None, "fsdp", None),
        P(None, None, "fsdp"),
        P(None, "fsdp", None),
        P(None, "fsdp", None),
        P(None, "fsdp", None),
        P(None, "fsdp", None),
        P(None, "fsdp", None),
        P(None, "fsdp", None),
        P(None, "fsdp", None),
        P("fsdp"),
        P("fsdp", None),
    )
    out_specs = (
        P("fsdp", "seq", None),
        P("fsdp", "seq", None),
        P("fsdp", "seq", None),
        P("fsdp", None, None),
        P("fsdp", None),
        P(None, "fsdp", None),
        P(None, None, "fsdp"),
        P(None, "fsdp", None),
        P(None, "fsdp", None),
        P(None, "fsdp", None),
        P(None, "fsdp", None),
        P(None, "fsdp", None),
        P(None, "fsdp", None),
        P(None, "fsdp", None),
        P("fsdp"),
        P("fsdp", None),
    )
    return jax.shard_map(body, mesh=mesh, in_specs=in_specs, out_specs=out_specs, check_vma=False)
```

```python
import functools
import math

import jax
import jax.numpy as jnp
from jax import lax
from jax.experimental import pallas as pl
from jax.experimental.pallas import tpu as pltpu
from jax.sharding import PartitionSpec as P

H = 16
NORM_EPSILON = 1e-06
EXACT = lax.Precision.HIGHEST
BF16 = jnp.bfloat16
F32 = jnp.float32
LOG2_E = 1.4426950408889634
GELU_SCALE = math.sqrt(2.0 / math.pi)
VMEM_LIMIT = 56 * 1024 * 1024


def dot_nn(a, b):
    return lax.dot_general(a, b, (((1,), (0,)), ((), ())), preferred_element_type=F32)


def dot_nt(a, b):
    return lax.dot_general(a, b, (((1,), (1,)), ((), ())), preferred_element_type=F32)


def dot_tn(a, b):
    return lax.dot_general(a, b, (((0,), (0,)), ((), ())), preferred_element_type=F32)


def padded_width(width):
    return -(-width // 128) * 128


def call(kernel, outs, scratch, micros, *operands, scalars=None, deps=(), outside=()):
    specs = [
        pl.BlockSpec(memory_space=pl.ANY if i in outside else pltpu.VMEM)
        for i in range(len(operands))
    ]
    if scalars is not None:
        specs = [pl.BlockSpec(memory_space=pltpu.SMEM)] + specs
        operands = (scalars,) + tuple(operands)
    used, held = len(operands), len(deps)

    def run(*refs):
        kernel(*refs[:used], *refs[used + held :])

    return pl.pallas_call(
        run,
        name=getattr(kernel, "func", kernel).__name__,
        out_shape=tuple(jax.ShapeDtypeStruct(s, d) for s, d in outs),
        in_specs=specs + [pl.BlockSpec(memory_space=pl.ANY)] * held,
        out_specs=tuple([pl.BlockSpec(memory_space=pltpu.VMEM)] * len(outs)),
        scratch_shapes=scratch,
        compiler_params=pltpu.CompilerParams(vmem_limit_bytes=VMEM_LIMIT),
        cost_estimate=pl.CostEstimate(
            flops=int(micros * 1000), bytes_accessed=1000, transcendentals=0
        ),
    )(*operands, *deps)


def gate_kernel(*refs):
    del refs


def gate(values, deps):
    values, deps = list(values), list(deps)
    return list(
        pl.pallas_call(
            gate_kernel,
            out_shape=tuple(jax.ShapeDtypeStruct(m.shape, m.dtype) for m in values),
            in_specs=[pl.BlockSpec(memory_space=pl.ANY)] * (len(values) + len(deps)),
            out_specs=tuple([pl.BlockSpec(memory_space=pl.ANY)] * len(values)),
            input_output_aliases={i: i for i in range(len(values))},
            cost_estimate=pl.CostEstimate(flops=1000, bytes_accessed=1000, transcendentals=0),
        )(*values, *deps)
    )


def cut_of(rows):
    return rows // 32 * 16


def piece_shapes(count, rows, columns):
    if count != 4:
        return [((rows, columns), BF16)] * (count - 1)
    cut = cut_of(rows)
    return [((m, columns), BF16) for m in (2 * cut, 2 * (rows - cut), rows - cut, cut)]


def put_pieces(refs, count, block, values):
    if count != 4:
        refs[block - 1][...] = values.astype(BF16)
        return
    to_x, to_y, x_bottom, y_top = refs
    rows = values.shape[0]
    cut = cut_of(rows)
    top, bottom = values[:cut].astype(BF16), values[cut:].astype(BF16)
    if block == 1:
        to_x[cut:, :] = top
        x_bottom[...] = bottom
    elif block == 2:
        y_top[...] = top
        to_y[rows - cut :, :] = bottom
    else:
        to_x[:cut, :] = top
        to_y[: rows - cut, :] = bottom


def add_terms(count, refs):
    total = refs[0][...].astype(F32)
    if count != 4:
        for ref in refs[1:]:
            total = total + ref[...].astype(F32)
        return total
    from_x, from_y, x_bottom, y_top = [ref[...] for ref in refs[1:]]
    cut, rest = y_top.shape[0], x_bottom.shape[0]
    by_x = jnp.concatenate([from_x[cut:], x_bottom], axis=0)
    by_y = jnp.concatenate([y_top, from_y[rest:]], axis=0)
    return total + by_x.astype(F32) + by_y.astype(F32)


def norm_stats(values):
    mean = jnp.mean(values, axis=1, keepdims=True)
    centered = values - mean
    var = jnp.mean(centered * centered, axis=1, keepdims=True)
    scale = lax.rsqrt(var + NORM_EPSILON)
    return centered * scale, scale


def norm_back(values, gain, grad):
    unit, scale = norm_stats(values)
    grad_unit = grad * gain
    inner = jnp.mean(grad_unit * unit, axis=1, keepdims=True)
    grad_values = scale * (grad_unit - jnp.mean(grad_unit, axis=1, keepdims=True) - unit * inner)
    return grad_values, jnp.sum(grad * unit, axis=0, keepdims=True)


def self_forward_kernel(count, parts, head_size, normed, *refs):
    part_refs, refs = refs[:parts], refs[parts:]
    weight_ref, gains_ref, shift_ref = refs[:3]
    rows_ref, triples_ref = refs[3:5]
    mixed_refs, (held_ref, done) = refs[5:-2], refs[-2:]
    copy = pltpu.make_async_copy(weight_ref.at[:, : held_ref.shape[1]], held_ref, done)
    copy.start()
    stride = held_ref.shape[1] // 3
    rows, width = mixed_refs[0].shape
    factor = LOG2_E / math.sqrt(head_size)
    start = 0
    for ref in part_refs:
        values = ref[...]
        if not normed:
            unit, _ = norm_stats(values.astype(F32))
            values = (unit * gains_ref[0:1, :] + shift_ref[...]).astype(BF16)
        rows_ref[start : start + ref.shape[0], :] = values
        start += ref.shape[0]
    copy.wait()
    for j in range(count):
        at = slice(j * rows, (j + 1) * rows)
        triples_ref[at, :] = dot_nn(rows_ref[at, :], held_ref[...]).astype(BF16)
    for j in range(count):
        at = slice(j * rows, (j + 1) * rows)
        for h in range(width // head_size):
            low = h * head_size
            q = triples_ref[at, low : low + head_size]
            k = triples_ref[:, stride + low : stride + low + head_size]
            v = triples_ref[:, 2 * stride + low : 2 * stride + low + head_size]
            scores = dot_nt(q, k)
            top = jnp.max(scores, axis=1, keepdims=True)
            weights = jnp.exp2((scores - top) * factor)
            total = jnp.sum(weights, axis=1, keepdims=True)
            mixed = dot_nn(weights.astype(BF16), v) * (1.0 / total)
            mixed_refs[j][:, low : low + head_size] = mixed.astype(BF16)


def self_forward(parts, weight, gains, shift, head_size, count, width, normed, deps=()):
    total = sum(m.shape[0] for m in parts)
    columns = parts[0].shape[1]
    held = (columns, 3 * padded_width(width))
    found = call(
        functools.partial(self_forward_kernel, count, len(parts), head_size, normed),
        [((total, columns), BF16), ((total, held[1]), BF16)]
        + [((total // count, width), BF16)] * count,
        [pltpu.VMEM(held, BF16), pltpu.SemaphoreType.DMA],
        24,
        *parts,
        weight,
        gains,
        shift[None],
        deps=deps,
        outside=(len(parts),),
    )
    return found[0], found[1], list(found[2:])


def attention_back(q, k, v, grad, valid, head_size):
    factor = LOG2_E / math.sqrt(head_size)
    scores = dot_nt(k, q)
    if valid is not None:
        scores = jnp.where(valid, scores, -1e30)
    top = jnp.max(scores, axis=0, keepdims=True)
    weights = jnp.exp2((scores - top) * factor)
    weights = weights * (1.0 / jnp.sum(weights, axis=0, keepdims=True))
    grad_weights = dot_nt(v, grad)
    delta = jnp.sum(grad_weights * weights, axis=0, keepdims=True)
    grad_scores = (weights * (grad_weights - delta)).astype(BF16)
    scale = 1.0 / math.sqrt(head_size)
    return (
        dot_tn(grad_scores, k) * scale,
        dot_nn(grad_scores, q) * scale,
        dot_nn(weights.astype(BF16), grad),
    )


def self_backward_kernel(count, head_size, step, triples_ref, *refs):
    grad_refs, (weight_ref, out_ref, own_ref) = refs[:count], refs[count : count + 3]
    piece_refs, (keys_ref, values_ref, held_ref, done) = refs[count + 3 : -4], refs[-4:]
    copy = pltpu.make_async_copy(weight_ref.at[:, : held_ref.shape[1]], held_ref, done)
    copy.start()
    total = triples_ref.shape[0]
    rows, width = grad_refs[0].shape
    stride = held_ref.shape[1] // 3
    for h in range(width // head_size):
        low = h * head_size
        k = triples_ref[:, stride + low : stride + low + head_size]
        v = triples_ref[:, 2 * stride + low : 2 * stride + low + head_size]
        for i in range(total // step):
            at = slice(i * step, (i + 1) * step)
            inside = (i * step) % rows
            q = triples_ref[at, low : low + head_size]
            grad = grad_refs[i * step // rows][inside : inside + step, low : low + head_size]
            grad_q, grad_k, grad_v = attention_back(q, k, v, grad, None, head_size)
            out_ref[at, low : low + head_size] = grad_q.astype(BF16)
            if i == 0:
                keys_ref[...] = grad_k
                values_ref[...] = grad_v
            else:
                keys_ref[...] += grad_k
                values_ref[...] += grad_v
        out_ref[:, stride + low : stride + low + head_size] = keys_ref[...].astype(BF16)
        out_ref[:, 2 * stride + low : 2 * stride + low + head_size] = values_ref[...].astype(BF16)
    if stride > width:
        for g in range(3):
            out_ref[:, g * stride + width : (g + 1) * stride] = jnp.zeros((total, stride - width), BF16)
    copy.wait()
    for j in range(count):
        found = dot_nt(out_ref[j * rows : (j + 1) * rows, :], held_ref[...])
        if j == 0:
            own_ref[...] = found
        else:
            put_pieces(piece_refs, count, j, found)


def self_backward(triples, grads, weight, head_size, deps=()):
    count = len(grads)
    total, rows, columns = triples.shape[0], grads[0].shape[0], weight.shape[0]
    step = min(256, rows)
    found = call(
        functools.partial(self_backward_kernel, count, head_size, step),
        [(triples.shape, BF16), ((rows, columns), F32)] + piece_shapes(count, rows, columns),
        [
            pltpu.VMEM((total, head_size), F32),
            pltpu.VMEM((total, head_size), F32),
            pltpu.VMEM((columns, triples.shape[1]), BF16),
            pltpu.SemaphoreType.DMA,
        ],
        32,
        triples,
        *grads,
        weight,
        deps=deps,
        outside=(1 + count,),
    )
    return found[0], found[1], list(found[2:])


def fill_corner(count, matrix_refs, scalars_ref, corner_ref):
    if len(matrix_refs) == count:
        return list(matrix_refs)
    odd = scalars_ref[2 * count]
    half = matrix_refs[-1].shape[0]
    corner_ref[pl.ds(pl.multiple_of(odd * half, half), half), :] = matrix_refs[-2][...]
    corner_ref[pl.ds(pl.multiple_of((1 - odd) * half, half), half), :] = matrix_refs[-1][...]
    return list(matrix_refs[:-2]) + [corner_ref]


def corner_scratch(count, matrices):
    rows, columns = matrices[0].shape
    return pltpu.VMEM((rows, columns) if len(matrices) > count else (16, 128), BF16)


def fill_pairs(count, block, pair_refs, pairs_ref):
    padded, columns = pairs_ref.shape[1:]
    place = 0
    for ref in pair_refs:
        j, low = divmod(place, padded)
        pairs_ref[j, low : low + ref.shape[0], :] = ref[:, block * columns : (block + 1) * columns]
        place += ref.shape[0]


def middle_forward_kernel(block, count, matrix_parts, pair_parts, head_size, scalars_ref, *refs):
    mixed_refs, refs = refs[:count], refs[count:]
    matrix_refs, refs = refs[:matrix_parts], refs[matrix_parts:]
    pair_refs, refs = refs[:pair_parts], refs[pair_parts:]
    hidden_ref, gains_ref = refs[:2]
    (self_ref, after_self_ref, norm_ref, queries_ref, cross_ref, after_cross_ref) = refs[2:8]
    mlp_ref = refs[8]
    wide_ref, narrow_ref, corner_ref, pairs_ref = refs[-4:]
    width = mixed_refs[0].shape[1]
    stride = matrix_refs[0].shape[1] // 3
    matrices = fill_corner(count, matrix_refs, scalars_ref, corner_ref)
    fill_pairs(count, block, pair_refs, pairs_ref)
    order = [scalars_ref[i] for i in range(count)]
    relative = [scalars_ref[count + j] for j in range(count)]
    length = scalars_ref[2 * count + 1]
    spans = [slice(a * width, (a + 1) * width) for a in range(count)]

    for j in range(count):
        narrow_ref[relative[j]] = mixed_refs[j][...]
    for a in range(count):
        self_ref[:, spans[a]] = narrow_ref[a]
    tokens = self_ref[...]
    for i in range(count):
        wide_ref[order[i]] = dot_nn(tokens, matrices[i][:, :width])
    for a in range(count):
        after_self_ref[:, spans[a]] = hidden_ref[:, spans[a]].astype(F32) + wide_ref[a]
    normed = (norm_stats(after_self_ref[...])[0] * gains_ref[1:2, :]).astype(BF16)
    norm_ref[...] = normed
    for i in range(count):
        found = dot_nn(normed, matrices[i][:, stride : stride + width])
        queries_ref[order[i] ^ relative[0]] = found.astype(BF16)

    factor = LOG2_E / math.sqrt(head_size)
    keys_rows = pairs_ref.shape[1]
    valid = lax.broadcasted_iota(jnp.int32, (1, keys_rows), 1) < length
    pair_stride = pairs_ref.shape[2] // 2
    for j in range(count):
        for h in range(width // head_size):
            at = slice(h * head_size, (h + 1) * head_size)
            values_at = slice(pair_stride + h * head_size, pair_stride + (h + 1) * head_size)
            scores = dot_nt(queries_ref[j, :, at], pairs_ref[j, :, at])
            scores = jnp.where(valid, scores, -1e30)
            top = jnp.max(scores, axis=1, keepdims=True)
            weights = jnp.exp2((scores - top) * factor)
            total = jnp.sum(weights, axis=1, keepdims=True)
            mixed = dot_nn(weights.astype(BF16), pairs_ref[j, :, values_at]) * (1.0 / total)
            narrow_ref[relative[j], :, at] = mixed.astype(BF16)
    for a in range(count):
        cross_ref[:, spans[a]] = narrow_ref[a]
    tokens = cross_ref[...]
    for i in range(count):
        wide_ref[order[i]] = dot_nn(tokens, matrices[i][:, 2 * stride : 2 * stride + width])
    for a in range(count):
        after_cross_ref[:, spans[a]] = after_self_ref[:, spans[a]] + wide_ref[a]
    mlp_ref[...] = (norm_stats(after_cross_ref[...])[0] * gains_ref[2:3, :]).astype(BF16)


def pairs_scratch(count, pairs):
    return pltpu.VMEM(
        (count, sum(m.shape[0] for m in pairs) // count, pairs[0].shape[1] // 2), BF16
    )


def middle_forward(block, scalars, mixed, matrices, pairs, hidden, gains, head_size, deps=()):
    count = len(mixed)
    rows, columns = hidden.shape
    width = columns // count
    return call(
        functools.partial(
            middle_forward_kernel, block, count, len(matrices), len(pairs), head_size
        ),
        [
            ((rows, columns), BF16),
            ((rows, columns), F32),
            ((rows, columns), BF16),
            ((count, rows, width), BF16),
            ((rows, columns), BF16),
            ((rows, columns), F32),
            ((rows, columns), BF16),
        ],
        [
            pltpu.VMEM((count, rows, width), F32),
            pltpu.VMEM((count, rows, width), BF16),
            corner_scratch(count, matrices),
            pairs_scratch(count, pairs),
        ],
        23,
        *mixed,
        *matrices,
        *pairs,
        hidden,
        gains,
        scalars=scalars,
        deps=deps,
    )


def middle_backward_kernel(block, count, matrix_parts, pair_parts, terms, head_size, scalars_ref, *refs):
    matrix_refs, refs = refs[:matrix_parts], refs[matrix_parts:]
    pair_refs, refs = refs[:pair_parts], refs[pair_parts:]
    term_refs, refs = refs[:terms], refs[terms:]
    grad_out_ref, after_cross_ref, after_self_ref, queries_ref, gains_ref = refs[:5]
    out_ref, self_branch_ref, query_branch_ref, cross_branch_ref, gain_ref = refs[5:10]
    mixed_grad_refs, refs = refs[10 : 10 + count], refs[10 + count :]
    own_pairs_ref, pair_grad_refs = refs[0], refs[1:-6]
    wide_ref, narrow_ref, query_ref, corner_ref, pairs_ref, pair_total_ref = refs[-6:]
    width = queries_ref.shape[2]
    stride = matrix_refs[0].shape[1] // 3
    matrices = fill_corner(count, matrix_refs, scalars_ref, corner_ref)
    fill_pairs(count, block, pair_refs, pairs_ref)
    order = [scalars_ref[i] for i in range(count)]
    relative = [scalars_ref[count + j] for j in range(count)]
    length = scalars_ref[2 * count + 1]
    spans = [slice(a * width, (a + 1) * width) for a in range(count)]

    def back(branch_ref, group):
        columns = slice(group * stride, group * stride + width)
        total = dot_nt(branch_ref[0], matrices[0][:, columns])
        for i in range(1, count):
            total = total + dot_nt(branch_ref[i], matrices[i][:, columns])
        return total

    def divide(values):
        for a in range(count):
            narrow_ref[a] = values[:, spans[a]].astype(BF16)

    grad, grad_gain = norm_back(
        after_cross_ref[...], gains_ref[2:3, :], add_terms(count, term_refs)
    )
    gain_ref[1:2, :] = grad_gain
    wide_ref[...] = grad + grad_out_ref[...].astype(F32)
    divide(wide_ref[...])
    for i in range(count):
        cross_branch_ref[i] = narrow_ref[order[i]]
    divide(back(cross_branch_ref, 2))

    keys_rows = pairs_ref.shape[1]
    valid = lax.broadcasted_iota(jnp.int32, (keys_rows, 1), 0) < length
    pair_stride = pairs_ref.shape[2] // 2
    if pair_stride > width:
        for g in range(2):
            pair_total_ref[:, g * pair_stride + width : (g + 1) * pair_stride] = jnp.zeros(
                (keys_rows, pair_stride - width), F32
            )
    for j in range(count):
        for h in range(width // head_size):
            at = slice(h * head_size, (h + 1) * head_size)
            values_at = slice(pair_stride + h * head_size, pair_stride + (h + 1) * head_size)
            grad_q, grad_k, grad_v = attention_back(
                queries_ref[j, :, at],
                pairs_ref[j, :, at],
                pairs_ref[j, :, values_at],
                narrow_ref[relative[j], :, at],
                valid,
                head_size,
            )
            query_ref[j, :, at] = grad_q.astype(BF16)
            pair_total_ref[:, at] = grad_k
            pair_total_ref[:, values_at] = grad_v
        if j == 0:
            own_pairs_ref[...] = pair_total_ref[...]
        else:
            pair_grad_refs[j - 1][...] = pair_total_ref[...].astype(BF16)
    for i in range(count):
        query_branch_ref[i] = query_ref[order[i] ^ relative[0]]
    grad, grad_gain = norm_back(after_self_ref[...], gains_ref[1:2, :], back(query_branch_ref, 1))
    gain_ref[0:1, :] = grad_gain
    out_ref[...] = grad + wide_ref[...]
    divide(out_ref[...])
    for i in range(count):
        self_branch_ref[i] = narrow_ref[order[i]]
    divide(back(self_branch_ref, 0))
    for j in range(count):
        mixed_grad_refs[j][...] = narrow_ref[relative[j]]


def middle_backward(
    block, scalars, matrices, pairs, terms, grad_out, after_cross, after_self, queries, gains, head_size, deps=()
):
    count, rows, width = queries.shape
    columns = count * width
    branch = ((count, rows, width), BF16)
    text = pairs_scratch(count, pairs)
    keys_rows, pair_columns = text.shape[1:]
    found = call(
        functools.partial(
            middle_backward_kernel, block, count, len(matrices), len(pairs), len(terms), head_size
        ),
        [((rows, columns), F32), branch, branch, branch, ((2, columns), F32)]
        + [((rows, width), BF16)] * count
        + [((keys_rows, pair_columns), F32)]
        + [((keys_rows, pair_columns), BF16)] * (count - 1),
        [
            pltpu.VMEM((rows, columns), F32),
            pltpu.VMEM((count, rows, width), BF16),
            pltpu.VMEM((count, rows, width), BF16),
            corner_scratch(count, matrices),
            text,
            pltpu.VMEM((keys_rows, pair_columns), F32),
        ],
        37,
        *matrices,
        *pairs,
        *terms,
        grad_out,
        after_cross,
        after_self,
        queries,
        gains,
        scalars=scalars,
        deps=deps,
    )
    found = list(found)
    return found[:5] + [found[5 : 5 + count], found[5 + count], found[6 + count :]]


def mlp_up_kernel(count, parts, *refs):
    part_refs, (up_ref, rows_ref, up_rows_ref, activated_ref) = refs[:parts], refs[parts:]
    start = 0
    for ref in part_refs:
        rows_ref[start : start + ref.shape[0], :] = ref[...]
        start += ref.shape[0]
    rows = start // count
    for j in range(count):
        at = slice(j * rows, (j + 1) * rows)
        values = dot_nn(rows_ref[at, :], up_ref[...])
        up_rows_ref[at, :] = values
        inner = GELU_SCALE * (values + 0.044715 * (values * values * values))
        activated_ref[at, :] = (0.5 * values * (1.0 + jnp.tanh(inner))).astype(BF16)


def mlp_up(parts, up, count, deps=()):
    total, columns, hidden = sum(m.shape[0] for m in parts), up.shape[0], up.shape[1]
    return call(
        functools.partial(mlp_up_kernel, count, len(parts)),
        [((total, columns), BF16), ((total, hidden), F32), ((total, hidden), BF16)],
        [],
        15,
        *parts,
        up,
        deps=deps,
    )


def mlp_down_kernel(count, activated_ref, down_ref, own_ref, *piece_refs):
    rows = own_ref.shape[0]
    for j in range(count - 1, -1, -1):
        found = dot_nn(activated_ref[j * rows : (j + 1) * rows, :], down_ref[...])
        if j == 0:
            own_ref[...] = found
        else:
            put_pieces(piece_refs, count, j, found)


def mlp_down(activated, down, count, deps=()):
    rows, columns = activated.shape[0] // count, down.shape[1]
    found = call(
        functools.partial(mlp_down_kernel, count),
        [((rows, columns), F32)] + piece_shapes(count, rows, columns),
        [],
        11,
        activated,
        down,
        deps=deps,
    )
    return found[0], list(found[1:])


def stack_kernel(*refs):
    start = 0
    for ref in refs[:-1]:
        refs[-1][start : start + ref.shape[0], :] = ref[...]
        start += ref.shape[0]


def stack_rows(parts, deps=()):
    shape = (sum(m.shape[0] for m in parts), parts[0].shape[1])
    return call(stack_kernel, [(shape, parts[0].dtype)], [], 3, *parts, deps=deps)[0]


def mlp_backward_kernel(count, parts, *refs):
    part_refs, refs = refs[:parts], refs[parts:]
    up_rows_ref, up_ref, down_ref, rows_ref, grad_up_ref, own_ref = refs[:6]
    piece_refs = refs[6:]
    start = 0
    for ref in part_refs:
        rows_ref[start : start + ref.shape[0], :] = ref[...]
        start += ref.shape[0]
    rows = start // count
    for j in range(count - 1, -1, -1):
        at = slice(j * rows, (j + 1) * rows)
        grad = dot_nt(rows_ref[at, :], down_ref[...])
        values = up_rows_ref[at, :]
        square = values * values
        bent = jnp.tanh(GELU_SCALE * (values + 0.044715 * (values * square)))
        slope = 0.5 * (1.0 + bent) + 0.5 * values * (1.0 - bent * bent) * (
            GELU_SCALE * (1.0 + 3.0 * 0.044715 * square)
        )
        grad_up_ref[at, :] = (grad * slope).astype(BF16)
        found = dot_nt(grad_up_ref[at, :], up_ref[...])
        if j == 0:
            own_ref[...] = found
        else:
            put_pieces(piece_refs, count, j, found)


def mlp_backward(parts, up_rows, up, down, count, deps=()):
    total, columns, hidden = sum(m.shape[0] for m in parts), up.shape[0], up.shape[1]
    rows = total // count
    found = call(
        functools.partial(mlp_backward_kernel, count, len(parts)),
        [((total, columns), BF16), ((total, hidden), BF16), ((rows, columns), F32)]
        + piece_shapes(count, rows, columns),
        [],
        22,
        *parts,
        up_rows,
        up,
        down,
        deps=deps,
    )
    return list(found[:3]) + [list(found[3:])]


def outer_kernel(count, groups, half, scalars_ref, *refs):
    rows_refs, branch_refs, refs = refs[:groups], refs[groups : 2 * groups], refs[2 * groups :]
    out_refs, turned_ref = refs[:-1], refs[-1]
    width = branch_refs[0].shape[2]
    stride = padded_width(width)
    odd = scalars_ref[2 * count]
    for g in range(groups):
        at = slice(g * stride, g * stride + width)
        turned_ref[...] = rows_refs[g][...].T
        out_refs[0][:, at] = dot_nn(turned_ref[...], branch_refs[g][0]).astype(BF16)
        for i in range(1, count):
            if not half:
                out_refs[i][:, at] = dot_nn(turned_ref[...], branch_refs[g][i]).astype(BF16)
                continue
            for k in range(2):
                low = pl.multiple_of((odd if k == 0 else 1 - odd) * half, half)
                found = dot_nn(turned_ref[pl.ds(low, half), :], branch_refs[g][i])
                out_refs[2 * i - 1 + k][:, at] = found.astype(BF16)
    if stride > width:
        for ref in out_refs:
            for g in range(groups):
                ref[:, g * stride + width : (g + 1) * stride] = jnp.zeros(
                    (ref.shape[0], stride - width), BF16
                )


def outer(scalars, rows, branches, deps=()):
    count, tokens, width = branches[0].shape
    groups, columns = len(rows), rows[0].shape[1]
    stride = padded_width(width)
    half = columns // 2 if count == 4 else 0
    shapes = [((columns, groups * stride), BF16)]
    if half:
        shapes += [((half, groups * stride), BF16)] * (2 * (count - 1))
    else:
        shapes = shapes * count
    return list(
        call(
            functools.partial(outer_kernel, count, groups, half),
            shapes,
            [pltpu.VMEM((columns, tokens), BF16)],
            3.5 * groups,
            *rows,
            *branches,
            scalars=scalars,
            deps=deps,
        )
    )


def join_kernel(count, scalars_ref, own_ref, mine_ref, other_ref, out_ref):
    odd = scalars_ref[2 * count]
    half = mine_ref.shape[0]
    for ref, place in ((mine_ref, odd), (other_ref, 1 - odd)):
        at = pl.ds(pl.multiple_of(place * half, half), half)
        out_ref[at, :] = (own_ref[at, :].astype(F32) + ref[...].astype(F32)).astype(BF16)


def join_halves(scalars, own, mine, other):
    count = lax.axis_size("seq")
    (found,) = call(
        functools.partial(join_kernel, count),
        [(own.shape, BF16)],
        [],
        4,
        own,
        mine,
        other,
        scalars=scalars,
    )
    return found


def joined_stats(first, second):
    count = first.shape[1] + second.shape[1]
    mean = (jnp.sum(first, axis=1, keepdims=True) + jnp.sum(second, axis=1, keepdims=True)) / count
    first, second = first - mean, second - mean
    var = (
        jnp.sum(first * first, axis=1, keepdims=True)
        + jnp.sum(second * second, axis=1, keepdims=True)
    ) / count
    scale = lax.rsqrt(var + NORM_EPSILON)
    return first * scale, second * scale, scale


def skip_forward_kernel(count, matrix_parts, terms, scalars_ref, *refs):
    matrix_refs, refs = refs[:matrix_parts], refs[matrix_parts:]
    term_refs, refs = refs[:terms], refs[terms:]
    residual_ref, second_ref, gains_ref, next_ref, shift_ref = refs[:5]
    first_ref, joined_ref, out_ref, norm_ref, wide_ref, corner_ref = refs[5:]
    rows, columns = first_ref.shape
    width = columns // count
    matrices = fill_corner(count, matrix_refs, scalars_ref, corner_ref)
    first_ref[...] = residual_ref[...] + add_terms(count, term_refs)
    first, second, _ = joined_stats(first_ref[...], second_ref[...].astype(F32))
    joined_ref[:, :columns] = (first * gains_ref[0:1, :]).astype(BF16)
    joined_ref[:, columns:] = (second * gains_ref[1:2, :]).astype(BF16)
    joined = joined_ref[...]
    for i in range(count):
        wide_ref[scalars_ref[i]] = dot_nn(joined, matrices[i][:, :width])
    for a in range(count):
        out_ref[:, a * width : (a + 1) * width] = wide_ref[a]
    normed = norm_stats(out_ref[...])[0] * next_ref[0:1, :] + shift_ref[...]
    norm_ref[...] = normed.astype(BF16)


def skip_forward(scalars, matrices, terms, residual, second, gains, next_gains, shift, deps=()):
    rows, columns = residual.shape
    count = lax.axis_size("seq")
    return call(
        functools.partial(skip_forward_kernel, count, len(matrices), len(terms)),
        [
            ((rows, columns), F32),
            ((rows, 2 * columns), BF16),
            ((rows, columns), F32),
            ((rows, columns), BF16),
        ],
        [pltpu.VMEM((count, rows, columns // count), F32), corner_scratch(count, matrices)],
        11,
        *matrices,
        *terms,
        residual,
        second,
        gains,
        next_gains,
        shift[None],
        scalars=scalars,
        deps=deps,
    )


def skip_backward_kernel(count, matrix_parts, terms, scalars_ref, *refs):
    matrix_refs, refs = refs[:matrix_parts], refs[matrix_parts:]
    term_refs, refs = refs[:terms], refs[terms:]
    hidden_ref, next_ref, residual_ref, first_ref, second_ref, gains_ref = refs[:6]
    branch_ref, grad_first_ref, grad_second_ref, vectors_ref, round_ref = refs[6:11]
    narrow_ref, corner_ref = refs[11:]
    rows, columns = first_ref.shape
    width = columns // count
    matrices = fill_corner(count, matrix_refs, scalars_ref, corner_ref)
    grad_norm = add_terms(count, term_refs)
    vectors_ref[0:1, :] = jnp.sum(grad_norm, axis=0, keepdims=True)
    grad, grad_gain = norm_back(hidden_ref[...], next_ref[0:1, :], grad_norm)
    vectors_ref[1:2, :] = grad_gain
    grad = grad + residual_ref[...]
    for a in range(count):
        narrow_ref[a] = grad[:, a * width : (a + 1) * width].astype(BF16)
    for i in range(count):
        branch_ref[i] = narrow_ref[scalars_ref[i]]

    def back(at):
        total = dot_nt(branch_ref[0], matrices[0][at, :width])
        for i in range(1, count):
            total = total + dot_nt(branch_ref[i], matrices[i][at, :width])
        return total

    grad_first_ref[...] = back(slice(0, columns))
    grad_second_ref[...] = back(slice(columns, 2 * columns))
    first, second, scale = joined_stats(first_ref[...], second_ref[...].astype(F32))
    vectors_ref[2:3, :] = jnp.sum(grad_first_ref[...] * first, axis=0, keepdims=True)
    vectors_ref[3:4, :] = jnp.sum(grad_second_ref[...] * second, axis=0, keepdims=True)
    grad_first = grad_first_ref[...] * gains_ref[0:1, :]
    grad_second = grad_second_ref[...] * gains_ref[1:2, :]
    mean = (
        jnp.sum(grad_first, axis=1, keepdims=True) + jnp.sum(grad_second, axis=1, keepdims=True)
    ) / (2 * columns)
    inner = (
        jnp.sum(grad_first * first, axis=1, keepdims=True)
        + jnp.sum(grad_second * second, axis=1, keepdims=True)
    ) / (2 * columns)
    grad_first_ref[...] = scale * (grad_first - mean - first * inner)
    grad_second_ref[...] = scale * (grad_second - mean - second * inner)
    round_ref[...] = grad_first_ref[...].astype(BF16)


def skip_backward(
    scalars, matrices, terms, hidden, next_gains, residual, first, second, gains, deps=()
):
    rows, columns = first.shape
    count = lax.axis_size("seq")
    narrow = (count, rows, columns // count)
    return call(
        functools.partial(skip_backward_kernel, count, len(matrices), len(terms)),
        [
            (narrow, BF16),
            ((rows, columns), F32),
            ((rows, columns), F32),
            ((4, columns), F32),
            ((rows, columns), BF16),
        ],
        [pltpu.VMEM(narrow, BF16), corner_scratch(count, matrices)],
        15,
        *matrices,
        *terms,
        hidden,
        next_gains,
        residual,
        first,
        second,
        gains,
        scalars=scalars,
        deps=deps,
    )


def open_backward_kernel(count, terms, *refs):
    term_refs, refs = refs[:terms], refs[terms:]
    hidden_ref, gains_ref, residual_ref, out_ref, vectors_ref = refs
    grad_norm = add_terms(count, term_refs)
    vectors_ref[0:1, :] = jnp.sum(grad_norm, axis=0, keepdims=True)
    grad, grad_gain = norm_back(hidden_ref[...].astype(F32), gains_ref[0:1, :], grad_norm)
    vectors_ref[1:2, :] = grad_gain
    out_ref[...] = grad + residual_ref[...]


def open_backward(terms, hidden, gains, residual, deps=()):
    count = lax.axis_size("seq")
    return call(
        functools.partial(open_backward_kernel, count, len(terms)),
        [(residual.shape, F32), ((2, residual.shape[1]), F32)],
        [],
        5,
        *terms,
        hidden,
        gains,
        residual,
        deps=deps,
    )


def close_kernel(count, terms, *refs):
    refs[terms + 1][...] = (refs[terms][...] + add_terms(count, refs[:terms])).astype(BF16)


def close_forward(terms, residual, deps=()):
    count = lax.axis_size("seq")
    (found,) = call(
        functools.partial(close_kernel, count, len(terms)),
        [(residual.shape, BF16)],
        [],
        3,
        *terms,
        residual,
        deps=deps,
    )
    return found


def pack_kernel(count, *refs):
    start = 0
    for ref in refs[:count]:
        refs[count][: ref.shape[0], start : start + ref.shape[1]] = ref[...]
        start += ref.shape[1]


def pack(shards, deps=()):
    rows = -(-max(m.shape[0] for m in shards) // 16) * 16
    shape = (rows, sum(m.shape[1] for m in shards))
    return call(functools.partial(pack_kernel, len(shards)), [(shape, BF16)], [], 3, *shards, deps=deps)[0]


def settle_kernel(count, parts, plan, scalars_ref, *refs):
    block_refs, refs = refs[:parts], refs[parts:]
    outs = sum(entry[3] for entry in plan)
    out_refs, stack_ref = refs[-outs - 1 : -1], refs[-1]
    ordered = parts == 1
    for j in range(count):
        if ordered:
            held = stack_ref.shape[1]
            stack_ref[j] = block_refs[0][j * held : (j + 1) * held, :]
            continue
        owner = scalars_ref[count + j]
        if j == count - 1 and parts > count:
            cut = block_refs[j].shape[0]
            stack_ref[owner, :cut] = block_refs[j][...]
            stack_ref[owner, cut:] = block_refs[j + 1][...]
        else:
            stack_ref[owner] = block_refs[j][...]
    place = 0
    for first, rows, groups, pieces, width, stride in plan:
        if not groups:
            for a in range(count):
                found = stack_ref[a, :rows, first : first + width]
                out_refs[place][0, a * rows : (a + 1) * rows, :] = found.astype(F32)
        for p in range(pieces):
            for g in range(groups):
                for a in range(count):
                    low = first + (p * groups + g) * stride
                    at = (g * count + a) * width
                    found = stack_ref[a, :rows, low : low + width]
                    out_refs[place + p][0, :, at : at + width] = found.astype(F32)
        place += pieces


def settle(scalars, blocks, plan, layer, layer_count, before):
    count = lax.axis_size("seq")
    shapes = []
    for _, rows, groups, pieces, width, _ in plan:
        shapes += [(rows, groups * count * width) if groups else (count * rows, width)] * pieces
    held = [] if before is None else list(before)
    inputs = [pl.BlockSpec(memory_space=pltpu.VMEM)] * len(blocks)
    inputs += [pl.BlockSpec(memory_space=pl.ANY)] * len(held)
    found = pl.pallas_call(
        functools.partial(settle_kernel, count, len(blocks), plan),
        grid=(1,),
        out_shape=[jax.ShapeDtypeStruct((layer_count,) + shape, F32) for shape in shapes],
        in_specs=[pl.BlockSpec(memory_space=pltpu.SMEM)] + inputs,
        out_specs=[pl.BlockSpec((1,) + shape, lambda i: (layer, 0, 0)) for shape in shapes],
        scratch_shapes=[
            pltpu.VMEM(
                (count, blocks[0].shape[0] // (count if len(blocks) == 1 else 1), blocks[0].shape[1]),
                BF16,
            )
        ],
        input_output_aliases={1 + len(blocks) + i: i for i in range(len(held))},
        compiler_params=pltpu.CompilerParams(vmem_limit_bytes=VMEM_LIMIT),
        cost_estimate=pl.CostEstimate(flops=8_000_000_000, bytes_accessed=1000, transcendentals=0),
    )(scalars, *blocks, *held)
    return list(found)


def plan_of(entries):
    plan, first = [], 0
    for shard, groups, pieces, width in entries:
        rows, columns = shard.shape
        stride = columns // (groups * pieces) if groups else columns
        plan.append((first, rows, groups, pieces, width, stride))
        first += columns
    return tuple(plan)


def finish(scalars, entries, layer, layer_count, before=None, deps=()):
    blocks = gather_parts(pack([entry[0] for entry in entries], deps))
    return settle(scalars, blocks, plan_of(entries), layer, layer_count, before)


def swap_seq(block, bits):
    seq_count = lax.axis_size("seq")
    return lax.ppermute(block, "seq", [(i, i ^ bits) for i in range(seq_count)])


def swap_fsdp(block, bits):
    fsdp_count = lax.axis_size("fsdp")
    return lax.ppermute(block, "fsdp", [(i, i ^ bits) for i in range(fsdp_count)])


def swap_core(block):
    return swap_fsdp(block, 1)


def swap_by_core(block, even_bits, odd_bits):
    seq_count, fsdp_count = lax.axis_size("seq"), lax.axis_size("fsdp")
    pairs = []
    for s in range(seq_count):
        for f in range(fsdp_count):
            other = s ^ (odd_bits if f % 2 else even_bits)
            pairs.append((s * fsdp_count + f, other * fsdp_count + f))
    return lax.ppermute(block, ("seq", "fsdp"), pairs)


def add_bf16(*terms):
    total = terms[0].astype(F32)
    for term in terms[1:]:
        total = total + term.astype(F32)
    return total.astype(BF16)


def scatter_first(pieces):
    seq_count = lax.axis_size("seq")
    if seq_count != 4:
        return [swap_seq(m, j + 1) for j, m in enumerate(pieces)]
    return [swap_seq(pieces[0], 1), swap_seq(pieces[1], 2), pieces[2], pieces[3]]


def scatter_last(own, first, ready=None):
    seq_count = lax.axis_size("seq")
    if seq_count != 4:
        return [own] + first
    from_x, from_y, x_bottom, y_top = first
    if ready is not None:
        from_x, from_y = gate([from_x, from_y], ready)
    cut, rest = y_top.shape[0], x_bottom.shape[0]
    to_y, to_x = add_bf16(y_top, from_x[:cut]), add_bf16(x_bottom, from_y[:rest])
    return [own, from_x, from_y, swap_seq(to_x, 1), swap_seq(to_y, 2)]


def exchange_rel(blocks):
    return [blocks[0]] + [swap_seq(blocks[j], j) for j in range(1, len(blocks))]


def gather_first(block):
    seq_count = lax.axis_size("seq")
    if seq_count != 4:
        return [block] + [swap_seq(block, j) for j in range(1, seq_count)]
    return [block, swap_seq(block, 1), swap_seq(block, 2)]


def gather_last(first, ready=None):
    seq_count = lax.axis_size("seq")
    if seq_count != 4:
        return first
    block, from_x, from_y = first
    if ready is not None:
        from_x, from_y = gate([from_x, from_y], ready)
    cut = cut_of(block.shape[0])
    return [block, from_x, from_y, swap_seq(from_y[:cut], 1), swap_seq(from_x[cut:], 2)]


def gather_parts(block):
    return gather_last(gather_first(block))


def list_order():
    s, seq_count = lax.axis_index("seq"), lax.axis_size("seq")
    if seq_count != 4:
        return [s ^ j for j in range(seq_count)]
    odd = lax.axis_index("fsdp") % 2
    return [s, s ^ (1 + odd), s ^ (2 - odd), s ^ 3]


def spread_first(block):
    seq_count = lax.axis_size("seq")
    if seq_count != 4:
        return [block] + [swap_seq(block, j) for j in range(1, seq_count)]
    return [block, swap_by_core(block, 1, 2)]


def spread_slice(blocks, ready):
    if lax.axis_size("seq") != 4:
        return blocks
    block, first = blocks
    if ready is not None:
        (first,) = gate([first], ready)
    half = block.shape[0] // 2
    odd = lax.axis_index("fsdp") % 2
    return [block, first, lax.dynamic_slice_in_dim(first, odd * half, half, 0)]


def spread_last(blocks, part_ready):
    seq_count = lax.axis_size("seq")
    if seq_count != 4:
        return blocks
    block, first, part = blocks
    part = swap_by_core(part, 2, 1)
    other = swap_core(first)
    if part_ready is not None:
        (part,) = gate([part], part_ready)
    return [block, first, other, part, swap_core(part)]


def unspread(scalars, blocks):
    seq_count = lax.axis_size("seq")
    if seq_count != 4:
        return add_bf16(blocks[0], *[swap_seq(blocks[j], j) for j in range(1, seq_count)])
    own, first_mine, first_other, second_mine, second_other, corner_mine, corner_other = blocks
    passed = swap_by_core(add_bf16(corner_mine, swap_core(corner_other)), 2, 1)
    other = swap_by_core(add_bf16(first_other, swap_core(second_mine)), 1, 2)
    mine = swap_by_core(add_bf16(first_mine, swap_core(second_other), passed), 1, 2)
    return join_halves(scalars, own, mine, other)


def own_part(matrix, groups, padded):
    s, seq_count = lax.axis_index("seq"), lax.axis_size("seq")
    width = matrix.shape[1] // (groups * seq_count)
    parts = [
        jnp.pad(
            lax.dynamic_slice_in_dim(matrix, (g * seq_count + s) * width, width, 1),
            ((0, 0), (0, padded - width)),
        )
        for g in range(groups)
    ]
    return jnp.concatenate(parts, axis=1)


def gather_fsdp(shard):
    return lax.all_gather(shard, "fsdp", axis=0, tiled=True)


def scatter_fsdp(full):
    return lax.psum_scatter(full.astype(BF16), "fsdp", scatter_dimension=0, tiled=True)


def layer_forward(parts, hidden, scalars, gains, shift, pairs, weights, normed, deps, hold=None):
    lead_part, square_parts, up_part = weights
    seq_count = lax.axis_size("seq")
    tok_rows, model_width = hidden.shape
    head_size, width = model_width // H, model_width // seq_count
    first_all, triples, mixed = self_forward(
        parts,
        lead_part,
        gains,
        shift,
        head_size,
        seq_count,
        width,
        normed,
        (square_parts[-1],) + deps,
    )
    mixed_rel = exchange_rel(mixed)
    square_parts = spread_last(square_parts, mixed_rel[1:])
    held = []
    if hold is not None:
        held = gate([hold], [square_parts[-1]])
    self_tokens, after_self, cross_norm, queries, cross_tokens, after_cross, mlp_norm = (
        middle_forward(
            int(normed), scalars, mixed_rel, square_parts, pairs, hidden, gains, head_size, held
        )
    )
    mlp_parts = gather_parts(mlp_norm)
    mlp_all, up_rows, activated = mlp_up(mlp_parts, up_part, seq_count)
    saved = (
        first_all,
        triples,
        self_tokens,
        after_self,
        cross_norm,
        queries,
        cross_tokens,
        after_cross,
        mlp_all,
        up_rows,
        activated,
    )
    return (saved, square_parts, mlp_parts, held)


def unspread_first(blocks, ready):
    own, first_mine, first_other, second_mine, second_other, corner_mine, corner_other = blocks
    from_corner, to_other = swap_core(corner_other), swap_core(second_mine)
    to_mine = swap_core(second_other)
    sums = [add_bf16(corner_mine, from_corner), add_bf16(first_other, to_other)]
    sums = gate(sums, ready)
    hops = [swap_by_core(sums[0], 2, 1), swap_by_core(sums[1], 1, 2)]
    return own, hops, [first_mine, to_mine], sums


def unspread_next(first, ready):
    own, hops, terms, _ = first
    passed, other = gate(hops, ready)
    return own, swap_by_core(add_bf16(*terms, passed), 1, 2), other


def unspread_last(scalars, second, ready):
    own, mine, other = second
    (mine,) = gate([mine], ready)
    return join_halves(scalars, own, mine, other)


def unspread_any(blocks):
    return add_bf16(blocks[0], *[swap_seq(m, j + 1) for j, m in enumerate(blocks[1:])])


def qkv_own(layer, qkv):
    return own_part(qkv[layer], 3, padded_width(qkv.shape[2] // (3 * lax.axis_size("seq"))))


def squares_own(layer, *stacks):
    padded = padded_width(stacks[0].shape[2] // lax.axis_size("seq"))
    return jnp.concatenate([own_part(m[layer], 1, padded) for m in stacks], axis=1)


def gather_rest(layer, up, down):
    s, seq_count, fsdp_count = lax.axis_index("seq"), lax.axis_size("seq"), lax.axis_size("fsdp")
    rows = down.shape[1] // seq_count
    return (
        gather_fsdp(own_part(up[layer], fsdp_count, up.shape[2] // (fsdp_count * seq_count))),
        gather_fsdp(lax.dynamic_slice_in_dim(down[layer], s * rows, rows, 0)),
    )


def sum_vectors(vectors):
    bits = 1
    while bits < lax.axis_size("seq"):
        vectors = vectors + swap_seq(vectors, bits)
        bits *= 2
    found, bits = vectors[None], 1
    while bits < lax.axis_size("fsdp"):
        found = jnp.concatenate([found, swap_fsdp(found, bits)], axis=0)
        bits *= 2
    return found


def body(
    latents,
    skip_input,
    text_tokens,
    text_lengths,
    condition,
    cotangent,
    mod_weight,
    norm_gains,
    qkv_weight,
    query_weight,
    text_kv_weight,
    self_out_weight,
    cross_out_weight,
    up_weight,
    down_weight,
    skip_gain,
    skip_weight,
):
    seq_count, fsdp_count = lax.axis_size("seq"), lax.axis_size("fsdp")
    s, f = lax.axis_index("seq"), lax.axis_index("fsdp")
    _, tok_rows, model_width = latents.shape
    width = model_width // seq_count
    shard_rows = mod_weight.shape[1]
    text_count = text_tokens.shape[1]
    padded = -(-text_count // 32) * 32
    text_rows = jnp.pad(text_tokens[0], ((0, padded - text_count), (0, 0)))
    scalars = jnp.stack(
        [*list_order(), *[s ^ j for j in range(seq_count)], f % 2, text_lengths[0]]
    ).astype(jnp.int32)

    gain_rows = jnp.concatenate(
        [norm_gains.reshape(-1, shard_rows), skip_gain.reshape(-1, shard_rows)], axis=0
    )
    small = jnp.concatenate(
        [
            condition.reshape(fsdp_count, 1, shard_rows),
            jnp.broadcast_to(gain_rows[None], (fsdp_count,) + gain_rows.shape),
        ],
        axis=1,
    ).astype(F32)
    latent_parts = gather_parts(latents[0])
    (small,) = gate([small], latent_parts[-2:])
    small = lax.all_to_all(small, "fsdp", 0, 0, tiled=True)
    cond_part = small[:, 0]
    gains = jnp.swapaxes(small[:, 1:7], 0, 1).reshape(2, 3, model_width)
    skip_gains = small[:, 7:].reshape(2, model_width)
    silu_part = jax.nn.silu(cond_part)
    shift_terms = jnp.einsum("br,lrd->bld", silu_part, mod_weight.astype(F32), precision=EXACT)
    padded_columns = padded_width(width)
    kv_both = gather_fsdp(
        jnp.concatenate([own_part(text_kv_weight[l], 2, padded_columns) for l in range(2)], axis=1)
    )
    pair_hops = gather_first(dot_nn(text_rows, kv_both).astype(BF16))
    pairs_all = gather_last(pair_hops)
    (shift_terms,) = gate([shift_terms], pair_hops[1:])
    shifts = jnp.sum(lax.all_to_all(shift_terms, "fsdp", 0, 0, tiled=True), axis=0)

    square_stacks = (self_out_weight, query_weight, cross_out_weight)
    rest_stacks = (up_weight, down_weight)
    head_size = model_width // H
    fours = seq_count == 4

    square_shard, qkv_shard = gate(
        [squares_own(0, *square_stacks), qkv_own(0, qkv_weight)], [kv_both] + latent_parts[-2:]
    )
    square_first, lead_first = gather_fsdp(square_shard), gather_fsdp(qkv_shard)
    up_first, down_first = gather_rest(0, *rest_stacks)
    spread_squares = spread_slice(spread_first(gate([square_first], [cond_part])[0]), [shifts])
    (lead_first,) = gate([lead_first], [shifts])
    pairs_first, pairs_second = pairs_all, pairs_all
    skip_matrix = gather_fsdp(own_part(skip_weight, 1, padded_width(width)))
    saved_first, squares_first, mlp_parts, (skip_matrix,) = layer_forward(
        latent_parts,
        latents[0],
        scalars,
        gains[0],
        shifts[0],
        pairs_first,
        (lead_first, spread_squares, up_first),
        False,
        tuple(pairs_all[-2:]),
        skip_matrix,
    )
    own, pieces = mlp_down(saved_first[10], down_first, seq_count)
    first = scatter_first(pieces)
    terms = scatter_last(own, first)

    skip_parts = spread_last(spread_slice(spread_first(skip_matrix), mlp_parts[-2:]), [own])
    square_second = gather_fsdp(squares_own(1, *square_stacks))
    lead_second = gather_fsdp(qkv_own(1, qkv_weight))
    (square_second,) = gate([square_second], first[:2])
    squares_second = spread_first(square_second)
    first_out, joined_norm, skip_out, second_norm = skip_forward(
        scalars,
        skip_parts,
        terms,
        saved_first[7],
        skip_input[0],
        skip_gains,
        gains[1],
        shifts[1],
        (square_second,),
    )

    up_second, down_second = gather_rest(1, *rest_stacks)
    out_hops = gather_first(gate([cotangent[0]], [skip_out])[0])
    second_parts = gather_parts(second_norm)
    squares_second = spread_slice(squares_second, second_parts[1:3])
    saved_second, squares_second, mlp_parts, _ = layer_forward(
        second_parts,
        skip_out,
        scalars,
        gains[1],
        shifts[1],
        pairs_second,
        (lead_second, squares_second, up_second),
        True,
        (),
    )
    out_parts = gather_last(out_hops, [squares_second[-1]])
    out_all = stack_rows(out_parts, (mlp_parts[1],))

    held = {}

    def block_backward(rows, grad_out, saved, block, weights, early, hooks):
        lead_matrix, square_parts, pairs, up_part, down_part = weights
        grad_down = dot_tn(saved[10], early).astype(BF16) if early is not None else None
        found_all, grad_up_rows, own, pieces = mlp_backward(
            rows,
            saved[9],
            up_part,
            down_part,
            seq_count,
            hooks[0] + ((grad_down,) if early is not None else ()),
        )
        first = scatter_first(gate(pieces, hooks[3]) if hooks[3] else pieces)
        terms = scatter_last(own, first)
        held["hops"] = first[:2]
        if early is None:
            grad_down = dot_tn(saved[10], found_all).astype(BF16)
            (grad_down,) = gate([grad_down], first[:2])
        grad_up = dot_tn(saved[8], grad_up_rows).astype(BF16)
        (grad_up,) = gate([grad_up], first[:2])
        down_shard, up_shard = scatter_fsdp(grad_down), scatter_fsdp(grad_up)
        (
            grad_after_self,
            self_branch,
            query_branch,
            cross_branch,
            gain_grads,
            mixed_grads,
            own_pairs,
            pair_blocks,
        ) = middle_backward(
            block,
            scalars,
            square_parts,
            pairs,
            terms,
            grad_out,
            saved[7],
            saved[3],
            saved[5],
            gains[block],
            head_size,
            (grad_down, grad_up) + hooks[1](grad_up_rows, terms),
        )
        mixed_rel = exchange_rel(mixed_grads)
        pair_blocks = gate(pair_blocks, mixed_rel[1:])
        pair_terms = [swap_seq(m, j + 1) for j, m in enumerate(pair_blocks)]
        grad_triples, own, pieces = self_backward(
            saved[1],
            mixed_rel,
            lead_matrix,
            head_size,
            (down_shard,) + hooks[2](mixed_rel[1]),
        )
        pair_terms = gate(pair_terms, [grad_triples])
        first = scatter_first(gate(pieces, pair_terms))
        terms = scatter_last(own, first)
        grad_qkv = dot_tn(saved[0], grad_triples).astype(BF16)
        (grad_qkv,) = gate([grad_qkv], first[:2])
        held["last"] = first[:2]
        squares = outer(
            scalars,
            [saved[2], saved[4], saved[6]],
            [self_branch, query_branch, cross_branch],
            (grad_triples,),
        )
        squares = gate(squares, first[:2])
        pair_terms = gate(pair_terms, first[:2])
        grad_pairs = add_bf16(own_pairs, *pair_terms)
        kv_part = kv_both[:, 2 * block * padded_columns : 2 * (block + 1) * padded_columns]
        grad_text = dot_nt(grad_pairs, kv_part)
        kv_shard = scatter_fsdp(dot_tn(text_rows, grad_pairs))
        return (
            terms,
            grad_after_self,
            gain_grads,
            grad_text,
            squares,
            grad_qkv,
            grad_triples,
            (scatter_fsdp(grad_qkv), kv_shard, up_shard, down_shard),
        )

    def second_own(grad_up_rows, terms):
        own, pieces = mlp_down(saved_second[10], down_second, seq_count, (grad_up_rows,))
        pieces = gate(pieces, terms[-2:])
        held["own"], held["own_hops"] = own, scatter_first(pieces)
        return tuple(pieces)

    def second_sum(ready):
        held["ready"] = ready
        return tuple(held["own_hops"][:2])

    (
        terms,
        grad_after_self,
        gain_grads,
        text_second,
        squares,
        grad_qkv,
        grad_triples,
        (qkv_shard, kv_shard, up_shard, down_shard),
    ) = block_backward(
        [out_all],
        cotangent[0],
        saved_second,
        1,
        (lead_second, squares_second, pairs_second, up_second, down_second),
        out_all,
        ((), second_own, second_sum, ()),
    )
    skip_branch, grad_first_out, grad_skip, vectors, first_round = skip_backward(
        scalars,
        skip_parts,
        terms,
        skip_out,
        gains[1],
        grad_after_self,
        first_out,
        skip_input[0],
        skip_gains,
        (grad_qkv, up_shard),
    )
    vectors_second = jnp.concatenate([vectors[:2], gain_grads, vectors[2:]], axis=0)
    first_hops = gather_first(first_round)
    first_parts = gather_last(first_hops)
    if fours:
        squares = unspread_first(squares, first_parts[-2:])
    own_terms = scatter_last(held["own"], held["own_hops"], terms[-2:])
    output = close_forward(own_terms, saved_second[7])
    skip_outer = outer(scalars, [joined_norm], [skip_branch], tuple(first_hops[1:]))

    def entries(layer):
        qkv, square, kv, up, down = layer
        return (
            [
                (up, fsdp_count, 1, up.shape[1] // fsdp_count),
                (down, 0, 1, down.shape[1]),
            ],
            [(qkv, 3, 1, width), (square, 1, 3, width), (kv, 2, 1, width)],
        )

    early, _ = entries((qkv_shard, qkv_shard, kv_shard, up_shard, down_shard))
    early_all = lax.all_gather(
        pack([entry[0] for entry in early], first_hops[1:]), "seq", axis=0, tiled=True
    )

    def first_middle(grad_up_rows, terms):
        del grad_up_rows, terms
        return (kv_shard,)

    def first_self(ready):
        if not fours:
            return (qkv_shard,)
        held["squares"] = unspread_next(squares, held["hops"])
        return (qkv_shard, held["squares"][1])

    (
        terms,
        grad_after_self,
        gain_grads,
        text_first,
        first_squares,
        grad_qkv,
        grad_triples,
        (first_qkv_shard, first_kv_shard, first_up_shard, first_down_shard),
    ) = block_backward(
        first_parts,
        grad_first_out,
        saved_first,
        0,
        (lead_first, squares_first, pairs_first, up_first, down_first),
        None,
        (
            (skip_outer[0],) + (tuple(squares[3]) if fours else ()),
            first_middle,
            first_self,
            squares[1] if fours else (),
        ),
    )
    if fours:
        outer_done = [first_squares[1]]
        joined = unspread_last(scalars, held["squares"], outer_done)
        first_squares = unspread_first(first_squares, outer_done)
        skip_first = unspread_first(skip_outer, first_squares[3])
        first_squares = unspread_next(first_squares, terms[-2:])
        first_joined = unspread_last(scalars, first_squares, terms[-2:])
        skip_joined = unspread_last(
            scalars, unspread_next(skip_first, [first_squares[1]]), [first_joined]
        )
    else:
        joined, skip_joined = unspread_any(squares), unspread_any(skip_outer)
        first_joined = unspread_any(first_squares)
        outer_done = [joined]
    square_shard, skip_shard = scatter_fsdp(joined), scatter_fsdp(skip_joined)
    early, _ = entries(
        (first_qkv_shard, first_qkv_shard, first_kv_shard, first_up_shard, first_down_shard)
    )
    first_hops = gather_first(pack([entry[0] for entry in early], outer_done))
    grad_latents, vectors = open_backward(
        terms, latents[0], gains[0], grad_after_self, (grad_qkv, early_all)
    )
    vectors_first = jnp.concatenate([vectors, gain_grads], axis=0)
    first_layer = (
        first_qkv_shard,
        scatter_fsdp(first_joined),
        first_kv_shard,
        first_up_shard,
        first_down_shard,
    )

    early_done = settle(
        scalars,
        [early_all],
        plan_of(early),
        1,
        2,
        None,
    )
    _, late = entries((qkv_shard, square_shard, kv_shard, up_shard, down_shard))
    late_done = finish(scalars, late, 1, 2, None)
    early, late = entries(first_layer)
    grad_up, grad_down = settle(
        scalars, gather_last(first_hops), plan_of(early), 0, 2, early_done
    )
    grad_qkv, grad_self_out, grad_query, grad_cross_out, grad_kv = finish(
        scalars, late, 0, 2, late_done
    )
    (grad_skip_weight,) = finish(scalars, [(skip_shard, 1, 1, width)], 0, 1)

    sums = sum_vectors(jnp.concatenate([vectors_first, vectors_second], axis=0))
    first_sums, second_sums = sums[:, :4], sums[:, 4:]
    shift_grads = jnp.stack([first_sums[:, 0], second_sums[:, 0]], axis=1)
    gain_sums = jnp.stack([first_sums[:, 1:4].sum(axis=0), second_sums[:, 1:4].sum(axis=0)])
    grad_norm_gains = lax.dynamic_slice_in_dim(gain_sums, f * shard_rows, shard_rows, 2)
    grad_skip_gain = lax.dynamic_slice_in_dim(
        second_sums[:, 4:].sum(axis=0).reshape(-1), f * skip_gain.shape[0], skip_gain.shape[0], 0
    )
    turned = jnp.stack(
        [lax.dynamic_index_in_dim(silu_part, f ^ j, 0, False) for j in range(fsdp_count)]
    )
    grad_mod = jnp.einsum("br,bld->lrd", turned, shift_grads, precision=EXACT)
    grad_silu = jnp.einsum("bld,lrd->br", shift_grads, mod_weight.astype(F32), precision=EXACT)
    grad_silu = jnp.stack(
        [lax.dynamic_index_in_dim(grad_silu, f ^ j, 0, False) for j in range(fsdp_count)]
    )
    _, silu_pull = jax.vjp(jax.nn.silu, cond_part)
    grad_cond_part = silu_pull(grad_silu)[0]
    grad_condition = lax.all_to_all(grad_cond_part, "fsdp", 0, 0, tiled=True).reshape(1, -1)

    text_sum, bits = text_first + text_second, 1
    while bits < seq_count:
        text_sum = text_sum + swap_seq(text_sum.astype(BF16), bits).astype(F32)
        bits *= 2
    return (
        output[None],
        grad_latents[None],
        grad_skip[None],
        text_sum[None, :text_count],
        grad_condition,
        grad_mod,
        grad_norm_gains,
        grad_qkv,
        grad_query,
        grad_kv,
        grad_self_out,
        grad_cross_out,
        grad_up,
        grad_down,
        grad_skip_gain,
        grad_skip_weight[0],
    )


def solution(mesh):
    in_specs = (
        P("fsdp", "seq", None),
        P("fsdp", "seq", None),
        P("fsdp", None, None),
        P("fsdp"),
        P("fsdp", None),
        P("fsdp", "seq", None),
        P(None, "fsdp", None),
        P(None, None, "fsdp"),
        P(None, "fsdp", None),
        P(None, "fsdp", None),
        P(None, "fsdp", None),
        P(None, "fsdp", None),
        P(None, "fsdp", None),
        P(None, "fsdp", None),
        P(None, "fsdp", None),
        P("fsdp"),
        P("fsdp", None),
    )
    out_specs = (
        P("fsdp", "seq", None),
        P("fsdp", "seq", None),
        P("fsdp", "seq", None),
        P("fsdp", None, None),
        P("fsdp", None),
        P(None, "fsdp", None),
        P(None, None, "fsdp"),
        P(None, "fsdp", None),
        P(None, "fsdp", None),
        P(None, "fsdp", None),
        P(None, "fsdp", None),
        P(None, "fsdp", None),
        P(None, "fsdp", None),
        P(None, "fsdp", None),
        P("fsdp"),
        P("fsdp", None),
    )
    return jax.shard_map(body, mesh=mesh, in_specs=in_specs, out_specs=out_specs, check_vma=False)
```

```python
import functools
import math

import jax
import jax.numpy as jnp
from jax import lax
from jax.experimental import pallas as pl
from jax.experimental.pallas import tpu as pltpu
from jax.sharding import PartitionSpec as P

H = 16
NORM_EPSILON = 1e-06
EXACT = lax.Precision.HIGHEST
BF16 = jnp.bfloat16
F32 = jnp.float32
LOG2_E = 1.4426950408889634
GELU_SCALE = math.sqrt(2.0 / math.pi)
VMEM_LIMIT = 56 * 1024 * 1024


def dot_nn(a, b):
    return lax.dot_general(a, b, (((1,), (0,)), ((), ())), preferred_element_type=F32)


def dot_nt(a, b):
    return lax.dot_general(a, b, (((1,), (1,)), ((), ())), preferred_element_type=F32)


def dot_tn(a, b):
    return lax.dot_general(a, b, (((0,), (0,)), ((), ())), preferred_element_type=F32)


def padded_width(width):
    return -(-width // 128) * 128


def call(kernel, outs, scratch, micros, *operands, scalars=None, deps=(), outside=()):
    specs = [
        pl.BlockSpec(memory_space=pl.ANY if i in outside else pltpu.VMEM)
        for i in range(len(operands))
    ]
    if scalars is not None:
        specs = [pl.BlockSpec(memory_space=pltpu.SMEM)] + specs
        operands = (scalars,) + tuple(operands)
    used, held = len(operands), len(deps)

    def run(*refs):
        kernel(*refs[:used], *refs[used + held :])

    return pl.pallas_call(
        run,
        name=getattr(kernel, "func", kernel).__name__,
        out_shape=tuple(jax.ShapeDtypeStruct(s, d) for s, d in outs),
        in_specs=specs + [pl.BlockSpec(memory_space=pl.ANY)] * held,
        out_specs=tuple([pl.BlockSpec(memory_space=pltpu.VMEM)] * len(outs)),
        scratch_shapes=scratch,
        compiler_params=pltpu.CompilerParams(vmem_limit_bytes=VMEM_LIMIT),
        cost_estimate=pl.CostEstimate(
            flops=int(micros * 1000), bytes_accessed=1000, transcendentals=0
        ),
    )(*operands, *deps)


def gate_kernel(*refs):
    del refs


def gate(values, deps):
    values, deps = list(values), list(deps)
    return list(
        pl.pallas_call(
            gate_kernel,
            out_shape=tuple(jax.ShapeDtypeStruct(m.shape, m.dtype) for m in values),
            in_specs=[pl.BlockSpec(memory_space=pl.ANY)] * (len(values) + len(deps)),
            out_specs=tuple([pl.BlockSpec(memory_space=pl.ANY)] * len(values)),
            input_output_aliases={i: i for i in range(len(values))},
            cost_estimate=pl.CostEstimate(flops=1000, bytes_accessed=1000, transcendentals=0),
        )(*values, *deps)
    )


def cut_of(rows):
    return rows // 32 * 16


def piece_shapes(count, rows, columns):
    if count != 4:
        return [((rows, columns), BF16)] * (count - 1)
    cut = cut_of(rows)
    return [((m, columns), BF16) for m in (2 * cut, 2 * (rows - cut), rows - cut, cut)]


def put_pieces(refs, count, block, values):
    if count != 4:
        refs[block - 1][...] = values.astype(BF16)
        return
    to_x, to_y, x_bottom, y_top = refs
    rows = values.shape[0]
    cut = cut_of(rows)
    top, bottom = values[:cut].astype(BF16), values[cut:].astype(BF16)
    if block == 1:
        to_x[cut:, :] = top
        x_bottom[...] = bottom
    elif block == 2:
        y_top[...] = top
        to_y[rows - cut :, :] = bottom
    else:
        to_x[:cut, :] = top
        to_y[: rows - cut, :] = bottom


def add_terms(count, refs):
    total = refs[0][...].astype(F32)
    if count != 4:
        for ref in refs[1:]:
            total = total + ref[...].astype(F32)
        return total
    from_x, from_y, x_bottom, y_top = [ref[...] for ref in refs[1:]]
    cut, rest = y_top.shape[0], x_bottom.shape[0]
    by_x = jnp.concatenate([from_x[cut:], x_bottom], axis=0)
    by_y = jnp.concatenate([y_top, from_y[rest:]], axis=0)
    return total + by_x.astype(F32) + by_y.astype(F32)


def norm_stats(values):
    mean = jnp.mean(values, axis=1, keepdims=True)
    centered = values - mean
    var = jnp.mean(centered * centered, axis=1, keepdims=True)
    scale = lax.rsqrt(var + NORM_EPSILON)
    return centered * scale, scale


def norm_back(values, gain, grad):
    unit, scale = norm_stats(values)
    grad_unit = grad * gain
    inner = jnp.mean(grad_unit * unit, axis=1, keepdims=True)
    grad_values = scale * (grad_unit - jnp.mean(grad_unit, axis=1, keepdims=True) - unit * inner)
    return grad_values, jnp.sum(grad * unit, axis=0, keepdims=True)


def self_forward_kernel(count, parts, head_size, normed, *refs):
    part_refs, refs = refs[:parts], refs[parts:]
    weight_ref, gains_ref, shift_ref = refs[:3]
    rows_ref, triples_ref = refs[3:5]
    mixed_refs, (held_ref, done) = refs[5:-2], refs[-2:]
    copy = pltpu.make_async_copy(weight_ref.at[:, : held_ref.shape[1]], held_ref, done)
    copy.start()
    stride = held_ref.shape[1] // 3
    rows, width = mixed_refs[0].shape
    factor = LOG2_E / math.sqrt(head_size)
    start = 0
    for ref in part_refs:
        values = ref[...]
        if not normed:
            unit, _ = norm_stats(values.astype(F32))
            values = (unit * gains_ref[0:1, :] + shift_ref[...]).astype(BF16)
        rows_ref[start : start + ref.shape[0], :] = values
        start += ref.shape[0]
    copy.wait()
    for j in range(count):
        at = slice(j * rows, (j + 1) * rows)
        triples_ref[at, :] = dot_nn(rows_ref[at, :], held_ref[...]).astype(BF16)
    for j in range(count):
        at = slice(j * rows, (j + 1) * rows)
        for h in range(width // head_size):
            low = h * head_size
            q = triples_ref[at, low : low + head_size]
            k = triples_ref[:, stride + low : stride + low + head_size]
            v = triples_ref[:, 2 * stride + low : 2 * stride + low + head_size]
            scores = dot_nt(q, k)
            top = jnp.max(scores, axis=1, keepdims=True)
            weights = jnp.exp2((scores - top) * factor)
            total = jnp.sum(weights, axis=1, keepdims=True)
            mixed = dot_nn(weights.astype(BF16), v) * (1.0 / total)
            mixed_refs[j][:, low : low + head_size] = mixed.astype(BF16)


def self_forward(parts, weight, gains, shift, head_size, count, width, normed, deps=()):
    total = sum(m.shape[0] for m in parts)
    columns = parts[0].shape[1]
    held = (columns, 3 * padded_width(width))
    found = call(
        functools.partial(self_forward_kernel, count, len(parts), head_size, normed),
        [((total, columns), BF16), ((total, held[1]), BF16)]
        + [((total // count, width), BF16)] * count,
        [pltpu.VMEM(held, BF16), pltpu.SemaphoreType.DMA],
        24,
        *parts,
        weight,
        gains,
        shift[None],
        deps=deps,
        outside=(len(parts),),
    )
    return found[0], found[1], list(found[2:])


def attention_back(q, k, v, grad, valid, head_size):
    factor = LOG2_E / math.sqrt(head_size)
    scores = dot_nt(k, q)
    if valid is not None:
        scores = jnp.where(valid, scores, -1e30)
    top = jnp.max(scores, axis=0, keepdims=True)
    weights = jnp.exp2((scores - top) * factor)
    weights = weights * (1.0 / jnp.sum(weights, axis=0, keepdims=True))
    grad_weights = dot_nt(v, grad)
    delta = jnp.sum(grad_weights * weights, axis=0, keepdims=True)
    grad_scores = (weights * (grad_weights - delta)).astype(BF16)
    scale = 1.0 / math.sqrt(head_size)
    return (
        dot_tn(grad_scores, k) * scale,
        dot_nn(grad_scores, q) * scale,
        dot_nn(weights.astype(BF16), grad),
    )


def self_backward_kernel(count, head_size, step, triples_ref, *refs):
    grad_refs, (weight_ref, out_ref, own_ref) = refs[:count], refs[count : count + 3]
    piece_refs, (keys_ref, values_ref, held_ref, done) = refs[count + 3 : -4], refs[-4:]
    copy = pltpu.make_async_copy(weight_ref.at[:, : held_ref.shape[1]], held_ref, done)
    copy.start()
    total = triples_ref.shape[0]
    rows, width = grad_refs[0].shape
    stride = held_ref.shape[1] // 3
    for h in range(width // head_size):
        low = h * head_size
        k = triples_ref[:, stride + low : stride + low + head_size]
        v = triples_ref[:, 2 * stride + low : 2 * stride + low + head_size]
        for i in range(total // step):
            at = slice(i * step, (i + 1) * step)
            inside = (i * step) % rows
            q = triples_ref[at, low : low + head_size]
            grad = grad_refs[i * step // rows][inside : inside + step, low : low + head_size]
            grad_q, grad_k, grad_v = attention_back(q, k, v, grad, None, head_size)
            out_ref[at, low : low + head_size] = grad_q.astype(BF16)
            if i == 0:
                keys_ref[...] = grad_k
                values_ref[...] = grad_v
            else:
                keys_ref[...] += grad_k
                values_ref[...] += grad_v
        out_ref[:, stride + low : stride + low + head_size] = keys_ref[...].astype(BF16)
        out_ref[:, 2 * stride + low : 2 * stride + low + head_size] = values_ref[...].astype(BF16)
    if stride > width:
        for g in range(3):
            out_ref[:, g * stride + width : (g + 1) * stride] = jnp.zeros((total, stride - width), BF16)
    copy.wait()
    for j in range(count):
        found = dot_nt(out_ref[j * rows : (j + 1) * rows, :], held_ref[...])
        if j == 0:
            own_ref[...] = found
        else:
            put_pieces(piece_refs, count, j, found)


def self_backward(triples, grads, weight, head_size, deps=()):
    count = len(grads)
    total, rows, columns = triples.shape[0], grads[0].shape[0], weight.shape[0]
    step = min(256, rows)
    found = call(
        functools.partial(self_backward_kernel, count, head_size, step),
        [(triples.shape, BF16), ((rows, columns), F32)] + piece_shapes(count, rows, columns),
        [
            pltpu.VMEM((total, head_size), F32),
            pltpu.VMEM((total, head_size), F32),
            pltpu.VMEM((columns, triples.shape[1]), BF16),
            pltpu.SemaphoreType.DMA,
        ],
        32,
        triples,
        *grads,
        weight,
        deps=deps,
        outside=(1 + count,),
    )
    return found[0], found[1], list(found[2:])


def fill_corner(count, matrix_refs, scalars_ref, corner_ref):
    if len(matrix_refs) == count:
        return list(matrix_refs)
    odd = scalars_ref[2 * count]
    half = matrix_refs[-1].shape[0]
    corner_ref[pl.ds(pl.multiple_of(odd * half, half), half), :] = matrix_refs[-2][...]
    corner_ref[pl.ds(pl.multiple_of((1 - odd) * half, half), half), :] = matrix_refs[-1][...]
    return list(matrix_refs[:-2]) + [corner_ref]


def corner_scratch(count, matrices):
    rows, columns = matrices[0].shape
    return pltpu.VMEM((rows, columns) if len(matrices) > count else (16, 128), BF16)


def fill_pairs(count, block, pair_refs, pairs_ref):
    padded, columns = pairs_ref.shape[1:]
    place = 0
    for ref in pair_refs:
        j, low = divmod(place, padded)
        pairs_ref[j, low : low + ref.shape[0], :] = ref[:, block * columns : (block + 1) * columns]
        place += ref.shape[0]


def middle_forward_kernel(block, count, matrix_parts, pair_parts, head_size, scalars_ref, *refs):
    mixed_refs, refs = refs[:count], refs[count:]
    matrix_refs, refs = refs[:matrix_parts], refs[matrix_parts:]
    pair_refs, refs = refs[:pair_parts], refs[pair_parts:]
    hidden_ref, gains_ref = refs[:2]
    (self_ref, after_self_ref, norm_ref, queries_ref, cross_ref, after_cross_ref) = refs[2:8]
    mlp_ref = refs[8]
    wide_ref, narrow_ref, corner_ref, pairs_ref = refs[-4:]
    width = mixed_refs[0].shape[1]
    stride = matrix_refs[0].shape[1] // 3
    matrices = fill_corner(count, matrix_refs, scalars_ref, corner_ref)
    fill_pairs(count, block, pair_refs, pairs_ref)
    order = [scalars_ref[i] for i in range(count)]
    relative = [scalars_ref[count + j] for j in range(count)]
    length = scalars_ref[2 * count + 1]
    spans = [slice(a * width, (a + 1) * width) for a in range(count)]

    for j in range(count):
        narrow_ref[relative[j]] = mixed_refs[j][...]
    for a in range(count):
        self_ref[:, spans[a]] = narrow_ref[a]
    tokens = self_ref[...]
    for i in range(count):
        wide_ref[order[i]] = dot_nn(tokens, matrices[i][:, :width])
    for a in range(count):
        after_self_ref[:, spans[a]] = hidden_ref[:, spans[a]].astype(F32) + wide_ref[a]
    normed = (norm_stats(after_self_ref[...])[0] * gains_ref[1:2, :]).astype(BF16)
    norm_ref[...] = normed
    for i in range(count):
        found = dot_nn(normed, matrices[i][:, stride : stride + width])
        queries_ref[order[i] ^ relative[0]] = found.astype(BF16)

    factor = LOG2_E / math.sqrt(head_size)
    keys_rows = pairs_ref.shape[1]
    valid = lax.broadcasted_iota(jnp.int32, (1, keys_rows), 1) < length
    pair_stride = pairs_ref.shape[2] // 2
    for j in range(count):
        for h in range(width // head_size):
            at = slice(h * head_size, (h + 1) * head_size)
            values_at = slice(pair_stride + h * head_size, pair_stride + (h + 1) * head_size)
            scores = dot_nt(queries_ref[j, :, at], pairs_ref[j, :, at])
            scores = jnp.where(valid, scores, -1e30)
            top = jnp.max(scores, axis=1, keepdims=True)
            weights = jnp.exp2((scores - top) * factor)
            total = jnp.sum(weights, axis=1, keepdims=True)
            mixed = dot_nn(weights.astype(BF16), pairs_ref[j, :, values_at]) * (1.0 / total)
            narrow_ref[relative[j], :, at] = mixed.astype(BF16)
    for a in range(count):
        cross_ref[:, spans[a]] = narrow_ref[a]
    tokens = cross_ref[...]
    for i in range(count):
        wide_ref[order[i]] = dot_nn(tokens, matrices[i][:, 2 * stride : 2 * stride + width])
    for a in range(count):
        after_cross_ref[:, spans[a]] = after_self_ref[:, spans[a]] + wide_ref[a]
    mlp_ref[...] = (norm_stats(after_cross_ref[...])[0] * gains_ref[2:3, :]).astype(BF16)


def pairs_scratch(count, pairs):
    return pltpu.VMEM(
        (count, sum(m.shape[0] for m in pairs) // count, pairs[0].shape[1] // 2), BF16
    )


def middle_forward(block, scalars, mixed, matrices, pairs, hidden, gains, head_size, deps=()):
    count = len(mixed)
    rows, columns = hidden.shape
    width = columns // count
    return call(
        functools.partial(
            middle_forward_kernel, block, count, len(matrices), len(pairs), head_size
        ),
        [
            ((rows, columns), BF16),
            ((rows, columns), F32),
            ((rows, columns), BF16),
            ((count, rows, width), BF16),
            ((rows, columns), BF16),
            ((rows, columns), F32),
            ((rows, columns), BF16),
        ],
        [
            pltpu.VMEM((count, rows, width), F32),
            pltpu.VMEM((count, rows, width), BF16),
            corner_scratch(count, matrices),
            pairs_scratch(count, pairs),
        ],
        23,
        *mixed,
        *matrices,
        *pairs,
        hidden,
        gains,
        scalars=scalars,
        deps=deps,
    )


def middle_backward_kernel(block, count, matrix_parts, pair_parts, terms, head_size, scalars_ref, *refs):
    matrix_refs, refs = refs[:matrix_parts], refs[matrix_parts:]
    pair_refs, refs = refs[:pair_parts], refs[pair_parts:]
    term_refs, refs = refs[:terms], refs[terms:]
    grad_out_ref, after_cross_ref, after_self_ref, queries_ref, gains_ref = refs[:5]
    out_ref, self_branch_ref, query_branch_ref, cross_branch_ref, gain_ref = refs[5:10]
    mixed_grad_refs, refs = refs[10 : 10 + count], refs[10 + count :]
    own_pairs_ref, pair_grad_refs = refs[0], refs[1:-6]
    wide_ref, narrow_ref, query_ref, corner_ref, pairs_ref, pair_total_ref = refs[-6:]
    width = queries_ref.shape[2]
    stride = matrix_refs[0].shape[1] // 3
    matrices = fill_corner(count, matrix_refs, scalars_ref, corner_ref)
    fill_pairs(count, block, pair_refs, pairs_ref)
    order = [scalars_ref[i] for i in range(count)]
    relative = [scalars_ref[count + j] for j in range(count)]
    length = scalars_ref[2 * count + 1]
    spans = [slice(a * width, (a + 1) * width) for a in range(count)]

    def back(branch_ref, group):
        columns = slice(group * stride, group * stride + width)
        total = dot_nt(branch_ref[order[0]], matrices[0][:, columns])
        for i in range(1, count):
            total = total + dot_nt(branch_ref[order[i]], matrices[i][:, columns])
        return total

    def divide(values):
        for a in range(count):
            narrow_ref[a] = values[:, spans[a]].astype(BF16)

    grad, grad_gain = norm_back(
        after_cross_ref[...], gains_ref[2:3, :], add_terms(count, term_refs)
    )
    gain_ref[1:2, :] = grad_gain
    wide_ref[...] = grad + grad_out_ref[...].astype(F32)
    cross_branch_ref[...] = wide_ref[...].astype(BF16)
    divide(wide_ref[...])
    divide(back(narrow_ref, 2))

    keys_rows = pairs_ref.shape[1]
    valid = lax.broadcasted_iota(jnp.int32, (keys_rows, 1), 0) < length
    pair_stride = pairs_ref.shape[2] // 2
    if pair_stride > width:
        for g in range(2):
            pair_total_ref[:, g * pair_stride + width : (g + 1) * pair_stride] = jnp.zeros(
                (keys_rows, pair_stride - width), F32
            )
    for j in range(count):
        for h in range(width // head_size):
            at = slice(h * head_size, (h + 1) * head_size)
            values_at = slice(pair_stride + h * head_size, pair_stride + (h + 1) * head_size)
            grad_q, grad_k, grad_v = attention_back(
                queries_ref[j, :, at],
                pairs_ref[j, :, at],
                pairs_ref[j, :, values_at],
                narrow_ref[relative[j], :, at],
                valid,
                head_size,
            )
            query_ref[relative[j], :, at] = grad_q.astype(BF16)
            pair_total_ref[:, at] = grad_k
            pair_total_ref[:, values_at] = grad_v
        if j == 0:
            own_pairs_ref[...] = pair_total_ref[...]
        else:
            pair_grad_refs[j - 1][...] = pair_total_ref[...].astype(BF16)
    for a in range(count):
        query_branch_ref[:, spans[a]] = query_ref[a]
    grad, grad_gain = norm_back(after_self_ref[...], gains_ref[1:2, :], back(query_ref, 1))
    gain_ref[0:1, :] = grad_gain
    out_ref[...] = grad + wide_ref[...]
    self_branch_ref[...] = out_ref[...].astype(BF16)
    divide(out_ref[...])
    divide(back(narrow_ref, 0))
    for j in range(count):
        mixed_grad_refs[j][...] = narrow_ref[relative[j]]


def middle_backward(
    block, scalars, matrices, pairs, terms, grad_out, after_cross, after_self, queries, gains, head_size, deps=()
):
    count, rows, width = queries.shape
    columns = count * width
    branch = ((rows, columns), BF16)
    text = pairs_scratch(count, pairs)
    keys_rows, pair_columns = text.shape[1:]
    found = call(
        functools.partial(
            middle_backward_kernel, block, count, len(matrices), len(pairs), len(terms), head_size
        ),
        [((rows, columns), F32), branch, branch, branch, ((2, columns), F32)]
        + [((rows, width), BF16)] * count
        + [((keys_rows, pair_columns), F32)]
        + [((keys_rows, pair_columns), BF16)] * (count - 1),
        [
            pltpu.VMEM((rows, columns), F32),
            pltpu.VMEM((count, rows, width), BF16),
            pltpu.VMEM((count, rows, width), BF16),
            corner_scratch(count, matrices),
            text,
            pltpu.VMEM((keys_rows, pair_columns), F32),
        ],
        37,
        *matrices,
        *pairs,
        *terms,
        grad_out,
        after_cross,
        after_self,
        queries,
        gains,
        scalars=scalars,
        deps=deps,
    )
    found = list(found)
    return found[:5] + [found[5 : 5 + count], found[5 + count], found[6 + count :]]


def mlp_up_kernel(count, parts, *refs):
    part_refs, (up_ref, rows_ref, up_rows_ref, activated_ref) = refs[:parts], refs[parts:]
    start = 0
    for ref in part_refs:
        rows_ref[start : start + ref.shape[0], :] = ref[...]
        start += ref.shape[0]
    rows = start // count
    for j in range(count):
        at = slice(j * rows, (j + 1) * rows)
        values = dot_nn(rows_ref[at, :], up_ref[...])
        up_rows_ref[at, :] = values
        inner = GELU_SCALE * (values + 0.044715 * (values * values * values))
        activated_ref[at, :] = (0.5 * values * (1.0 + jnp.tanh(inner))).astype(BF16)


def mlp_up(parts, up, count, deps=()):
    total, columns, hidden = sum(m.shape[0] for m in parts), up.shape[0], up.shape[1]
    return call(
        functools.partial(mlp_up_kernel, count, len(parts)),
        [((total, columns), BF16), ((total, hidden), F32), ((total, hidden), BF16)],
        [],
        15,
        *parts,
        up,
        deps=deps,
    )


def mlp_down_kernel(count, activated_ref, down_ref, own_ref, *piece_refs):
    rows = own_ref.shape[0]
    for j in range(count - 1, -1, -1):
        found = dot_nn(activated_ref[j * rows : (j + 1) * rows, :], down_ref[...])
        if j == 0:
            own_ref[...] = found
        else:
            put_pieces(piece_refs, count, j, found)


def mlp_down(activated, down, count, deps=()):
    rows, columns = activated.shape[0] // count, down.shape[1]
    found = call(
        functools.partial(mlp_down_kernel, count),
        [((rows, columns), F32)] + piece_shapes(count, rows, columns),
        [],
        11,
        activated,
        down,
        deps=deps,
    )
    return found[0], list(found[1:])


def stack_kernel(*refs):
    start = 0
    for ref in refs[:-1]:
        refs[-1][start : start + ref.shape[0], :] = ref[...]
        start += ref.shape[0]


def stack_rows(parts, deps=()):
    shape = (sum(m.shape[0] for m in parts), parts[0].shape[1])
    return call(stack_kernel, [(shape, parts[0].dtype)], [], 3, *parts, deps=deps)[0]


def mlp_backward_kernel(count, parts, *refs):
    part_refs, refs = refs[:parts], refs[parts:]
    up_rows_ref, up_ref, down_ref, rows_ref, grad_up_ref, own_ref = refs[:6]
    piece_refs = refs[6:]
    start = 0
    for ref in part_refs:
        rows_ref[start : start + ref.shape[0], :] = ref[...]
        start += ref.shape[0]
    rows = start // count
    for j in range(count - 1, -1, -1):
        at = slice(j * rows, (j + 1) * rows)
        grad = dot_nt(rows_ref[at, :], down_ref[...])
        values = up_rows_ref[at, :]
        square = values * values
        bent = jnp.tanh(GELU_SCALE * (values + 0.044715 * (values * square)))
        slope = 0.5 * (1.0 + bent) + 0.5 * values * (1.0 - bent * bent) * (
            GELU_SCALE * (1.0 + 3.0 * 0.044715 * square)
        )
        grad_up_ref[at, :] = (grad * slope).astype(BF16)
        found = dot_nt(grad_up_ref[at, :], up_ref[...])
        if j == 0:
            own_ref[...] = found
        else:
            put_pieces(piece_refs, count, j, found)


def mlp_backward(parts, up_rows, up, down, count, deps=()):
    total, columns, hidden = sum(m.shape[0] for m in parts), up.shape[0], up.shape[1]
    rows = total // count
    found = call(
        functools.partial(mlp_backward_kernel, count, len(parts)),
        [((total, columns), BF16), ((total, hidden), BF16), ((rows, columns), F32)]
        + piece_shapes(count, rows, columns),
        [],
        22,
        *parts,
        up_rows,
        up,
        down,
        deps=deps,
    )
    return list(found[:3]) + [list(found[3:])]


def outer_kernel(groups, *refs):
    rows_refs, branch_refs, out_ref = refs[:groups], refs[groups : 2 * groups], refs[2 * groups]
    width = branch_refs[0].shape[1]
    for g in range(groups):
        turned = rows_refs[g][...].T
        out_ref[:, g * width : (g + 1) * width] = dot_nn(turned, branch_refs[g][...]).astype(BF16)


def outer(rows, branches, deps=()):
    groups, columns = len(rows), rows[0].shape[1]
    shape = (columns, groups * branches[0].shape[1])
    return call(
        functools.partial(outer_kernel, groups),
        [(shape, BF16)],
        [],
        3.5 * groups,
        *rows,
        *branches,
        deps=deps,
    )[0]


def fold_kernel(count, groups, scalars_ref, shard_ref, own_ref, *refs):
    piece_refs, stack_ref = refs[:-1], refs[-1]
    stride = stack_ref.shape[2] // groups
    width = shard_ref.shape[1] // (groups * count)
    for a in range(count):
        for g in range(groups):
            low = (g * count + a) * width
            stack_ref[a, :, g * stride : g * stride + width] = shard_ref[:, low : low + width]
            if stride > width:
                stack_ref[a, :, g * stride + width : (g + 1) * stride] = jnp.zeros(
                    (shard_ref.shape[0], stride - width), BF16
                )
    for j in range(count):
        values = stack_ref[scalars_ref[count + j]]
        if j == 0:
            own_ref[...] = values.astype(F32)
        else:
            put_pieces(piece_refs, count, j, values)


def fold(scalars, shard, groups):
    count = lax.axis_size("seq")
    rows = shard.shape[0]
    columns = groups * padded_width(shard.shape[1] // (groups * count))
    found = call(
        functools.partial(fold_kernel, count, groups),
        [((rows, columns), F32)] + piece_shapes(count, rows, columns),
        [pltpu.VMEM((count, rows, columns), BF16)],
        3,
        shard,
        scalars=scalars,
    )
    return found[0], list(found[1:])


def sum_kernel(count, terms, *refs):
    refs[terms][...] = add_terms(count, refs[:terms]).astype(BF16)


def sum_terms(terms):
    count = lax.axis_size("seq")
    shape = terms[0].shape
    return call(functools.partial(sum_kernel, count, len(terms)), [(shape, BF16)], [], 2, *terms)[0]


def joined_stats(first, second):
    count = first.shape[1] + second.shape[1]
    mean = (jnp.sum(first, axis=1, keepdims=True) + jnp.sum(second, axis=1, keepdims=True)) / count
    first, second = first - mean, second - mean
    var = (
        jnp.sum(first * first, axis=1, keepdims=True)
        + jnp.sum(second * second, axis=1, keepdims=True)
    ) / count
    scale = lax.rsqrt(var + NORM_EPSILON)
    return first * scale, second * scale, scale


def skip_forward_kernel(count, terms, matrix_ref, *refs):
    term_refs, refs = refs[:terms], refs[terms:]
    residual_ref, second_ref, gains_ref, next_ref, shift_ref = refs[:5]
    first_ref, joined_ref, out_ref, norm_ref = refs[5:]
    columns = first_ref.shape[1]
    first_ref[...] = residual_ref[...] + add_terms(count, term_refs)
    first, second, _ = joined_stats(first_ref[...], second_ref[...].astype(F32))
    joined_ref[:, :columns] = (first * gains_ref[0:1, :]).astype(BF16)
    joined_ref[:, columns:] = (second * gains_ref[1:2, :]).astype(BF16)
    out_ref[...] = dot_nn(joined_ref[...], matrix_ref[...])
    normed = norm_stats(out_ref[...])[0] * next_ref[0:1, :] + shift_ref[...]
    norm_ref[...] = normed.astype(BF16)


def skip_forward(matrix, terms, residual, second, gains, next_gains, shift, deps=()):
    rows, columns = residual.shape
    return call(
        functools.partial(skip_forward_kernel, lax.axis_size("seq"), len(terms)),
        [
            ((rows, columns), F32),
            ((rows, 2 * columns), BF16),
            ((rows, columns), F32),
            ((rows, columns), BF16),
        ],
        [],
        11,
        matrix,
        *terms,
        residual,
        second,
        gains,
        next_gains,
        shift[None],
        deps=deps,
    )


def skip_backward_kernel(count, terms, matrix_ref, *refs):
    term_refs, refs = refs[:terms], refs[terms:]
    hidden_ref, next_ref, residual_ref, first_ref, second_ref, gains_ref = refs[:6]
    branch_ref, grad_first_ref, grad_second_ref, vectors_ref, round_ref = refs[6:]
    columns = first_ref.shape[1]
    grad_norm = add_terms(count, term_refs)
    vectors_ref[0:1, :] = jnp.sum(grad_norm, axis=0, keepdims=True)
    grad, grad_gain = norm_back(hidden_ref[...], next_ref[0:1, :], grad_norm)
    vectors_ref[1:2, :] = grad_gain
    branch_ref[...] = (grad + residual_ref[...]).astype(BF16)
    grad_first_ref[...] = dot_nt(branch_ref[...], matrix_ref[:columns, :])
    grad_second_ref[...] = dot_nt(branch_ref[...], matrix_ref[columns:, :])
    first, second, scale = joined_stats(first_ref[...], second_ref[...].astype(F32))
    vectors_ref[2:3, :] = jnp.sum(grad_first_ref[...] * first, axis=0, keepdims=True)
    vectors_ref[3:4, :] = jnp.sum(grad_second_ref[...] * second, axis=0, keepdims=True)
    grad_first = grad_first_ref[...] * gains_ref[0:1, :]
    grad_second = grad_second_ref[...] * gains_ref[1:2, :]
    mean = (
        jnp.sum(grad_first, axis=1, keepdims=True) + jnp.sum(grad_second, axis=1, keepdims=True)
    ) / (2 * columns)
    inner = (
        jnp.sum(grad_first * first, axis=1, keepdims=True)
        + jnp.sum(grad_second * second, axis=1, keepdims=True)
    ) / (2 * columns)
    grad_first_ref[...] = scale * (grad_first - mean - first * inner)
    grad_second_ref[...] = scale * (grad_second - mean - second * inner)
    round_ref[...] = grad_first_ref[...].astype(BF16)


def skip_backward(
    matrix, terms, hidden, next_gains, residual, first, second, gains, deps=()
):
    rows, columns = first.shape
    return call(
        functools.partial(skip_backward_kernel, lax.axis_size("seq"), len(terms)),
        [
            ((rows, columns), BF16),
            ((rows, columns), F32),
            ((rows, columns), F32),
            ((4, columns), F32),
            ((rows, columns), BF16),
        ],
        [],
        15,
        matrix,
        *terms,
        hidden,
        next_gains,
        residual,
        first,
        second,
        gains,
        deps=deps,
    )


def open_backward_kernel(count, terms, *refs):
    term_refs, refs = refs[:terms], refs[terms:]
    hidden_ref, gains_ref, residual_ref, out_ref, vectors_ref = refs
    grad_norm = add_terms(count, term_refs)
    vectors_ref[0:1, :] = jnp.sum(grad_norm, axis=0, keepdims=True)
    grad, grad_gain = norm_back(hidden_ref[...].astype(F32), gains_ref[0:1, :], grad_norm)
    vectors_ref[1:2, :] = grad_gain
    out_ref[...] = grad + residual_ref[...]


def open_backward(terms, hidden, gains, residual, deps=()):
    count = lax.axis_size("seq")
    return call(
        functools.partial(open_backward_kernel, count, len(terms)),
        [(residual.shape, F32), ((2, residual.shape[1]), F32)],
        [],
        5,
        *terms,
        hidden,
        gains,
        residual,
        deps=deps,
    )


def close_kernel(count, terms, *refs):
    refs[terms + 1][...] = (refs[terms][...] + add_terms(count, refs[:terms])).astype(BF16)


def close_forward(terms, residual, deps=()):
    count = lax.axis_size("seq")
    (found,) = call(
        functools.partial(close_kernel, count, len(terms)),
        [(residual.shape, BF16)],
        [],
        3,
        *terms,
        residual,
        deps=deps,
    )
    return found


def pack_kernel(count, *refs):
    start = 0
    for ref in refs[:count]:
        refs[count][: ref.shape[0], start : start + ref.shape[1]] = ref[...]
        start += ref.shape[1]


def pack(shards, deps=()):
    rows = -(-max(m.shape[0] for m in shards) // 16) * 16
    shape = (rows, sum(m.shape[1] for m in shards))
    return call(functools.partial(pack_kernel, len(shards)), [(shape, BF16)], [], 3, *shards, deps=deps)[0]


def settle_kernel(count, parts, plan, scalars_ref, *refs):
    block_refs, refs = refs[:parts], refs[parts:]
    outs = sum(entry[3] for entry in plan)
    out_refs, stack_ref = refs[-outs - 1 : -1], refs[-1]
    ordered = parts == 1
    for j in range(count):
        if ordered:
            held = stack_ref.shape[1]
            stack_ref[j] = block_refs[0][j * held : (j + 1) * held, :]
            continue
        owner = scalars_ref[count + j]
        if j == count - 1 and parts > count:
            cut = block_refs[j].shape[0]
            stack_ref[owner, :cut] = block_refs[j][...]
            stack_ref[owner, cut:] = block_refs[j + 1][...]
        else:
            stack_ref[owner] = block_refs[j][...]
    place = 0
    for first, rows, groups, pieces, width, stride in plan:
        if not groups:
            for a in range(count):
                found = stack_ref[a, :rows, first : first + width]
                out_refs[place][0, a * rows : (a + 1) * rows, :] = found.astype(F32)
        for p in range(pieces):
            for g in range(groups):
                for a in range(count):
                    low = first + (p * groups + g) * stride
                    at = (g * count + a) * width
                    found = stack_ref[a, :rows, low : low + width]
                    out_refs[place + p][0, :, at : at + width] = found.astype(F32)
        place += pieces


def settle(scalars, blocks, plan, layer, layer_count, before):
    count = lax.axis_size("seq")
    shapes = []
    for _, rows, groups, pieces, width, _ in plan:
        shapes += [(rows, groups * count * width) if groups else (count * rows, width)] * pieces
    held = [] if before is None else list(before)
    inputs = [pl.BlockSpec(memory_space=pltpu.VMEM)] * len(blocks)
    inputs += [pl.BlockSpec(memory_space=pl.ANY)] * len(held)
    found = pl.pallas_call(
        functools.partial(settle_kernel, count, len(blocks), plan),
        grid=(1,),
        out_shape=[jax.ShapeDtypeStruct((layer_count,) + shape, F32) for shape in shapes],
        in_specs=[pl.BlockSpec(memory_space=pltpu.SMEM)] + inputs,
        out_specs=[pl.BlockSpec((1,) + shape, lambda i: (layer, 0, 0)) for shape in shapes],
        scratch_shapes=[
            pltpu.VMEM(
                (count, blocks[0].shape[0] // (count if len(blocks) == 1 else 1), blocks[0].shape[1]),
                BF16,
            )
        ],
        input_output_aliases={1 + len(blocks) + i: i for i in range(len(held))},
        compiler_params=pltpu.CompilerParams(vmem_limit_bytes=VMEM_LIMIT),
        cost_estimate=pl.CostEstimate(flops=8_000_000_000, bytes_accessed=1000, transcendentals=0),
    )(scalars, *blocks, *held)
    return list(found)


def plan_of(entries):
    plan, first = [], 0
    for shard, groups, pieces, width in entries:
        rows, columns = shard.shape
        stride = columns // (groups * pieces) if groups else columns
        plan.append((first, rows, groups, pieces, width, stride))
        first += columns
    return tuple(plan)


def finish(scalars, entries, layer, layer_count, before=None, deps=()):
    blocks = gather_parts(pack([entry[0] for entry in entries], deps))
    return settle(scalars, blocks, plan_of(entries), layer, layer_count, before)


def swap_seq(block, bits):
    seq_count = lax.axis_size("seq")
    return lax.ppermute(block, "seq", [(i, i ^ bits) for i in range(seq_count)])


def swap_fsdp(block, bits):
    fsdp_count = lax.axis_size("fsdp")
    return lax.ppermute(block, "fsdp", [(i, i ^ bits) for i in range(fsdp_count)])


def swap_core(block):
    return swap_fsdp(block, 1)


def swap_by_core(block, even_bits, odd_bits):
    seq_count, fsdp_count = lax.axis_size("seq"), lax.axis_size("fsdp")
    pairs = []
    for s in range(seq_count):
        for f in range(fsdp_count):
            other = s ^ (odd_bits if f % 2 else even_bits)
            pairs.append((s * fsdp_count + f, other * fsdp_count + f))
    return lax.ppermute(block, ("seq", "fsdp"), pairs)


def add_bf16(*terms):
    total = terms[0].astype(F32)
    for term in terms[1:]:
        total = total + term.astype(F32)
    return total.astype(BF16)


def scatter_first(pieces):
    seq_count = lax.axis_size("seq")
    if seq_count != 4:
        return [swap_seq(m, j + 1) for j, m in enumerate(pieces)]
    return [swap_seq(pieces[0], 1), swap_seq(pieces[1], 2), pieces[2], pieces[3]]


def scatter_last(own, first, ready=None):
    seq_count = lax.axis_size("seq")
    if seq_count != 4:
        return [own] + first
    from_x, from_y, x_bottom, y_top = first
    if ready is not None:
        from_x, from_y = gate([from_x, from_y], ready)
    cut, rest = y_top.shape[0], x_bottom.shape[0]
    to_y, to_x = add_bf16(y_top, from_x[:cut]), add_bf16(x_bottom, from_y[:rest])
    return [own, from_x, from_y, swap_seq(to_x, 1), swap_seq(to_y, 2)]


def exchange_rel(blocks):
    return [blocks[0]] + [swap_seq(blocks[j], j) for j in range(1, len(blocks))]


def gather_first(block):
    seq_count = lax.axis_size("seq")
    if seq_count != 4:
        return [block] + [swap_seq(block, j) for j in range(1, seq_count)]
    return [block, swap_seq(block, 1), swap_seq(block, 2)]


def gather_last(first, ready=None):
    seq_count = lax.axis_size("seq")
    if seq_count != 4:
        return first
    block, from_x, from_y = first
    if ready is not None:
        from_x, from_y = gate([from_x, from_y], ready)
    cut = cut_of(block.shape[0])
    return [block, from_x, from_y, swap_seq(from_y[:cut], 1), swap_seq(from_x[cut:], 2)]


def gather_parts(block):
    return gather_last(gather_first(block))


def list_order():
    s, seq_count = lax.axis_index("seq"), lax.axis_size("seq")
    if seq_count != 4:
        return [s ^ j for j in range(seq_count)]
    odd = lax.axis_index("fsdp") % 2
    return [s, s ^ (1 + odd), s ^ (2 - odd), s ^ 3]


def spread_first(block):
    seq_count = lax.axis_size("seq")
    if seq_count != 4:
        return [block] + [swap_seq(block, j) for j in range(1, seq_count)]
    return [block, swap_by_core(block, 1, 2)]


def spread_slice(blocks, ready):
    if lax.axis_size("seq") != 4:
        return blocks
    block, first = blocks
    if ready is not None:
        (first,) = gate([first], ready)
    half = block.shape[0] // 2
    odd = lax.axis_index("fsdp") % 2
    return [block, first, lax.dynamic_slice_in_dim(first, odd * half, half, 0)]


def spread_last(blocks, part_ready):
    seq_count = lax.axis_size("seq")
    if seq_count != 4:
        return blocks
    block, first, part = blocks
    part = swap_by_core(part, 2, 1)
    other = swap_core(first)
    if part_ready is not None:
        (part,) = gate([part], part_ready)
    return [block, first, other, part, swap_core(part)]


def own_part(matrix, groups, padded):
    s, seq_count = lax.axis_index("seq"), lax.axis_size("seq")
    width = matrix.shape[1] // (groups * seq_count)
    parts = [
        jnp.pad(
            lax.dynamic_slice_in_dim(matrix, (g * seq_count + s) * width, width, 1),
            ((0, 0), (0, padded - width)),
        )
        for g in range(groups)
    ]
    return jnp.concatenate(parts, axis=1)


def gather_fsdp(shard):
    return lax.all_gather(shard, "fsdp", axis=0, tiled=True)


def scatter_fsdp(full):
    return lax.psum_scatter(full.astype(BF16), "fsdp", scatter_dimension=0, tiled=True)


def layer_forward(parts, hidden, scalars, gains, shift, pairs, weights, normed, deps, hold=None):
    lead_part, square_parts, up_part = weights
    seq_count = lax.axis_size("seq")
    tok_rows, model_width = hidden.shape
    head_size, width = model_width // H, model_width // seq_count
    first_all, triples, mixed = self_forward(
        parts,
        lead_part,
        gains,
        shift,
        head_size,
        seq_count,
        width,
        normed,
        (square_parts[-1],) + deps,
    )
    mixed_rel = exchange_rel(mixed)
    square_parts = spread_last(square_parts, mixed_rel[1:])
    held = []
    if hold is not None:
        held = gate([hold], [square_parts[-1]])
    self_tokens, after_self, cross_norm, queries, cross_tokens, after_cross, mlp_norm = (
        middle_forward(
            int(normed), scalars, mixed_rel, square_parts, pairs, hidden, gains, head_size, held
        )
    )
    mlp_parts = gather_parts(mlp_norm)
    mlp_all, up_rows, activated = mlp_up(mlp_parts, up_part, seq_count)
    saved = (
        first_all,
        triples,
        self_tokens,
        after_self,
        cross_norm,
        queries,
        cross_tokens,
        after_cross,
        mlp_all,
        up_rows,
        activated,
    )
    return (saved, square_parts, mlp_parts, held)


def sum_shard(scalars, shard, groups, ready=None):
    if ready is not None:
        (shard,) = gate([shard], ready)
    own, pieces = fold(scalars, shard, groups)
    return sum_terms(scatter_last(own, scatter_first(pieces)))


def qkv_own(layer, qkv):
    return own_part(qkv[layer], 3, padded_width(qkv.shape[2] // (3 * lax.axis_size("seq"))))


def squares_own(layer, *stacks):
    padded = padded_width(stacks[0].shape[2] // lax.axis_size("seq"))
    return jnp.concatenate([own_part(m[layer], 1, padded) for m in stacks], axis=1)


def gather_rest(layer, up, down):
    s, seq_count, fsdp_count = lax.axis_index("seq"), lax.axis_size("seq"), lax.axis_size("fsdp")
    rows = down.shape[1] // seq_count
    return (
        gather_fsdp(own_part(up[layer], fsdp_count, up.shape[2] // (fsdp_count * seq_count))),
        gather_fsdp(lax.dynamic_slice_in_dim(down[layer], s * rows, rows, 0)),
    )


def sum_vectors(vectors):
    bits = 1
    while bits < lax.axis_size("seq"):
        vectors = vectors + swap_seq(vectors, bits)
        bits *= 2
    found, bits = vectors[None], 1
    while bits < lax.axis_size("fsdp"):
        found = jnp.concatenate([found, swap_fsdp(found, bits)], axis=0)
        bits *= 2
    return found


def body(
    latents,
    skip_input,
    text_tokens,
    text_lengths,
    condition,
    cotangent,
    mod_weight,
    norm_gains,
    qkv_weight,
    query_weight,
    text_kv_weight,
    self_out_weight,
    cross_out_weight,
    up_weight,
    down_weight,
    skip_gain,
    skip_weight,
):
    seq_count, fsdp_count = lax.axis_size("seq"), lax.axis_size("fsdp")
    s, f = lax.axis_index("seq"), lax.axis_index("fsdp")
    _, tok_rows, model_width = latents.shape
    width = model_width // seq_count
    shard_rows = mod_weight.shape[1]
    text_count = text_tokens.shape[1]
    padded = -(-text_count // 32) * 32
    text_rows = jnp.pad(text_tokens[0], ((0, padded - text_count), (0, 0)))
    scalars = jnp.stack(
        [*list_order(), *[s ^ j for j in range(seq_count)], f % 2, text_lengths[0]]
    ).astype(jnp.int32)

    gain_rows = jnp.concatenate(
        [norm_gains.reshape(-1, shard_rows), skip_gain.reshape(-1, shard_rows)], axis=0
    )
    small = jnp.concatenate(
        [
            condition.reshape(fsdp_count, 1, shard_rows),
            jnp.broadcast_to(gain_rows[None], (fsdp_count,) + gain_rows.shape),
        ],
        axis=1,
    ).astype(F32)
    latent_parts = gather_parts(latents[0])
    (small,) = gate([small], latent_parts[-2:])
    small = lax.all_to_all(small, "fsdp", 0, 0, tiled=True)
    cond_part = small[:, 0]
    gains = jnp.swapaxes(small[:, 1:7], 0, 1).reshape(2, 3, model_width)
    skip_gains = small[:, 7:].reshape(2, model_width)
    silu_part = jax.nn.silu(cond_part)
    shift_terms = jnp.einsum("br,lrd->bld", silu_part, mod_weight.astype(F32), precision=EXACT)
    padded_columns = padded_width(width)
    kv_both = gather_fsdp(
        jnp.concatenate([own_part(text_kv_weight[l], 2, padded_columns) for l in range(2)], axis=1)
    )
    pair_hops = gather_first(dot_nn(text_rows, kv_both).astype(BF16))
    pairs_all = gather_last(pair_hops)
    (shift_terms,) = gate([shift_terms], pair_hops[1:])
    shifts = jnp.sum(lax.all_to_all(shift_terms, "fsdp", 0, 0, tiled=True), axis=0)

    square_stacks = (self_out_weight, query_weight, cross_out_weight)
    rest_stacks = (up_weight, down_weight)
    head_size = model_width // H

    square_shard, qkv_shard = gate(
        [squares_own(0, *square_stacks), qkv_own(0, qkv_weight)], [kv_both] + latent_parts[-2:]
    )
    square_first, lead_first = gather_fsdp(square_shard), gather_fsdp(qkv_shard)
    up_first, down_first = gather_rest(0, *rest_stacks)
    spread_squares = spread_slice(spread_first(gate([square_first], pair_hops[1:])[0]), [shifts])
    (lead_first,) = gate([lead_first], [shifts])
    pairs_first, pairs_second = pairs_all, pairs_all
    saved_first, squares_first, mlp_parts, _ = layer_forward(
        latent_parts,
        latents[0],
        scalars,
        gains[0],
        shifts[0],
        pairs_first,
        (lead_first, spread_squares, up_first),
        False,
        (),
    )
    own, pieces = mlp_down(saved_first[10], down_first, seq_count)
    first = scatter_first(pieces)
    terms = scatter_last(own, first)

    skip_matrix = gather_fsdp(skip_weight)
    square_second = gather_fsdp(gate([squares_own(1, *square_stacks)], mlp_parts[-2:])[0])
    lead_second = gather_fsdp(qkv_own(1, qkv_weight))
    (square_second,) = gate([square_second], first[:2])
    squares_second = spread_first(square_second)
    first_out, joined_norm, skip_out, second_norm = skip_forward(
        skip_matrix,
        terms,
        saved_first[7],
        skip_input[0],
        skip_gains,
        gains[1],
        shifts[1],
        (square_second,),
    )

    up_second, down_second = gather_rest(1, *rest_stacks)
    out_hops = gather_first(gate([cotangent[0]], [skip_out])[0])
    second_parts = gather_parts(second_norm)
    squares_second = spread_slice(squares_second, second_parts[1:3])
    saved_second, squares_second, mlp_parts, _ = layer_forward(
        second_parts,
        skip_out,
        scalars,
        gains[1],
        shifts[1],
        pairs_second,
        (lead_second, squares_second, up_second),
        True,
        (),
    )
    out_parts = gather_last(out_hops, [squares_second[-1]])
    out_all = stack_rows(out_parts, (mlp_parts[1],))

    held = {}

    def block_backward(rows, grad_out, saved, block, weights, early, hooks):
        lead_matrix, square_parts, pairs, up_part, down_part = weights
        grad_down = dot_tn(saved[10], early).astype(BF16) if early is not None else None
        found_all, grad_up_rows, own, pieces = mlp_backward(
            rows,
            saved[9],
            up_part,
            down_part,
            seq_count,
            hooks[0] + ((grad_down,) if early is not None else ()),
        )
        first = scatter_first(gate(pieces, hooks[3]) if hooks[3] else pieces)
        terms = scatter_last(own, first)
        held["hops"] = first[:2]
        if early is None:
            grad_down = dot_tn(saved[10], found_all).astype(BF16)
            (grad_down,) = gate([grad_down], first[:2])
        grad_up = dot_tn(saved[8], grad_up_rows).astype(BF16)
        (grad_up,) = gate([grad_up], first[:2])
        down_shard, up_shard = scatter_fsdp(grad_down), scatter_fsdp(grad_up)
        (
            grad_after_self,
            self_branch,
            query_branch,
            cross_branch,
            gain_grads,
            mixed_grads,
            own_pairs,
            pair_blocks,
        ) = middle_backward(
            block,
            scalars,
            square_parts,
            pairs,
            terms,
            grad_out,
            saved[7],
            saved[3],
            saved[5],
            gains[block],
            head_size,
            (grad_down, grad_up) + hooks[1](grad_up_rows, terms),
        )
        mixed_rel = exchange_rel(mixed_grads)
        pair_blocks = gate(pair_blocks, mixed_rel[1:])
        pair_terms = [swap_seq(m, j + 1) for j, m in enumerate(pair_blocks)]
        grad_triples, own, pieces = self_backward(
            saved[1],
            mixed_rel,
            lead_matrix,
            head_size,
            (down_shard,) + hooks[2](mixed_rel[1]),
        )
        pair_terms = gate(pair_terms, [grad_triples])
        first = scatter_first(gate(pieces, pair_terms))
        terms = scatter_last(own, first)
        grad_qkv = dot_tn(saved[0], grad_triples).astype(BF16)
        (grad_qkv,) = gate([grad_qkv], first[:2])
        held["last"] = first[:2]
        squares = outer(
            [saved[2], saved[4], saved[6]],
            [self_branch, query_branch, cross_branch],
            (grad_triples,),
        )
        held["outer"] = squares
        square_shard = scatter_fsdp(gate([squares], first[:2])[0])
        pair_terms = gate(pair_terms, first[:2])
        grad_pairs = add_bf16(own_pairs, *pair_terms)
        kv_part = kv_both[:, 2 * block * padded_columns : 2 * (block + 1) * padded_columns]
        grad_text = dot_nt(grad_pairs, kv_part)
        kv_shard = scatter_fsdp(dot_tn(text_rows, grad_pairs))
        return (
            terms,
            grad_after_self,
            gain_grads,
            grad_text,
            square_shard,
            grad_qkv,
            grad_triples,
            (scatter_fsdp(grad_qkv), kv_shard, up_shard, down_shard),
        )

    def second_own(grad_up_rows, terms):
        own, pieces = mlp_down(saved_second[10], down_second, seq_count, (grad_up_rows,))
        pieces = gate(pieces, terms[-2:])
        held["own"], held["own_hops"] = own, scatter_first(pieces)
        return tuple(pieces)

    def second_sum(ready):
        held["ready"] = ready
        return tuple(held["own_hops"][:2])

    (
        terms,
        grad_after_self,
        gain_grads,
        text_second,
        square_shard,
        grad_qkv,
        grad_triples,
        (qkv_shard, kv_shard, up_shard, down_shard),
    ) = block_backward(
        [out_all],
        cotangent[0],
        saved_second,
        1,
        (lead_second, squares_second, pairs_second, up_second, down_second),
        out_all,
        ((), second_own, second_sum, ()),
    )
    skip_branch, grad_first_out, grad_skip, vectors, first_round = skip_backward(
        skip_matrix,
        terms,
        skip_out,
        gains[1],
        grad_after_self,
        first_out,
        skip_input[0],
        skip_gains,
        (grad_qkv, up_shard, held["outer"]),
    )
    vectors_second = jnp.concatenate([vectors[:2], gain_grads, vectors[2:]], axis=0)
    first_hops = gather_first(first_round)
    first_parts = gather_last(first_hops)
    own_terms = scatter_last(held["own"], held["own_hops"], terms[-2:])
    output = close_forward(own_terms, saved_second[7])
    skip_outer = outer([joined_norm], [skip_branch], tuple(first_hops[1:]))
    skip_shard = scatter_fsdp(skip_outer)

    def entries(layer):
        qkv, square, kv, up, down = layer
        return (
            [
                (up, fsdp_count, 1, up.shape[1] // fsdp_count),
                (down, 0, 1, down.shape[1]),
            ],
            [(qkv, 3, 1, width), (square, 1, 3, width), (kv, 2, 1, width)],
        )

    early, _ = entries((qkv_shard, qkv_shard, kv_shard, up_shard, down_shard))
    def first_middle(grad_up_rows, terms):
        del grad_up_rows, terms
        return (kv_shard,)

    def first_self(ready):
        del ready
        return (qkv_shard,)

    (
        terms,
        grad_after_self,
        gain_grads,
        text_first,
        first_square_shard,
        grad_qkv,
        grad_triples,
        (first_qkv_shard, first_kv_shard, first_up_shard, first_down_shard),
    ) = block_backward(
        first_parts,
        grad_first_out,
        saved_first,
        0,
        (lead_first, squares_first, pairs_first, up_first, down_first),
        None,
        (
            (skip_outer,),
            first_middle,
            first_self,
            (),
        ),
    )
    early_hops = gather_first(pack([entry[0] for entry in early], held["last"]))
    square_sum = sum_shard(scalars, square_shard, 3, held["last"])
    skip_sum = sum_shard(scalars, skip_shard, 1, held["last"])
    early, _ = entries(
        (first_qkv_shard, first_qkv_shard, first_kv_shard, first_up_shard, first_down_shard)
    )
    first_hops = gather_first(pack([entry[0] for entry in early], terms[-2:]))
    grad_latents, vectors = open_backward(
        terms, latents[0], gains[0], grad_after_self, (grad_qkv,)
    )
    vectors_first = jnp.concatenate([vectors, gain_grads], axis=0)
    first_layer = (
        first_qkv_shard,
        sum_shard(scalars, first_square_shard, 3),
        first_kv_shard,
        first_up_shard,
        first_down_shard,
    )

    early_done = settle(
        scalars,
        gather_last(early_hops),
        plan_of(early),
        1,
        2,
        None,
    )
    _, late = entries((qkv_shard, square_sum, kv_shard, up_shard, down_shard))
    late_done = finish(scalars, late, 1, 2, None)
    early, late = entries(first_layer)
    grad_up, grad_down = settle(
        scalars, gather_last(first_hops), plan_of(early), 0, 2, early_done
    )
    grad_qkv, grad_self_out, grad_query, grad_cross_out, grad_kv = finish(
        scalars, late, 0, 2, late_done
    )
    (grad_skip_weight,) = finish(scalars, [(skip_sum, 1, 1, width)], 0, 1)

    sums = sum_vectors(jnp.concatenate([vectors_first, vectors_second], axis=0))
    first_sums, second_sums = sums[:, :4], sums[:, 4:]
    shift_grads = jnp.stack([first_sums[:, 0], second_sums[:, 0]], axis=1)
    gain_sums = jnp.stack([first_sums[:, 1:4].sum(axis=0), second_sums[:, 1:4].sum(axis=0)])
    grad_norm_gains = lax.dynamic_slice_in_dim(gain_sums, f * shard_rows, shard_rows, 2)
    grad_skip_gain = lax.dynamic_slice_in_dim(
        second_sums[:, 4:].sum(axis=0).reshape(-1), f * skip_gain.shape[0], skip_gain.shape[0], 0
    )
    turned = jnp.stack(
        [lax.dynamic_index_in_dim(silu_part, f ^ j, 0, False) for j in range(fsdp_count)]
    )
    grad_mod = jnp.einsum("br,bld->lrd", turned, shift_grads, precision=EXACT)
    grad_silu = jnp.einsum("bld,lrd->br", shift_grads, mod_weight.astype(F32), precision=EXACT)
    grad_silu = jnp.stack(
        [lax.dynamic_index_in_dim(grad_silu, f ^ j, 0, False) for j in range(fsdp_count)]
    )
    _, silu_pull = jax.vjp(jax.nn.silu, cond_part)
    grad_cond_part = silu_pull(grad_silu)[0]
    grad_condition = lax.all_to_all(grad_cond_part, "fsdp", 0, 0, tiled=True).reshape(1, -1)

    text_sum, bits = text_first + text_second, 1
    while bits < seq_count:
        text_sum = text_sum + swap_seq(text_sum.astype(BF16), bits).astype(F32)
        bits *= 2
    return (
        output[None],
        grad_latents[None],
        grad_skip[None],
        text_sum[None, :text_count],
        grad_condition,
        grad_mod,
        grad_norm_gains,
        grad_qkv,
        grad_query,
        grad_kv,
        grad_self_out,
        grad_cross_out,
        grad_up,
        grad_down,
        grad_skip_gain,
        grad_skip_weight[0],
    )


def solution(mesh):
    in_specs = (
        P("fsdp", "seq", None),
        P("fsdp", "seq", None),
        P("fsdp", None, None),
        P("fsdp"),
        P("fsdp", None),
        P("fsdp", "seq", None),
        P(None, "fsdp", None),
        P(None, None, "fsdp"),
        P(None, "fsdp", None),
        P(None, "fsdp", None),
        P(None, "fsdp", None),
        P(None, "fsdp", None),
        P(None, "fsdp", None),
        P(None, "fsdp", None),
        P(None, "fsdp", None),
        P("fsdp"),
        P("fsdp", None),
    )
    out_specs = (
        P("fsdp", "seq", None),
        P("fsdp", "seq", None),
        P("fsdp", "seq", None),
        P("fsdp", None, None),
        P("fsdp", None),
        P(None, "fsdp", None),
        P(None, None, "fsdp"),
        P(None, "fsdp", None),
        P(None, "fsdp", None),
        P(None, "fsdp", None),
        P(None, "fsdp", None),
        P(None, "fsdp", None),
        P(None, "fsdp", None),
        P(None, "fsdp", None),
        P("fsdp"),
        P("fsdp", None),
    )
    return jax.shard_map(body, mesh=mesh, in_specs=in_specs, out_specs=out_specs, check_vma=False)
```

```python
import functools
import math

import jax
import jax.numpy as jnp
from jax import lax
from jax.experimental import pallas as pl
from jax.experimental.pallas import tpu as pltpu
from jax.sharding import PartitionSpec as P

H = 16
NORM_EPSILON = 1e-06
EXACT = lax.Precision.HIGHEST
BF16 = jnp.bfloat16
F32 = jnp.float32
LOG2_E = 1.4426950408889634
GELU_SCALE = math.sqrt(2.0 / math.pi)
VMEM_LIMIT = 56 * 1024 * 1024


def dot_nn(a, b):
    return lax.dot_general(a, b, (((1,), (0,)), ((), ())), preferred_element_type=F32)


def dot_nt(a, b):
    return lax.dot_general(a, b, (((1,), (1,)), ((), ())), preferred_element_type=F32)


def dot_tn(a, b):
    return lax.dot_general(a, b, (((0,), (0,)), ((), ())), preferred_element_type=F32)


def padded_width(width):
    return -(-width // 128) * 128


def call(kernel, outs, scratch, micros, *operands, scalars=None, deps=(), outside=()):
    specs = [
        pl.BlockSpec(memory_space=pl.ANY if i in outside else pltpu.VMEM)
        for i in range(len(operands))
    ]
    if scalars is not None:
        specs = [pl.BlockSpec(memory_space=pltpu.SMEM)] + specs
        operands = (scalars,) + tuple(operands)
    used, held = len(operands), len(deps)

    def run(*refs):
        kernel(*refs[:used], *refs[used + held :])

    return pl.pallas_call(
        run,
        name=getattr(kernel, "func", kernel).__name__,
        out_shape=tuple(jax.ShapeDtypeStruct(s, d) for s, d in outs),
        in_specs=specs + [pl.BlockSpec(memory_space=pl.ANY)] * held,
        out_specs=tuple([pl.BlockSpec(memory_space=pltpu.VMEM)] * len(outs)),
        scratch_shapes=scratch,
        compiler_params=pltpu.CompilerParams(vmem_limit_bytes=VMEM_LIMIT),
        cost_estimate=pl.CostEstimate(
            flops=int(micros * 1000), bytes_accessed=1000, transcendentals=0
        ),
    )(*operands, *deps)


def gate_kernel(*refs):
    del refs


def gate(values, deps):
    values, deps = list(values), list(deps)
    return list(
        pl.pallas_call(
            gate_kernel,
            out_shape=tuple(jax.ShapeDtypeStruct(m.shape, m.dtype) for m in values),
            in_specs=[pl.BlockSpec(memory_space=pl.ANY)] * (len(values) + len(deps)),
            out_specs=tuple([pl.BlockSpec(memory_space=pl.ANY)] * len(values)),
            input_output_aliases={i: i for i in range(len(values))},
            cost_estimate=pl.CostEstimate(flops=1000, bytes_accessed=1000, transcendentals=0),
        )(*values, *deps)
    )


def cut_of(rows):
    return rows // 32 * 16


def piece_shapes(count, rows, columns):
    if count != 4:
        return [((rows, columns), BF16)] * (count - 1)
    cut = cut_of(rows)
    return [((m, columns), BF16) for m in (2 * cut, 2 * (rows - cut), rows - cut, cut)]


def put_pieces(refs, count, block, values):
    if count != 4:
        refs[block - 1][...] = values.astype(BF16)
        return
    to_x, to_y, x_bottom, y_top = refs
    rows = values.shape[0]
    cut = cut_of(rows)
    top, bottom = values[:cut].astype(BF16), values[cut:].astype(BF16)
    if block == 1:
        to_x[cut:, :] = top
        x_bottom[...] = bottom
    elif block == 2:
        y_top[...] = top
        to_y[rows - cut :, :] = bottom
    else:
        to_x[:cut, :] = top
        to_y[: rows - cut, :] = bottom


def add_terms(count, refs):
    total = refs[0][...].astype(F32)
    if count != 4:
        for ref in refs[1:]:
            total = total + ref[...].astype(F32)
        return total
    from_x, from_y, x_bottom, y_top = [ref[...] for ref in refs[1:]]
    cut, rest = y_top.shape[0], x_bottom.shape[0]
    by_x = jnp.concatenate([from_x[cut:], x_bottom], axis=0)
    by_y = jnp.concatenate([y_top, from_y[rest:]], axis=0)
    return total + by_x.astype(F32) + by_y.astype(F32)


def norm_stats(values):
    mean = jnp.mean(values, axis=1, keepdims=True)
    centered = values - mean
    var = jnp.mean(centered * centered, axis=1, keepdims=True)
    scale = lax.rsqrt(var + NORM_EPSILON)
    return centered * scale, scale


def norm_back(values, gain, grad):
    unit, scale = norm_stats(values)
    grad_unit = grad * gain
    inner = jnp.mean(grad_unit * unit, axis=1, keepdims=True)
    grad_values = scale * (grad_unit - jnp.mean(grad_unit, axis=1, keepdims=True) - unit * inner)
    return grad_values, jnp.sum(grad * unit, axis=0, keepdims=True)


def self_forward_kernel(count, parts, head_size, normed, *refs):
    part_refs, refs = refs[:parts], refs[parts:]
    weight_ref, gains_ref, shift_ref = refs[:3]
    rows_ref, triples_ref = refs[3:5]
    mixed_refs, (held_ref, done) = refs[5:-2], refs[-2:]
    copy = pltpu.make_async_copy(weight_ref.at[:, : held_ref.shape[1]], held_ref, done)
    copy.start()
    stride = held_ref.shape[1] // 3
    rows, width = mixed_refs[0].shape
    factor = LOG2_E / math.sqrt(head_size)
    start = 0
    for ref in part_refs:
        values = ref[...]
        if not normed:
            unit, _ = norm_stats(values.astype(F32))
            values = (unit * gains_ref[0:1, :] + shift_ref[...]).astype(BF16)
        rows_ref[start : start + ref.shape[0], :] = values
        start += ref.shape[0]
    copy.wait()
    for j in range(count):
        at = slice(j * rows, (j + 1) * rows)
        triples_ref[at, :] = dot_nn(rows_ref[at, :], held_ref[...]).astype(BF16)
    for j in range(count):
        at = slice(j * rows, (j + 1) * rows)
        for h in range(width // head_size):
            low = h * head_size
            q = triples_ref[at, low : low + head_size]
            k = triples_ref[:, stride + low : stride + low + head_size]
            v = triples_ref[:, 2 * stride + low : 2 * stride + low + head_size]
            scores = dot_nt(q, k)
            top = jnp.max(scores, axis=1, keepdims=True)
            weights = jnp.exp2((scores - top) * factor)
            total = jnp.sum(weights, axis=1, keepdims=True)
            mixed = dot_nn(weights.astype(BF16), v) * (1.0 / total)
            mixed_refs[j][:, low : low + head_size] = mixed.astype(BF16)


def self_forward(parts, weight, gains, shift, head_size, count, width, normed, deps=()):
    total = sum(m.shape[0] for m in parts)
    columns = parts[0].shape[1]
    held = (columns, 3 * padded_width(width))
    found = call(
        functools.partial(self_forward_kernel, count, len(parts), head_size, normed),
        [((total, columns), BF16), ((total, held[1]), BF16)]
        + [((total // count, width), BF16)] * count,
        [pltpu.VMEM(held, BF16), pltpu.SemaphoreType.DMA],
        24,
        *parts,
        weight,
        gains,
        shift[None],
        deps=deps,
        outside=(len(parts),),
    )
    return found[0], found[1], list(found[2:])


def attention_back(q, k, v, grad, valid, head_size):
    factor = LOG2_E / math.sqrt(head_size)
    scores = dot_nt(k, q)
    if valid is not None:
        scores = jnp.where(valid, scores, -1e30)
    top = jnp.max(scores, axis=0, keepdims=True)
    weights = jnp.exp2((scores - top) * factor)
    weights = weights * (1.0 / jnp.sum(weights, axis=0, keepdims=True))
    grad_weights = dot_nt(v, grad)
    delta = jnp.sum(grad_weights * weights, axis=0, keepdims=True)
    grad_scores = (weights * (grad_weights - delta)).astype(BF16)
    scale = 1.0 / math.sqrt(head_size)
    return (
        dot_tn(grad_scores, k) * scale,
        dot_nn(grad_scores, q) * scale,
        dot_nn(weights.astype(BF16), grad),
    )


def self_backward_kernel(count, head_size, step, triples_ref, *refs):
    grad_refs, (weight_ref, out_ref, own_ref) = refs[:count], refs[count : count + 3]
    piece_refs, (keys_ref, values_ref, held_ref, done) = refs[count + 3 : -4], refs[-4:]
    copy = pltpu.make_async_copy(weight_ref.at[:, : held_ref.shape[1]], held_ref, done)
    copy.start()
    total = triples_ref.shape[0]
    rows, width = grad_refs[0].shape
    stride = held_ref.shape[1] // 3
    for h in range(width // head_size):
        low = h * head_size
        k = triples_ref[:, stride + low : stride + low + head_size]
        v = triples_ref[:, 2 * stride + low : 2 * stride + low + head_size]
        for i in range(total // step):
            at = slice(i * step, (i + 1) * step)
            inside = (i * step) % rows
            q = triples_ref[at, low : low + head_size]
            grad = grad_refs[i * step // rows][inside : inside + step, low : low + head_size]
            grad_q, grad_k, grad_v = attention_back(q, k, v, grad, None, head_size)
            out_ref[at, low : low + head_size] = grad_q.astype(BF16)
            if i == 0:
                keys_ref[...] = grad_k
                values_ref[...] = grad_v
            else:
                keys_ref[...] += grad_k
                values_ref[...] += grad_v
        out_ref[:, stride + low : stride + low + head_size] = keys_ref[...].astype(BF16)
        out_ref[:, 2 * stride + low : 2 * stride + low + head_size] = values_ref[...].astype(BF16)
    if stride > width:
        for g in range(3):
            out_ref[:, g * stride + width : (g + 1) * stride] = jnp.zeros((total, stride - width), BF16)
    copy.wait()
    for j in range(count):
        found = dot_nt(out_ref[j * rows : (j + 1) * rows, :], held_ref[...])
        if j == 0:
            own_ref[...] = found
        else:
            put_pieces(piece_refs, count, j, found)


def self_backward(triples, grads, weight, head_size, deps=()):
    count = len(grads)
    total, rows, columns = triples.shape[0], grads[0].shape[0], weight.shape[0]
    step = min(256, rows)
    found = call(
        functools.partial(self_backward_kernel, count, head_size, step),
        [(triples.shape, BF16), ((rows, columns), F32)] + piece_shapes(count, rows, columns),
        [
            pltpu.VMEM((total, head_size), F32),
            pltpu.VMEM((total, head_size), F32),
            pltpu.VMEM((columns, triples.shape[1]), BF16),
            pltpu.SemaphoreType.DMA,
        ],
        32,
        triples,
        *grads,
        weight,
        deps=deps,
        outside=(1 + count,),
    )
    return found[0], found[1], list(found[2:])


def fill_corner(count, matrix_refs, scalars_ref, corner_ref):
    if len(matrix_refs) == count:
        return list(matrix_refs)
    odd = scalars_ref[2 * count]
    half = matrix_refs[-1].shape[0]
    corner_ref[pl.ds(pl.multiple_of(odd * half, half), half), :] = matrix_refs[-2][...]
    corner_ref[pl.ds(pl.multiple_of((1 - odd) * half, half), half), :] = matrix_refs[-1][...]
    return list(matrix_refs[:-2]) + [corner_ref]


def corner_scratch(count, matrices):
    rows, columns = matrices[0].shape
    return pltpu.VMEM((rows, columns) if len(matrices) > count else (16, 128), BF16)


def fill_pairs(count, block, pair_refs, pairs_ref):
    padded, columns = pairs_ref.shape[1:]
    place = 0
    for ref in pair_refs:
        j, low = divmod(place, padded)
        pairs_ref[j, low : low + ref.shape[0], :] = ref[:, block * columns : (block + 1) * columns]
        place += ref.shape[0]


def middle_forward_kernel(block, count, matrix_parts, pair_parts, head_size, scalars_ref, *refs):
    mixed_refs, refs = refs[:count], refs[count:]
    matrix_refs, refs = refs[:matrix_parts], refs[matrix_parts:]
    pair_refs, refs = refs[:pair_parts], refs[pair_parts:]
    hidden_ref, gains_ref = refs[:2]
    (self_ref, after_self_ref, norm_ref, queries_ref, cross_ref, after_cross_ref) = refs[2:8]
    mlp_ref = refs[8]
    wide_ref, narrow_ref, corner_ref, pairs_ref = refs[-4:]
    width = mixed_refs[0].shape[1]
    stride = matrix_refs[0].shape[1] // 3
    matrices = fill_corner(count, matrix_refs, scalars_ref, corner_ref)
    fill_pairs(count, block, pair_refs, pairs_ref)
    order = [scalars_ref[i] for i in range(count)]
    relative = [scalars_ref[count + j] for j in range(count)]
    length = scalars_ref[2 * count + 1]
    spans = [slice(a * width, (a + 1) * width) for a in range(count)]

    for j in range(count):
        narrow_ref[relative[j]] = mixed_refs[j][...]
    for a in range(count):
        self_ref[:, spans[a]] = narrow_ref[a]
    tokens = self_ref[...]
    for i in range(count):
        wide_ref[order[i]] = dot_nn(tokens, matrices[i][:, :width])
    for a in range(count):
        after_self_ref[:, spans[a]] = hidden_ref[:, spans[a]].astype(F32) + wide_ref[a]
    normed = (norm_stats(after_self_ref[...])[0] * gains_ref[1:2, :]).astype(BF16)
    norm_ref[...] = normed
    for i in range(count):
        found = dot_nn(normed, matrices[i][:, stride : stride + width])
        queries_ref[order[i] ^ relative[0]] = found.astype(BF16)

    factor = LOG2_E / math.sqrt(head_size)
    keys_rows = pairs_ref.shape[1]
    valid = lax.broadcasted_iota(jnp.int32, (1, keys_rows), 1) < length
    pair_stride = pairs_ref.shape[2] // 2
    for j in range(count):
        for h in range(width // head_size):
            at = slice(h * head_size, (h + 1) * head_size)
            values_at = slice(pair_stride + h * head_size, pair_stride + (h + 1) * head_size)
            scores = dot_nt(queries_ref[j, :, at], pairs_ref[j, :, at])
            scores = jnp.where(valid, scores, -1e30)
            top = jnp.max(scores, axis=1, keepdims=True)
            weights = jnp.exp2((scores - top) * factor)
            total = jnp.sum(weights, axis=1, keepdims=True)
            mixed = dot_nn(weights.astype(BF16), pairs_ref[j, :, values_at]) * (1.0 / total)
            narrow_ref[relative[j], :, at] = mixed.astype(BF16)
    for a in range(count):
        cross_ref[:, spans[a]] = narrow_ref[a]
    tokens = cross_ref[...]
    for i in range(count):
        wide_ref[order[i]] = dot_nn(tokens, matrices[i][:, 2 * stride : 2 * stride + width])
    for a in range(count):
        after_cross_ref[:, spans[a]] = after_self_ref[:, spans[a]] + wide_ref[a]
    mlp_ref[...] = (norm_stats(after_cross_ref[...])[0] * gains_ref[2:3, :]).astype(BF16)


def pairs_scratch(count, pairs):
    return pltpu.VMEM(
        (count, sum(m.shape[0] for m in pairs) // count, pairs[0].shape[1] // 2), BF16
    )


def middle_forward(block, scalars, mixed, matrices, pairs, hidden, gains, head_size, deps=()):
    count = len(mixed)
    rows, columns = hidden.shape
    width = columns // count
    return call(
        functools.partial(
            middle_forward_kernel, block, count, len(matrices), len(pairs), head_size
        ),
        [
            ((rows, columns), BF16),
            ((rows, columns), F32),
            ((rows, columns), BF16),
            ((count, rows, width), BF16),
            ((rows, columns), BF16),
            ((rows, columns), F32),
            ((rows, columns), BF16),
        ],
        [
            pltpu.VMEM((count, rows, width), F32),
            pltpu.VMEM((count, rows, width), BF16),
            corner_scratch(count, matrices),
            pairs_scratch(count, pairs),
        ],
        23,
        *mixed,
        *matrices,
        *pairs,
        hidden,
        gains,
        scalars=scalars,
        deps=deps,
    )


def middle_backward_kernel(block, count, matrix_parts, pair_parts, terms, head_size, scalars_ref, *refs):
    matrix_refs, refs = refs[:matrix_parts], refs[matrix_parts:]
    pair_refs, refs = refs[:pair_parts], refs[pair_parts:]
    term_refs, refs = refs[:terms], refs[terms:]
    grad_out_ref, after_cross_ref, after_self_ref, queries_ref, gains_ref = refs[:5]
    out_ref, self_branch_ref, query_branch_ref, cross_branch_ref, gain_ref = refs[5:10]
    mixed_grad_refs, refs = refs[10 : 10 + count], refs[10 + count :]
    own_pairs_ref, pair_grad_refs = refs[0], refs[1:-6]
    wide_ref, narrow_ref, query_ref, corner_ref, pairs_ref, pair_total_ref = refs[-6:]
    width = queries_ref.shape[2]
    stride = matrix_refs[0].shape[1] // 3
    matrices = fill_corner(count, matrix_refs, scalars_ref, corner_ref)
    fill_pairs(count, block, pair_refs, pairs_ref)
    order = [scalars_ref[i] for i in range(count)]
    relative = [scalars_ref[count + j] for j in range(count)]
    length = scalars_ref[2 * count + 1]
    spans = [slice(a * width, (a + 1) * width) for a in range(count)]

    def back(branch_ref, group):
        columns = slice(group * stride, group * stride + width)
        total = dot_nt(branch_ref[order[0]], matrices[0][:, columns])
        for i in range(1, count):
            total = total + dot_nt(branch_ref[order[i]], matrices[i][:, columns])
        return total

    def divide(values):
        for a in range(count):
            narrow_ref[a] = values[:, spans[a]].astype(BF16)

    grad, grad_gain = norm_back(
        after_cross_ref[...], gains_ref[2:3, :], add_terms(count, term_refs)
    )
    gain_ref[1:2, :] = grad_gain
    wide_ref[...] = grad + grad_out_ref[...].astype(F32)
    cross_branch_ref[...] = wide_ref[...].astype(BF16)
    divide(wide_ref[...])
    divide(back(narrow_ref, 2))

    keys_rows = pairs_ref.shape[1]
    valid = lax.broadcasted_iota(jnp.int32, (keys_rows, 1), 0) < length
    pair_stride = pairs_ref.shape[2] // 2
    if pair_stride > width:
        for g in range(2):
            pair_total_ref[:, g * pair_stride + width : (g + 1) * pair_stride] = jnp.zeros(
                (keys_rows, pair_stride - width), F32
            )
    for j in range(count):
        for h in range(width // head_size):
            at = slice(h * head_size, (h + 1) * head_size)
            values_at = slice(pair_stride + h * head_size, pair_stride + (h + 1) * head_size)
            grad_q, grad_k, grad_v = attention_back(
                queries_ref[j, :, at],
                pairs_ref[j, :, at],
                pairs_ref[j, :, values_at],
                narrow_ref[relative[j], :, at],
                valid,
                head_size,
            )
            query_ref[relative[j], :, at] = grad_q.astype(BF16)
            pair_total_ref[:, at] = grad_k
            pair_total_ref[:, values_at] = grad_v
        if j == 0:
            own_pairs_ref[...] = pair_total_ref[...]
        else:
            pair_grad_refs[j - 1][...] = pair_total_ref[...].astype(BF16)
    for a in range(count):
        query_branch_ref[:, spans[a]] = query_ref[a]
    grad, grad_gain = norm_back(after_self_ref[...], gains_ref[1:2, :], back(query_ref, 1))
    gain_ref[0:1, :] = grad_gain
    out_ref[...] = grad + wide_ref[...]
    self_branch_ref[...] = out_ref[...].astype(BF16)
    divide(out_ref[...])
    divide(back(narrow_ref, 0))
    for j in range(count):
        mixed_grad_refs[j][...] = narrow_ref[relative[j]]


def middle_backward(
    block, scalars, matrices, pairs, terms, grad_out, after_cross, after_self, queries, gains, head_size, deps=()
):
    count, rows, width = queries.shape
    columns = count * width
    branch = ((rows, columns), BF16)
    text = pairs_scratch(count, pairs)
    keys_rows, pair_columns = text.shape[1:]
    found = call(
        functools.partial(
            middle_backward_kernel, block, count, len(matrices), len(pairs), len(terms), head_size
        ),
        [((rows, columns), F32), branch, branch, branch, ((2, columns), F32)]
        + [((rows, width), BF16)] * count
        + [((keys_rows, pair_columns), F32)]
        + [((keys_rows, pair_columns), BF16)] * (count - 1),
        [
            pltpu.VMEM((rows, columns), F32),
            pltpu.VMEM((count, rows, width), BF16),
            pltpu.VMEM((count, rows, width), BF16),
            corner_scratch(count, matrices),
            text,
            pltpu.VMEM((keys_rows, pair_columns), F32),
        ],
        37,
        *matrices,
        *pairs,
        *terms,
        grad_out,
        after_cross,
        after_self,
        queries,
        gains,
        scalars=scalars,
        deps=deps,
    )
    found = list(found)
    return found[:5] + [found[5 : 5 + count], found[5 + count], found[6 + count :]]


def mlp_up_kernel(count, parts, *refs):
    part_refs, (up_ref, rows_ref, up_rows_ref, activated_ref) = refs[:parts], refs[parts:]
    start = 0
    for ref in part_refs:
        rows_ref[start : start + ref.shape[0], :] = ref[...]
        start += ref.shape[0]
    rows = start // count
    for j in range(count):
        at = slice(j * rows, (j + 1) * rows)
        values = dot_nn(rows_ref[at, :], up_ref[...])
        up_rows_ref[at, :] = values
        inner = GELU_SCALE * (values + 0.044715 * (values * values * values))
        activated_ref[at, :] = (0.5 * values * (1.0 + jnp.tanh(inner))).astype(BF16)


def mlp_up(parts, up, count, deps=()):
    total, columns, hidden = sum(m.shape[0] for m in parts), up.shape[0], up.shape[1]
    return call(
        functools.partial(mlp_up_kernel, count, len(parts)),
        [((total, columns), BF16), ((total, hidden), F32), ((total, hidden), BF16)],
        [],
        15,
        *parts,
        up,
        deps=deps,
    )


def mlp_down_kernel(count, activated_ref, down_ref, own_ref, *piece_refs):
    rows = own_ref.shape[0]
    for j in range(count - 1, -1, -1):
        found = dot_nn(activated_ref[j * rows : (j + 1) * rows, :], down_ref[...])
        if j == 0:
            own_ref[...] = found
        else:
            put_pieces(piece_refs, count, j, found)


def mlp_down(activated, down, count, deps=()):
    rows, columns = activated.shape[0] // count, down.shape[1]
    found = call(
        functools.partial(mlp_down_kernel, count),
        [((rows, columns), F32)] + piece_shapes(count, rows, columns),
        [],
        11,
        activated,
        down,
        deps=deps,
    )
    return found[0], list(found[1:])


def stack_kernel(*refs):
    start = 0
    for ref in refs[:-1]:
        refs[-1][start : start + ref.shape[0], :] = ref[...]
        start += ref.shape[0]


def stack_rows(parts, deps=()):
    shape = (sum(m.shape[0] for m in parts), parts[0].shape[1])
    return call(stack_kernel, [(shape, parts[0].dtype)], [], 3, *parts, deps=deps)[0]


def mlp_backward_kernel(count, parts, *refs):
    part_refs, refs = refs[:parts], refs[parts:]
    up_rows_ref, up_ref, down_ref, rows_ref, grad_up_ref, own_ref = refs[:6]
    piece_refs = refs[6:]
    start = 0
    for ref in part_refs:
        rows_ref[start : start + ref.shape[0], :] = ref[...]
        start += ref.shape[0]
    rows = start // count
    for j in range(count - 1, -1, -1):
        at = slice(j * rows, (j + 1) * rows)
        grad = dot_nt(rows_ref[at, :], down_ref[...])
        values = up_rows_ref[at, :]
        square = values * values
        bent = jnp.tanh(GELU_SCALE * (values + 0.044715 * (values * square)))
        slope = 0.5 * (1.0 + bent) + 0.5 * values * (1.0 - bent * bent) * (
            GELU_SCALE * (1.0 + 3.0 * 0.044715 * square)
        )
        grad_up_ref[at, :] = (grad * slope).astype(BF16)
        found = dot_nt(grad_up_ref[at, :], up_ref[...])
        if j == 0:
            own_ref[...] = found
        else:
            put_pieces(piece_refs, count, j, found)


def mlp_backward(parts, up_rows, up, down, count, deps=()):
    total, columns, hidden = sum(m.shape[0] for m in parts), up.shape[0], up.shape[1]
    rows = total // count
    found = call(
        functools.partial(mlp_backward_kernel, count, len(parts)),
        [((total, columns), BF16), ((total, hidden), BF16), ((rows, columns), F32)]
        + piece_shapes(count, rows, columns),
        [],
        22,
        *parts,
        up_rows,
        up,
        down,
        deps=deps,
    )
    return list(found[:3]) + [list(found[3:])]


def outer_kernel(groups, *refs):
    rows_refs, branch_refs, out_ref = refs[:groups], refs[groups : 2 * groups], refs[2 * groups]
    width = branch_refs[0].shape[1]
    for g in range(groups):
        turned = rows_refs[g][...].T
        out_ref[:, g * width : (g + 1) * width] = dot_nn(turned, branch_refs[g][...]).astype(BF16)


def outer(rows, branches, deps=()):
    groups, columns = len(rows), rows[0].shape[1]
    shape = (columns, groups * branches[0].shape[1])
    return call(
        functools.partial(outer_kernel, groups),
        [(shape, BF16)],
        [],
        3.5 * groups,
        *rows,
        *branches,
        deps=deps,
    )[0]


def spread_outer_kernel(count, groups, half, scalars_ref, *refs):
    rows_refs, branch_refs, refs = refs[:groups], refs[groups : 2 * groups], refs[2 * groups :]
    out_refs, (turned_ref, stack_ref) = refs[:-2], refs[-2:]
    width = stack_ref.shape[2]
    stride = padded_width(width)
    odd = scalars_ref[2 * count]
    for g in range(groups):
        at = slice(g * stride, g * stride + width)
        turned_ref[...] = rows_refs[g][...].T
        for a in range(count):
            stack_ref[a] = branch_refs[g][:, a * width : (a + 1) * width]
        out_refs[0][:, at] = dot_nn(turned_ref[...], stack_ref[scalars_ref[0]]).astype(BF16)
        for i in range(1, count):
            if not half:
                out_refs[i][:, at] = dot_nn(turned_ref[...], stack_ref[scalars_ref[i]]).astype(BF16)
                continue
            for k in range(2):
                low = pl.multiple_of((odd if k == 0 else 1 - odd) * half, half)
                found = dot_nn(turned_ref[pl.ds(low, half), :], stack_ref[scalars_ref[i]])
                out_refs[2 * i - 1 + k][:, at] = found.astype(BF16)
    if stride > width:
        for ref in out_refs:
            for g in range(groups):
                ref[:, g * stride + width : (g + 1) * stride] = jnp.zeros(
                    (ref.shape[0], stride - width), BF16
                )


def spread_outer(scalars, rows, branches, deps=()):
    count = lax.axis_size("seq")
    tokens, width = branches[0].shape[0], branches[0].shape[1] // count
    groups, columns = len(rows), rows[0].shape[1]
    stride = padded_width(width)
    half = columns // 2 if count == 4 else 0
    shapes = [((columns, groups * stride), BF16)]
    if half:
        shapes += [((half, groups * stride), BF16)] * (2 * (count - 1))
    else:
        shapes = shapes * count
    return list(
        call(
            functools.partial(spread_outer_kernel, count, groups, half),
            shapes,
            [pltpu.VMEM((columns, tokens), BF16), pltpu.VMEM((count, tokens, width), BF16)],
            3.5 * groups,
            *rows,
            *branches,
            scalars=scalars,
            deps=deps,
        )
    )


def join_kernel(count, scalars_ref, own_ref, mine_ref, other_ref, out_ref):
    odd = scalars_ref[2 * count]
    half = mine_ref.shape[0]
    for ref, place in ((mine_ref, odd), (other_ref, 1 - odd)):
        at = pl.ds(pl.multiple_of(place * half, half), half)
        out_ref[at, :] = (own_ref[at, :].astype(F32) + ref[...].astype(F32)).astype(BF16)


def join_halves(scalars, own, mine, other):
    count = lax.axis_size("seq")
    (found,) = call(
        functools.partial(join_kernel, count),
        [(own.shape, BF16)],
        [],
        4,
        own,
        mine,
        other,
        scalars=scalars,
    )
    return found


def fold_kernel(count, groups, scalars_ref, shard_ref, own_ref, *refs):
    piece_refs, stack_ref = refs[:-1], refs[-1]
    stride = stack_ref.shape[2] // groups
    width = shard_ref.shape[1] // (groups * count)
    for a in range(count):
        for g in range(groups):
            low = (g * count + a) * width
            stack_ref[a, :, g * stride : g * stride + width] = shard_ref[:, low : low + width]
            if stride > width:
                stack_ref[a, :, g * stride + width : (g + 1) * stride] = jnp.zeros(
                    (shard_ref.shape[0], stride - width), BF16
                )
    for j in range(count):
        values = stack_ref[scalars_ref[count + j]]
        if j == 0:
            own_ref[...] = values.astype(F32)
        else:
            put_pieces(piece_refs, count, j, values)


def fold(scalars, shard, groups):
    count = lax.axis_size("seq")
    rows = shard.shape[0]
    columns = groups * padded_width(shard.shape[1] // (groups * count))
    found = call(
        functools.partial(fold_kernel, count, groups),
        [((rows, columns), F32)] + piece_shapes(count, rows, columns),
        [pltpu.VMEM((count, rows, columns), BF16)],
        3,
        shard,
        scalars=scalars,
    )
    return found[0], list(found[1:])


def sum_kernel(count, terms, *refs):
    refs[terms][...] = add_terms(count, refs[:terms]).astype(BF16)


def sum_terms(terms):
    count = lax.axis_size("seq")
    shape = terms[0].shape
    return call(functools.partial(sum_kernel, count, len(terms)), [(shape, BF16)], [], 2, *terms)[0]


def joined_stats(first, second):
    count = first.shape[1] + second.shape[1]
    mean = (jnp.sum(first, axis=1, keepdims=True) + jnp.sum(second, axis=1, keepdims=True)) / count
    first, second = first - mean, second - mean
    var = (
        jnp.sum(first * first, axis=1, keepdims=True)
        + jnp.sum(second * second, axis=1, keepdims=True)
    ) / count
    scale = lax.rsqrt(var + NORM_EPSILON)
    return first * scale, second * scale, scale


def skip_forward_kernel(count, terms, matrix_ref, *refs):
    term_refs, refs = refs[:terms], refs[terms:]
    residual_ref, second_ref, gains_ref, next_ref, shift_ref = refs[:5]
    first_ref, joined_ref, out_ref, norm_ref = refs[5:]
    columns = first_ref.shape[1]
    first_ref[...] = residual_ref[...] + add_terms(count, term_refs)
    first, second, _ = joined_stats(first_ref[...], second_ref[...].astype(F32))
    joined_ref[:, :columns] = (first * gains_ref[0:1, :]).astype(BF16)
    joined_ref[:, columns:] = (second * gains_ref[1:2, :]).astype(BF16)
    out_ref[...] = dot_nn(joined_ref[...], matrix_ref[...])
    normed = norm_stats(out_ref[...])[0] * next_ref[0:1, :] + shift_ref[...]
    norm_ref[...] = normed.astype(BF16)


def skip_forward(matrix, terms, residual, second, gains, next_gains, shift, deps=()):
    rows, columns = residual.shape
    return call(
        functools.partial(skip_forward_kernel, lax.axis_size("seq"), len(terms)),
        [
            ((rows, columns), F32),
            ((rows, 2 * columns), BF16),
            ((rows, columns), F32),
            ((rows, columns), BF16),
        ],
        [],
        11,
        matrix,
        *terms,
        residual,
        second,
        gains,
        next_gains,
        shift[None],
        deps=deps,
    )


def skip_backward_kernel(count, terms, matrix_ref, *refs):
    term_refs, refs = refs[:terms], refs[terms:]
    hidden_ref, next_ref, residual_ref, first_ref, second_ref, gains_ref = refs[:6]
    branch_ref, grad_first_ref, grad_second_ref, vectors_ref, round_ref = refs[6:]
    columns = first_ref.shape[1]
    grad_norm = add_terms(count, term_refs)
    vectors_ref[0:1, :] = jnp.sum(grad_norm, axis=0, keepdims=True)
    grad, grad_gain = norm_back(hidden_ref[...], next_ref[0:1, :], grad_norm)
    vectors_ref[1:2, :] = grad_gain
    branch_ref[...] = (grad + residual_ref[...]).astype(BF16)
    grad_first_ref[...] = dot_nt(branch_ref[...], matrix_ref[:columns, :])
    grad_second_ref[...] = dot_nt(branch_ref[...], matrix_ref[columns:, :])
    first, second, scale = joined_stats(first_ref[...], second_ref[...].astype(F32))
    vectors_ref[2:3, :] = jnp.sum(grad_first_ref[...] * first, axis=0, keepdims=True)
    vectors_ref[3:4, :] = jnp.sum(grad_second_ref[...] * second, axis=0, keepdims=True)
    grad_first = grad_first_ref[...] * gains_ref[0:1, :]
    grad_second = grad_second_ref[...] * gains_ref[1:2, :]
    mean = (
        jnp.sum(grad_first, axis=1, keepdims=True) + jnp.sum(grad_second, axis=1, keepdims=True)
    ) / (2 * columns)
    inner = (
        jnp.sum(grad_first * first, axis=1, keepdims=True)
        + jnp.sum(grad_second * second, axis=1, keepdims=True)
    ) / (2 * columns)
    grad_first_ref[...] = scale * (grad_first - mean - first * inner)
    grad_second_ref[...] = scale * (grad_second - mean - second * inner)
    round_ref[...] = grad_first_ref[...].astype(BF16)


def skip_backward(
    matrix, terms, hidden, next_gains, residual, first, second, gains, deps=()
):
    rows, columns = first.shape
    return call(
        functools.partial(skip_backward_kernel, lax.axis_size("seq"), len(terms)),
        [
            ((rows, columns), BF16),
            ((rows, columns), F32),
            ((rows, columns), F32),
            ((4, columns), F32),
            ((rows, columns), BF16),
        ],
        [],
        15,
        matrix,
        *terms,
        hidden,
        next_gains,
        residual,
        first,
        second,
        gains,
        deps=deps,
    )


def open_backward_kernel(count, terms, *refs):
    term_refs, refs = refs[:terms], refs[terms:]
    hidden_ref, gains_ref, residual_ref, out_ref, vectors_ref = refs
    grad_norm = add_terms(count, term_refs)
    vectors_ref[0:1, :] = jnp.sum(grad_norm, axis=0, keepdims=True)
    grad, grad_gain = norm_back(hidden_ref[...].astype(F32), gains_ref[0:1, :], grad_norm)
    vectors_ref[1:2, :] = grad_gain
    out_ref[...] = grad + residual_ref[...]


def open_backward(terms, hidden, gains, residual, deps=()):
    count = lax.axis_size("seq")
    return call(
        functools.partial(open_backward_kernel, count, len(terms)),
        [(residual.shape, F32), ((2, residual.shape[1]), F32)],
        [],
        5,
        *terms,
        hidden,
        gains,
        residual,
        deps=deps,
    )


def close_kernel(count, terms, *refs):
    refs[terms + 1][...] = (refs[terms][...] + add_terms(count, refs[:terms])).astype(BF16)


def close_forward(terms, residual, deps=()):
    count = lax.axis_size("seq")
    (found,) = call(
        functools.partial(close_kernel, count, len(terms)),
        [(residual.shape, BF16)],
        [],
        3,
        *terms,
        residual,
        deps=deps,
    )
    return found


def pack_kernel(count, *refs):
    start = 0
    for ref in refs[:count]:
        refs[count][: ref.shape[0], start : start + ref.shape[1]] = ref[...]
        start += ref.shape[1]


def pack(shards, deps=()):
    rows = -(-max(m.shape[0] for m in shards) // 16) * 16
    shape = (rows, sum(m.shape[1] for m in shards))
    return call(functools.partial(pack_kernel, len(shards)), [(shape, BF16)], [], 3, *shards, deps=deps)[0]


def settle_kernel(count, parts, plan, scalars_ref, *refs):
    block_refs, refs = refs[:parts], refs[parts:]
    outs = sum(entry[3] for entry in plan)
    out_refs, stack_ref = refs[-outs - 1 : -1], refs[-1]
    ordered = parts == 1
    for j in range(count):
        if ordered:
            held = stack_ref.shape[1]
            stack_ref[j] = block_refs[0][j * held : (j + 1) * held, :]
            continue
        owner = scalars_ref[count + j]
        if j == count - 1 and parts > count:
            cut = block_refs[j].shape[0]
            stack_ref[owner, :cut] = block_refs[j][...]
            stack_ref[owner, cut:] = block_refs[j + 1][...]
        else:
            stack_ref[owner] = block_refs[j][...]
    place = 0
    for first, rows, groups, pieces, width, stride in plan:
        if not groups:
            for a in range(count):
                found = stack_ref[a, :rows, first : first + width]
                out_refs[place][0, a * rows : (a + 1) * rows, :] = found.astype(F32)
        for p in range(pieces):
            for g in range(groups):
                for a in range(count):
                    low = first + (p * groups + g) * stride
                    at = (g * count + a) * width
                    found = stack_ref[a, :rows, low : low + width]
                    out_refs[place + p][0, :, at : at + width] = found.astype(F32)
        place += pieces


def settle(scalars, blocks, plan, layer, layer_count, before):
    count = lax.axis_size("seq")
    shapes = []
    for _, rows, groups, pieces, width, _ in plan:
        shapes += [(rows, groups * count * width) if groups else (count * rows, width)] * pieces
    held = [] if before is None else list(before)
    inputs = [pl.BlockSpec(memory_space=pltpu.VMEM)] * len(blocks)
    inputs += [pl.BlockSpec(memory_space=pl.ANY)] * len(held)
    found = pl.pallas_call(
        functools.partial(settle_kernel, count, len(blocks), plan),
        grid=(1,),
        out_shape=[jax.ShapeDtypeStruct((layer_count,) + shape, F32) for shape in shapes],
        in_specs=[pl.BlockSpec(memory_space=pltpu.SMEM)] + inputs,
        out_specs=[pl.BlockSpec((1,) + shape, lambda i: (layer, 0, 0)) for shape in shapes],
        scratch_shapes=[
            pltpu.VMEM(
                (count, blocks[0].shape[0] // (count if len(blocks) == 1 else 1), blocks[0].shape[1]),
                BF16,
            )
        ],
        input_output_aliases={1 + len(blocks) + i: i for i in range(len(held))},
        compiler_params=pltpu.CompilerParams(vmem_limit_bytes=VMEM_LIMIT),
        cost_estimate=pl.CostEstimate(flops=8_000_000_000, bytes_accessed=1000, transcendentals=0),
    )(scalars, *blocks, *held)
    return list(found)


def plan_of(entries):
    plan, first = [], 0
    for shard, groups, pieces, width in entries:
        rows, columns = shard.shape
        stride = columns // (groups * pieces) if groups else columns
        plan.append((first, rows, groups, pieces, width, stride))
        first += columns
    return tuple(plan)


def finish(scalars, entries, layer, layer_count, before=None, deps=()):
    blocks = gather_parts(pack([entry[0] for entry in entries], deps))
    return settle(scalars, blocks, plan_of(entries), layer, layer_count, before)


def swap_seq(block, bits):
    seq_count = lax.axis_size("seq")
    return lax.ppermute(block, "seq", [(i, i ^ bits) for i in range(seq_count)])


def swap_fsdp(block, bits):
    fsdp_count = lax.axis_size("fsdp")
    return lax.ppermute(block, "fsdp", [(i, i ^ bits) for i in range(fsdp_count)])


def swap_core(block):
    return swap_fsdp(block, 1)


def swap_by_core(block, even_bits, odd_bits):
    seq_count, fsdp_count = lax.axis_size("seq"), lax.axis_size("fsdp")
    pairs = []
    for s in range(seq_count):
        for f in range(fsdp_count):
            other = s ^ (odd_bits if f % 2 else even_bits)
            pairs.append((s * fsdp_count + f, other * fsdp_count + f))
    return lax.ppermute(block, ("seq", "fsdp"), pairs)


def add_bf16(*terms):
    total = terms[0].astype(F32)
    for term in terms[1:]:
        total = total + term.astype(F32)
    return total.astype(BF16)


def scatter_first(pieces):
    seq_count = lax.axis_size("seq")
    if seq_count != 4:
        return [swap_seq(m, j + 1) for j, m in enumerate(pieces)]
    return [swap_seq(pieces[0], 1), swap_seq(pieces[1], 2), pieces[2], pieces[3]]


def scatter_last(own, first, ready=None):
    seq_count = lax.axis_size("seq")
    if seq_count != 4:
        return [own] + first
    from_x, from_y, x_bottom, y_top = first
    if ready is not None:
        from_x, from_y = gate([from_x, from_y], ready)
    cut, rest = y_top.shape[0], x_bottom.shape[0]
    to_y, to_x = add_bf16(y_top, from_x[:cut]), add_bf16(x_bottom, from_y[:rest])
    return [own, from_x, from_y, swap_seq(to_x, 1), swap_seq(to_y, 2)]


def exchange_rel(blocks):
    return [blocks[0]] + [swap_seq(blocks[j], j) for j in range(1, len(blocks))]


def gather_first(block):
    seq_count = lax.axis_size("seq")
    if seq_count != 4:
        return [block] + [swap_seq(block, j) for j in range(1, seq_count)]
    return [block, swap_seq(block, 1), swap_seq(block, 2)]


def gather_last(first, ready=None):
    seq_count = lax.axis_size("seq")
    if seq_count != 4:
        return first
    block, from_x, from_y = first
    if ready is not None:
        from_x, from_y = gate([from_x, from_y], ready)
    cut = cut_of(block.shape[0])
    return [block, from_x, from_y, swap_seq(from_y[:cut], 1), swap_seq(from_x[cut:], 2)]


def gather_parts(block):
    return gather_last(gather_first(block))


def list_order():
    s, seq_count = lax.axis_index("seq"), lax.axis_size("seq")
    if seq_count != 4:
        return [s ^ j for j in range(seq_count)]
    odd = lax.axis_index("fsdp") % 2
    return [s, s ^ (1 + odd), s ^ (2 - odd), s ^ 3]


def spread_first(block):
    seq_count = lax.axis_size("seq")
    if seq_count != 4:
        return [block] + [swap_seq(block, j) for j in range(1, seq_count)]
    return [block, swap_by_core(block, 1, 2)]


def spread_slice(blocks, ready):
    if lax.axis_size("seq") != 4:
        return blocks
    block, first = blocks
    if ready is not None:
        (first,) = gate([first], ready)
    half = block.shape[0] // 2
    odd = lax.axis_index("fsdp") % 2
    return [block, first, lax.dynamic_slice_in_dim(first, odd * half, half, 0)]


def spread_last(blocks, part_ready):
    seq_count = lax.axis_size("seq")
    if seq_count != 4:
        return blocks
    block, first, part = blocks
    part = swap_by_core(part, 2, 1)
    other = swap_core(first)
    if part_ready is not None:
        (part,) = gate([part], part_ready)
    return [block, first, other, part, swap_core(part)]


def own_part(matrix, groups, padded):
    s, seq_count = lax.axis_index("seq"), lax.axis_size("seq")
    width = matrix.shape[1] // (groups * seq_count)
    parts = [
        jnp.pad(
            lax.dynamic_slice_in_dim(matrix, (g * seq_count + s) * width, width, 1),
            ((0, 0), (0, padded - width)),
        )
        for g in range(groups)
    ]
    return jnp.concatenate(parts, axis=1)


def gather_fsdp(shard):
    return lax.all_gather(shard, "fsdp", axis=0, tiled=True)


def scatter_fsdp(full):
    return lax.psum_scatter(full.astype(BF16), "fsdp", scatter_dimension=0, tiled=True)


def layer_forward(parts, hidden, scalars, gains, shift, pairs, weights, normed, deps, hold=None):
    lead_part, square_parts, up_part = weights
    seq_count = lax.axis_size("seq")
    tok_rows, model_width = hidden.shape
    head_size, width = model_width // H, model_width // seq_count
    first_all, triples, mixed = self_forward(
        parts,
        lead_part,
        gains,
        shift,
        head_size,
        seq_count,
        width,
        normed,
        (square_parts[-1],) + deps,
    )
    mixed_rel = exchange_rel(mixed)
    square_parts = spread_last(square_parts, mixed_rel[1:])
    held = []
    if hold is not None:
        held = gate([hold], [square_parts[-1]])
    self_tokens, after_self, cross_norm, queries, cross_tokens, after_cross, mlp_norm = (
        middle_forward(
            int(normed), scalars, mixed_rel, square_parts, pairs, hidden, gains, head_size, held
        )
    )
    mlp_parts = gather_parts(mlp_norm)
    mlp_all, up_rows, activated = mlp_up(mlp_parts, up_part, seq_count)
    saved = (
        first_all,
        triples,
        self_tokens,
        after_self,
        cross_norm,
        queries,
        cross_tokens,
        after_cross,
        mlp_all,
        up_rows,
        activated,
    )
    return (saved, square_parts, mlp_parts, held)


def unspread_first(blocks, ready):
    own, first_mine, first_other, second_mine, second_other, corner_mine, corner_other = blocks
    from_corner, to_other = swap_core(corner_other), swap_core(second_mine)
    to_mine = swap_core(second_other)
    sums = [add_bf16(corner_mine, from_corner), add_bf16(first_other, to_other)]
    sums = gate(sums, ready)
    hops = [swap_by_core(sums[0], 2, 1), swap_by_core(sums[1], 1, 2)]
    return own, hops, [first_mine, to_mine], sums


def unspread_next(first, ready):
    own, hops, terms, _ = first
    passed, other = gate(hops, ready)
    return own, swap_by_core(add_bf16(*terms, passed), 1, 2), other


def unspread_last(scalars, second, ready):
    own, mine, other = second
    (mine,) = gate([mine], ready)
    return join_halves(scalars, own, mine, other)


def unspread_any(blocks):
    return add_bf16(blocks[0], *[swap_seq(m, j + 1) for j, m in enumerate(blocks[1:])])


def sum_shard(scalars, shard, groups, ready=None):
    if ready is not None:
        (shard,) = gate([shard], ready)
    own, pieces = fold(scalars, shard, groups)
    return sum_terms(scatter_last(own, scatter_first(pieces)))


def qkv_own(layer, qkv):
    return own_part(qkv[layer], 3, padded_width(qkv.shape[2] // (3 * lax.axis_size("seq"))))


def squares_own(layer, *stacks):
    padded = padded_width(stacks[0].shape[2] // lax.axis_size("seq"))
    return jnp.concatenate([own_part(m[layer], 1, padded) for m in stacks], axis=1)


def gather_rest(layer, up, down):
    s, seq_count, fsdp_count = lax.axis_index("seq"), lax.axis_size("seq"), lax.axis_size("fsdp")
    rows = down.shape[1] // seq_count
    return (
        gather_fsdp(own_part(up[layer], fsdp_count, up.shape[2] // (fsdp_count * seq_count))),
        gather_fsdp(lax.dynamic_slice_in_dim(down[layer], s * rows, rows, 0)),
    )


def sum_vectors(vectors):
    bits = 1
    while bits < lax.axis_size("seq"):
        vectors = vectors + swap_seq(vectors, bits)
        bits *= 2
    found, bits = vectors[None], 1
    while bits < lax.axis_size("fsdp"):
        found = jnp.concatenate([found, swap_fsdp(found, bits)], axis=0)
        bits *= 2
    return found


def body(
    latents,
    skip_input,
    text_tokens,
    text_lengths,
    condition,
    cotangent,
    mod_weight,
    norm_gains,
    qkv_weight,
    query_weight,
    text_kv_weight,
    self_out_weight,
    cross_out_weight,
    up_weight,
    down_weight,
    skip_gain,
    skip_weight,
):
    seq_count, fsdp_count = lax.axis_size("seq"), lax.axis_size("fsdp")
    s, f = lax.axis_index("seq"), lax.axis_index("fsdp")
    _, tok_rows, model_width = latents.shape
    width = model_width // seq_count
    shard_rows = mod_weight.shape[1]
    text_count = text_tokens.shape[1]
    padded = -(-text_count // 32) * 32
    text_rows = jnp.pad(text_tokens[0], ((0, padded - text_count), (0, 0)))
    scalars = jnp.stack(
        [*list_order(), *[s ^ j for j in range(seq_count)], f % 2, text_lengths[0]]
    ).astype(jnp.int32)

    gain_rows = jnp.concatenate(
        [norm_gains.reshape(-1, shard_rows), skip_gain.reshape(-1, shard_rows)], axis=0
    )
    small = jnp.concatenate(
        [
            condition.reshape(fsdp_count, 1, shard_rows),
            jnp.broadcast_to(gain_rows[None], (fsdp_count,) + gain_rows.shape),
        ],
        axis=1,
    ).astype(F32)
    latent_parts = gather_parts(latents[0])
    (small,) = gate([small], latent_parts[-2:])
    small = lax.all_to_all(small, "fsdp", 0, 0, tiled=True)
    cond_part = small[:, 0]
    gains = jnp.swapaxes(small[:, 1:7], 0, 1).reshape(2, 3, model_width)
    skip_gains = small[:, 7:].reshape(2, model_width)
    silu_part = jax.nn.silu(cond_part)
    shift_terms = jnp.einsum("br,lrd->bld", silu_part, mod_weight.astype(F32), precision=EXACT)
    padded_columns = padded_width(width)
    kv_both = gather_fsdp(
        jnp.concatenate([own_part(text_kv_weight[l], 2, padded_columns) for l in range(2)], axis=1)
    )
    pair_hops = gather_first(dot_nn(text_rows, kv_both).astype(BF16))
    pairs_all = gather_last(pair_hops)
    (shift_terms,) = gate([shift_terms], pair_hops[1:])
    shifts = jnp.sum(lax.all_to_all(shift_terms, "fsdp", 0, 0, tiled=True), axis=0)

    square_stacks = (self_out_weight, query_weight, cross_out_weight)
    rest_stacks = (up_weight, down_weight)
    head_size = model_width // H

    square_shard, qkv_shard = gate(
        [squares_own(0, *square_stacks), qkv_own(0, qkv_weight)], [kv_both] + latent_parts[-2:]
    )
    square_first, lead_first = gather_fsdp(square_shard), gather_fsdp(qkv_shard)
    up_first, down_first = gather_rest(0, *rest_stacks)
    spread_squares = spread_slice(spread_first(gate([square_first], pair_hops[1:])[0]), [shifts])
    (lead_first,) = gate([lead_first], [shifts])
    pairs_first, pairs_second = pairs_all, pairs_all
    saved_first, squares_first, mlp_parts, _ = layer_forward(
        latent_parts,
        latents[0],
        scalars,
        gains[0],
        shifts[0],
        pairs_first,
        (lead_first, spread_squares, up_first),
        False,
        (),
    )
    own, pieces = mlp_down(saved_first[10], down_first, seq_count)
    first = scatter_first(pieces)
    terms = scatter_last(own, first)

    skip_matrix = gather_fsdp(skip_weight)
    square_second = gather_fsdp(gate([squares_own(1, *square_stacks)], mlp_parts[-2:])[0])
    lead_second = gather_fsdp(qkv_own(1, qkv_weight))
    (square_second,) = gate([square_second], first[:2])
    squares_second = spread_first(square_second)
    first_out, joined_norm, skip_out, second_norm = skip_forward(
        skip_matrix,
        terms,
        saved_first[7],
        skip_input[0],
        skip_gains,
        gains[1],
        shifts[1],
        (square_second,),
    )

    up_second, down_second = gather_rest(1, *rest_stacks)
    out_hops = gather_first(gate([cotangent[0]], [skip_out])[0])
    second_parts = gather_parts(second_norm)
    squares_second = spread_slice(squares_second, second_parts[1:3])
    saved_second, squares_second, mlp_parts, _ = layer_forward(
        second_parts,
        skip_out,
        scalars,
        gains[1],
        shifts[1],
        pairs_second,
        (lead_second, squares_second, up_second),
        True,
        (),
    )
    out_parts = gather_last(out_hops, [squares_second[-1]])
    out_all = stack_rows(out_parts, (mlp_parts[1],))

    held = {}

    def block_backward(rows, grad_out, saved, block, weights, early, hooks):
        lead_matrix, square_parts, pairs, up_part, down_part = weights
        grad_down = dot_tn(saved[10], early).astype(BF16) if early is not None else None
        found_all, grad_up_rows, own, pieces = mlp_backward(
            rows,
            saved[9],
            up_part,
            down_part,
            seq_count,
            hooks[0] + ((grad_down,) if early is not None else ()),
        )
        first = scatter_first(gate(pieces, hooks[3]) if hooks[3] else pieces)
        terms = scatter_last(own, first)
        held["hops"] = first[:2]
        if early is None:
            grad_down = dot_tn(saved[10], found_all).astype(BF16)
            (grad_down,) = gate([grad_down], first[:2])
        grad_up = dot_tn(saved[8], grad_up_rows).astype(BF16)
        (grad_up,) = gate([grad_up], first[:2])
        down_shard, up_shard = scatter_fsdp(grad_down), scatter_fsdp(grad_up)
        (
            grad_after_self,
            self_branch,
            query_branch,
            cross_branch,
            gain_grads,
            mixed_grads,
            own_pairs,
            pair_blocks,
        ) = middle_backward(
            block,
            scalars,
            square_parts,
            pairs,
            terms,
            grad_out,
            saved[7],
            saved[3],
            saved[5],
            gains[block],
            head_size,
            (grad_down, grad_up) + hooks[1](grad_up_rows, terms),
        )
        mixed_rel = exchange_rel(mixed_grads)
        pair_blocks = gate(pair_blocks, mixed_rel[1:])
        pair_terms = [swap_seq(m, j + 1) for j, m in enumerate(pair_blocks)]
        grad_triples, own, pieces = self_backward(
            saved[1],
            mixed_rel,
            lead_matrix,
            head_size,
            (down_shard,) + hooks[2](mixed_rel[1]),
        )
        pair_terms = gate(pair_terms, [grad_triples])
        first = scatter_first(gate(pieces, pair_terms))
        terms = scatter_last(own, first)
        grad_qkv = dot_tn(saved[0], grad_triples).astype(BF16)
        (grad_qkv,) = gate([grad_qkv], first[:2])
        held["last"] = first[:2]
        squares = spread_outer(
            scalars,
            [saved[2], saved[4], saved[6]],
            [self_branch, query_branch, cross_branch],
            (grad_triples,),
        )
        held["outer"] = squares[0]
        squares = gate(squares, first[:2])
        pair_terms = gate(pair_terms, first[:2])
        grad_pairs = add_bf16(own_pairs, *pair_terms)
        kv_part = kv_both[:, 2 * block * padded_columns : 2 * (block + 1) * padded_columns]
        grad_text = dot_nt(grad_pairs, kv_part)
        kv_shard = scatter_fsdp(dot_tn(text_rows, grad_pairs))
        return (
            terms,
            grad_after_self,
            gain_grads,
            grad_text,
            squares,
            grad_qkv,
            grad_triples,
            (scatter_fsdp(grad_qkv), kv_shard, up_shard, down_shard),
        )

    def second_own(grad_up_rows, terms):
        own, pieces = mlp_down(saved_second[10], down_second, seq_count, (grad_up_rows,))
        pieces = gate(pieces, terms[-2:])
        held["own"], held["own_hops"] = own, scatter_first(pieces)
        return tuple(pieces)

    def second_sum(ready):
        held["ready"] = ready
        return tuple(held["own_hops"][:2])

    (
        terms,
        grad_after_self,
        gain_grads,
        text_second,
        squares,
        grad_qkv,
        grad_triples,
        (qkv_shard, kv_shard, up_shard, down_shard),
    ) = block_backward(
        [out_all],
        cotangent[0],
        saved_second,
        1,
        (lead_second, squares_second, pairs_second, up_second, down_second),
        out_all,
        ((), second_own, second_sum, ()),
    )
    skip_branch, grad_first_out, grad_skip, vectors, first_round = skip_backward(
        skip_matrix,
        terms,
        skip_out,
        gains[1],
        grad_after_self,
        first_out,
        skip_input[0],
        skip_gains,
        (grad_qkv, up_shard, held["outer"]),
    )
    vectors_second = jnp.concatenate([vectors[:2], gain_grads, vectors[2:]], axis=0)
    first_hops = gather_first(first_round)
    first_parts = gather_last(first_hops)
    fours = seq_count == 4
    if fours:
        squares = unspread_first(squares, first_parts[-2:])
    own_terms = scatter_last(held["own"], held["own_hops"], terms[-2:])
    output = close_forward(own_terms, saved_second[7])
    skip_outer = outer([joined_norm], [skip_branch], tuple(first_hops[1:]))
    skip_shard = scatter_fsdp(skip_outer)

    def entries(layer):
        qkv, square, kv, up, down = layer
        return (
            [
                (up, fsdp_count, 1, up.shape[1] // fsdp_count),
                (down, 0, 1, down.shape[1]),
            ],
            [(qkv, 3, 1, width), (square, 1, 3, width), (kv, 2, 1, width)],
        )

    early, _ = entries((qkv_shard, qkv_shard, kv_shard, up_shard, down_shard))
    def first_middle(grad_up_rows, terms):
        del grad_up_rows, terms
        return (kv_shard,)

    def first_self(ready):
        del ready
        return (qkv_shard,)

    (
        terms,
        grad_after_self,
        gain_grads,
        text_first,
        first_squares,
        grad_qkv,
        grad_triples,
        (first_qkv_shard, first_kv_shard, first_up_shard, first_down_shard),
    ) = block_backward(
        first_parts,
        grad_first_out,
        saved_first,
        0,
        (lead_first, squares_first, pairs_first, up_first, down_first),
        None,
        (
            (skip_outer,) + (tuple(squares[3]) if fours else ()),
            first_middle,
            first_self,
            squares[1] if fours else (),
        ),
    )
    early_hops = gather_first(pack([entry[0] for entry in early], held["last"]))
    if fours:
        joined = unspread_last(scalars, unspread_next(squares, held["last"]), terms[-2:])
        first_squares = unspread_next(unspread_first(first_squares, terms[3:4]), terms[-2:])
        first_joined = unspread_last(scalars, first_squares, terms[-2:])
    else:
        joined, first_joined = unspread_any(squares), unspread_any(first_squares)
    square_sum = scatter_fsdp(joined)
    skip_sum = sum_shard(scalars, skip_shard, 1, held["last"])
    early, _ = entries(
        (first_qkv_shard, first_qkv_shard, first_kv_shard, first_up_shard, first_down_shard)
    )
    first_hops = gather_first(pack([entry[0] for entry in early], terms[-2:]))
    grad_latents, vectors = open_backward(
        terms, latents[0], gains[0], grad_after_self, (grad_qkv,)
    )
    vectors_first = jnp.concatenate([vectors, gain_grads], axis=0)
    first_layer = (
        first_qkv_shard,
        scatter_fsdp(first_joined),
        first_kv_shard,
        first_up_shard,
        first_down_shard,
    )

    early_done = settle(
        scalars,
        gather_last(early_hops),
        plan_of(early),
        1,
        2,
        None,
    )
    _, late = entries((qkv_shard, square_sum, kv_shard, up_shard, down_shard))
    late_done = finish(scalars, late, 1, 2, None)
    early, late = entries(first_layer)
    grad_up, grad_down = settle(
        scalars, gather_last(first_hops), plan_of(early), 0, 2, early_done
    )
    grad_qkv, grad_self_out, grad_query, grad_cross_out, grad_kv = finish(
        scalars, late, 0, 2, late_done
    )
    (grad_skip_weight,) = finish(scalars, [(skip_sum, 1, 1, width)], 0, 1)

    sums = sum_vectors(jnp.concatenate([vectors_first, vectors_second], axis=0))
    first_sums, second_sums = sums[:, :4], sums[:, 4:]
    shift_grads = jnp.stack([first_sums[:, 0], second_sums[:, 0]], axis=1)
    gain_sums = jnp.stack([first_sums[:, 1:4].sum(axis=0), second_sums[:, 1:4].sum(axis=0)])
    grad_norm_gains = lax.dynamic_slice_in_dim(gain_sums, f * shard_rows, shard_rows, 2)
    grad_skip_gain = lax.dynamic_slice_in_dim(
        second_sums[:, 4:].sum(axis=0).reshape(-1), f * skip_gain.shape[0], skip_gain.shape[0], 0
    )
    turned = jnp.stack(
        [lax.dynamic_index_in_dim(silu_part, f ^ j, 0, False) for j in range(fsdp_count)]
    )
    grad_mod = jnp.einsum("br,bld->lrd", turned, shift_grads, precision=EXACT)
    grad_silu = jnp.einsum("bld,lrd->br", shift_grads, mod_weight.astype(F32), precision=EXACT)
    grad_silu = jnp.stack(
        [lax.dynamic_index_in_dim(grad_silu, f ^ j, 0, False) for j in range(fsdp_count)]
    )
    _, silu_pull = jax.vjp(jax.nn.silu, cond_part)
    grad_cond_part = silu_pull(grad_silu)[0]
    grad_condition = lax.all_to_all(grad_cond_part, "fsdp", 0, 0, tiled=True).reshape(1, -1)

    text_sum, bits = text_first + text_second, 1
    while bits < seq_count:
        text_sum = text_sum + swap_seq(text_sum.astype(BF16), bits).astype(F32)
        bits *= 2
    return (
        output[None],
        grad_latents[None],
        grad_skip[None],
        text_sum[None, :text_count],
        grad_condition,
        grad_mod,
        grad_norm_gains,
        grad_qkv,
        grad_query,
        grad_kv,
        grad_self_out,
        grad_cross_out,
        grad_up,
        grad_down,
        grad_skip_gain,
        grad_skip_weight[0],
    )


def solution(mesh):
    in_specs = (
        P("fsdp", "seq", None),
        P("fsdp", "seq", None),
        P("fsdp", None, None),
        P("fsdp"),
        P("fsdp", None),
        P("fsdp", "seq", None),
        P(None, "fsdp", None),
        P(None, None, "fsdp"),
        P(None, "fsdp", None),
        P(None, "fsdp", None),
        P(None, "fsdp", None),
        P(None, "fsdp", None),
        P(None, "fsdp", None),
        P(None, "fsdp", None),
        P(None, "fsdp", None),
        P("fsdp"),
        P("fsdp", None),
    )
    out_specs = (
        P("fsdp", "seq", None),
        P("fsdp", "seq", None),
        P("fsdp", "seq", None),
        P("fsdp", None, None),
        P("fsdp", None),
        P(None, "fsdp", None),
        P(None, None, "fsdp"),
        P(None, "fsdp", None),
        P(None, "fsdp", None),
        P(None, "fsdp", None),
        P(None, "fsdp", None),
        P(None, "fsdp", None),
        P(None, "fsdp", None),
        P(None, "fsdp", None),
        P("fsdp"),
        P("fsdp", None),
    )
    return jax.shard_map(body, mesh=mesh, in_specs=in_specs, out_specs=out_specs, check_vma=False)
```
